128 devices in a mesh: section: 4 (over x), lat: 32 (over z, y, core).
Axes of the slice: x: 4, y: 4, z: 4, core: 2. Of those that a mesh axis runs over, the one named last changes fastest.
Arguments:
- saved_input: bfloat16 [4, 384, 192, 768], P('section', 'lat'), may hold values from -6 to 6
- incoming: bfloat16 [4, 384, 192, 768], P('section', 'lat'), may hold values from -6 to 6
- spectral_gain: float32 [4, 384, 192], P('section'), may hold values from 0.5 to 2
- mix_weight: bfloat16 [4, 2, 192, 192], P('section'), may hold values from -0.3125 to 0.3125
- proj_weight: bfloat16 [4, 192, 192], P('section'), may hold values from -0.4375 to 0.4375
Outputs:
- received: bfloat16 [4, 384, 192, 768], P('section', 'lat')
- grad_w2: float32 [4, 192, 192], P('section')
- grad_mix: float32 [4, 2, 192, 192], P('section')
- grad_gain: float32 [4, 384, 192], P('section')
The draws below stay inside these ranges and needn't reach their ends.
All inputs are finite; a program needn't handle non-finite values.
Results may differ from the reference program's by a relative error of at most 0.025.
Values may be sent and summed in bfloat16 or wider, within the bound.
No kernel may reach another device: no remote copies, remote signals or barrier semaphores. Data moves between devices by JAX's collectives and lax.ppermute only.
A program may use at most 192 MiB of HBM per device.

```python
import math
import jax
import jax.numpy as jnp
from jax import lax

C = 192
NLAT = 384
NLON = 768
MODES = 384
SECTIONS = 4
N_SECTION = 4


def block_levels(stream_key, shape, split, low, high):
    factor_of, own = 1.0, jax.random.fold_in(stream_key, 6)
    for axis_at, blocks in split:
        steps = jnp.exp(jax.random.uniform(jax.random.fold_in(own, axis_at), (blocks,), jnp.float32, low / len(split), high / len(split)))
        factor_of = factor_of * jnp.repeat(steps, shape[axis_at] // blocks).reshape([-1 if axis == axis_at else 1 for axis in range(len(shape))])
    return factor_of


def normal_values(rng, extent, deviation, limit, shards=(), kind=jnp.bfloat16):
    array = deviation * jax.random.normal(rng, extent, jnp.float32)
    if shards:
        array = array * block_levels(rng, extent, shards, -0.22, 0.18)
    return jnp.clip(array, -limit, limit).astype(kind)


def setup_inputs(seed: int = 0) -> dict:
    seeds = jax.random.split(jax.random.key(seed), 6)
    saved_input = normal_values(seeds[0], (SECTIONS, NLAT, C, NLON), 1.0, 6.0, ((0, 4), (1, 32)))
    incoming = normal_values(seeds[1], (SECTIONS, NLAT, C, NLON), 1.0, 6.0, ((0, 4), (1, 32)))
    spectral_gain = jnp.clip(jnp.exp(math.log(2.0) - 1.3862944 * jax.random.uniform(seeds[2], (SECTIONS, MODES, C), jnp.float32) ** block_levels(seeds[2], (SECTIONS, MODES, C), ((0, 4),), -0.2, 0.2)), 0.5, 2.0)
    mix_weight = normal_values(seeds[3], (SECTIONS, 2, C, C), (2 * C) ** -0.5, 0.3125, ((0, 4),))
    proj_weight = normal_values(seeds[4], (SECTIONS, C, C), C ** -0.5, 0.4375, ((0, 4),))
    return {"saved_input": saved_input, "incoming": incoming, "spectral_gain": spectral_gain, "mix_weight": mix_weight, "proj_weight": proj_weight}


log_gamma_half = 0.5723649429247001

def quadrature(colatitude):
    harmonic = jnp.arange(1, NLAT // 2 + 1, dtype=jnp.float32)
    terms = jnp.cos(2.0 * harmonic[None, :] * colatitude[:, None]) / (4.0 * harmonic * harmonic - 1.0)[None, :]
    return 2.0 / NLAT * (1.0 - 2.0 * lax.optimization_barrier(jnp.sum(terms, axis=1)))

def legendre_table(orders, cos_lat, sin_lat, degrees):
    order_col = orders[:, None]
    cosine = cos_lat[None, :]
    log_start = 0.5 * jnp.log((2.0 * order_col + 1.0) / 2.0) + 0.5 * (jax.scipy.special.gammaln(order_col + 0.5) - log_gamma_half - jax.scipy.special.gammaln(order_col + 1.0)) + order_col * jnp.log(sin_lat)[None, :]
    zero_state = jnp.zeros(log_start.shape, jnp.float32)

    def block_step(state_in, block_index):
        previous, current, log_scale = state_in
        row_list = []
        for inner_step in range(16):
            degree = (block_index * 16 + inner_step).astype(jnp.float32)
            factor_up = jnp.sqrt(jnp.maximum(4.0 * degree * degree - 1.0, 1.0) / jnp.maximum(degree * degree - order_col * order_col, 1.0))
            lower_degree = degree - 1.0
            factor_down = jnp.sqrt(jnp.maximum(lower_degree * lower_degree - order_col * order_col, 0.0) / jnp.maximum(4.0 * lower_degree * lower_degree - 1.0, 1.0))
            general = factor_up * (cosine * current - factor_down * previous)
            second = jnp.sqrt(2.0 * order_col + 3.0) * cosine * current
            new_row = jnp.where(degree == order_col, 1.0, jnp.where(degree == order_col + 1.0, second, jnp.where(degree > order_col + 1.0, general, 0.0)))
            row_list.append(new_row * jnp.exp(log_scale))
            previous, current = (current, new_row)
        largest = jnp.maximum(jnp.abs(previous), jnp.abs(current))
        largest = jnp.where(largest > 0.0, largest, 1.0)
        return ((previous / largest, current / largest, log_scale + jnp.log(largest)), jnp.stack(row_list))
    _, blocks = lax.scan(block_step, (zero_state, zero_state, log_start), jnp.arange(degrees // 16, dtype=jnp.int32))
    stacked = blocks.reshape(degrees, orders.shape[0], cos_lat.shape[0])
    return jnp.transpose(stacked, (1, 0, 2))

def fourier_tables(orders):
    longitude = jnp.arange(NLON, dtype=jnp.int32)
    phase_index = longitude[:, None] * orders[None, :] % NLON
    angle_table = phase_index.astype(jnp.float32) * (2.0 * math.pi / NLON)
    cosine_table = jnp.cos(angle_table)
    sine_table = jnp.sin(angle_table)
    forward_table = jnp.stack([cosine_table, -sine_table]).astype(jnp.bfloat16)
    factor = jnp.where(orders == 0, 1.0, 2.0).astype(jnp.float32) / NLON
    inverse_table = jnp.stack([factor[:, None] * cosine_table.T, -factor[:, None] * sine_table.T]).astype(jnp.bfloat16)
    return (forward_table, inverse_table)

def gelu_slope(pre_act):
    return 0.5 * (1.0 + jax.scipy.special.erf(pre_act * (1.0 / math.sqrt(2.0)))) + pre_act * jnp.exp(-0.5 * pre_act * pre_act) * (1.0 / math.sqrt(2.0 * math.pi))

def reference(saved_input, incoming, spectral_gain, mix_weight, proj_weight):
    colatitude = (jnp.arange(NLAT, dtype=jnp.float32) + 0.5) * (math.pi / NLAT)
    quad_weight = quadrature(colatitude)
    orders = jnp.arange(MODES, dtype=jnp.int32)
    forward_table, inverse_table = fourier_tables(orders)
    legendre = legendre_table(orders.astype(jnp.float32), jnp.cos(colatitude), jnp.sin(colatitude), MODES)
    analysis_table = (quad_weight[None, None, :] * legendre).astype(jnp.bfloat16).astype(jnp.float32)
    synthesis_table = legendre.astype(jnp.bfloat16).astype(jnp.float32)
    forward_wide = forward_table.astype(jnp.float32)
    inverse_wide = inverse_table.astype(jnp.float32)
    grid_scale = 1.0 / math.sqrt(NLAT * NLON)
    mode_scale = 1.0 / math.sqrt(MODES)
    input_grads = []
    proj_grads = []
    mix_grads = []
    gain_grads = []
    for section_index in range(N_SECTION):
        grid_field = saved_input[section_index].astype(jnp.float32)
        upstream = incoming[section_index]
        spectrum = jnp.einsum('jck,pkm->mjpc', grid_field, forward_wide).astype(jnp.bfloat16)
        spectrum = spectrum.reshape(MODES, NLAT, 2 * C)
        coefficients = jnp.einsum('mlj,mjc->mlc', analysis_table, spectrum.astype(jnp.float32))
        gain_pair = jnp.concatenate([spectral_gain[section_index], spectral_gain[section_index]], axis=1)
        scaled = (gain_pair[None, :, :] * coefficients).astype(jnp.bfloat16)
        real_part = mix_weight[section_index, 0]
        imag_part = mix_weight[section_index, 1]
        block_weight = jnp.concatenate([jnp.concatenate([real_part, imag_part], axis=1), jnp.concatenate([-imag_part, real_part], axis=1)], axis=0)
        scaled_rows = scaled.reshape(MODES * MODES, 2 * C)
        mixed_modes = jnp.dot(scaled_rows, block_weight, preferred_element_type=jnp.float32).astype(jnp.bfloat16)
        mixed_modes = mixed_modes.reshape(MODES, MODES, 2 * C)
        grid_modes = jnp.einsum('mlj,mlc->mjc', synthesis_table, mixed_modes.astype(jnp.float32)).astype(jnp.bfloat16)
        pre_act = jnp.einsum('mjpc,pmk->jck', grid_modes.reshape(MODES, NLAT, 2, C).astype(jnp.float32), inverse_wide)
        activated = jax.nn.gelu(pre_act, approximate=False).astype(jnp.bfloat16)
        grad_act = jnp.einsum('cd,jdk->jck', proj_weight[section_index].astype(jnp.float32), upstream.astype(jnp.float32))
        proj_grads.append(grid_scale * jnp.einsum('jck,jdk->cd', activated.astype(jnp.float32), upstream.astype(jnp.float32)))
        grad_pre = (grad_act * gelu_slope(pre_act)).astype(jnp.bfloat16)
        grad_modes = jnp.einsum('jck,pmk->mjpc', grad_pre.astype(jnp.float32), inverse_wide).astype(jnp.bfloat16)
        grad_modes = grad_modes.reshape(MODES, NLAT, 2 * C)
        grad_mixed = jnp.einsum('mlj,mjc->mlc', synthesis_table, grad_modes.astype(jnp.float32)).astype(jnp.bfloat16)
        grad_rows = grad_mixed.reshape(MODES * MODES, 2 * C)
        grad_scaled = jnp.dot(grad_rows, block_weight.T, preferred_element_type=jnp.float32).reshape(MODES, MODES, 2 * C)
        block_grad = jnp.dot(scaled_rows.T, grad_rows, preferred_element_type=jnp.float32)
        grad_real = block_grad[:C, :C] + block_grad[C:, C:]
        grad_imag = block_grad[:C, C:] - block_grad[C:, :C]
        mix_grads.append(grid_scale * jnp.stack([grad_real, grad_imag]))
        gain_sum = lax.optimization_barrier(jnp.sum(grad_scaled * coefficients, axis=0))
        gain_grads.append(mode_scale * (gain_sum[:, :C] + gain_sum[:, C:]))
        grad_coeffs = (gain_pair[None, :, :] * grad_scaled).astype(jnp.bfloat16)
        grad_spectrum = jnp.einsum('mlj,mlc->mjc', analysis_table, grad_coeffs.astype(jnp.float32)).astype(jnp.bfloat16)
        grad_input = upstream.astype(jnp.float32) + jnp.einsum('mjpc,pkm->jck', grad_spectrum.reshape(MODES, NLAT, 2, C).astype(jnp.float32), forward_wide)
        input_grads.append(grad_input.astype(jnp.bfloat16))
    received = jnp.stack([input_grads[(section_index + 1) % N_SECTION] for section_index in range(N_SECTION)])
    return (received, jnp.stack(proj_grads), jnp.stack(mix_grads), jnp.stack(gain_grads))
```

```python
import functools
import math

import jax
import jax.numpy as jnp
import ml_dtypes
import numpy as np
from jax import lax
from jax.experimental import pallas as pl
from jax.experimental.pallas import tpu as pltpu
from jax.sharding import PartitionSpec as P

NLAT = 384
NLON = 768
MODES = 384
C = 192
DEVICES = 32
LAT_LOCAL = 12
ORDERS = 12
GROUPS = 3
GROUP_ORDERS = 4
HALF = 64
LANES = 128
TILE = 16
TILES = 9
GROUP_TILES = 3
SPAN = DEVICES * TILE
VMEM_LIMIT = 56 * 1024 * 1024
F32 = jnp.float32
BF16 = jnp.bfloat16
NT = (((1,), (1,)), ((), ()))

PAIRS = ((0, 0), (1, 0), (1, 1), (2, 1), (2, 2), (3, 2))


def degrees_of(group):
    return MODES - LANES * group


def params(**extra):
    return pltpu.CompilerParams(vmem_limit_bytes=VMEM_LIMIT, **extra)


def cost(flops, bytes_accessed, transcendentals=0):
    return pl.CostEstimate(
        flops=int(flops), bytes_accessed=int(bytes_accessed), transcendentals=int(transcendentals)
    )


def dot(left, right):
    return jnp.dot(left, right, preferred_element_type=F32)


def dot_nt(left, right):
    return lax.dot_general(left, right, NT, preferred_element_type=F32)


def order_rows(group):
    device = np.arange(DEVICES)[:, None]
    local = np.arange(GROUP_ORDERS)[None, :] + GROUP_ORDERS * group
    return (DEVICES * local + device).reshape(-1)


def fourier_rows(orders):
    phase = (orders[:, None] * np.arange(NLON)[None, :]) % NLON
    angle = phase * (2.0 * math.pi / NLON)
    return np.cos(angle), -np.sin(angle)


def forward_groups():
    tables = []
    for group in range(GROUPS):
        cosine, sine = fourier_rows(order_rows(group))
        tables.append(np.concatenate([cosine, sine], axis=0))
    return np.stack(tables).astype(np.float32).astype(ml_dtypes.bfloat16)


def inverse_rows():
    device = np.arange(DEVICES)[:, None]
    orders = (DEVICES * np.arange(ORDERS)[None, :] + device).reshape(-1)
    factor = np.where(orders == 0, 1.0, 2.0)[:, None] / NLON
    cosine, sine = fourier_rows(orders)
    table = np.concatenate([factor * cosine, factor * sine], axis=0)
    return table.astype(np.float32).astype(ml_dtypes.bfloat16)


def spread_tables():
    rows = np.arange(SPAN)
    source, inner = rows // TILE, rows % TILE
    tables = np.zeros((len(PAIRS), SPAN, NLAT), np.float32)
    for index, (order, tile) in enumerate(PAIRS):
        lat = TILE * tile + inner - LAT_LOCAL * order
        valid = (lat >= 0) & (lat < LAT_LOCAL)
        tables[index, rows[valid], (source * LAT_LOCAL + lat)[valid]] = 1.0
    return tables.astype(ml_dtypes.bfloat16)


def log_starts():
    table = np.zeros((DEVICES, TILE, LANES), np.float32)
    numbers = np.zeros((DEVICES, TILE, LANES), np.float32)
    for device in range(DEVICES):
        for local in range(ORDERS):
            order = DEVICES * local + device
            numbers[device, local] = order
            table[device, local] = 0.5 * math.log((2.0 * order + 1.0) / 2.0) + 0.5 * (
                math.lgamma(order + 0.5) - math.lgamma(0.5) - math.lgamma(order + 1.0)
            )
    return table, numbers


def latitude_rows():
    colatitude = (np.arange(NLAT) + 0.5) * (math.pi / NLAT)
    harmonic = np.arange(1, NLAT // 2 + 1)
    terms = np.cos(2.0 * harmonic[None, :] * colatitude[:, None]) / (4.0 * harmonic**2 - 1.0)
    weight = 2.0 / NLAT * (1.0 - 2.0 * np.sum(terms, axis=1))
    rows = np.stack([np.cos(colatitude), np.log(np.sin(colatitude)), weight])
    return np.concatenate([rows, np.zeros((5, NLAT))]).astype(np.float32)


def legendre_kernel(start_ref, order_ref, lat_ref, out_ref):
    order = jnp.concatenate([order_ref[...]] * 3, axis=1)
    cosine = jnp.broadcast_to(lat_ref[0:1, :], (TILE, NLAT))
    log_sin = jnp.broadcast_to(lat_ref[1:2, :], (TILE, NLAT))
    log_start = jnp.concatenate([start_ref[...]] * 3, axis=1) + order * log_sin
    narrow = order_ref[...]
    narrow_square = narrow * narrow
    second_factor = jnp.concatenate([jnp.sqrt(2.0 * narrow + 3.0)] * 3, axis=1)
    zeros = jnp.zeros((TILE, NLAT), F32)

    def block(index, state):
        previous, current, log_scale = state
        scale = jnp.exp(log_scale)
        for inner in range(16):
            row = index * 16 + inner
            degree = row.astype(F32)
            lower = degree - 1.0
            up = jnp.sqrt(
                jnp.maximum(4.0 * degree * degree - 1.0, 1.0)
                / jnp.maximum(degree * degree - narrow_square, 1.0)
            )
            down = jnp.sqrt(
                jnp.maximum(lower * lower - narrow_square, 0.0)
                / jnp.maximum(4.0 * lower * lower - 1.0, 1.0)
            )
            up = jnp.concatenate([up] * 3, axis=1)
            down = jnp.concatenate([down] * 3, axis=1)
            general = up * (cosine * current - down * previous)
            second = second_factor * cosine * current
            new_row = jnp.where(
                degree == order,
                1.0,
                jnp.where(
                    degree == order + 1.0, second, jnp.where(degree > order + 1.0, general, 0.0)
                ),
            )
            out_ref[row] = new_row * scale
            previous, current = current, new_row
        largest = jnp.maximum(jnp.abs(previous), jnp.abs(current))
        largest = jnp.where(largest > 0.0, largest, 1.0)
        return previous / largest, current / largest, log_scale + jnp.log(largest)

    lax.fori_loop(0, MODES // 16, block, (zeros, zeros, log_start))


def legendre_rows(start, order, lat):
    return pl.pallas_call(
        legendre_kernel,
        out_shape=jax.ShapeDtypeStruct((MODES, TILE, NLAT), F32),
        compiler_params=params(),
        cost_estimate=cost(MODES * TILE * NLAT * 25, MODES * TILE * NLAT * 4),
        name="legendre_rows",
    )(start, order, lat)


def expand_kernel(group, rows_ref, lat_ref, spread_ref, a_ref, s_ref, at_ref, st_ref):
    weight = lat_ref[2:3, :]
    for local in range(GROUP_ORDERS):
        legendre = rows_ref[:, GROUP_ORDERS * group + local, :]
        synthesis = legendre.astype(BF16)
        analysis = (weight * legendre).astype(BF16)
        for index, (order, _) in enumerate(PAIRS):
            if order != local:
                continue
            spread = spread_ref[index]
            a_ref[index] = dot_nt(analysis, spread).astype(BF16)
            s_ref[index] = dot_nt(synthesis, spread).astype(BF16)
            at_ref[index] = dot_nt(spread, analysis).astype(BF16)
            st_ref[index] = dot_nt(spread, synthesis).astype(BF16)


def expand_tables(group, rows, lat, spread):
    degrees = degrees_of(group)
    pairs = len(PAIRS)
    flat = jax.ShapeDtypeStruct((pairs, degrees, SPAN), BF16)
    turned = jax.ShapeDtypeStruct((pairs, SPAN, degrees), BF16)
    flat_spec = pl.BlockSpec((pairs, LANES, SPAN), lambda b: (0, b, 0))
    turned_spec = pl.BlockSpec((pairs, SPAN, LANES), lambda b: (0, 0, b))
    return pl.pallas_call(
        functools.partial(expand_kernel, group),
        grid=(degrees // LANES,),
        in_specs=[
            pl.BlockSpec((LANES, TILE, NLAT), lambda b: (b + group, 0, 0)),
            pl.BlockSpec((8, NLAT), lambda b: (0, 0)),
            pl.BlockSpec((pairs, SPAN, NLAT), lambda b: (0, 0, 0)),
        ],
        out_specs=[flat_spec, flat_spec, turned_spec, turned_spec],
        out_shape=[flat, flat, turned, turned],
        compiler_params=params(),
        cost_estimate=cost(
            8 * pairs * degrees * SPAN * NLAT, degrees * TILE * NLAT * 4 + pairs * degrees * SPAN * 8
        ),
        name=f"expand_tables_{group}",
    )(rows, lat, spread)


def half_lanes(shape):
    return lax.broadcasted_iota(jnp.int32, shape, 1) < HALF


def spectrum_kernel(field_ref, table_ref, out_ref, scratch):
    step = pl.program_id(0)
    rows = DEVICES * GROUP_ORDERS
    low = half_lanes((rows, LANES))
    for inner in range(4):
        product = dot_nt(table_ref[...], field_ref[inner])
        real, imag = product[:rows], product[rows:]
        real_a, imag_a = real[:, :LANES], imag[:, :LANES]
        tiles = (
            jnp.where(low, real_a, pltpu.roll(imag_a, HALF, 1)),
            jnp.where(low, pltpu.roll(real_a, HALF, 1), imag_a),
            jnp.concatenate([real[:, LANES:], imag[:, LANES:]], axis=1),
        )
        for index, tile in enumerate(tiles):
            scratch[index, pl.ds(step * 4 + inner, rows, stride=LAT_LOCAL), :] = tile

    @pl.when(step == LAT_LOCAL // 4 - 1)
    def _():
        for index in range(GROUPS):
            out_ref[:, index * LANES : (index + 1) * LANES] = scratch[index].astype(BF16)


def spectrum_rows(field, table):
    rows = DEVICES * GROUP_ORDERS * LAT_LOCAL
    return pl.pallas_call(
        spectrum_kernel,
        grid=(LAT_LOCAL // 4,),
        in_specs=[
            pl.BlockSpec((4, C, NLON), lambda b: (b, 0, 0)),
            pl.BlockSpec((2 * DEVICES * GROUP_ORDERS, NLON), lambda b: (0, 0)),
        ],
        out_specs=pl.BlockSpec((rows, 2 * C), lambda b: (0, 0)),
        out_shape=jax.ShapeDtypeStruct((rows, 2 * C), BF16),
        scratch_shapes=[pltpu.VMEM((GROUPS, rows, LANES), F32)],
        compiler_params=params(),
        cost_estimate=cost(
            2 * LAT_LOCAL * C * NLON * 256, LAT_LOCAL * C * NLON * 2 + rows * 2 * C * 2
        ),
        name="spectrum_rows",
    )(field, table)


def spectral_kernel(
    group, recv_ref, a_ref, st_ref, gain_ref, mix_ref, *rest
):
    outs = rest[-5:]
    coef_ref, scaled_ref = outs[0], outs[1]
    out_refs = outs[2:]
    degrees = degrees_of(group)
    tiles = [recv_ref[:, tile].reshape(SPAN, 2 * C) for tile in range(GROUP_TILES)]
    mixed = []
    for local in range(GROUP_ORDERS):
        coef = None
        for index, (order, tile) in enumerate(PAIRS):
            if order == local:
                part = dot(a_ref[index], tiles[tile])
                coef = part if coef is None else coef + part
        rows = slice(local * degrees, (local + 1) * degrees)
        coef_ref[rows, :] = coef
        scaled = (gain_ref[LANES * group :, :] * coef).astype(BF16)
        scaled_ref[rows, :] = scaled
        mixed.append(dot(scaled, mix_ref[...]).astype(BF16))
    for tile in range(GROUP_TILES):
        grid = (
            dot(st_ref[2 * tile], mixed[tile]) + dot(st_ref[2 * tile + 1], mixed[tile + 1])
        ).astype(BF16)
        for index, out_ref in enumerate(out_refs):
            out_ref[:, tile] = grid[:, index * LANES : (index + 1) * LANES].reshape(
                DEVICES, TILE, LANES
            )


def whole(shape):
    return pl.BlockSpec(shape, lambda *_: (0,) * len(shape))


def spectral_forward(group, recv, a, st, gain, mix, earlier):
    degrees = degrees_of(group)
    rows = GROUP_ORDERS * degrees
    pairs = len(PAIRS)
    payload = jax.ShapeDtypeStruct((DEVICES, TILES, TILE, LANES), BF16)
    payload_spec = pl.BlockSpec(
        (DEVICES, GROUP_TILES, TILE, LANES), lambda b: (0, group, 0, 0)
    )
    return pl.pallas_call(
        functools.partial(spectral_kernel, group),
        grid=(1,),
        in_specs=[
            whole((DEVICES, GROUP_TILES, TILE, 2 * C)),
            whole((pairs, degrees, SPAN)),
            whole((pairs, SPAN, degrees)),
            whole((MODES, 2 * C)),
            whole((2 * C, 2 * C)),
        ]
        + [pl.BlockSpec(memory_space=pl.ANY)] * len(earlier),
        out_specs=[whole((rows, 2 * C)), whole((rows, 2 * C))] + [payload_spec] * 3,
        out_shape=[
            jax.ShapeDtypeStruct((rows, 2 * C), F32),
            jax.ShapeDtypeStruct((rows, 2 * C), BF16),
        ]
        + [payload] * 3,
        input_output_aliases={5 + index: 2 + index for index in range(len(earlier))},
        compiler_params=params(),
        cost_estimate=cost(
            2 * rows * 2 * C * (2 * 768 + 384), rows * SPAN * 6 + rows * 2 * C * 6 + SPAN * 48 * 48
        ),
        name=f"spectral_forward_{group}",
    )(recv, a, st, gain, mix, *earlier)


def grid_kernel(
    recv_ref, up_ref, turned_ref, proj_ref, table_ref, turned_table_ref,
    out_ref, grad_ref, scratch, out_scratch, act_scratch, pre_scratch,
):
    step = pl.program_id(0)
    low = half_lanes((MODES, LANES))
    block = 128

    @pl.when(step == 0)
    def _():
        scratch[...] = recv_ref[...].astype(F32)
        grad_ref[...] = jnp.zeros_like(grad_ref)

    columns = []
    for pair in range(2):
        first = scratch[pl.ds(step * 4 + 2 * pair, MODES, stride=LAT_LOCAL), :]
        second = scratch[pl.ds(step * 4 + 2 * pair + 1, MODES, stride=LAT_LOCAL), :]
        real = jnp.where(low, first, pltpu.roll(second, HALF, 1))
        imag = jnp.where(low, pltpu.roll(first, HALF, 1), second)
        columns.append(jnp.concatenate([real, imag], axis=0).astype(BF16))
    modes = jnp.concatenate(columns, axis=1)
    low_block = half_lanes((block, LANES))
    for part in range(NLON // block):
        rows = slice(part * block, (part + 1) * block)
        pre = dot(turned_table_ref[rows, :], modes)
        grad_act = jnp.concatenate(
            [
                jnp.where(
                    low_block,
                    dot(turned_ref[2 * pair, rows, :], proj_ref[...]),
                    dot(turned_ref[2 * pair + 1, rows, :], proj_ref[...]),
                )
                for pair in range(2)
            ],
            axis=1,
        )
        cumulative = 0.5 * (1.0 + lax.erf(pre * (1.0 / math.sqrt(2.0))))
        slope = cumulative + pre * jnp.exp(-0.5 * pre * pre) * (1.0 / math.sqrt(2.0 * math.pi))
        act_scratch[rows, :] = (pre * cumulative).astype(BF16)
        pre_scratch[rows, :] = (grad_act * slope).astype(BF16)
    low_grad = half_lanes((C, LANES))
    for pair in range(2):
        lanes = slice(pair * LANES, (pair + 1) * LANES)
        act = act_scratch[:, lanes]
        grad_ref[...] += jnp.where(
            low_grad, dot(up_ref[2 * pair], act), dot(up_ref[2 * pair + 1], act)
        )
    grad_modes = dot(table_ref[...], pre_scratch[...])
    for pair in range(2):
        lanes = slice(pair * LANES, (pair + 1) * LANES)
        real, imag = grad_modes[:MODES, lanes], grad_modes[MODES:, lanes]
        out_scratch[pl.ds(step * 4 + 2 * pair, MODES, stride=LAT_LOCAL), :] = jnp.where(
            low, real, pltpu.roll(imag, HALF, 1)
        )
        out_scratch[pl.ds(step * 4 + 2 * pair + 1, MODES, stride=LAT_LOCAL), :] = jnp.where(
            low, pltpu.roll(real, HALF, 1), imag
        )

    @pl.when(step == LAT_LOCAL // 4 - 1)
    def _():
        out_ref[...] = out_scratch[...].astype(BF16)


def grid_stage(recv, up, turned, proj, table, turned_table):
    rows = MODES * LAT_LOCAL
    return pl.pallas_call(
        grid_kernel,
        grid=(LAT_LOCAL // 4,),
        in_specs=[
            whole((rows, LANES)),
            pl.BlockSpec((4, C, NLON), lambda b: (b, 0, 0)),
            pl.BlockSpec((4, NLON, C), lambda b: (b, 0, 0)),
            whole((C, LANES)),
            whole((2 * MODES, NLON)),
            whole((NLON, 2 * MODES)),
        ],
        out_specs=[whole((rows, LANES)), whole((C, LANES))],
        out_shape=[
            jax.ShapeDtypeStruct((rows, LANES), BF16),
            jax.ShapeDtypeStruct((C, LANES), F32),
        ],
        scratch_shapes=[
            pltpu.VMEM((rows, LANES), F32),
            pltpu.VMEM((rows, LANES), F32),
            pltpu.VMEM((NLON, 2 * LANES), BF16),
            pltpu.VMEM((NLON, 2 * LANES), BF16),
        ],
        compiler_params=params(),
        cost_estimate=cost(
            2 * LAT_LOCAL * HALF * NLON * (2 * 768 + 4 * 192) + LAT_LOCAL * HALF * NLON * 60,
            2 * LAT_LOCAL * C * NLON * 2 + 2 * rows * LANES * 2 + 4 * 768 * 768,
            LAT_LOCAL * HALF * NLON * 2,
        ),
        name="grid_stage",
    )(recv, up, turned, proj, table, turned_table)


def backward_kernel(group, recv_a, recv_b, recv_c, s_ref, gain_ref, mix_ref, mixed_ref, coeff_ref):
    degrees = degrees_of(group)
    tiles = [
        jnp.concatenate(
            [ref[:, tile].reshape(SPAN, LANES) for ref in (recv_a, recv_b, recv_c)], axis=1
        )
        for tile in range(GROUP_TILES)
    ]
    for local in range(GROUP_ORDERS):
        total = None
        for index, (order, tile) in enumerate(PAIRS):
            if order == local:
                part = dot(s_ref[index], tiles[tile])
                total = part if total is None else total + part
        rows = slice(local * degrees, (local + 1) * degrees)
        mixed = total.astype(BF16)
        mixed_ref[rows, :] = mixed
        scaled = dot_nt(mixed, mix_ref[...])
        coeff_ref[rows, :] = (gain_ref[LANES * group :, :] * scaled).astype(BF16)


def spectral_backward(group, recv, s, gain, mix):
    degrees = degrees_of(group)
    rows = GROUP_ORDERS * degrees
    recv_spec = pl.BlockSpec((DEVICES, GROUP_TILES, TILE, LANES), lambda b: (0, group, 0, 0))
    result = jax.ShapeDtypeStruct((rows, 2 * C), BF16)
    return pl.pallas_call(
        functools.partial(backward_kernel, group),
        grid=(1,),
        in_specs=[recv_spec] * 3
        + [whole((len(PAIRS), degrees, SPAN)), whole((MODES, 2 * C)), whole((2 * C, 2 * C))],
        out_specs=[whole((rows, 2 * C))] * 2,
        out_shape=[result] * 2,
        compiler_params=params(),
        cost_estimate=cost(
            2 * rows * 2 * C * (768 + 384), rows * SPAN * 3 + rows * 2 * C * 4 + SPAN * 48 * 48
        ),
        name=f"spectral_backward_{group}",
    )(*recv, s, gain, mix)


def synthesis_kernel(group, coeff_ref, at_ref, out_ref):
    degrees = degrees_of(group)
    for tile in range(GROUP_TILES):
        first = coeff_ref[tile * degrees : (tile + 1) * degrees, :]
        second = coeff_ref[(tile + 1) * degrees : (tile + 2) * degrees, :]
        out = dot(at_ref[2 * tile], first) + dot(at_ref[2 * tile + 1], second)
        out_ref[:, tile] = out.astype(BF16).reshape(DEVICES, TILE, 2 * C)


def analysis_back(group, coeffs, at):
    degrees = degrees_of(group)
    rows = GROUP_ORDERS * degrees
    shape = (DEVICES, GROUP_TILES, TILE, 2 * C)
    return pl.pallas_call(
        functools.partial(synthesis_kernel, group),
        grid=(1,),
        in_specs=[whole((rows, 2 * C)), whole((len(PAIRS), SPAN, degrees))],
        out_specs=whole(shape),
        out_shape=jax.ShapeDtypeStruct(shape, BF16),
        compiler_params=params(),
        cost_estimate=cost(
            2 * rows * 2 * C * 768, rows * SPAN * 3 + rows * 2 * C * 2 + SPAN * 48 * 48
        ),
        name=f"analysis_back_{group}",
    )(coeffs, at)


def weight_kernel(group, scaled_ref, mixed_ref, coef_ref, mix_ref, block_ref, gain_ref):
    degrees = degrees_of(group)
    block_ref[...] = lax.dot_general(
        scaled_ref[...], mixed_ref[...], (((0,), (0,)), ((), ())), preferred_element_type=F32
    )
    total = None
    for local in range(GROUP_ORDERS):
        rows = slice(local * degrees, (local + 1) * degrees)
        part = dot_nt(mixed_ref[rows, :], mix_ref[...]) * coef_ref[rows, :]
        total = part if total is None else total + part
    gain_ref[...] = total


def weight_grads(group, scaled, mixed, coef, mix):
    degrees = degrees_of(group)
    rows = GROUP_ORDERS * degrees
    return pl.pallas_call(
        functools.partial(weight_kernel, group),
        out_shape=[
            jax.ShapeDtypeStruct((2 * C, 2 * C), F32),
            jax.ShapeDtypeStruct((degrees, 2 * C), F32),
        ],
        compiler_params=params(),
        cost_estimate=cost(2 * rows * 2 * C * 2 * 384, rows * 2 * C * 8),
        name=f"weight_grads_{group}",
    )(scaled, mixed, coef, mix)


def field_kernel(recv_ref, table_ref, base_ref, out_ref, scratch):
    step = pl.program_id(0)
    orders = DEVICES * GROUP_ORDERS

    @pl.when(step == 0)
    def _():
        for index in range(GROUPS):
            scratch[index] = recv_ref[:, index * LANES : (index + 1) * LANES].astype(F32)

    for inner in range(4):
        real, imag = [], []
        for index in range(GROUPS):
            rows = scratch[index, pl.ds(step * 4 + inner, orders, stride=LAT_LOCAL), :]
            turned = rows.T.astype(BF16)
            real.append(turned[:HALF])
            imag.append(turned[HALF:])
        left = jnp.concatenate(
            [jnp.concatenate(real, axis=0), jnp.concatenate(imag, axis=0)], axis=1
        )
        total = base_ref[inner].astype(F32) + dot(left, table_ref[...])
        out_ref[inner] = total.astype(out_ref.dtype)


def field_stage(recv, table, base, kind):
    rows = DEVICES * GROUP_ORDERS * LAT_LOCAL
    block = pl.BlockSpec((4, C, NLON), lambda b: (b, 0, 0))
    return pl.pallas_call(
        field_kernel,
        grid=(LAT_LOCAL // 4,),
        in_specs=[whole((rows, 2 * C)), whole((2 * DEVICES * GROUP_ORDERS, NLON)), block],
        out_specs=block,
        out_shape=jax.ShapeDtypeStruct((LAT_LOCAL, C, NLON), kind),
        scratch_shapes=[pltpu.VMEM((GROUPS, rows, LANES), F32)],
        compiler_params=params(),
        cost_estimate=cost(
            2 * LAT_LOCAL * C * NLON * 256, LAT_LOCAL * C * NLON * 7 + rows * 2 * C * 2
        ),
        name="field_stage",
    )(recv, table, base)


def exchange(payload):
    return lax.all_to_all(payload, "lat", split_axis=0, concat_axis=0, tiled=True)


def shards(saved_input, incoming, spectral_gain, mix_weight, proj_weight):
    device = lax.axis_index("lat")
    section_count = lax.axis_size("section")
    shift = [(source, (source - 1) % section_count) for source in range(section_count)]

    forward = jnp.asarray(forward_groups())
    inverse_np = inverse_rows()
    inverse = jnp.asarray(inverse_np)
    inverse_turned = jnp.asarray(np.ascontiguousarray(inverse_np.T))
    spread = jnp.asarray(spread_tables())
    lat = jnp.asarray(latitude_rows())
    starts, numbers = log_starts()
    start = lax.dynamic_index_in_dim(jnp.asarray(starts), device, 0, keepdims=False)
    order = lax.dynamic_index_in_dim(jnp.asarray(numbers), device, 0, keepdims=False)

    field = saved_input[0]
    upstream = incoming[0]
    upstream_next = lax.ppermute(upstream, "section", shift)
    turned = jnp.swapaxes(upstream, 1, 2)
    gain = jnp.broadcast_to(
        spectral_gain[0].reshape(MODES, GROUPS, 1, HALF), (MODES, GROUPS, 2, HALF)
    ).reshape(MODES, 2 * C)
    real, imag = mix_weight[0, 0], mix_weight[0, 1]
    mix = (
        jnp.stack([jnp.stack([real, imag]), jnp.stack([-imag, real])])
        .reshape(2, 2, GROUPS, HALF, GROUPS, HALF)
        .transpose(2, 0, 3, 4, 1, 5)
        .reshape(2 * C, 2 * C)
    )
    proj = proj_weight[0].T.reshape(C, GROUPS, 1, HALF)
    proj = jnp.broadcast_to(proj, (C, GROUPS, 2, HALF)).transpose(1, 0, 2, 3)
    proj = proj.reshape(GROUPS, C, LANES)

    group_rows = GROUP_ORDERS * LAT_LOCAL
    received = []
    for group in range(GROUPS):
        rows = spectrum_rows(field, forward[group])
        received.append(exchange(rows.reshape(DEVICES, group_rows, 2 * C)))
    legendre = legendre_rows(start, order, lat)
    tables = [expand_tables(group, legendre, lat, spread) for group in range(GROUPS)]

    coefs, scaleds, payloads = [], [], []
    for group in range(GROUPS):
        coef, scaled, *payloads = spectral_forward(
            group,
            received[group].reshape(DEVICES, GROUP_TILES, TILE, 2 * C),
            tables[group][0],
            tables[group][3],
            gain,
            mix,
            payloads,
        )
        coefs.append(coef)
        scaleds.append(scaled)

    back, proj_parts = [], []
    for block in range(GROUPS):
        recv = exchange(payloads[block].reshape(DEVICES, ORDERS * LAT_LOCAL, LANES))
        rows, proj_part = grid_stage(
            recv.reshape(MODES * LAT_LOCAL, LANES),
            upstream,
            turned,
            proj[block],
            inverse,
            inverse_turned,
        )
        proj_parts.append(proj_part[:, :HALF] + proj_part[:, HALF:])
        back.append(
            exchange(rows.reshape(DEVICES, ORDERS * LAT_LOCAL, LANES)).reshape(
                DEVICES, TILES, TILE, LANES
            )
        )
    proj_local = jnp.concatenate(proj_parts, axis=1).T
    proj_total = lax.psum(proj_local.astype(BF16), "lat").astype(F32)

    base = upstream_next
    mixeds = [None] * GROUPS
    for group in reversed(range(GROUPS)):
        mixeds[group], coeffs = spectral_backward(group, back, tables[group][1], gain, mix)
        moved = lax.ppermute(coeffs, "section", shift)
        rows = exchange(
            analysis_back(group, moved, tables[group][2]).reshape(DEVICES, group_rows, 2 * C)
        )
        base = field_stage(
            rows.reshape(DEVICES * group_rows, 2 * C),
            forward[group],
            base,
            BF16 if group == 0 else F32,
        )

    block_grad, gain_sum = None, None
    for group in reversed(range(GROUPS)):
        part, gain_part = weight_grads(group, scaleds[group], mixeds[group], coefs[group], mix)
        block_grad = part if block_grad is None else block_grad + part
        gain_part = jnp.pad(gain_part, ((LANES * group, 0), (0, 0)))
        gain_sum = gain_part if gain_sum is None else gain_sum + gain_part
    block_grad = block_grad.reshape(GROUPS, 2, HALF, GROUPS, 2, HALF)
    grad_real = (block_grad[:, 0, :, :, 0] + block_grad[:, 1, :, :, 1]).reshape(C, C)
    grad_imag = (block_grad[:, 0, :, :, 1] - block_grad[:, 1, :, :, 0]).reshape(C, C)
    gain_local = gain_sum.reshape(MODES, GROUPS, 2, HALF).sum(axis=2).reshape(MODES, C)

    real_total, imag_total, gain_total = (
        lax.psum(grad_real.astype(BF16), "lat").astype(F32),
        lax.psum(grad_imag.astype(BF16), "lat").astype(F32),
        lax.psum(gain_local.astype(BF16), "lat").astype(F32),
    )
    grid_scale = 1.0 / math.sqrt(NLAT * NLON)
    mode_scale = 1.0 / math.sqrt(MODES)
    grad_w2 = grid_scale * proj_total
    grad_mix = grid_scale * jnp.stack([real_total, imag_total])
    grad_gain = mode_scale * gain_total
    return (base[None], grad_w2[None], grad_mix[None], grad_gain[None])


def solution(mesh):
    in_specs = (
        P("section", "lat", None, None),
        P("section", "lat", None, None),
        P("section", None, None),
        P("section", None, None, None),
        P("section", None, None),
    )
    out_specs = (
        P("section", "lat", None, None),
        P("section", None, None),
        P("section", None, None, None),
        P("section", None, None),
    )
    return jax.shard_map(shards, mesh=mesh, in_specs=in_specs, out_specs=out_specs, check_vma=False)
```

```python
import functools
import math

import jax
import jax.numpy as jnp
import ml_dtypes
import numpy as np
from jax import lax
from jax.experimental import pallas as pl
from jax.experimental.pallas import tpu as pltpu
from jax.sharding import PartitionSpec as P

NLAT = 384
NLON = 768
MODES = 384
C = 192
DEVICES = 32
LAT_LOCAL = 12
ORDERS = 12
GROUPS = 3
GROUP_ORDERS = 4
HALF = 64
LANES = 128
TILE = 16
TILES = 9
GROUP_TILES = 3
SPAN = DEVICES * TILE
LAT_BLOCKS = 4
BLOCK_LATS = NLAT // LAT_BLOCKS
VMEM_LIMIT = 56 * 1024 * 1024
F32 = jnp.float32
BF16 = jnp.bfloat16
NT = (((1,), (1,)), ((), ()))

PAIRS = ((0, 0), (1, 0), (1, 1), (2, 1), (2, 2), (3, 2))


def degrees_of(group):
    return MODES - LANES * group


def half_lanes(shape):
    return lax.broadcasted_iota(jnp.int32, shape, 1) < HALF


def dot(left, right):
    return jnp.dot(left, right, preferred_element_type=F32)


def dot_nt(left, right):
    return lax.dot_general(left, right, NT, preferred_element_type=F32)


def whole(shape):
    return pl.BlockSpec(shape, lambda *_: (0,) * len(shape))


def call(kernel, inputs, in_specs, out_specs, out_shape, grid, flops, after=(), aliases=None, **extra):
    count = len(inputs)

    def body(*refs):
        kernel(*refs[:count], *refs[count + len(after) :])

    outs = jax.tree.leaves(out_shape)
    moved = sum(value.size * value.dtype.itemsize for value in list(inputs) + outs)
    return pl.pallas_call(
        body,
        grid=grid,
        in_specs=list(in_specs) + [pl.BlockSpec(memory_space=pl.ANY)] * len(after),
        out_specs=out_specs,
        out_shape=out_shape,
        input_output_aliases=aliases or {},
        compiler_params=pltpu.CompilerParams(vmem_limit_bytes=VMEM_LIMIT),
        cost_estimate=pl.CostEstimate(
            flops=int(flops), bytes_accessed=int(moved), transcendentals=0
        ),
        **extra,
    )(*inputs, *after)


def order_rows(first, count):
    device = np.arange(DEVICES)[:, None]
    local = np.arange(GROUP_ORDERS * count)[None, :] + GROUP_ORDERS * first
    return (DEVICES * local + device).reshape(-1)


def fourier_rows(orders):
    phase = (orders[:, None] * np.arange(NLON)[None, :]) % NLON
    angle = phase * (2.0 * math.pi / NLON)
    return np.cos(angle), -np.sin(angle)


def forward_rows(first, count):
    cosine, sine = fourier_rows(order_rows(first, count))
    table = np.concatenate([cosine, sine], axis=0)
    return jnp.asarray(table.astype(np.float32).astype(ml_dtypes.bfloat16))


def inverse_rows():
    device = np.arange(DEVICES)[:, None]
    orders = (DEVICES * np.arange(ORDERS)[None, :] + device).reshape(-1)
    factor = np.where(orders == 0, 1.0, 2.0)[:, None] / NLON
    cosine, sine = fourier_rows(orders)
    table = np.concatenate([factor * cosine, factor * sine], axis=0)
    return table.astype(np.float32).astype(ml_dtypes.bfloat16)


def spread_tables():
    rows = np.arange(LANES)
    source, inner = rows // TILE, rows % TILE
    tables = np.zeros((len(PAIRS), LANES, LANES), np.float32)
    for index, (order, tile) in enumerate(PAIRS):
        lat = TILE * tile + inner - LAT_LOCAL * order
        valid = (lat >= 0) & (lat < LAT_LOCAL)
        tables[index, (source * LAT_LOCAL + lat)[valid], rows[valid]] = 1.0
    flat = jnp.asarray(tables.astype(ml_dtypes.bfloat16))
    turned = jnp.asarray(np.swapaxes(tables, 1, 2).astype(ml_dtypes.bfloat16))
    return flat, turned


def log_starts():
    table = np.zeros((DEVICES, TILE, LANES), np.float32)
    numbers = np.zeros((DEVICES, TILE, LANES), np.float32)
    for device in range(DEVICES):
        for local in range(ORDERS):
            order = DEVICES * local + device
            numbers[device, local] = order
            table[device, local] = 0.5 * math.log((2.0 * order + 1.0) / 2.0) + 0.5 * (
                math.lgamma(order + 0.5) - math.lgamma(0.5) - math.lgamma(order + 1.0)
            )
    return table, numbers


def latitude_rows():
    colatitude = (np.arange(NLAT) + 0.5) * (math.pi / NLAT)
    harmonic = np.arange(1, NLAT // 2 + 1)
    terms = np.cos(2.0 * harmonic[None, :] * colatitude[:, None]) / (4.0 * harmonic**2 - 1.0)
    weight = 2.0 / NLAT * (1.0 - 2.0 * np.sum(terms, axis=1))
    rows = np.stack([np.cos(colatitude), np.log(np.sin(colatitude)), weight])
    rows = np.concatenate([rows, np.zeros((5, NLAT))]).reshape(8, LAT_BLOCKS, BLOCK_LATS)
    rows = np.pad(rows, ((0, 0), (0, 0), (0, LANES - BLOCK_LATS)))
    return rows.reshape(8, SPAN).astype(np.float32)


def legendre_rows(start_ref, order_ref, lat_ref, rows_ref):
    order = jnp.concatenate([order_ref[...]] * LAT_BLOCKS, axis=1)
    cosine = jnp.broadcast_to(lat_ref[0:1, :], (TILE, SPAN))
    log_sin = jnp.broadcast_to(lat_ref[1:2, :], (TILE, SPAN))
    log_start = jnp.concatenate([start_ref[...]] * LAT_BLOCKS, axis=1) + order * log_sin
    narrow = order_ref[...]
    narrow_square = narrow * narrow
    second_factor = jnp.concatenate([jnp.sqrt(2.0 * narrow + 3.0)] * LAT_BLOCKS, axis=1)
    zeros = jnp.zeros((TILE, SPAN), F32)

    def block(index, state):
        previous, current, log_scale = state
        scale = jnp.exp(log_scale)
        for inner in range(16):
            row = index * 16 + inner
            degree = row.astype(F32)
            lower = degree - 1.0
            up = jnp.sqrt(
                jnp.maximum(4.0 * degree * degree - 1.0, 1.0)
                / jnp.maximum(degree * degree - narrow_square, 1.0)
            )
            down = jnp.sqrt(
                jnp.maximum(lower * lower - narrow_square, 0.0)
                / jnp.maximum(4.0 * lower * lower - 1.0, 1.0)
            )
            up = jnp.concatenate([up] * LAT_BLOCKS, axis=1)
            down = jnp.concatenate([down] * LAT_BLOCKS, axis=1)
            general = up * (cosine * current - down * previous)
            second = second_factor * cosine * current
            new_row = jnp.where(
                degree == order,
                1.0,
                jnp.where(
                    degree == order + 1.0, second, jnp.where(degree > order + 1.0, general, 0.0)
                ),
            )
            scaled = new_row * scale
            for part in range(LAT_BLOCKS):
                rows_ref[part, row] = scaled[:, part * LANES : (part + 1) * LANES]
            previous, current = current, new_row
        largest = jnp.maximum(jnp.abs(previous), jnp.abs(current))
        largest = jnp.where(largest > 0.0, largest, 1.0)
        return previous / largest, current / largest, log_scale + jnp.log(largest)

    lax.fori_loop(0, MODES // 16, block, (zeros, zeros, log_start))


def table_kernel(start_ref, order_ref, lat_ref, flat_ref, turned_ref, *rest):
    outs, rows_ref, buffers, sems = rest[:12], rest[12], rest[13:25], rest[25]
    legendre_rows(start_ref, order_ref, lat_ref, rows_ref)
    copies = []
    for group in range(GROUPS):
        ahead_flat, ahead_turned, behind_flat, behind_turned = buffers[4 * group : 4 * group + 4]

        def part_step(part, carry):
            lats = pl.ds(pl.multiple_of(part * LANES, LANES), LANES)
            weight = lat_ref[2:3, lats]
            for local in range(GROUP_ORDERS):
                legendre = rows_ref[part, LANES * group :, GROUP_ORDERS * group + local, :]
                synthesis = legendre.astype(BF16)
                analysis = (weight * legendre).astype(BF16)
                pairs = [index for index, (order, _) in enumerate(PAIRS) if order == local]
                flat = jnp.concatenate([flat_ref[index] for index in pairs], axis=1)
                turned = jnp.concatenate([turned_ref[index] for index in pairs], axis=0)
                products = (
                    dot(analysis, flat).astype(BF16),
                    dot_nt(turned, synthesis).astype(BF16),
                    dot(synthesis, flat).astype(BF16),
                    dot_nt(turned, analysis).astype(BF16),
                )
                for place, index in enumerate(pairs):
                    cut = slice(place * LANES, (place + 1) * LANES)
                    ahead_flat[index, :, lats] = products[0][:, cut]
                    ahead_turned[index, lats, :] = products[1][cut]
                    behind_flat[index, :, lats] = products[2][:, cut]
                    behind_turned[index, lats, :] = products[3][cut]
            return carry

        lax.fori_loop(0, LAT_BLOCKS, part_step, 0)
        for place in range(4):
            at = 4 * group + place
            copy = pltpu.make_async_copy(buffers[at], outs[at], sems.at[at])
            copy.start()
            copies.append(copy)
    for copy in copies:
        copy.wait()


def legendre_tables(start, order, lat, flat, turned, after):
    shapes = []
    for group in range(GROUPS):
        degrees = degrees_of(group)
        shapes += [(len(PAIRS), degrees, SPAN), (len(PAIRS), SPAN, degrees)] * 2
    inputs = (start, order, lat, flat, turned)
    return call(
        table_kernel,
        inputs,
        [whole(value.shape) for value in inputs],
        [pl.BlockSpec(memory_space=pl.ANY)] * len(shapes),
        [jax.ShapeDtypeStruct(shape, BF16) for shape in shapes],
        (1,),
        16 * sum(math.prod(shape) for shape in shapes) * 8,
        after,
        scratch_shapes=[pltpu.VMEM((LAT_BLOCKS, MODES, TILE, LANES), F32)]
        + [pltpu.VMEM(shape, BF16) for shape in shapes]
        + [pltpu.SemaphoreType.DMA((len(shapes),))],
        name="legendre_tables",
    )


def spectrum_kernel(field_ref, table_ref, out_ref, scratch):
    step = pl.program_id(0)
    rows = table_ref.shape[0] // 2
    low = half_lanes((rows, LANES))
    for inner in range(4):
        product = dot_nt(table_ref[...], field_ref[inner])
        real, imag = product[:rows], product[rows:]
        real_a, imag_a = real[:, :LANES], imag[:, :LANES]
        tiles = (
            jnp.where(low, real_a, pltpu.roll(imag_a, HALF, 1)),
            jnp.where(low, pltpu.roll(real_a, HALF, 1), imag_a),
            jnp.concatenate([real[:, LANES:], imag[:, LANES:]], axis=1),
        )
        for index, tile in enumerate(tiles):
            scratch[index, pl.ds(step * 4 + inner, rows, stride=LAT_LOCAL), :] = tile

    @pl.when(step == LAT_LOCAL // 4 - 1)
    def _():
        for index in range(GROUPS):
            out_ref[:, index * LANES : (index + 1) * LANES] = scratch[index].astype(BF16)


def spectrum_rows(field, table, after=()):
    rows = table.shape[0] // 2 * LAT_LOCAL
    return call(
        spectrum_kernel,
        (field, table),
        [pl.BlockSpec((4, C, NLON), lambda b: (b, 0, 0)), whole(table.shape)],
        whole((rows, 2 * C)),
        jax.ShapeDtypeStruct((rows, 2 * C), BF16),
        (LAT_LOCAL // 4,),
        2 * LAT_LOCAL * C * NLON * table.shape[0],
        after,
        scratch_shapes=[pltpu.VMEM((GROUPS, rows, LANES), F32)],
        name="spectrum_rows",
    )


def pair_sum(local, table_ref, tiles):
    total = None
    for index, (order, tile) in enumerate(PAIRS):
        if order == local:
            part = dot(table_ref[index], tiles[tile])
            total = part if total is None else total + part
    return total


def spectral_kernel(recv_ref, *refs):
    a_refs, st_refs = refs[0:3], refs[3:6]
    gain_ref, mix_ref = refs[6:8]
    scaled_outs, payload_ref = refs[8:11], refs[11]
    recv, payload = refs[12:14]
    a_buffers, st_buffers, scaled_buffers = refs[14:17], refs[17:20], refs[20:23]
    in_sems, out_sems = refs[23:25]
    schedule = (2, 0, 1)
    arrivals, departures = {}, []
    for group in schedule:
        tiles = pl.ds(GROUP_TILES * group, GROUP_TILES)
        arrivals[group] = [
            pltpu.make_async_copy(recv_ref.at[:, tiles], recv.at[group], in_sems.at[group, 0]),
            pltpu.make_async_copy(a_refs[group], a_buffers[group], in_sems.at[group, 1]),
            pltpu.make_async_copy(st_refs[group], st_buffers[group], in_sems.at[group, 2]),
        ]
        for copy in arrivals[group]:
            copy.start()
    for group in schedule:
        degrees = degrees_of(group)
        for copy in arrivals[group]:
            copy.wait()
        tiles = [recv[group, :, tile].reshape(SPAN, 2 * C) for tile in range(GROUP_TILES)]
        mixed = []
        for local in range(GROUP_ORDERS):
            rows = slice(local * degrees, (local + 1) * degrees)
            coef = pair_sum(local, a_buffers[group], tiles)
            scaled = (gain_ref[LANES * group :, :] * coef).astype(BF16)
            scaled_buffers[group][rows, :] = scaled
            mixed.append(dot(scaled, mix_ref[...]).astype(BF16))
        for tile in range(GROUP_TILES):
            grid = dot(st_buffers[group][2 * tile], mixed[tile]) + dot(
                st_buffers[group][2 * tile + 1], mixed[tile + 1]
            )
            payload[group, :, tile] = grid.astype(BF16).reshape(DEVICES, TILE, 2 * C)
        tiles = pl.ds(GROUP_TILES * group, GROUP_TILES)
        copies = (
            pltpu.make_async_copy(
                payload.at[group], payload_ref.at[:, tiles], out_sems.at[group, 0]
            ),
            pltpu.make_async_copy(
                scaled_buffers[group], scaled_outs[group], out_sems.at[group, 1]
            ),
        )
        for copy in copies:
            copy.start()
            departures.append(copy)
    for copy in departures:
        copy.wait()


def spectral_forward(recv, a, st, gain, mix, after=()):
    shapes = [(GROUP_ORDERS * degrees_of(group), 2 * C) for group in range(GROUPS)]
    held = pl.BlockSpec(memory_space=pl.ANY)
    slots = (GROUPS, DEVICES, GROUP_TILES, TILE, 2 * C)
    return call(
        spectral_kernel,
        (recv, *a, *st, gain, mix),
        [held] * 7 + [whole(gain.shape), whole(mix.shape)],
        [held] * 4,
        [jax.ShapeDtypeStruct(shape, BF16) for shape in shapes]
        + [jax.ShapeDtypeStruct(recv.shape, BF16)],
        (1,),
        sum(2 * rows * 2 * C * (2 * 768 + 384) for rows, _ in shapes),
        after,
        scratch_shapes=[pltpu.VMEM(slots, BF16), pltpu.VMEM(slots, BF16)]
        + [pltpu.VMEM(value.shape, BF16) for value in a]
        + [pltpu.VMEM(value.shape, BF16) for value in st]
        + [pltpu.VMEM(shape, BF16) for shape in shapes]
        + [pltpu.SemaphoreType.DMA((GROUPS, 3)), pltpu.SemaphoreType.DMA((GROUPS, 2))],
        name="spectral_forward",
    )


def grid_kernel(
    recv_ref, up_ref, turned_ref, proj_ref, table_ref, turned_table_ref,
    out_ref, grad_ref, scratch, out_scratch, act_scratch, pre_scratch,
):
    step = pl.program_id(1)
    low = half_lanes((MODES, LANES))
    block = 128

    @pl.when(step == 0)
    def _():
        scratch[...] = recv_ref[...].astype(F32)
        grad_ref[...] = jnp.zeros_like(grad_ref)

    columns = []
    for pair in range(2):
        first = scratch[pl.ds(step * 4 + 2 * pair, MODES, stride=LAT_LOCAL), :]
        second = scratch[pl.ds(step * 4 + 2 * pair + 1, MODES, stride=LAT_LOCAL), :]
        real = jnp.where(low, first, pltpu.roll(second, HALF, 1))
        imag = jnp.where(low, pltpu.roll(first, HALF, 1), second)
        columns.append(jnp.concatenate([real, imag], axis=0).astype(BF16))
    modes = jnp.concatenate(columns, axis=1)
    low_block = half_lanes((block, LANES))
    for part in range(NLON // block):
        rows = slice(part * block, (part + 1) * block)
        pre = dot(turned_table_ref[rows, :], modes)
        grad_act = jnp.concatenate(
            [
                jnp.where(
                    low_block,
                    dot(turned_ref[2 * pair, rows, :], proj_ref[...]),
                    dot(turned_ref[2 * pair + 1, rows, :], proj_ref[...]),
                )
                for pair in range(2)
            ],
            axis=1,
        )
        cumulative = 0.5 * (1.0 + lax.erf(pre * (1.0 / math.sqrt(2.0))))
        slope = cumulative + pre * jnp.exp(-0.5 * pre * pre) * (1.0 / math.sqrt(2.0 * math.pi))
        act_scratch[rows, :] = (pre * cumulative).astype(BF16)
        pre_scratch[rows, :] = (grad_act * slope).astype(BF16)
    low_grad = half_lanes((C, LANES))
    for pair in range(2):
        lanes = slice(pair * LANES, (pair + 1) * LANES)
        act = act_scratch[:, lanes]
        grad_ref[...] += jnp.where(
            low_grad, dot(up_ref[2 * pair], act), dot(up_ref[2 * pair + 1], act)
        )
    grad_modes = dot(table_ref[...], pre_scratch[...])
    for pair in range(2):
        lanes = slice(pair * LANES, (pair + 1) * LANES)
        real, imag = grad_modes[:MODES, lanes], grad_modes[MODES:, lanes]
        out_scratch[pl.ds(step * 4 + 2 * pair, MODES, stride=LAT_LOCAL), :] = jnp.where(
            low, real, pltpu.roll(imag, HALF, 1)
        )
        out_scratch[pl.ds(step * 4 + 2 * pair + 1, MODES, stride=LAT_LOCAL), :] = jnp.where(
            low, pltpu.roll(real, HALF, 1), imag
        )

    @pl.when(step == LAT_LOCAL // 4 - 1)
    def _():
        out_ref[...] = out_scratch[...].astype(BF16)


def grid_stage(first, blocks, recv, up, turned, proj, table, turned_table, after=()):
    rows = MODES * LAT_LOCAL
    lanes_spec = pl.BlockSpec((rows, LANES), lambda q, b: (0, q))
    grad_spec = pl.BlockSpec((C, LANES), lambda q, b: (0, q))
    return call(
        grid_kernel,
        (recv, up, turned, proj, table, turned_table),
        [
            pl.BlockSpec((rows, LANES), lambda q, b: (0, q + first)),
            pl.BlockSpec((4, C, NLON), lambda q, b: (b, 0, 0)),
            pl.BlockSpec((4, NLON, C), lambda q, b: (b, 0, 0)),
            pl.BlockSpec((C, LANES), lambda q, b: (0, q + first)),
            whole(table.shape),
            whole(turned_table.shape),
        ],
        [lanes_spec, grad_spec],
        [
            jax.ShapeDtypeStruct((rows, LANES * blocks), BF16),
            jax.ShapeDtypeStruct((C, LANES * blocks), F32),
        ],
        (blocks, LAT_LOCAL // 4),
        blocks * LAT_LOCAL * HALF * NLON * (4 * 768 + 8 * 192 + 60),
        after,
        scratch_shapes=[
            pltpu.VMEM((rows, LANES), F32),
            pltpu.VMEM((rows, LANES), F32),
            pltpu.VMEM((NLON, 2 * LANES), BF16),
            pltpu.VMEM((NLON, 2 * LANES), BF16),
        ],
        name=f"grid_stage_{blocks}",
    )


def backward_kernel(group, small_ref, large_ref, s_ref, gain_ref, mix_ref, mixed_ref, coeff_ref):
    degrees = degrees_of(group)
    tiles = [
        jnp.concatenate(
            [
                small_ref[:, tile].reshape(SPAN, LANES),
                large_ref[:, tile].reshape(SPAN, 2 * LANES),
            ],
            axis=1,
        )
        for tile in range(GROUP_TILES)
    ]
    for local in range(GROUP_ORDERS):
        rows = slice(local * degrees, (local + 1) * degrees)
        mixed = pair_sum(local, s_ref, tiles).astype(BF16)
        mixed_ref[rows, :] = mixed
        scaled = dot_nt(mixed, mix_ref[...])
        coeffs = (gain_ref[LANES * group :, :] * scaled).astype(BF16)
        coeff_ref[packed_rows(degrees, local), :] = coeffs[DEVICES * local :]


def packed_rows(degrees, local):
    first = sum(degrees - DEVICES * other for other in range(local))
    return slice(first, first + degrees - DEVICES * local)


def spectral_backward(group, small, large, s, gain, mix, after=()):
    degrees = degrees_of(group)
    rows = GROUP_ORDERS * degrees
    packed = packed_rows(degrees, GROUP_ORDERS - 1).stop
    return call(
        functools.partial(backward_kernel, group),
        (small, large, s, gain, mix),
        [
            pl.BlockSpec((DEVICES, GROUP_TILES, TILE, lanes), lambda b: (0, group, 0, 0))
            for lanes in (LANES, 2 * LANES)
        ]
        + [whole(s.shape), whole(gain.shape), whole(mix.shape)],
        [whole((rows, 2 * C)), whole((packed, 2 * C))],
        [
            jax.ShapeDtypeStruct((rows, 2 * C), BF16),
            jax.ShapeDtypeStruct((packed, 2 * C), BF16),
        ],
        (1,),
        2 * rows * 2 * C * (768 + 384),
        after,
        name=f"spectral_backward_{group}",
    )


def hold_kernel(value_ref, out_ref):
    pass


def hold(value, after):
    held = pl.BlockSpec(memory_space=pl.ANY)
    return call(
        hold_kernel,
        (value,),
        [held],
        held,
        jax.ShapeDtypeStruct(value.shape, value.dtype),
        (1,),
        0,
        after,
        aliases={0: 0},
        name="hold",
    )


def synthesis_kernel(group, packed_ref, at_ref, *rest):
    out_ref, coeff_ref = rest[-2:]
    rest = rest[:-1]
    degrees = degrees_of(group)
    for local in range(GROUP_ORDERS):
        first = local * degrees
        skipped = DEVICES * local
        if local:
            coeff_ref[first : first + skipped, :] = jnp.zeros((skipped, 2 * C), BF16)
        coeff_ref[first + skipped : first + degrees, :] = packed_ref[
            packed_rows(degrees, local), :
        ]
    for tile in range(GROUP_TILES):
        first = coeff_ref[tile * degrees : (tile + 1) * degrees, :]
        second = coeff_ref[(tile + 1) * degrees : (tile + 2) * degrees, :]
        out = dot(at_ref[2 * tile], first) + dot(at_ref[2 * tile + 1], second)
        out_ref[:, tile] = out.astype(BF16).reshape(DEVICES, TILE, 2 * C)
    if len(rest) == 2:
        out_ref[:, GROUP_TILES] = rest[0][...]


def analysis_back(group, coeffs, at, tiles, extra=(), after=()):
    degrees = degrees_of(group)
    rows = GROUP_ORDERS * degrees
    block = GROUP_TILES + len(extra)
    return call(
        functools.partial(synthesis_kernel, group),
        (coeffs, at, *extra),
        [whole(coeffs.shape), whole(at.shape)] + [whole(value.shape) for value in extra],
        whole((DEVICES, block, TILE, 2 * C)),
        jax.ShapeDtypeStruct((DEVICES, tiles, TILE, 2 * C), BF16),
        (1,),
        2 * rows * 2 * C * 768,
        after,
        scratch_shapes=[pltpu.VMEM((rows, 2 * C), BF16)],
        name=f"analysis_back_{group}",
    )


def fold(tile):
    return tile + pltpu.roll(tile, HALF, 1)


def weight_kernel(*refs):
    scaled_refs, mixed_refs = refs[:3], refs[3:6]
    mix_ref, factor_ref, proj_small, proj_large, out_ref, gain, packed, spaced = refs[6:]
    block = None
    for scaled_ref, mixed_ref in zip(scaled_refs, mixed_refs):
        part = lax.dot_general(
            scaled_ref[...], mixed_ref[...], (((0,), (0,)), ((), ())), preferred_element_type=F32
        )
        block = part if block is None else block + part
    for group in range(GROUPS):
        degrees = degrees_of(group)
        total = None
        for local in range(GROUP_ORDERS):
            rows = slice(local * degrees, (local + 1) * degrees)
            part = dot_nt(mixed_refs[group][rows, :], mix_ref[...])
            part = part * scaled_refs[group][rows, :].astype(F32)
            total = part if total is None else total + part
        if group == 0:
            gain[...] = total
        else:
            gain[LANES * group :, :] += total
    gain[...] = gain[...] / factor_ref[...]
    low = half_lanes((HALF, LANES))
    low_gain = half_lanes((C, LANES))
    low_proj = half_lanes((C // 2, LANES))
    for index in range(GROUPS):
        lanes = slice(index * LANES, (index + 1) * LANES)
        for row_block in range(GROUPS):
            start = row_block * LANES
            first = block[start : start + HALF, lanes]
            second = pltpu.roll(block[start + HALF : start + LANES, lanes], HALF, 1)
            packed[index, row_block * HALF : (row_block + 1) * HALF, :] = jnp.where(
                low, first + second, first - second
            )
        packed[index, C : 2 * C, :] = jnp.where(
            low_gain, fold(gain[:C, lanes]), fold(gain[C:, lanes])
        )
        if index == 0:
            proj = fold(proj_small[...])
        else:
            proj = fold(proj_large[:, (index - 1) * LANES : index * LANES])
        packed[index, 2 * C :, :] = jnp.where(low_proj, proj[: C // 2], proj[C // 2 :])
        for row in range(TILE - 1):
            spaced[index, pl.ds(row, DEVICES, stride=TILE), :] = packed[
                index, row * DEVICES : (row + 1) * DEVICES, :
            ]
        spaced[index, pl.ds(TILE - 1, DEVICES, stride=TILE), :] = jnp.zeros((DEVICES, LANES), F32)
        out_ref[:, :, lanes] = spaced[index].astype(BF16).reshape(DEVICES, TILE, LANES)


def weight_grads(scaleds, mixeds, mix, gain, proj_small, proj_large, after=()):
    out = (DEVICES, TILE, 2 * C)
    inputs = (*scaleds, *mixeds, mix, gain, proj_small, proj_large)
    return call(
        weight_kernel,
        inputs,
        [whole(value.shape) for value in inputs],
        whole(out),
        jax.ShapeDtypeStruct(out, BF16),
        (1,),
        sum(4 * value.shape[0] * 2 * C * 2 * C for value in scaleds),
        after,
        scratch_shapes=[
            pltpu.VMEM((MODES, 2 * C), F32),
            pltpu.VMEM((GROUPS, 15 * DEVICES, LANES), F32),
            pltpu.VMEM((GROUPS, TILE * DEVICES, LANES), F32),
        ],
        name="weight_grads",
    )


def total_kernel(recv_ref, payload_ref, out_ref):
    total = jnp.sum(recv_ref[:, 0].astype(F32), axis=0)
    out_ref[:, 0] = jnp.broadcast_to(total.astype(BF16)[None], (DEVICES, TILE, 2 * C))


def attach_totals(recv, payload):
    spec = pl.BlockSpec((DEVICES, 1, TILE, 2 * C), lambda b: (0, GROUP_TILES, 0, 0))
    return call(
        total_kernel,
        (recv, payload),
        [spec, pl.BlockSpec(memory_space=pl.ANY)],
        spec,
        jax.ShapeDtypeStruct(payload.shape, BF16),
        (1,),
        DEVICES * TILE * 2 * C,
        aliases={1: 0},
        name="attach_totals",
    )


def unpack_kernel(recv_ref, proj_ref, mix_ref, gain_ref, spaced, packed):
    grid_scale = 1.0 / math.sqrt(NLAT * NLON)
    mode_scale = 1.0 / math.sqrt(MODES)
    lows, highs = [], []
    for index in range(GROUPS):
        lanes = slice(index * LANES, (index + 1) * LANES)
        spaced[index] = recv_ref[:, 0, :, lanes].reshape(DEVICES * TILE, LANES).astype(F32)
        for row in range(TILE - 1):
            packed[index, row * DEVICES : (row + 1) * DEVICES, :] = spaced[
                index, pl.ds(row, DEVICES, stride=TILE), :
            ]
        lows.append(packed[index, :, :HALF])
        highs.append(packed[index, :, HALF:])
    low = jnp.concatenate(lows, axis=1)
    high = jnp.concatenate(highs, axis=1)
    mix_ref[0] = grid_scale * low[:C]
    mix_ref[1] = grid_scale * high[:C]
    gain = jnp.concatenate([low[C : 2 * C], high[C : 2 * C]], axis=0)
    gain_ref[...] = mode_scale * gain.T
    proj = jnp.concatenate([low[2 * C :], high[2 * C :]], axis=0)
    proj_ref[...] = grid_scale * proj.T


def unpack_totals(recv, after=()):
    shapes = ((C, C), (2, C, C), (C, MODES))
    return call(
        unpack_kernel,
        (recv,),
        [pl.BlockSpec((DEVICES, 1, TILE, 2 * C), lambda b: (0, GROUP_TILES, 0, 0))],
        [whole(shape) for shape in shapes],
        [jax.ShapeDtypeStruct(shape, F32) for shape in shapes],
        (1,),
        4 * MODES * C,
        after,
        scratch_shapes=[
            pltpu.VMEM((GROUPS, TILE * DEVICES, LANES), F32),
            pltpu.VMEM((GROUPS, 15 * DEVICES, LANES), F32),
        ],
        name="unpack_totals",
    )


def field_kernel(recv_ref, table_ref, base_ref, out_ref, scratch):
    step = pl.program_id(0)
    orders = DEVICES * GROUP_ORDERS
    rows = orders * LAT_LOCAL

    @pl.when(step == 0)
    def _():
        for index in range(GROUPS):
            lanes = slice(index * LANES, (index + 1) * LANES)
            values = recv_ref[:, :, :, lanes].astype(F32)
            scratch[index] = values.reshape(rows, LANES)

    lefts = []
    for inner in range(4):
        real, imag = [], []
        for index in range(GROUPS):
            values = scratch[index, pl.ds(step * 4 + inner, orders, stride=LAT_LOCAL), :]
            turned = values.T.astype(BF16)
            real.append(turned[:HALF])
            imag.append(turned[HALF:])
        lefts.append(
            jnp.concatenate(
                [jnp.concatenate(real, axis=0), jnp.concatenate(imag, axis=0)], axis=1
            )
        )
    product = dot(jnp.concatenate(lefts, axis=0), table_ref[...])
    for inner in range(4):
        total = base_ref[inner].astype(F32) + product[inner * C : (inner + 1) * C]
        out_ref[inner] = total.astype(out_ref.dtype)


def field_stage(recv, table, base, kind, after=()):
    rows = DEVICES * GROUP_ORDERS * LAT_LOCAL
    block = pl.BlockSpec((4, C, NLON), lambda b: (b, 0, 0))
    return call(
        field_kernel,
        (recv, table, base),
        [
            pl.BlockSpec((DEVICES, GROUP_TILES, TILE, 2 * C), lambda b: (0, 0, 0, 0)),
            whole(table.shape),
            block,
        ],
        block,
        jax.ShapeDtypeStruct((LAT_LOCAL, C, NLON), kind),
        (LAT_LOCAL // 4,),
        2 * LAT_LOCAL * C * NLON * 256,
        after,
        scratch_shapes=[pltpu.VMEM((GROUPS, rows, LANES), F32)],
        name="field_stage",
    )


def exchange(payload):
    tiles, lanes = payload.shape[1], payload.shape[3]
    flat = payload.reshape(DEVICES, tiles * TILE, lanes)
    moved = lax.all_to_all(flat, "lat", split_axis=0, concat_axis=0, tiled=True)
    return moved.reshape(DEVICES, tiles, TILE, lanes)


def shards(saved_input, incoming, spectral_gain, mix_weight, proj_weight):
    device = lax.axis_index("lat")
    section_count = lax.axis_size("section")
    shift = [(source, (source - 1) % section_count) for source in range(section_count)]

    forward_all = forward_rows(0, GROUPS)
    forward = [forward_rows(group, 1) for group in range(GROUPS)]
    inverse_np = inverse_rows()
    inverse = jnp.asarray(inverse_np)
    inverse_turned = jnp.asarray(np.ascontiguousarray(inverse_np.T))
    spread, spread_turned = spread_tables()
    lat = jnp.asarray(latitude_rows())
    starts, numbers = log_starts()
    start = lax.dynamic_index_in_dim(jnp.asarray(starts), device, 0, keepdims=False)
    order = lax.dynamic_index_in_dim(jnp.asarray(numbers), device, 0, keepdims=False)

    field = saved_input[0]
    upstream = incoming[0]
    upstream_next = lax.ppermute(upstream, "section", shift)
    turned = jnp.swapaxes(upstream, 1, 2)
    gain = jnp.broadcast_to(
        spectral_gain[0].reshape(MODES, GROUPS, 1, HALF), (MODES, GROUPS, 2, HALF)
    ).reshape(MODES, 2 * C)
    real, imag = mix_weight[0, 0], mix_weight[0, 1]
    mix = (
        jnp.stack([jnp.stack([real, imag]), jnp.stack([-imag, real])])
        .reshape(2, 2, GROUPS, HALF, GROUPS, HALF)
        .transpose(2, 0, 3, 4, 1, 5)
        .reshape(2 * C, 2 * C)
    )
    proj = jnp.broadcast_to(
        proj_weight[0].T.reshape(C, GROUPS, 1, HALF), (C, GROUPS, 2, HALF)
    ).reshape(C, 2 * C)

    rows = MODES * LAT_LOCAL
    spectrum = spectrum_rows(field, forward_all)
    recv = exchange(spectrum.reshape(DEVICES, TILES, TILE, 2 * C))
    tables = legendre_tables(start, order, lat, spread, spread_turned, (spectrum,))
    behind = [tables[4 * group + 2 : 4 * group + 4] for group in range(GROUPS)]
    *scaleds, payload = spectral_forward(
        recv, tables[0::4], tables[1::4], gain, mix, (turned, proj)
    )
    recv = exchange(payload).reshape(rows, 2 * C)
    small_rows, proj_small = grid_stage(
        0, 1, recv, upstream, turned, proj, inverse, inverse_turned, (upstream_next,)
    )
    small = exchange(small_rows.reshape(DEVICES, TILES, TILE, LANES))
    large, proj_large = grid_stage(
        1, 2, recv, upstream, turned, proj, inverse, inverse_turned, (small_rows,)
    )
    large = exchange(large.reshape(DEVICES, TILES, TILE, 2 * LANES))

    mixeds, moved = [None] * GROUPS, [None] * GROUPS
    mixeds[2], coeffs_2 = spectral_backward(2, small, large, behind[2][0], gain, mix)
    moved[2] = lax.ppermute(coeffs_2, "section", shift)
    mixeds[1], coeffs_1 = spectral_backward(1, small, large, behind[1][0], gain, mix, (coeffs_2,))
    moved[1] = lax.ppermute(hold(coeffs_1, (moved[2],)), "section", shift)

    out_2 = analysis_back(2, moved[2], behind[2][1], GROUP_TILES, after=(coeffs_1,))
    mixeds[0], coeffs_0 = spectral_backward(0, small, large, behind[0][0], gain, mix, (out_2,))
    moved[0] = lax.ppermute(coeffs_0, "section", shift)
    recv_2 = exchange(out_2)
    partial_grads = weight_grads(
        scaleds, mixeds, mix, gain, proj_small, proj_large, after=(out_2, coeffs_0)
    )
    out_1 = analysis_back(1, moved[1], behind[1][1], GROUP_TILES + 1, (partial_grads,))
    recv_1 = exchange(out_1)
    out_0 = analysis_back(0, moved[0], behind[0][1], GROUP_TILES + 1, after=(out_1,))
    base = field_stage(recv_2, forward[2], upstream_next, F32, (out_0,))
    out_0 = attach_totals(recv_1, out_0)
    recv_0 = exchange(out_0)
    base = field_stage(recv_1, forward[1], base, F32, (out_0,))
    grad_w2, grad_mix, grad_gain = unpack_totals(recv_0)
    received = field_stage(recv_0, forward[0], base, BF16)
    return (
        received[None],
        grad_w2[None],
        grad_mix[None],
        jnp.swapaxes(grad_gain, 0, 1)[None],
    )


def solution(mesh):
    in_specs = (
        P("section", "lat", None, None),
        P("section", "lat", None, None),
        P("section", None, None),
        P("section", None, None, None),
        P("section", None, None),
    )
    out_specs = (
        P("section", "lat", None, None),
        P("section", None, None),
        P("section", None, None, None),
        P("section", None, None),
    )
    return jax.shard_map(shards, mesh=mesh, in_specs=in_specs, out_specs=out_specs, check_vma=False)
```

```python
import functools
import math

import jax
import jax.numpy as jnp
import ml_dtypes
import numpy as np
from jax import lax
from jax.experimental import pallas as pl
from jax.experimental.pallas import tpu as pltpu
from jax.sharding import PartitionSpec as P

NLAT = 384
NLON = 768
MODES = 384
C = 192
DEVICES = 32
LAT_LOCAL = 12
ORDERS = 12
GROUPS = 3
GROUP_ORDERS = 4
HALF = 64
LANES = 128
TILE = 16
TILES = 9
GROUP_TILES = 3
SPAN = DEVICES * TILE
LAT_BLOCKS = 4
BLOCK_LATS = NLAT // LAT_BLOCKS
VMEM_LIMIT = 56 * 1024 * 1024
F32 = jnp.float32
BF16 = jnp.bfloat16
NT = (((1,), (1,)), ((), ()))

PAIRS = ((0, 0), (1, 0), (1, 1), (2, 1), (2, 2), (3, 2))


def degrees_of(group):
    return MODES - LANES * group


def half_lanes(shape):
    return lax.broadcasted_iota(jnp.int32, shape, 1) < HALF


def dot(left, right):
    return jnp.dot(left, right, preferred_element_type=F32)


def dot_nt(left, right):
    return lax.dot_general(left, right, NT, preferred_element_type=F32)


def whole(shape):
    return pl.BlockSpec(shape, lambda *_: (0,) * len(shape))


def call(kernel, inputs, in_specs, out_specs, out_shape, grid, after=(), aliases=None, **extra):
    count = len(inputs)

    def body(*refs):
        kernel(*refs[:count], *refs[count + len(after) :])

    return pl.pallas_call(
        body,
        grid=grid,
        in_specs=list(in_specs) + [pl.BlockSpec(memory_space=pl.ANY)] * len(after),
        out_specs=out_specs,
        out_shape=out_shape,
        input_output_aliases=aliases or {},
        compiler_params=pltpu.CompilerParams(vmem_limit_bytes=VMEM_LIMIT),
        cost_estimate=pl.CostEstimate(flops=1, bytes_accessed=1, transcendentals=0),
        **extra,
    )(*inputs, *after)


def order_rows(first, count):
    device = np.arange(DEVICES)[:, None]
    local = np.arange(GROUP_ORDERS * count)[None, :] + GROUP_ORDERS * first
    return (DEVICES * local + device).reshape(-1)


def fourier_rows(orders):
    phase = (orders[:, None] * np.arange(NLON)[None, :]) % NLON
    angle = phase * (2.0 * math.pi / NLON)
    return np.cos(angle), -np.sin(angle)


def forward_rows(first, count):
    cosine, sine = fourier_rows(order_rows(first, count))
    table = np.concatenate([cosine, sine], axis=0)
    return jnp.asarray(table.astype(np.float32).astype(ml_dtypes.bfloat16))


def inverse_rows():
    device = np.arange(DEVICES)[:, None]
    orders = (DEVICES * np.arange(ORDERS)[None, :] + device).reshape(-1)
    factor = np.where(orders == 0, 1.0, 2.0)[:, None] / NLON
    cosine, sine = fourier_rows(orders)
    table = np.concatenate([factor * cosine, factor * sine], axis=0)
    return table.astype(np.float32).astype(ml_dtypes.bfloat16)


def spread_tables():
    rows = np.arange(LANES)
    source, inner = rows // TILE, rows % TILE
    tables = np.zeros((len(PAIRS), LANES, LANES), np.float32)
    for index, (order, tile) in enumerate(PAIRS):
        lat = TILE * tile + inner - LAT_LOCAL * order
        valid = (lat >= 0) & (lat < LAT_LOCAL)
        tables[index, (source * LAT_LOCAL + lat)[valid], rows[valid]] = 1.0
    flat = jnp.asarray(tables.astype(ml_dtypes.bfloat16))
    turned = jnp.asarray(np.swapaxes(tables, 1, 2).astype(ml_dtypes.bfloat16))
    return flat, turned


def log_starts():
    table = np.zeros((DEVICES, TILE, LANES), np.float32)
    numbers = np.zeros((DEVICES, TILE, LANES), np.float32)
    for device in range(DEVICES):
        for local in range(ORDERS):
            order = DEVICES * local + device
            numbers[device, local] = order
            table[device, local] = 0.5 * math.log((2.0 * order + 1.0) / 2.0) + 0.5 * (
                math.lgamma(order + 0.5) - math.lgamma(0.5) - math.lgamma(order + 1.0)
            )
    return table, numbers


def latitude_rows():
    colatitude = (np.arange(NLAT) + 0.5) * (math.pi / NLAT)
    harmonic = np.arange(1, NLAT // 2 + 1)
    terms = np.cos(2.0 * harmonic[None, :] * colatitude[:, None]) / (4.0 * harmonic**2 - 1.0)
    weight = 2.0 / NLAT * (1.0 - 2.0 * np.sum(terms, axis=1))
    rows = np.stack([np.cos(colatitude), np.log(np.sin(colatitude)), weight])
    rows = np.concatenate([rows, np.zeros((5, NLAT))]).reshape(8, LAT_BLOCKS, BLOCK_LATS)
    rows = np.pad(rows, ((0, 0), (0, 0), (0, LANES - BLOCK_LATS)))
    return rows.reshape(8, SPAN).astype(np.float32)


def legendre_rows(start_ref, order_ref, lat_ref, rows_ref):
    order = jnp.concatenate([order_ref[...]] * LAT_BLOCKS, axis=1)
    cosine = jnp.broadcast_to(lat_ref[0:1, :], (TILE, SPAN))
    log_sin = jnp.broadcast_to(lat_ref[1:2, :], (TILE, SPAN))
    log_start = jnp.concatenate([start_ref[...]] * LAT_BLOCKS, axis=1) + order * log_sin
    narrow = order_ref[...]
    narrow_square = narrow * narrow
    second_factor = jnp.concatenate([jnp.sqrt(2.0 * narrow + 3.0)] * LAT_BLOCKS, axis=1)
    zeros = jnp.zeros((TILE, SPAN), F32)

    def block(index, state):
        previous, current, log_scale = state
        scale = jnp.exp(log_scale)
        for inner in range(16):
            row = index * 16 + inner
            degree = row.astype(F32)
            lower = degree - 1.0
            up = jnp.sqrt(
                jnp.maximum(4.0 * degree * degree - 1.0, 1.0)
                / jnp.maximum(degree * degree - narrow_square, 1.0)
            )
            down = jnp.sqrt(
                jnp.maximum(lower * lower - narrow_square, 0.0)
                / jnp.maximum(4.0 * lower * lower - 1.0, 1.0)
            )
            up = jnp.concatenate([up] * LAT_BLOCKS, axis=1)
            down = jnp.concatenate([down] * LAT_BLOCKS, axis=1)
            general = up * (cosine * current - down * previous)
            second = second_factor * cosine * current
            new_row = jnp.where(
                degree == order,
                1.0,
                jnp.where(
                    degree == order + 1.0, second, jnp.where(degree > order + 1.0, general, 0.0)
                ),
            )
            scaled = new_row * scale
            for part in range(LAT_BLOCKS):
                rows_ref[part, row] = scaled[:, part * LANES : (part + 1) * LANES]
            previous, current = current, new_row
        largest = jnp.maximum(jnp.abs(previous), jnp.abs(current))
        largest = jnp.where(largest > 0.0, largest, 1.0)
        return previous / largest, current / largest, log_scale + jnp.log(largest)

    lax.fori_loop(0, MODES // 16, block, (zeros, zeros, log_start))


def table_kernel(start_ref, order_ref, lat_ref, flat_ref, turned_ref, *rest):
    outs, rows_ref, buffers, sems = rest[:12], rest[12], rest[13:25], rest[25]
    legendre_rows(start_ref, order_ref, lat_ref, rows_ref)
    copies = []
    for group in range(GROUPS):
        ahead_flat, ahead_turned, behind_flat, behind_turned = buffers[4 * group : 4 * group + 4]

        def part_step(part, carry):
            lats = pl.ds(pl.multiple_of(part * LANES, LANES), LANES)
            weight = lat_ref[2:3, lats]
            for local in range(GROUP_ORDERS):
                legendre = rows_ref[part, LANES * group :, GROUP_ORDERS * group + local, :]
                synthesis = legendre.astype(BF16)
                analysis = (weight * legendre).astype(BF16)
                pairs = [index for index, (order, _) in enumerate(PAIRS) if order == local]
                flat = jnp.concatenate([flat_ref[index] for index in pairs], axis=1)
                turned = jnp.concatenate([turned_ref[index] for index in pairs], axis=0)
                products = (
                    dot(analysis, flat).astype(BF16),
                    dot_nt(turned, synthesis).astype(BF16),
                    dot(synthesis, flat).astype(BF16),
                    dot_nt(turned, analysis).astype(BF16),
                )
                for place, index in enumerate(pairs):
                    cut = slice(place * LANES, (place + 1) * LANES)
                    ahead_flat[index, :, lats] = products[0][:, cut]
                    ahead_turned[index, lats, :] = products[1][cut]
                    behind_flat[index, :, lats] = products[2][:, cut]
                    behind_turned[index, lats, :] = products[3][cut]
            return carry

        lax.fori_loop(0, LAT_BLOCKS, part_step, 0)
        for place in range(4):
            at = 4 * group + place
            copy = pltpu.make_async_copy(buffers[at], outs[at], sems.at[at])
            copy.start()
            copies.append(copy)
    for copy in copies:
        copy.wait()


def legendre_tables(start, order, lat, flat, turned, after):
    shapes = []
    for group in range(GROUPS):
        degrees = degrees_of(group)
        shapes += [(len(PAIRS), degrees, SPAN), (len(PAIRS), SPAN, degrees)] * 2
    inputs = (start, order, lat, flat, turned)
    return call(
        table_kernel,
        inputs,
        [whole(value.shape) for value in inputs],
        [pl.BlockSpec(memory_space=pl.ANY)] * len(shapes),
        [jax.ShapeDtypeStruct(shape, BF16) for shape in shapes],
        (1,),
        after,
        scratch_shapes=[pltpu.VMEM((LAT_BLOCKS, MODES, TILE, LANES), F32)]
        + [pltpu.VMEM(shape, BF16) for shape in shapes]
        + [pltpu.SemaphoreType.DMA((len(shapes),))],
        name="legendre_tables",
    )


def blocks_of(value):
    return [value[:, index * HALF : (index + 1) * HALF] for index in range(GROUPS)]


def interleave(first, second):
    pairs = zip(blocks_of(first), blocks_of(second))
    return jnp.concatenate([block for pair in pairs for block in pair], axis=1)


def prepare_kernel(gain_ref, mix_ref, proj_ref, gain_out, mix_out, proj_out):
    gain = gain_ref[...].T
    gain_out[...] = interleave(gain, gain)
    real, imag = mix_ref[0].astype(F32), mix_ref[1].astype(F32)
    upper, lower = interleave(real, imag), interleave(-imag, real)
    for index in range(GROUPS):
        rows = slice(index * HALF, (index + 1) * HALF)
        start = index * LANES
        mix_out[start : start + HALF, :] = upper[rows].astype(BF16)
        mix_out[start + HALF : start + LANES, :] = lower[rows].astype(BF16)
    proj = proj_ref[...].astype(F32).T
    proj_out[...] = interleave(proj, proj).astype(BF16)


def prepare(gain, mix, proj, after):
    shapes = ((MODES, 2 * C), (2 * C, 2 * C), (C, 2 * C))
    kinds = (F32, BF16, BF16)
    return call(
        prepare_kernel,
        (gain, mix, proj),
        [whole(gain.shape), whole(mix.shape), whole(proj.shape)],
        [whole(shape) for shape in shapes],
        [jax.ShapeDtypeStruct(shape, kind) for shape, kind in zip(shapes, kinds)],
        (1,),
        after,
        name="prepare",
    )


def spectrum_kernel(field_ref, table_ref, out_ref, scratch):
    step = pl.program_id(0)
    rows = table_ref.shape[0] // 2
    low = half_lanes((rows, LANES))
    for inner in range(4):
        product = dot_nt(table_ref[...], field_ref[inner])
        real, imag = product[:rows], product[rows:]
        real_a, imag_a = real[:, :LANES], imag[:, :LANES]
        tiles = (
            jnp.where(low, real_a, pltpu.roll(imag_a, HALF, 1)),
            jnp.where(low, pltpu.roll(real_a, HALF, 1), imag_a),
            jnp.concatenate([real[:, LANES:], imag[:, LANES:]], axis=1),
        )
        for index, tile in enumerate(tiles):
            scratch[index, pl.ds(step * 4 + inner, rows, stride=LAT_LOCAL), :] = tile

    @pl.when(step == LAT_LOCAL // 4 - 1)
    def _():
        for index in range(GROUPS):
            out_ref[:, index * LANES : (index + 1) * LANES] = scratch[index].astype(BF16)


def spectrum_rows(field, table, after=()):
    rows = table.shape[0] // 2 * LAT_LOCAL
    return call(
        spectrum_kernel,
        (field, table),
        [pl.BlockSpec((4, C, NLON), lambda b: (b, 0, 0)), whole(table.shape)],
        whole((rows, 2 * C)),
        jax.ShapeDtypeStruct((rows, 2 * C), BF16),
        (LAT_LOCAL // 4,),
        after,
        scratch_shapes=[pltpu.VMEM((GROUPS, rows, LANES), F32)],
        name="spectrum_rows",
    )


def pair_sum(local, table_ref, tiles):
    total = None
    for index, (order, tile) in enumerate(PAIRS):
        if order == local:
            part = dot(table_ref[index], tiles[tile])
            total = part if total is None else total + part
    return total


def spectral_kernel(recv_ref, *refs):
    a_refs, st_refs = refs[0:3], refs[3:6]
    gain_ref, mix_ref = refs[6:8]
    scaled_outs, payload_ref = refs[8:11], refs[11]
    recv, payload = refs[12:14]
    a_buffers, st_buffers, scaled_buffers = refs[14:17], refs[17:20], refs[20:23]
    in_sems, out_sems = refs[23:25]
    schedule = (2, 0, 1)
    arrivals, departures = {}, []
    for group in schedule:
        tiles = pl.ds(GROUP_TILES * group, GROUP_TILES)
        arrivals[group] = [
            pltpu.make_async_copy(recv_ref.at[:, tiles], recv.at[group], in_sems.at[group, 0]),
            pltpu.make_async_copy(a_refs[group], a_buffers[group], in_sems.at[group, 1]),
            pltpu.make_async_copy(st_refs[group], st_buffers[group], in_sems.at[group, 2]),
        ]
        for copy in arrivals[group]:
            copy.start()
    for group in schedule:
        degrees = degrees_of(group)
        for copy in arrivals[group]:
            copy.wait()
        tiles = [recv[group, :, tile].reshape(SPAN, 2 * C) for tile in range(GROUP_TILES)]
        mixed = []
        for local in range(GROUP_ORDERS):
            rows = slice(local * degrees, (local + 1) * degrees)
            coef = pair_sum(local, a_buffers[group], tiles)
            scaled = (gain_ref[LANES * group :, :] * coef).astype(BF16)
            scaled_buffers[group][rows, :] = scaled
            mixed.append(dot(scaled, mix_ref[...]).astype(BF16))
        for tile in range(GROUP_TILES):
            grid = dot(st_buffers[group][2 * tile], mixed[tile]) + dot(
                st_buffers[group][2 * tile + 1], mixed[tile + 1]
            )
            payload[group, :, tile] = grid.astype(BF16).reshape(DEVICES, TILE, 2 * C)
        tiles = pl.ds(GROUP_TILES * group, GROUP_TILES)
        copies = (
            pltpu.make_async_copy(
                payload.at[group], payload_ref.at[:, tiles], out_sems.at[group, 0]
            ),
            pltpu.make_async_copy(
                scaled_buffers[group], scaled_outs[group], out_sems.at[group, 1]
            ),
        )
        for copy in copies:
            copy.start()
            departures.append(copy)
    for copy in departures:
        copy.wait()


def spectral_forward(recv, a, st, gain, mix, after=()):
    shapes = [(GROUP_ORDERS * degrees_of(group), 2 * C) for group in range(GROUPS)]
    held = pl.BlockSpec(memory_space=pl.ANY)
    slots = (GROUPS, DEVICES, GROUP_TILES, TILE, 2 * C)
    return call(
        spectral_kernel,
        (recv, *a, *st, gain, mix),
        [held] * 7 + [whole(gain.shape), whole(mix.shape)],
        [held] * 4,
        [jax.ShapeDtypeStruct(shape, BF16) for shape in shapes]
        + [jax.ShapeDtypeStruct(recv.shape, BF16)],
        (1,),
        after,
        scratch_shapes=[pltpu.VMEM(slots, BF16), pltpu.VMEM(slots, BF16)]
        + [pltpu.VMEM(value.shape, BF16) for value in a]
        + [pltpu.VMEM(value.shape, BF16) for value in st]
        + [pltpu.VMEM(shape, BF16) for shape in shapes]
        + [pltpu.SemaphoreType.DMA((GROUPS, 3)), pltpu.SemaphoreType.DMA((GROUPS, 2))],
        name="spectral_forward",
    )


def grid_kernel(
    recv_ref, up_ref, turned_ref, proj_ref, table_ref, turned_table_ref,
    out_ref, grad_ref, scratch, out_scratch, act_scratch, pre_scratch,
):
    step = pl.program_id(1)
    low = half_lanes((MODES, LANES))
    block = 128

    @pl.when(step == 0)
    def _():
        scratch[...] = recv_ref[...].astype(F32)
        grad_ref[...] = jnp.zeros_like(grad_ref)

    columns = []
    for pair in range(2):
        first = scratch[pl.ds(step * 4 + 2 * pair, MODES, stride=LAT_LOCAL), :]
        second = scratch[pl.ds(step * 4 + 2 * pair + 1, MODES, stride=LAT_LOCAL), :]
        real = jnp.where(low, first, pltpu.roll(second, HALF, 1))
        imag = jnp.where(low, pltpu.roll(first, HALF, 1), second)
        columns.append(jnp.concatenate([real, imag], axis=0).astype(BF16))
    modes = jnp.concatenate(columns, axis=1)
    low_block = half_lanes((block, LANES))
    for part in range(NLON // block):
        rows = slice(part * block, (part + 1) * block)
        pre = dot(turned_table_ref[rows, :], modes)
        grad_act = jnp.concatenate(
            [
                jnp.where(
                    low_block,
                    dot(turned_ref[2 * pair, rows, :], proj_ref[...]),
                    dot(turned_ref[2 * pair + 1, rows, :], proj_ref[...]),
                )
                for pair in range(2)
            ],
            axis=1,
        )
        cumulative = 0.5 * (1.0 + lax.erf(pre * (1.0 / math.sqrt(2.0))))
        slope = cumulative + pre * jnp.exp(-0.5 * pre * pre) * (1.0 / math.sqrt(2.0 * math.pi))
        act_scratch[rows, :] = (pre * cumulative).astype(BF16)
        pre_scratch[rows, :] = (grad_act * slope).astype(BF16)
    low_grad = half_lanes((C, LANES))
    for pair in range(2):
        lanes = slice(pair * LANES, (pair + 1) * LANES)
        act = act_scratch[:, lanes]
        grad_ref[...] += jnp.where(
            low_grad, dot(up_ref[2 * pair], act), dot(up_ref[2 * pair + 1], act)
        )
    grad_modes = dot(table_ref[...], pre_scratch[...])
    for pair in range(2):
        lanes = slice(pair * LANES, (pair + 1) * LANES)
        real, imag = grad_modes[:MODES, lanes], grad_modes[MODES:, lanes]
        out_scratch[pl.ds(step * 4 + 2 * pair, MODES, stride=LAT_LOCAL), :] = jnp.where(
            low, real, pltpu.roll(imag, HALF, 1)
        )
        out_scratch[pl.ds(step * 4 + 2 * pair + 1, MODES, stride=LAT_LOCAL), :] = jnp.where(
            low, pltpu.roll(real, HALF, 1), imag
        )

    @pl.when(step == LAT_LOCAL // 4 - 1)
    def _():
        out_ref[...] = out_scratch[...].astype(BF16)


def grid_stage(first, blocks, recv, up, turned, proj, table, turned_table, after=()):
    rows = MODES * LAT_LOCAL
    lanes_spec = pl.BlockSpec((rows, LANES), lambda q, b: (0, q))
    grad_spec = pl.BlockSpec((C, LANES), lambda q, b: (0, q))
    return call(
        grid_kernel,
        (recv, up, turned, proj, table, turned_table),
        [
            pl.BlockSpec((rows, LANES), lambda q, b: (0, q + first)),
            pl.BlockSpec((4, C, NLON), lambda q, b: (b, 0, 0)),
            pl.BlockSpec((4, NLON, C), lambda q, b: (b, 0, 0)),
            pl.BlockSpec((C, LANES), lambda q, b: (0, q + first)),
            whole(table.shape),
            whole(turned_table.shape),
        ],
        [lanes_spec, grad_spec],
        [
            jax.ShapeDtypeStruct((rows, LANES * blocks), BF16),
            jax.ShapeDtypeStruct((C, LANES * blocks), F32),
        ],
        (blocks, LAT_LOCAL // 4),
        after,
        scratch_shapes=[
            pltpu.VMEM((rows, LANES), F32),
            pltpu.VMEM((rows, LANES), F32),
            pltpu.VMEM((NLON, 2 * LANES), BF16),
            pltpu.VMEM((NLON, 2 * LANES), BF16),
        ],
        name=f"grid_stage_{blocks}",
    )


def backward_kernel(group, small_ref, large_ref, s_ref, gain_ref, mix_ref, mixed_ref, coeff_ref):
    degrees = degrees_of(group)
    tiles = [
        jnp.concatenate(
            [
                small_ref[:, tile].reshape(SPAN, LANES),
                large_ref[:, tile].reshape(SPAN, 2 * LANES),
            ],
            axis=1,
        )
        for tile in range(GROUP_TILES)
    ]
    for local in range(GROUP_ORDERS):
        rows = slice(local * degrees, (local + 1) * degrees)
        mixed = pair_sum(local, s_ref, tiles).astype(BF16)
        mixed_ref[rows, :] = mixed
        scaled = dot_nt(mixed, mix_ref[...])
        coeffs = (gain_ref[LANES * group :, :] * scaled).astype(BF16)
        coeff_ref[packed_rows(degrees, local), :] = coeffs[DEVICES * local :]


def packed_rows(degrees, local):
    first = sum(degrees - DEVICES * other for other in range(local))
    return slice(first, first + degrees - DEVICES * local)


def spectral_backward(group, small, large, s, gain, mix, after=()):
    degrees = degrees_of(group)
    rows = GROUP_ORDERS * degrees
    packed = packed_rows(degrees, GROUP_ORDERS - 1).stop
    return call(
        functools.partial(backward_kernel, group),
        (small, large, s, gain, mix),
        [
            pl.BlockSpec((DEVICES, GROUP_TILES, TILE, lanes), lambda b: (0, group, 0, 0))
            for lanes in (LANES, 2 * LANES)
        ]
        + [whole(s.shape), whole(gain.shape), whole(mix.shape)],
        [whole((rows, 2 * C)), whole((packed, 2 * C))],
        [
            jax.ShapeDtypeStruct((rows, 2 * C), BF16),
            jax.ShapeDtypeStruct((packed, 2 * C), BF16),
        ],
        (1,),
        after,
        name=f"spectral_backward_{group}",
    )


def hold_kernel(value_ref, out_ref):
    pass


def hold(value, after):
    held = pl.BlockSpec(memory_space=pl.ANY)
    return call(
        hold_kernel,
        (value,),
        [held],
        held,
        jax.ShapeDtypeStruct(value.shape, value.dtype),
        (1,),
        after,
        aliases={0: 0},
        name="hold",
    )


def synthesis_kernel(group, packed_ref, at_ref, *rest):
    out_ref, coeff_ref = rest[-2:]
    rest = rest[:-1]
    degrees = degrees_of(group)
    for local in range(GROUP_ORDERS):
        first = local * degrees
        skipped = DEVICES * local
        if local:
            coeff_ref[first : first + skipped, :] = jnp.zeros((skipped, 2 * C), BF16)
        coeff_ref[first + skipped : first + degrees, :] = packed_ref[
            packed_rows(degrees, local), :
        ]
    for tile in range(GROUP_TILES):
        first = coeff_ref[tile * degrees : (tile + 1) * degrees, :]
        second = coeff_ref[(tile + 1) * degrees : (tile + 2) * degrees, :]
        out = dot(at_ref[2 * tile], first) + dot(at_ref[2 * tile + 1], second)
        out_ref[:, tile] = out.astype(BF16).reshape(DEVICES, TILE, 2 * C)
    if len(rest) == 2:
        out_ref[:, GROUP_TILES] = rest[0][...]


def analysis_back(group, coeffs, at, tiles, extra=(), after=()):
    degrees = degrees_of(group)
    rows = GROUP_ORDERS * degrees
    block = GROUP_TILES + len(extra)
    return call(
        functools.partial(synthesis_kernel, group),
        (coeffs, at, *extra),
        [whole(coeffs.shape), whole(at.shape)] + [whole(value.shape) for value in extra],
        whole((DEVICES, block, TILE, 2 * C)),
        jax.ShapeDtypeStruct((DEVICES, tiles, TILE, 2 * C), BF16),
        (1,),
        after,
        scratch_shapes=[pltpu.VMEM((rows, 2 * C), BF16)],
        name=f"analysis_back_{group}",
    )


def fold(tile):
    return tile + pltpu.roll(tile, HALF, 1)


def weight_kernel(*refs):
    scaled_refs, mixed_refs = refs[:3], refs[3:6]
    mix_ref, factor_ref, proj_small, proj_large, out_ref, gain, packed, spaced = refs[6:]
    block = None
    for scaled_ref, mixed_ref in zip(scaled_refs, mixed_refs):
        part = lax.dot_general(
            scaled_ref[...], mixed_ref[...], (((0,), (0,)), ((), ())), preferred_element_type=F32
        )
        block = part if block is None else block + part
    for group in range(GROUPS):
        degrees = degrees_of(group)
        total = None
        for local in range(GROUP_ORDERS):
            rows = slice(local * degrees, (local + 1) * degrees)
            part = dot_nt(mixed_refs[group][rows, :], mix_ref[...])
            part = part * scaled_refs[group][rows, :].astype(F32)
            total = part if total is None else total + part
        if group == 0:
            gain[...] = total
        else:
            gain[LANES * group :, :] += total
    gain[...] = gain[...] / factor_ref[...]
    low = half_lanes((HALF, LANES))
    low_gain = half_lanes((C, LANES))
    low_proj = half_lanes((C // 2, LANES))
    for index in range(GROUPS):
        lanes = slice(index * LANES, (index + 1) * LANES)
        for row_block in range(GROUPS):
            start = row_block * LANES
            first = block[start : start + HALF, lanes]
            second = pltpu.roll(block[start + HALF : start + LANES, lanes], HALF, 1)
            packed[index, row_block * HALF : (row_block + 1) * HALF, :] = jnp.where(
                low, first + second, first - second
            )
        packed[index, C : 2 * C, :] = jnp.where(
            low_gain, fold(gain[:C, lanes]), fold(gain[C:, lanes])
        )
        if index == 0:
            proj = fold(proj_small[...])
        else:
            proj = fold(proj_large[:, (index - 1) * LANES : index * LANES])
        packed[index, 2 * C :, :] = jnp.where(low_proj, proj[: C // 2], proj[C // 2 :])
        for row in range(TILE - 1):
            spaced[index, pl.ds(row, DEVICES, stride=TILE), :] = packed[
                index, row * DEVICES : (row + 1) * DEVICES, :
            ]
        spaced[index, pl.ds(TILE - 1, DEVICES, stride=TILE), :] = jnp.zeros((DEVICES, LANES), F32)
        out_ref[:, :, lanes] = spaced[index].astype(BF16).reshape(DEVICES, TILE, LANES)


def weight_grads(scaleds, mixeds, mix, gain, proj_small, proj_large, after=()):
    out = (DEVICES, TILE, 2 * C)
    inputs = (*scaleds, *mixeds, mix, gain, proj_small, proj_large)
    return call(
        weight_kernel,
        inputs,
        [whole(value.shape) for value in inputs],
        whole(out),
        jax.ShapeDtypeStruct(out, BF16),
        (1,),
        after,
        scratch_shapes=[
            pltpu.VMEM((MODES, 2 * C), F32),
            pltpu.VMEM((GROUPS, 15 * DEVICES, LANES), F32),
            pltpu.VMEM((GROUPS, TILE * DEVICES, LANES), F32),
        ],
        name="weight_grads",
    )


def total_kernel(recv_ref, payload_ref, out_ref):
    total = jnp.sum(recv_ref[:, 0].astype(F32), axis=0)
    out_ref[:, 0] = jnp.broadcast_to(total.astype(BF16)[None], (DEVICES, TILE, 2 * C))


def attach_totals(recv, payload):
    spec = pl.BlockSpec((DEVICES, 1, TILE, 2 * C), lambda b: (0, GROUP_TILES, 0, 0))
    return call(
        total_kernel,
        (recv, payload),
        [spec, pl.BlockSpec(memory_space=pl.ANY)],
        spec,
        jax.ShapeDtypeStruct(payload.shape, BF16),
        (1,),
        aliases={1: 0},
        name="attach_totals",
    )


def unpack_kernel(recv_ref, proj_ref, mix_ref, gain_ref, spaced, packed):
    grid_scale = 1.0 / math.sqrt(NLAT * NLON)
    mode_scale = 1.0 / math.sqrt(MODES)
    lows, highs = [], []
    for index in range(GROUPS):
        lanes = slice(index * LANES, (index + 1) * LANES)
        spaced[index] = recv_ref[:, 0, :, lanes].reshape(DEVICES * TILE, LANES).astype(F32)
        for row in range(TILE - 1):
            packed[index, row * DEVICES : (row + 1) * DEVICES, :] = spaced[
                index, pl.ds(row, DEVICES, stride=TILE), :
            ]
        lows.append(packed[index, :, :HALF])
        highs.append(packed[index, :, HALF:])
    low = jnp.concatenate(lows, axis=1)
    high = jnp.concatenate(highs, axis=1)
    mix_ref[0] = grid_scale * low[:C]
    mix_ref[1] = grid_scale * high[:C]
    gain = jnp.concatenate([low[C : 2 * C], high[C : 2 * C]], axis=0)
    gain_ref[...] = mode_scale * gain.T
    proj = jnp.concatenate([low[2 * C :], high[2 * C :]], axis=0)
    proj_ref[...] = grid_scale * proj.T


def unpack_totals(recv, after=()):
    shapes = ((C, C), (2, C, C), (C, MODES))
    return call(
        unpack_kernel,
        (recv,),
        [pl.BlockSpec((DEVICES, 1, TILE, 2 * C), lambda b: (0, GROUP_TILES, 0, 0))],
        [whole(shape) for shape in shapes],
        [jax.ShapeDtypeStruct(shape, F32) for shape in shapes],
        (1,),
        after,
        scratch_shapes=[
            pltpu.VMEM((GROUPS, TILE * DEVICES, LANES), F32),
            pltpu.VMEM((GROUPS, 15 * DEVICES, LANES), F32),
        ],
        name="unpack_totals",
    )


def field_kernel(recv_ref, table_ref, base_ref, out_ref, scratch):
    step = pl.program_id(0)
    orders = DEVICES * GROUP_ORDERS
    rows = orders * LAT_LOCAL

    @pl.when(step == 0)
    def _():
        for index in range(GROUPS):
            lanes = slice(index * LANES, (index + 1) * LANES)
            values = recv_ref[:, :, :, lanes].astype(F32)
            scratch[index] = values.reshape(rows, LANES)

    lefts = []
    for inner in range(4):
        real, imag = [], []
        for index in range(GROUPS):
            values = scratch[index, pl.ds(step * 4 + inner, orders, stride=LAT_LOCAL), :]
            turned = values.T.astype(BF16)
            real.append(turned[:HALF])
            imag.append(turned[HALF:])
        lefts.append(
            jnp.concatenate(
                [jnp.concatenate(real, axis=0), jnp.concatenate(imag, axis=0)], axis=1
            )
        )
    product = dot(jnp.concatenate(lefts, axis=0), table_ref[...])
    for inner in range(4):
        total = base_ref[inner].astype(F32) + product[inner * C : (inner + 1) * C]
        out_ref[inner] = total.astype(out_ref.dtype)


def field_stage(recv, table, base, kind, after=()):
    rows = DEVICES * GROUP_ORDERS * LAT_LOCAL
    block = pl.BlockSpec((4, C, NLON), lambda b: (b, 0, 0))
    return call(
        field_kernel,
        (recv, table, base),
        [
            pl.BlockSpec((DEVICES, GROUP_TILES, TILE, 2 * C), lambda b: (0, 0, 0, 0)),
            whole(table.shape),
            block,
        ],
        block,
        jax.ShapeDtypeStruct((LAT_LOCAL, C, NLON), kind),
        (LAT_LOCAL // 4,),
        after,
        scratch_shapes=[pltpu.VMEM((GROUPS, rows, LANES), F32)],
        name="field_stage",
    )


def exchange(payload):
    tiles, lanes = payload.shape[1], payload.shape[3]
    flat = payload.reshape(DEVICES, tiles * TILE, lanes)
    moved = lax.all_to_all(flat, "lat", split_axis=0, concat_axis=0, tiled=True)
    return moved.reshape(DEVICES, tiles, TILE, lanes)


def shards(saved_input, incoming, spectral_gain, mix_weight, proj_weight):
    device = lax.axis_index("lat")
    section_count = lax.axis_size("section")
    shift = [(source, (source - 1) % section_count) for source in range(section_count)]

    forward_all = forward_rows(0, GROUPS)
    forward = [forward_rows(group, 1) for group in range(GROUPS)]
    inverse_np = inverse_rows()
    inverse = jnp.asarray(inverse_np)
    inverse_turned = jnp.asarray(np.ascontiguousarray(inverse_np.T))
    spread, spread_turned = spread_tables()
    lat = jnp.asarray(latitude_rows())
    starts, numbers = log_starts()
    start = lax.dynamic_index_in_dim(jnp.asarray(starts), device, 0, keepdims=False)
    order = lax.dynamic_index_in_dim(jnp.asarray(numbers), device, 0, keepdims=False)

    field = saved_input[0]
    upstream = incoming[0]
    upstream_next = lax.ppermute(upstream, "section", shift)
    turned = jnp.swapaxes(upstream, 1, 2)
    rows = MODES * LAT_LOCAL
    spectrum = spectrum_rows(field, forward_all)
    recv = exchange(spectrum.reshape(DEVICES, TILES, TILE, 2 * C))
    gain, mix, proj = prepare(
        jnp.swapaxes(spectral_gain[0], 0, 1), mix_weight[0], proj_weight[0], (spectrum,)
    )
    tables = legendre_tables(start, order, lat, spread, spread_turned, (spectrum,))
    behind = [tables[4 * group + 2 : 4 * group + 4] for group in range(GROUPS)]
    *scaleds, payload = spectral_forward(
        recv, tables[0::4], tables[1::4], gain, mix, (turned, proj)
    )
    recv = exchange(payload).reshape(rows, 2 * C)
    small_rows, proj_small = grid_stage(
        0, 1, recv, upstream, turned, proj, inverse, inverse_turned, (upstream_next,)
    )
    small = exchange(small_rows.reshape(DEVICES, TILES, TILE, LANES))
    large, proj_large = grid_stage(
        1, 2, recv, upstream, turned, proj, inverse, inverse_turned, (small_rows,)
    )
    large = exchange(large.reshape(DEVICES, TILES, TILE, 2 * LANES))

    mixeds, moved = [None] * GROUPS, [None] * GROUPS
    mixeds[2], coeffs_2 = spectral_backward(2, small, large, behind[2][0], gain, mix)
    out_2 = analysis_back(2, coeffs_2, behind[2][1], GROUP_TILES)
    recv_2 = exchange(out_2)
    mixeds[1], coeffs_1 = spectral_backward(1, small, large, behind[1][0], gain, mix, (out_2,))
    moved[1] = lax.ppermute(coeffs_1, "section", shift)
    mixeds[0], coeffs_0 = spectral_backward(0, small, large, behind[0][0], gain, mix, (coeffs_1,))
    partial_grads = weight_grads(
        scaleds, mixeds, mix, gain, proj_small, proj_large, after=(coeffs_0,)
    )
    moved[0] = lax.ppermute(hold(coeffs_0, (moved[1], partial_grads)), "section", shift)
    out_1 = analysis_back(1, moved[1], behind[1][1], GROUP_TILES + 1, (partial_grads,))
    recv_1 = exchange(hold(out_1, (recv_2,)))
    out_0 = analysis_back(0, moved[0], behind[0][1], GROUP_TILES + 1, after=(out_1,))
    moved_2 = lax.ppermute(hold(recv_2, (moved[0],)), "section", shift)
    out_0 = attach_totals(recv_1, out_0)
    base = field_stage(recv_1, forward[1], upstream_next, F32, (out_0,))
    recv_0 = exchange(out_0)
    base = field_stage(moved_2, forward[2], base, F32)
    grad_w2, grad_mix, grad_gain = unpack_totals(recv_0)
    received = field_stage(recv_0, forward[0], base, BF16)
    return (
        received[None],
        grad_w2[None],
        grad_mix[None],
        jnp.swapaxes(grad_gain, 0, 1)[None],
    )


def solution(mesh):
    in_specs = (
        P("section", "lat", None, None),
        P("section", "lat", None, None),
        P("section", None, None),
        P("section", None, None, None),
        P("section", None, None),
    )
    out_specs = (
        P("section", "lat", None, None),
        P("section", None, None),
        P("section", None, None, None),
        P("section", None, None),
    )
    return jax.shard_map(shards, mesh=mesh, in_specs=in_specs, out_specs=out_specs, check_vma=False)
```

```python
import functools
import math

import jax
import jax.numpy as jnp
import ml_dtypes
import numpy as np
from jax import lax
from jax.experimental import pallas as pl
from jax.experimental.pallas import tpu as pltpu
from jax.sharding import PartitionSpec as P

NLAT = 384
NLON = 768
MODES = 384
C = 192
DEVICES = 32
LAT_LOCAL = 12
ORDERS = 12
GROUPS = 3
GROUP_ORDERS = 4
HALF = 64
LANES = 128
TILE = 16
TILES = 9
GROUP_TILES = 3
SPAN = DEVICES * TILE
LAT_BLOCKS = 4
BLOCK_LATS = NLAT // LAT_BLOCKS
MIB = 1024 * 1024
F32 = jnp.float32
BF16 = jnp.bfloat16
NT = (((1,), (1,)), ((), ()))

PAIRS = ((0, 0), (1, 0), (1, 1), (2, 1), (2, 2), (3, 2))


def degrees_of(group):
    return MODES - LANES * group


def half_lanes(shape):
    return lax.broadcasted_iota(jnp.int32, shape, 1) < HALF


def packed_rows(group):
    rows, first = [], 0
    for local in range(GROUP_ORDERS):
        rows.append(slice(first, first + degrees_of(group) - DEVICES * local))
        first = rows[-1].stop
    return rows


PACKED = [packed_rows(group)[-1].stop for group in range(GROUPS)]
BASES = [sum(PACKED[:group]) for group in range(GROUPS)]


def dot(left, right):
    return jnp.dot(left, right, preferred_element_type=F32)


def dot_nt(left, right):
    return lax.dot_general(left, right, NT, preferred_element_type=F32)


def whole(shape):
    return pl.BlockSpec(shape, lambda *_: (0,) * len(shape), pipeline_mode=pl.Buffered(1))


HELD = pl.BlockSpec(memory_space=pltpu.HBM)


def call(
    kernel, inputs, in_specs, out_specs, out_shape, grid, after=(), aliases=None, vmem=56, **extra
):
    count = len(inputs)

    def body(*refs):
        kernel(*refs[:count], *refs[count + len(after) :])

    return pl.pallas_call(
        body,
        grid=grid,
        in_specs=list(in_specs) + [pl.BlockSpec(memory_space=pl.ANY)] * len(after),
        out_specs=out_specs,
        out_shape=out_shape,
        input_output_aliases=aliases or {},
        compiler_params=pltpu.CompilerParams(vmem_limit_bytes=vmem * MIB),
        cost_estimate=pl.CostEstimate(flops=1, bytes_accessed=1, transcendentals=0),
        **extra,
    )(*inputs, *after)


def order_rows(first, count):
    device = np.arange(DEVICES)[:, None]
    local = np.arange(GROUP_ORDERS * count)[None, :] + GROUP_ORDERS * first
    return (DEVICES * local + device).reshape(-1)


def fourier_rows(orders):
    phase = (orders[:, None] * np.arange(NLON)[None, :]) % NLON
    angle = phase * (2.0 * math.pi / NLON)
    return np.cos(angle), -np.sin(angle)


def forward_rows(first, count):
    cosine, sine = fourier_rows(order_rows(first, count))
    table = np.concatenate([cosine, sine], axis=0)
    return jnp.asarray(table.astype(np.float32).astype(ml_dtypes.bfloat16))


def inverse_rows():
    device = np.arange(DEVICES)[:, None]
    orders = (DEVICES * np.arange(ORDERS)[None, :] + device).reshape(-1)
    factor = np.where(orders == 0, 1.0, 2.0)[:, None] / NLON
    cosine, sine = fourier_rows(orders)
    table = np.concatenate([factor * cosine, factor * sine], axis=0)
    return table.astype(np.float32).astype(ml_dtypes.bfloat16)


def spread_tables():
    rows = np.arange(LANES)
    source, inner = rows // TILE, rows % TILE
    tables = np.zeros((len(PAIRS), LANES, LANES), np.float32)
    for index, (order, tile) in enumerate(PAIRS):
        lat = TILE * tile + inner - LAT_LOCAL * order
        valid = (lat >= 0) & (lat < LAT_LOCAL)
        tables[index, (source * LAT_LOCAL + lat)[valid], rows[valid]] = 1.0
    flat = jnp.asarray(tables.astype(ml_dtypes.bfloat16))
    turned = jnp.asarray(np.swapaxes(tables, 1, 2).astype(ml_dtypes.bfloat16))
    return flat, turned


def log_starts():
    table = np.zeros((DEVICES, TILE, LANES), np.float32)
    numbers = np.zeros((DEVICES, TILE, LANES), np.float32)
    for device in range(DEVICES):
        for local in range(ORDERS):
            order = DEVICES * local + device
            numbers[device, local] = order
            table[device, local] = 0.5 * math.log((2.0 * order + 1.0) / 2.0) + 0.5 * (
                math.lgamma(order + 0.5) - math.lgamma(0.5) - math.lgamma(order + 1.0)
            )
    return table, numbers


def latitude_rows():
    colatitude = (np.arange(NLAT) + 0.5) * (math.pi / NLAT)
    harmonic = np.arange(1, NLAT // 2 + 1)
    terms = np.cos(2.0 * harmonic[None, :] * colatitude[:, None]) / (4.0 * harmonic**2 - 1.0)
    weight = 2.0 / NLAT * (1.0 - 2.0 * np.sum(terms, axis=1))
    rows = np.stack([np.cos(colatitude), np.log(np.sin(colatitude)), weight])
    rows = np.concatenate([rows, np.zeros((5, NLAT))]).reshape(8, LAT_BLOCKS, BLOCK_LATS)
    rows = np.pad(rows, ((0, 0), (0, 0), (0, LANES - BLOCK_LATS)))
    return rows.reshape(8, SPAN).astype(np.float32)


def legendre_rows(start_ref, order_ref, lat_ref, rows_ref):
    order = jnp.concatenate([order_ref[...]] * LAT_BLOCKS, axis=1)
    cosine = jnp.broadcast_to(lat_ref[0:1, :], (TILE, SPAN))
    log_sin = jnp.broadcast_to(lat_ref[1:2, :], (TILE, SPAN))
    log_start = jnp.concatenate([start_ref[...]] * LAT_BLOCKS, axis=1) + order * log_sin
    narrow = order_ref[...]
    narrow_square = narrow * narrow
    second_factor = jnp.concatenate([jnp.sqrt(2.0 * narrow + 3.0)] * LAT_BLOCKS, axis=1)
    zeros = jnp.zeros((TILE, SPAN), F32)

    def block(index, state):
        previous, current, log_scale = state
        scale = jnp.exp(log_scale)
        for inner in range(16):
            row = index * 16 + inner
            degree = row.astype(F32)
            lower = degree - 1.0
            up = jnp.sqrt(
                jnp.maximum(4.0 * degree * degree - 1.0, 1.0)
                / jnp.maximum(degree * degree - narrow_square, 1.0)
            )
            down = jnp.sqrt(
                jnp.maximum(lower * lower - narrow_square, 0.0)
                / jnp.maximum(4.0 * lower * lower - 1.0, 1.0)
            )
            up = jnp.concatenate([up] * LAT_BLOCKS, axis=1)
            down = jnp.concatenate([down] * LAT_BLOCKS, axis=1)
            general = up * (cosine * current - down * previous)
            second = second_factor * cosine * current
            new_row = jnp.where(
                degree == order,
                1.0,
                jnp.where(
                    degree == order + 1.0, second, jnp.where(degree > order + 1.0, general, 0.0)
                ),
            )
            scaled = new_row * scale
            for part in range(LAT_BLOCKS):
                rows_ref[part, row] = scaled[:, part * LANES : (part + 1) * LANES]
            previous, current = current, new_row
        largest = jnp.maximum(jnp.abs(previous), jnp.abs(current))
        largest = jnp.where(largest > 0.0, largest, 1.0)
        return previous / largest, current / largest, log_scale + jnp.log(largest)

    lax.fori_loop(0, MODES // 16, block, (zeros, zeros, log_start))


def table_kernel(start_ref, order_ref, lat_ref, flat_ref, turned_ref, *rest):
    outs, rows_ref, buffers, sems = rest[:12], rest[12], rest[13:25], rest[25]
    legendre_rows(start_ref, order_ref, lat_ref, rows_ref)
    copies = []
    for group in range(GROUPS):
        ahead_flat, ahead_turned, behind_flat, behind_turned = buffers[4 * group : 4 * group + 4]

        def part_step(part, carry):
            lats = pl.ds(pl.multiple_of(part * LANES, LANES), LANES)
            weight = lat_ref[2:3, lats]
            for local in range(GROUP_ORDERS):
                legendre = rows_ref[part, LANES * group :, GROUP_ORDERS * group + local, :]
                synthesis = legendre.astype(BF16)
                analysis = (weight * legendre).astype(BF16)
                pairs = [index for index, (order, _) in enumerate(PAIRS) if order == local]
                flat = jnp.concatenate([flat_ref[index] for index in pairs], axis=1)
                turned = jnp.concatenate([turned_ref[index] for index in pairs], axis=0)
                products = (
                    dot(analysis, flat).astype(BF16),
                    dot_nt(turned, synthesis).astype(BF16),
                    dot(synthesis, flat).astype(BF16),
                    dot_nt(turned, analysis).astype(BF16),
                )
                for place, index in enumerate(pairs):
                    cut = slice(place * LANES, (place + 1) * LANES)
                    ahead_flat[index, :, lats] = products[0][:, cut]
                    ahead_turned[index, lats, :] = products[1][cut]
                    behind_flat[index, :, lats] = products[2][:, cut]
                    behind_turned[index, lats, :] = products[3][cut]
            return carry

        lax.fori_loop(0, LAT_BLOCKS, part_step, 0)
        for place in range(4):
            at = 4 * group + place
            copy = pltpu.make_async_copy(buffers[at], outs[at], sems.at[at])
            copy.start()
            copies.append(copy)
    for copy in copies:
        copy.wait()


def legendre_tables(start, order, lat, flat, turned, after):
    shapes = []
    for group in range(GROUPS):
        degrees = degrees_of(group)
        shapes += [(len(PAIRS), degrees, SPAN), (len(PAIRS), SPAN, degrees)] * 2
    inputs = (start, order, lat, flat, turned)
    return call(
        table_kernel,
        inputs,
        [whole(value.shape) for value in inputs],
        [HELD] * len(shapes),
        [jax.ShapeDtypeStruct(shape, BF16) for shape in shapes],
        (1,),
        after,
        scratch_shapes=[pltpu.VMEM((LAT_BLOCKS, MODES, TILE, LANES), F32)]
        + [pltpu.VMEM(shape, BF16) for shape in shapes]
        + [pltpu.SemaphoreType.DMA((len(shapes),))],
        name="legendre_tables",
    )


def blocks_of(value):
    return [value[:, index * HALF : (index + 1) * HALF] for index in range(GROUPS)]


def interleave(first, second):
    pairs = zip(blocks_of(first), blocks_of(second))
    return jnp.concatenate([block for pair in pairs for block in pair], axis=1)


def prepare_kernel(gain_ref, mix_ref, proj_ref, gain_out, mix_out, proj_out):
    gain = gain_ref[...].T
    gain_out[...] = interleave(gain, gain)
    real, imag = mix_ref[0].astype(F32), mix_ref[1].astype(F32)
    upper, lower = interleave(real, imag), interleave(-imag, real)
    for index in range(GROUPS):
        rows = slice(index * HALF, (index + 1) * HALF)
        start = index * LANES
        mix_out[start : start + HALF, :] = upper[rows].astype(BF16)
        mix_out[start + HALF : start + LANES, :] = lower[rows].astype(BF16)
    proj = proj_ref[...].astype(F32).T
    proj_out[...] = interleave(proj, proj).astype(BF16)


def prepare(gain, mix, proj, after):
    shapes = ((MODES, 2 * C), (2 * C, 2 * C), (C, 2 * C))
    kinds = (F32, BF16, BF16)
    return call(
        prepare_kernel,
        (gain, mix, proj),
        [whole(gain.shape), whole(mix.shape), whole(proj.shape)],
        [whole(shape) for shape in shapes],
        [jax.ShapeDtypeStruct(shape, kind) for shape, kind in zip(shapes, kinds)],
        (1,),
        after,
        name="prepare",
    )


def spectrum_kernel(field_ref, table_ref, out_ref, scratch):
    step = pl.program_id(0)
    rows = table_ref.shape[0] // 2
    low = half_lanes((rows, LANES))
    for inner in range(4):
        product = dot_nt(table_ref[...], field_ref[inner])
        real, imag = product[:rows], product[rows:]
        real_a, imag_a = real[:, :LANES], imag[:, :LANES]
        tiles = (
            jnp.where(low, real_a, pltpu.roll(imag_a, HALF, 1)),
            jnp.where(low, pltpu.roll(real_a, HALF, 1), imag_a),
            jnp.concatenate([real[:, LANES:], imag[:, LANES:]], axis=1),
        )
        for index, tile in enumerate(tiles):
            scratch[index, pl.ds(step * 4 + inner, rows, stride=LAT_LOCAL), :] = tile

    @pl.when(step == LAT_LOCAL // 4 - 1)
    def _():
        for index in range(GROUPS):
            out_ref[:, index * LANES : (index + 1) * LANES] = scratch[index].astype(BF16)


def spectrum_rows(field, table, after=()):
    rows = table.shape[0] // 2 * LAT_LOCAL
    return call(
        spectrum_kernel,
        (field, table),
        [pl.BlockSpec((4, C, NLON), lambda b: (b, 0, 0)), whole(table.shape)],
        whole((rows, 2 * C)),
        jax.ShapeDtypeStruct((rows, 2 * C), BF16),
        (LAT_LOCAL // 4,),
        after,
        scratch_shapes=[pltpu.VMEM((GROUPS, rows, LANES), F32)],
        name="spectrum_rows",
    )


def pair_sum(local, table_ref, tiles):
    total = None
    for index, (order, tile) in enumerate(PAIRS):
        if order == local:
            part = dot(table_ref[index, DEVICES * local :, :], tiles[tile])
            total = part if total is None else total + part
    return total


def spectral_kernel(recv_ref, *refs):
    a_refs, st_refs = refs[0:3], refs[3:6]
    gain_ref, mix_ref = refs[6:8]
    scaled_ref, payload_ref, recv, payload = refs[8:12]
    a_buffers, st_buffers, scaled_buffers = refs[12:15], refs[15:18], refs[18:21]
    in_sems, out_sems = refs[21:23]
    schedule = (2, 0, 1)
    arrivals, departures = {}, []
    for group in schedule:
        tiles = pl.ds(GROUP_TILES * group, GROUP_TILES)
        arrivals[group] = [
            pltpu.make_async_copy(recv_ref.at[:, tiles], recv.at[group], in_sems.at[group, 0]),
            pltpu.make_async_copy(a_refs[group], a_buffers[group], in_sems.at[group, 1]),
            pltpu.make_async_copy(st_refs[group], st_buffers[group], in_sems.at[group, 2]),
        ]
        for copy in arrivals[group]:
            copy.start()
    for group in schedule:
        for copy in arrivals[group]:
            copy.wait()
        tiles = [recv[group, :, tile].reshape(SPAN, 2 * C) for tile in range(GROUP_TILES)]
        mixed = []
        for local in range(GROUP_ORDERS):
            skipped = DEVICES * local
            coef = pair_sum(local, a_buffers[group], tiles)
            scaled = (gain_ref[LANES * group + skipped :, :] * coef).astype(BF16)
            scaled_buffers[group][packed_rows(group)[local], :] = scaled
            product = dot(scaled, mix_ref[...]).astype(BF16)
            if skipped:
                zeros = jnp.zeros((skipped, 2 * C), BF16)
                product = jnp.concatenate([zeros, product], axis=0)
            mixed.append(product)
        for tile in range(GROUP_TILES):
            grid = dot(st_buffers[group][2 * tile], mixed[tile]) + dot(
                st_buffers[group][2 * tile + 1], mixed[tile + 1]
            )
            payload[group, :, tile] = grid.astype(BF16).reshape(DEVICES, TILE, 2 * C)
        tiles = pl.ds(GROUP_TILES * group, GROUP_TILES)
        copies = (
            pltpu.make_async_copy(
                payload.at[group], payload_ref.at[:, tiles], out_sems.at[group, 0]
            ),
            pltpu.make_async_copy(
                scaled_buffers[group],
                scaled_ref.at[pl.ds(BASES[group], PACKED[group])],
                out_sems.at[group, 1],
            ),
        )
        for copy in copies:
            copy.start()
            departures.append(copy)
    for copy in departures:
        copy.wait()


def spectral_forward(recv, a, st, gain, mix, after=()):
    slots = (GROUPS, DEVICES, GROUP_TILES, TILE, 2 * C)
    return call(
        spectral_kernel,
        (recv, *a, *st, gain, mix),
        [HELD] * 7 + [whole(gain.shape), whole(mix.shape)],
        [HELD] * 2,
        [
            jax.ShapeDtypeStruct((sum(PACKED), 2 * C), BF16),
            jax.ShapeDtypeStruct(recv.shape, BF16),
        ],
        (1,),
        after,
        scratch_shapes=[pltpu.VMEM(slots, BF16), pltpu.VMEM(slots, BF16)]
        + [pltpu.VMEM(value.shape, BF16) for value in a]
        + [pltpu.VMEM(value.shape, BF16) for value in st]
        + [pltpu.VMEM((rows, 2 * C), BF16) for rows in PACKED]
        + [pltpu.SemaphoreType.DMA((GROUPS, 3)), pltpu.SemaphoreType.DMA((GROUPS, 2))],
        name="spectral_forward",
    )


def normal_cumulative(value, bell):
    denominator = 1.0 + (0.3275911 / math.sqrt(2.0)) * jnp.abs(value)
    inverse = pl.reciprocal(denominator, approx=True)
    inverse = inverse * (2.0 - denominator * inverse)
    series = 0.5 * 1.061405429 * inverse - 0.5 * 1.453152027
    series = series * inverse + 0.5 * 1.421413741
    series = series * inverse - 0.5 * 0.284496736
    series = series * inverse + 0.5 * 0.254829592
    tail = series * inverse * bell
    return jnp.where(value < 0.0, tail, 1.0 - tail)


def grid_kernel(
    recv_ref, up_ref, turned_ref, proj_ref, table_ref, turned_table_ref,
    out_ref, grad_ref, scratch, out_scratch, act_scratch, pre_scratch,
):
    step = pl.program_id(1)
    low = half_lanes((MODES, LANES))
    block = 128

    @pl.when(step == 0)
    def _():
        scratch[...] = recv_ref[...].astype(F32)
        grad_ref[...] = jnp.zeros_like(grad_ref)

    columns = []
    for pair in range(2):
        first = scratch[pl.ds(step * 4 + 2 * pair, MODES, stride=LAT_LOCAL), :]
        second = scratch[pl.ds(step * 4 + 2 * pair + 1, MODES, stride=LAT_LOCAL), :]
        real = jnp.where(low, first, pltpu.roll(second, HALF, 1))
        imag = jnp.where(low, pltpu.roll(first, HALF, 1), second)
        columns.append(jnp.concatenate([real, imag], axis=0).astype(BF16))
    modes = jnp.concatenate(columns, axis=1)
    low_block = half_lanes((block, LANES))
    for part in range(NLON // block):
        rows = slice(part * block, (part + 1) * block)
        pre = dot(turned_table_ref[rows, :], modes)
        grad_act = jnp.concatenate(
            [
                jnp.where(
                    low_block,
                    dot(turned_ref[2 * pair, rows, :], proj_ref[...]),
                    dot(turned_ref[2 * pair + 1, rows, :], proj_ref[...]),
                )
                for pair in range(2)
            ],
            axis=1,
        )
        bell = jnp.exp(-0.5 * pre * pre)
        cumulative = normal_cumulative(pre, bell)
        slope = cumulative + pre * bell * (1.0 / math.sqrt(2.0 * math.pi))
        act_scratch[rows, :] = (pre * cumulative).astype(BF16)
        pre_scratch[rows, :] = (grad_act * slope).astype(BF16)
    low_grad = half_lanes((C, LANES))
    for pair in range(2):
        lanes = slice(pair * LANES, (pair + 1) * LANES)
        act = act_scratch[:, lanes]
        grad_ref[...] += jnp.where(
            low_grad, dot(up_ref[2 * pair], act), dot(up_ref[2 * pair + 1], act)
        )
    grad_modes = dot(table_ref[...], pre_scratch[...])
    for pair in range(2):
        lanes = slice(pair * LANES, (pair + 1) * LANES)
        real, imag = grad_modes[:MODES, lanes], grad_modes[MODES:, lanes]
        out_scratch[pl.ds(step * 4 + 2 * pair, MODES, stride=LAT_LOCAL), :] = jnp.where(
            low, real, pltpu.roll(imag, HALF, 1)
        )
        out_scratch[pl.ds(step * 4 + 2 * pair + 1, MODES, stride=LAT_LOCAL), :] = jnp.where(
            low, pltpu.roll(real, HALF, 1), imag
        )

    @pl.when(step == LAT_LOCAL // 4 - 1)
    def _():
        out_ref[...] = out_scratch[...].astype(BF16)


def grid_stage(first, blocks, recv, up, turned, proj, table, turned_table, after=()):
    rows = MODES * LAT_LOCAL
    lanes_spec = pl.BlockSpec((rows, LANES), lambda q, b: (0, q))
    grad_spec = pl.BlockSpec((C, LANES), lambda q, b: (0, q))
    return call(
        grid_kernel,
        (recv, up, turned, proj, table, turned_table),
        [
            pl.BlockSpec((rows, LANES), lambda q, b: (0, q + first)),
            pl.BlockSpec((4, C, NLON), lambda q, b: (b, 0, 0)),
            pl.BlockSpec((4, NLON, C), lambda q, b: (b, 0, 0)),
            pl.BlockSpec((C, LANES), lambda q, b: (0, q + first)),
            whole(table.shape),
            whole(turned_table.shape),
        ],
        [lanes_spec, grad_spec],
        [
            jax.ShapeDtypeStruct((rows, LANES * blocks), BF16),
            jax.ShapeDtypeStruct((C, LANES * blocks), F32),
        ],
        (blocks, LAT_LOCAL // 4),
        after,
        scratch_shapes=[
            pltpu.VMEM((rows, LANES), F32),
            pltpu.VMEM((rows, LANES), F32),
            pltpu.VMEM((NLON, 2 * LANES), BF16),
            pltpu.VMEM((NLON, 2 * LANES), BF16),
        ],
        name=f"grid_stage_{blocks}",
    )


def backward_kernel(groups, *refs):
    recv_ref, table_refs, out_ref = refs[0], refs[1 : 1 + len(groups)], refs[1 + len(groups)]
    buffers, sems = refs[2 + len(groups) : -1], refs[-1]
    copies = [
        pltpu.make_async_copy(table_refs[place], buffers[place], sems.at[place])
        for place in range(len(groups))
    ]
    for copy in copies:
        copy.start()
    lanes = recv_ref.shape[-1]
    first = 0
    for place, group in enumerate(groups):
        start = GROUP_TILES * place
        tiles = [
            recv_ref[:, start + tile].reshape(SPAN, lanes) for tile in range(GROUP_TILES)
        ]
        copies[place].wait()
        for local, rows in enumerate(packed_rows(group)):
            mixed = pair_sum(local, buffers[place], tiles).astype(BF16)
            out_ref[first + rows.start : first + rows.stop, :] = mixed
        first += PACKED[group]


def spectral_backward(groups, recv, tables, after=()):
    lanes = recv.shape[-1]
    tiles = GROUP_TILES * len(groups)
    block = groups[0] if len(groups) == 1 else 0
    out = (sum(PACKED[group] for group in groups), lanes)
    return call(
        functools.partial(backward_kernel, groups),
        (recv, *tables),
        [
            pl.BlockSpec(
                (DEVICES, tiles, TILE, lanes),
                lambda b: (0, block, 0, 0),
                pipeline_mode=pl.Buffered(1),
            )
        ]
        + [HELD] * len(groups),
        whole(out),
        jax.ShapeDtypeStruct(out, BF16),
        (1,),
        after,
        scratch_shapes=[pltpu.VMEM(table.shape, BF16) for table in tables]
        + [pltpu.SemaphoreType.DMA((len(groups),))],
        vmem=20,
        name="spectral_backward_" + "_".join(str(group) for group in groups),
    )


def hold_kernel(value_ref, out_ref):
    pass


def hold(value, after):
    held = pl.BlockSpec(memory_space=pl.ANY)
    return call(
        hold_kernel,
        (value,),
        [held],
        held,
        jax.ShapeDtypeStruct(value.shape, value.dtype),
        (1,),
        after,
        aliases={0: 0},
        vmem=1,
        name="hold",
    )


def synthesis_kernel(group, table_ref, small_ref, large_ref, gain_ref, mix_ref, *refs):
    extra, (out_ref, coeff_ref, at_ref, part_ref, sems) = refs[:-5], refs[-5:]
    degrees = degrees_of(group)
    copies = (
        pltpu.make_async_copy(
            small_ref.at[pl.ds(BASES[group], PACKED[group])], part_ref, sems.at[0]
        ),
        pltpu.make_async_copy(table_ref, at_ref, sems.at[1]),
    )
    for copy in copies:
        copy.start()
    copies[0].wait()
    for local, rows in enumerate(packed_rows(group)):
        first = local * degrees
        skipped = DEVICES * local
        mixed = jnp.concatenate([part_ref[rows, :], large_ref[rows, :]], axis=1)
        scaled = dot_nt(mixed, mix_ref[...])
        if skipped:
            coeff_ref[first : first + skipped, :] = jnp.zeros((skipped, 2 * C), BF16)
        coeff_ref[first + skipped : first + degrees, :] = (
            gain_ref[LANES * group + skipped :, :] * scaled
        ).astype(BF16)
    copies[1].wait()
    for tile in range(GROUP_TILES):
        first = coeff_ref[tile * degrees : (tile + 1) * degrees, :]
        second = coeff_ref[(tile + 1) * degrees : (tile + 2) * degrees, :]
        out = dot(at_ref[2 * tile], first) + dot(at_ref[2 * tile + 1], second)
        out_ref[:, tile] = out.astype(BF16).reshape(DEVICES, TILE, 2 * C)
    if extra:
        out_ref[:, GROUP_TILES] = extra[0][...]


def analysis_back(group, at, small, large, gain, mix, tiles, extra=(), after=()):
    inputs = (at, small, large, gain, mix, *extra)
    return call(
        functools.partial(synthesis_kernel, group),
        inputs,
        [HELD] * 2 + [whole(value.shape) for value in inputs[2:]],
        whole((DEVICES, GROUP_TILES + len(extra), TILE, 2 * C)),
        jax.ShapeDtypeStruct((DEVICES, tiles, TILE, 2 * C), BF16),
        (1,),
        after,
        scratch_shapes=[
            pltpu.VMEM((GROUP_ORDERS * degrees_of(group), 2 * C), BF16),
            pltpu.VMEM(at.shape, BF16),
            pltpu.VMEM((PACKED[group], LANES), BF16),
            pltpu.SemaphoreType.DMA((2,)),
        ],
        vmem=20,
        name=f"analysis_back_{group}",
    )


def fold(tile):
    return tile + pltpu.roll(tile, HALF, 1)


def weight_kernel(held_ref, small_ref, *refs):
    large_refs, (mix_ref, factor_ref, proj_small, proj_large) = refs[:3], refs[3:7]
    out_ref, gain, packed, spaced, scaled_ref, sem = refs[7:]
    copy = pltpu.make_async_copy(held_ref, scaled_ref, sem)
    copy.start()
    copy.wait()
    block = None
    for group in range(GROUPS):
        rows = slice(BASES[group], BASES[group] + PACKED[group])
        mixed = jnp.concatenate([small_ref[rows, :], large_refs[group][...]], axis=1)
        part = lax.dot_general(
            scaled_ref[rows, :], mixed, (((0,), (0,)), ((), ())), preferred_element_type=F32
        )
        block = part if block is None else block + part
        for local, rows in enumerate(packed_rows(group)):
            here = slice(BASES[group] + rows.start, BASES[group] + rows.stop)
            mixed = jnp.concatenate([small_ref[here, :], large_refs[group][rows, :]], axis=1)
            part = dot_nt(mixed, mix_ref[...]) * scaled_ref[here, :].astype(F32)
            first = LANES * group + DEVICES * local
            if first:
                gain[first:, :] += part
            else:
                gain[...] = part
    gain[...] = gain[...] / factor_ref[...]
    low = half_lanes((HALF, LANES))
    low_gain = half_lanes((C, LANES))
    low_proj = half_lanes((C // 2, LANES))
    for index in range(GROUPS):
        lanes = slice(index * LANES, (index + 1) * LANES)
        for row_block in range(GROUPS):
            start = row_block * LANES
            first = block[start : start + HALF, lanes]
            second = pltpu.roll(block[start + HALF : start + LANES, lanes], HALF, 1)
            packed[index, row_block * HALF : (row_block + 1) * HALF, :] = jnp.where(
                low, first + second, first - second
            )
        packed[index, C : 2 * C, :] = jnp.where(
            low_gain, fold(gain[:C, lanes]), fold(gain[C:, lanes])
        )
        if index == 0:
            proj = fold(proj_small[...])
        else:
            proj = fold(proj_large[:, (index - 1) * LANES : index * LANES])
        packed[index, 2 * C :, :] = jnp.where(low_proj, proj[: C // 2], proj[C // 2 :])
        for row in range(TILE - 1):
            spaced[index, pl.ds(row, DEVICES, stride=TILE), :] = packed[
                index, row * DEVICES : (row + 1) * DEVICES, :
            ]
        spaced[index, pl.ds(TILE - 1, DEVICES, stride=TILE), :] = jnp.zeros((DEVICES, LANES), F32)
        out_ref[:, :, lanes] = spaced[index].astype(BF16).reshape(DEVICES, TILE, LANES)


def weight_grads(scaled, small, large, mix, gain, proj_small, proj_large, after=()):
    out = (DEVICES, TILE, 2 * C)
    inputs = (scaled, small, *large, mix, gain, proj_small, proj_large)
    return call(
        weight_kernel,
        inputs,
        [HELD] + [whole(value.shape) for value in inputs[1:]],
        whole(out),
        jax.ShapeDtypeStruct(out, BF16),
        (1,),
        after,
        scratch_shapes=[
            pltpu.VMEM((MODES, 2 * C), F32),
            pltpu.VMEM((GROUPS, 15 * DEVICES, LANES), F32),
            pltpu.VMEM((GROUPS, TILE * DEVICES, LANES), F32),
            pltpu.VMEM(scaled.shape, BF16),
            pltpu.SemaphoreType.DMA,
        ],
        vmem=24,
        name="weight_grads",
    )


def total_kernel(recv_ref, payload_ref, out_ref):
    total = jnp.sum(recv_ref[:, 0].astype(F32), axis=0)
    out_ref[:, 0] = jnp.broadcast_to(total.astype(BF16)[None], (DEVICES, TILE, 2 * C))


def attach_totals(recv, payload):
    spec = pl.BlockSpec((DEVICES, 1, TILE, 2 * C), lambda b: (0, GROUP_TILES, 0, 0))
    return call(
        total_kernel,
        (recv, payload),
        [spec, pl.BlockSpec(memory_space=pl.ANY)],
        spec,
        jax.ShapeDtypeStruct(payload.shape, BF16),
        (1,),
        aliases={1: 0},
        vmem=8,
        name="attach_totals",
    )


def unpack_kernel(recv_ref, proj_ref, mix_ref, gain_ref, spaced, packed):
    grid_scale = 1.0 / math.sqrt(NLAT * NLON)
    mode_scale = 1.0 / math.sqrt(MODES)
    lows, highs = [], []
    for index in range(GROUPS):
        lanes = slice(index * LANES, (index + 1) * LANES)
        spaced[index] = recv_ref[:, 0, :, lanes].reshape(DEVICES * TILE, LANES).astype(F32)
        for row in range(TILE - 1):
            packed[index, row * DEVICES : (row + 1) * DEVICES, :] = spaced[
                index, pl.ds(row, DEVICES, stride=TILE), :
            ]
        lows.append(packed[index, :, :HALF])
        highs.append(packed[index, :, HALF:])
    low = jnp.concatenate(lows, axis=1)
    high = jnp.concatenate(highs, axis=1)
    mix_ref[0] = grid_scale * low[:C]
    mix_ref[1] = grid_scale * high[:C]
    gain = jnp.concatenate([low[C : 2 * C], high[C : 2 * C]], axis=0)
    gain_ref[...] = mode_scale * gain.T
    proj = jnp.concatenate([low[2 * C :], high[2 * C :]], axis=0)
    proj_ref[...] = grid_scale * proj.T


def unpack_totals(recv, after=()):
    shapes = ((C, C), (2, C, C), (C, MODES))
    return call(
        unpack_kernel,
        (recv,),
        [pl.BlockSpec((DEVICES, 1, TILE, 2 * C), lambda b: (0, GROUP_TILES, 0, 0))],
        [whole(shape) for shape in shapes],
        [jax.ShapeDtypeStruct(shape, F32) for shape in shapes],
        (1,),
        after,
        scratch_shapes=[
            pltpu.VMEM((GROUPS, TILE * DEVICES, LANES), F32),
            pltpu.VMEM((GROUPS, 15 * DEVICES, LANES), F32),
        ],
        vmem=12,
        name="unpack_totals",
    )


def field_kernel(*refs):
    recv_refs, (table_ref, base_ref, out_ref, scratch) = refs[:-4], refs[-4:]
    step = pl.program_id(0)
    orders = DEVICES * GROUP_ORDERS
    rows = orders * LAT_LOCAL // len(recv_refs)

    @pl.when(step == 0)
    def _():
        for index in range(GROUPS):
            lanes = slice(index * LANES, (index + 1) * LANES)
            for place, recv_ref in enumerate(recv_refs):
                values = recv_ref[:, :, :, lanes].astype(F32)
                scratch[index, place * rows : (place + 1) * rows] = values.reshape(rows, LANES)

    lefts = []
    for inner in range(4):
        real, imag = [], []
        for index in range(GROUPS):
            values = scratch[index, pl.ds(step * 4 + inner, orders, stride=LAT_LOCAL), :]
            turned = values.T.astype(BF16)
            real.append(turned[:HALF])
            imag.append(turned[HALF:])
        lefts.append(
            jnp.concatenate(
                [jnp.concatenate(real, axis=0), jnp.concatenate(imag, axis=0)], axis=1
            )
        )
    product = dot(jnp.concatenate(lefts, axis=0), table_ref[...])
    for inner in range(4):
        total = base_ref[inner].astype(F32) + product[inner * C : (inner + 1) * C]
        out_ref[inner] = total.astype(out_ref.dtype)


def field_stage(recv, table, base, after=()):
    rows = DEVICES * GROUP_ORDERS * LAT_LOCAL
    block = pl.BlockSpec((4, C, NLON), lambda b: (b, 0, 0))
    return call(
        field_kernel,
        (*recv, table, base),
        [
            pl.BlockSpec(
                (DEVICES // len(recv), GROUP_TILES, TILE, 2 * C),
                lambda b: (0, 0, 0, 0),
                pipeline_mode=pl.Buffered(1),
            )
        ]
        * len(recv)
        + [whole(table.shape), block],
        block,
        jax.ShapeDtypeStruct((LAT_LOCAL, C, NLON), BF16),
        (LAT_LOCAL // 4,),
        after,
        scratch_shapes=[pltpu.VMEM((GROUPS, rows, LANES), F32)],
        vmem=20,
        name="field_stage",
    )


def exchange(payload):
    tiles, lanes = payload.shape[1], payload.shape[3]
    flat = payload.reshape(DEVICES, tiles * TILE, lanes)
    moved = lax.all_to_all(flat, "lat", split_axis=0, concat_axis=0, tiled=True)
    return moved.reshape(DEVICES, tiles, TILE, lanes)


def shards(saved_input, incoming, spectral_gain, mix_weight, proj_weight):
    device = lax.axis_index("lat")
    section_count = lax.axis_size("section")
    shift = [(source, (source - 1) % section_count) for source in range(section_count)]

    forward_all = forward_rows(0, GROUPS)
    forward = [forward_rows(group, 1) for group in range(GROUPS)]
    inverse_np = inverse_rows()
    inverse = jnp.asarray(inverse_np)
    inverse_turned = jnp.asarray(np.ascontiguousarray(inverse_np.T))
    spread, spread_turned = spread_tables()
    lat = jnp.asarray(latitude_rows())
    starts, numbers = log_starts()
    start = lax.dynamic_index_in_dim(jnp.asarray(starts), device, 0, keepdims=False)
    order = lax.dynamic_index_in_dim(jnp.asarray(numbers), device, 0, keepdims=False)

    field = saved_input[0]
    upstream = incoming[0]
    upstream_next = lax.ppermute(upstream, "section", shift)
    turned = jnp.swapaxes(upstream, 1, 2)
    rows = MODES * LAT_LOCAL
    spectrum = spectrum_rows(field, forward_all)
    recv = exchange(spectrum.reshape(DEVICES, TILES, TILE, 2 * C))
    gain, mix, proj = prepare(
        jnp.swapaxes(spectral_gain[0], 0, 1), mix_weight[0], proj_weight[0], (spectrum,)
    )
    gain_next, mix_next, _ = prepare(
        lax.ppermute(jnp.swapaxes(spectral_gain[0], 0, 1), "section", shift),
        lax.ppermute(mix_weight[0], "section", shift),
        proj_weight[0],
        (spectrum,),
    )
    tables = legendre_tables(start, order, lat, spread, spread_turned, (spectrum,))
    behind = [tables[4 * group + 2 : 4 * group + 4] for group in range(GROUPS)]
    scaled, payload = spectral_forward(
        recv, tables[0::4], tables[1::4], gain, mix, (turned, proj)
    )
    recv = exchange(payload).reshape(rows, 2 * C)
    small_rows, proj_small = grid_stage(
        0,
        1,
        recv,
        upstream,
        turned,
        proj,
        inverse,
        inverse_turned,
        (upstream_next, gain_next, mix_next),
    )
    small = exchange(small_rows.reshape(DEVICES, TILES, TILE, LANES))
    large, proj_large = grid_stage(
        1, 2, recv, upstream, turned, proj, inverse, inverse_turned, (small_rows,)
    )
    large = exchange(large.reshape(DEVICES, TILES, TILE, 2 * LANES))

    mixeds, moved = [None] * GROUPS, [None] * GROUPS
    every = tuple(range(GROUPS))
    mixed_small = spectral_backward(every, small, [table[0] for table in behind])
    moved_small = lax.ppermute(mixed_small, "section", shift)
    mixed_2 = spectral_backward((2,), large, [behind[2][0]], (moved_small,))
    moved_2 = lax.ppermute(mixed_2, "section", shift)
    out_2 = analysis_back(
        2, behind[2][1], moved_small, moved_2, gain_next, mix_next, GROUP_TILES
    )
    recv_2 = exchange(out_2)
    mixed_1 = spectral_backward((1,), large, [behind[1][0]], (out_2,))
    moved_1 = lax.ppermute(mixed_1, "section", shift)
    mixed_0 = spectral_backward((0,), large, [behind[0][0]], (mixed_1,))
    moved_0 = lax.ppermute(mixed_0, "section", shift)
    partial_grads = weight_grads(
        scaled, mixed_small, (mixed_0, mixed_1, mixed_2), mix, gain, proj_small, proj_large
    )
    out_1 = analysis_back(
        1,
        behind[1][1],
        moved_small,
        moved_1,
        gain_next,
        mix_next,
        GROUP_TILES + 1,
        (partial_grads,),
    )
    out_1 = hold(out_1, (recv_2,))
    recv_1 = exchange(out_1)
    out_0 = analysis_back(
        0,
        behind[0][1],
        moved_small,
        moved_0,
        gain_next,
        mix_next,
        GROUP_TILES + 1,
        after=(recv_2,),
    )
    out_0 = attach_totals(recv_1, out_0)
    recv_0 = exchange(out_0)
    base = field_stage((recv_2,), forward[2], upstream_next, (out_0,))
    base = field_stage((recv_1,), forward[1], base)
    grad_w2, grad_mix, grad_gain = unpack_totals(recv_0)
    received = field_stage((recv_0,), forward[0], base)
    return (
        received[None],
        grad_w2[None],
        grad_mix[None],
        jnp.swapaxes(grad_gain, 0, 1)[None],
    )


def solution(mesh):
    in_specs = (
        P("section", "lat", None, None),
        P("section", "lat", None, None),
        P("section", None, None),
        P("section", None, None, None),
        P("section", None, None),
    )
    out_specs = (
        P("section", "lat", None, None),
        P("section", None, None),
        P("section", None, None, None),
        P("section", None, None),
    )
    return jax.shard_map(shards, mesh=mesh, in_specs=in_specs, out_specs=out_specs, check_vma=False)
```

```python
import functools
import math

import jax
import jax.numpy as jnp
import ml_dtypes
import numpy as np
from jax import lax
from jax.experimental import pallas as pl
from jax.experimental.pallas import tpu as pltpu
from jax.sharding import PartitionSpec as P

NLAT = 384
NLON = 768
MODES = 384
C = 192
DEVICES = 32
LAT_LOCAL = 12
ORDERS = 12
GROUPS = 3
GROUP_ORDERS = 4
HALF = 64
LANES = 128
TILE = 16
TILES = 9
GROUP_TILES = 3
SPAN = DEVICES * TILE
LAT_BLOCKS = 4
BLOCK_LATS = NLAT // LAT_BLOCKS
MIB = 1024 * 1024
F32 = jnp.float32
BF16 = jnp.bfloat16
NT = (((1,), (1,)), ((), ()))

PAIRS = ((0, 0), (1, 0), (1, 1), (2, 1), (2, 2), (3, 2))


def degrees_of(group):
    return MODES - LANES * group


def half_lanes(shape):
    return lax.broadcasted_iota(jnp.int32, shape, 1) < HALF


def packed_rows(group):
    rows, first = [], 0
    for local in range(GROUP_ORDERS):
        rows.append(slice(first, first + degrees_of(group) - DEVICES * local))
        first = rows[-1].stop
    return rows


PACKED = [packed_rows(group)[-1].stop for group in range(GROUPS)]
BASES = [sum(PACKED[:group]) for group in range(GROUPS)]


def dot(left, right):
    return jnp.dot(left, right, preferred_element_type=F32)


def dot_nt(left, right):
    return lax.dot_general(left, right, NT, preferred_element_type=F32)


def whole(shape):
    return pl.BlockSpec(shape, lambda *_: (0,) * len(shape), pipeline_mode=pl.Buffered(1))


HELD = pl.BlockSpec(memory_space=pltpu.HBM)


def call(
    kernel, inputs, in_specs, out_specs, out_shape, grid, after=(), aliases=None, vmem=56, **extra
):
    count = len(inputs)

    def body(*refs):
        kernel(*refs[:count], *refs[count + len(after) :])

    return pl.pallas_call(
        body,
        grid=grid,
        in_specs=list(in_specs) + [pl.BlockSpec(memory_space=pl.ANY)] * len(after),
        out_specs=out_specs,
        out_shape=out_shape,
        input_output_aliases=aliases or {},
        compiler_params=pltpu.CompilerParams(vmem_limit_bytes=vmem * MIB),
        cost_estimate=pl.CostEstimate(flops=1, bytes_accessed=1, transcendentals=0),
        **extra,
    )(*inputs, *after)


def order_rows(first, count):
    device = np.arange(DEVICES)[:, None]
    local = np.arange(GROUP_ORDERS * count)[None, :] + GROUP_ORDERS * first
    return (DEVICES * local + device).reshape(-1)


def fourier_rows(orders):
    phase = (orders[:, None] * np.arange(NLON)[None, :]) % NLON
    angle = phase * (2.0 * math.pi / NLON)
    return np.cos(angle), -np.sin(angle)


def forward_rows(first, count):
    cosine, sine = fourier_rows(order_rows(first, count))
    table = np.concatenate([cosine, sine], axis=0)
    return jnp.asarray(table.astype(np.float32).astype(ml_dtypes.bfloat16))


def inverse_rows():
    device = np.arange(DEVICES)[:, None]
    orders = (DEVICES * np.arange(ORDERS)[None, :] + device).reshape(-1)
    factor = np.where(orders == 0, 1.0, 2.0)[:, None] / NLON
    cosine, sine = fourier_rows(orders)
    table = np.concatenate([factor * cosine, factor * sine], axis=0)
    return table.astype(np.float32).astype(ml_dtypes.bfloat16)


def spread_tables():
    rows = np.arange(LANES)
    source, inner = rows // TILE, rows % TILE
    tables = np.zeros((len(PAIRS), LANES, LANES), np.float32)
    for index, (order, tile) in enumerate(PAIRS):
        lat = TILE * tile + inner - LAT_LOCAL * order
        valid = (lat >= 0) & (lat < LAT_LOCAL)
        tables[index, (source * LAT_LOCAL + lat)[valid], rows[valid]] = 1.0
    flat = jnp.asarray(tables.astype(ml_dtypes.bfloat16))
    turned = jnp.asarray(np.swapaxes(tables, 1, 2).astype(ml_dtypes.bfloat16))
    return flat, turned


def log_starts():
    table = np.zeros((DEVICES, TILE, LANES), np.float32)
    numbers = np.zeros((DEVICES, TILE, LANES), np.float32)
    for device in range(DEVICES):
        for local in range(ORDERS):
            order = DEVICES * local + device
            numbers[device, local] = order
            table[device, local] = 0.5 * math.log((2.0 * order + 1.0) / 2.0) + 0.5 * (
                math.lgamma(order + 0.5) - math.lgamma(0.5) - math.lgamma(order + 1.0)
            )
    return table, numbers


def latitude_rows():
    colatitude = (np.arange(NLAT) + 0.5) * (math.pi / NLAT)
    harmonic = np.arange(1, NLAT // 2 + 1)
    terms = np.cos(2.0 * harmonic[None, :] * colatitude[:, None]) / (4.0 * harmonic**2 - 1.0)
    weight = 2.0 / NLAT * (1.0 - 2.0 * np.sum(terms, axis=1))
    rows = np.stack([np.cos(colatitude), np.log(np.sin(colatitude)), weight])
    rows = np.concatenate([rows, np.zeros((5, NLAT))]).reshape(8, LAT_BLOCKS, BLOCK_LATS)
    rows = np.pad(rows, ((0, 0), (0, 0), (0, LANES - BLOCK_LATS)))
    return rows.reshape(8, SPAN).astype(np.float32)


def legendre_rows(start_ref, order_ref, lat_ref, rows_ref):
    order = jnp.concatenate([order_ref[...]] * LAT_BLOCKS, axis=1)
    cosine = jnp.broadcast_to(lat_ref[0:1, :], (TILE, SPAN))
    log_sin = jnp.broadcast_to(lat_ref[1:2, :], (TILE, SPAN))
    log_start = jnp.concatenate([start_ref[...]] * LAT_BLOCKS, axis=1) + order * log_sin
    narrow = order_ref[...]
    narrow_square = narrow * narrow
    second_factor = jnp.concatenate([jnp.sqrt(2.0 * narrow + 3.0)] * LAT_BLOCKS, axis=1)
    zeros = jnp.zeros((TILE, SPAN), F32)

    def block(index, state):
        previous, current, log_scale = state
        scale = jnp.exp(log_scale)
        for inner in range(16):
            row = index * 16 + inner
            degree = row.astype(F32)
            lower = degree - 1.0
            up = jnp.sqrt(
                jnp.maximum(4.0 * degree * degree - 1.0, 1.0)
                / jnp.maximum(degree * degree - narrow_square, 1.0)
            )
            down = jnp.sqrt(
                jnp.maximum(lower * lower - narrow_square, 0.0)
                / jnp.maximum(4.0 * lower * lower - 1.0, 1.0)
            )
            up = jnp.concatenate([up] * LAT_BLOCKS, axis=1)
            down = jnp.concatenate([down] * LAT_BLOCKS, axis=1)
            general = up * (cosine * current - down * previous)
            second = second_factor * cosine * current
            new_row = jnp.where(
                degree == order,
                1.0,
                jnp.where(
                    degree == order + 1.0, second, jnp.where(degree > order + 1.0, general, 0.0)
                ),
            )
            scaled = new_row * scale
            for part in range(LAT_BLOCKS):
                rows_ref[part, row] = scaled[:, part * LANES : (part + 1) * LANES]
            previous, current = current, new_row
        largest = jnp.maximum(jnp.abs(previous), jnp.abs(current))
        largest = jnp.where(largest > 0.0, largest, 1.0)
        return previous / largest, current / largest, log_scale + jnp.log(largest)

    lax.fori_loop(0, MODES // 16, block, (zeros, zeros, log_start))


def table_kernel(start_ref, order_ref, lat_ref, flat_ref, turned_ref, *rest):
    outs, rows_ref, buffers, sems = rest[:12], rest[12], rest[13:25], rest[25]
    legendre_rows(start_ref, order_ref, lat_ref, rows_ref)
    copies = []
    for group in range(GROUPS):
        ahead_flat, ahead_turned, behind_flat, behind_turned = buffers[4 * group : 4 * group + 4]

        def part_step(part, carry):
            lats = pl.ds(pl.multiple_of(part * LANES, LANES), LANES)
            weight = lat_ref[2:3, lats]
            for local in range(GROUP_ORDERS):
                legendre = rows_ref[part, LANES * group :, GROUP_ORDERS * group + local, :]
                synthesis = legendre.astype(BF16)
                analysis = (weight * legendre).astype(BF16)
                pairs = [index for index, (order, _) in enumerate(PAIRS) if order == local]
                flat = jnp.concatenate([flat_ref[index] for index in pairs], axis=1)
                turned = jnp.concatenate([turned_ref[index] for index in pairs], axis=0)
                products = (
                    dot(analysis, flat).astype(BF16),
                    dot_nt(turned, synthesis).astype(BF16),
                    dot(synthesis, flat).astype(BF16),
                    dot_nt(turned, analysis).astype(BF16),
                )
                for place, index in enumerate(pairs):
                    cut = slice(place * LANES, (place + 1) * LANES)
                    ahead_flat[index, :, lats] = products[0][:, cut]
                    ahead_turned[index, lats, :] = products[1][cut]
                    behind_flat[index, :, lats] = products[2][:, cut]
                    behind_turned[index, lats, :] = products[3][cut]
            return carry

        lax.fori_loop(0, LAT_BLOCKS, part_step, 0)
        for place in range(4):
            at = 4 * group + place
            copy = pltpu.make_async_copy(buffers[at], outs[at], sems.at[at])
            copy.start()
            copies.append(copy)
    for copy in copies:
        copy.wait()


def legendre_tables(start, order, lat, flat, turned, after):
    shapes = []
    for group in range(GROUPS):
        degrees = degrees_of(group)
        shapes += [(len(PAIRS), degrees, SPAN), (len(PAIRS), SPAN, degrees)] * 2
    inputs = (start, order, lat, flat, turned)
    return call(
        table_kernel,
        inputs,
        [whole(value.shape) for value in inputs],
        [HELD] * len(shapes),
        [jax.ShapeDtypeStruct(shape, BF16) for shape in shapes],
        (1,),
        after,
        scratch_shapes=[pltpu.VMEM((LAT_BLOCKS, MODES, TILE, LANES), F32)]
        + [pltpu.VMEM(shape, BF16) for shape in shapes]
        + [pltpu.SemaphoreType.DMA((len(shapes),))],
        name="legendre_tables",
    )


def blocks_of(value):
    return [value[:, index * HALF : (index + 1) * HALF] for index in range(GROUPS)]


def interleave(first, second):
    pairs = zip(blocks_of(first), blocks_of(second))
    return jnp.concatenate([block for pair in pairs for block in pair], axis=1)


def prepare_kernel(gain_ref, mix_ref, proj_ref, gain_out, mix_out, proj_out):
    gain = gain_ref[...].T
    gain_out[...] = interleave(gain, gain)
    real, imag = mix_ref[0].astype(F32), mix_ref[1].astype(F32)
    upper, lower = interleave(real, imag), interleave(-imag, real)
    for index in range(GROUPS):
        rows = slice(index * HALF, (index + 1) * HALF)
        start = index * LANES
        mix_out[start : start + HALF, :] = upper[rows].astype(BF16)
        mix_out[start + HALF : start + LANES, :] = lower[rows].astype(BF16)
    proj = proj_ref[...].astype(F32).T
    proj_out[...] = interleave(proj, proj).astype(BF16)


def prepare(gain, mix, proj, after):
    shapes = ((MODES, 2 * C), (2 * C, 2 * C), (C, 2 * C))
    kinds = (F32, BF16, BF16)
    return call(
        prepare_kernel,
        (gain, mix, proj),
        [whole(gain.shape), whole(mix.shape), whole(proj.shape)],
        [whole(shape) for shape in shapes],
        [jax.ShapeDtypeStruct(shape, kind) for shape, kind in zip(shapes, kinds)],
        (1,),
        after,
        name="prepare",
    )


def spectrum_kernel(field_ref, table_ref, out_ref, scratch):
    step = pl.program_id(0)
    rows = table_ref.shape[0] // 2
    low = half_lanes((rows, LANES))
    for inner in range(4):
        product = dot_nt(table_ref[...], field_ref[inner])
        real, imag = product[:rows], product[rows:]
        real_a, imag_a = real[:, :LANES], imag[:, :LANES]
        tiles = (
            jnp.where(low, real_a, pltpu.roll(imag_a, HALF, 1)),
            jnp.where(low, pltpu.roll(real_a, HALF, 1), imag_a),
            jnp.concatenate([real[:, LANES:], imag[:, LANES:]], axis=1),
        )
        for index, tile in enumerate(tiles):
            scratch[index, pl.ds(step * 4 + inner, rows, stride=LAT_LOCAL), :] = tile

    @pl.when(step == LAT_LOCAL // 4 - 1)
    def _():
        for index in range(GROUPS):
            out_ref[:, index * LANES : (index + 1) * LANES] = scratch[index].astype(BF16)


def spectrum_rows(field, table, after=()):
    rows = table.shape[0] // 2 * LAT_LOCAL
    return call(
        spectrum_kernel,
        (field, table),
        [pl.BlockSpec((4, C, NLON), lambda b: (b, 0, 0)), whole(table.shape)],
        whole((rows, 2 * C)),
        jax.ShapeDtypeStruct((rows, 2 * C), BF16),
        (LAT_LOCAL // 4,),
        after,
        scratch_shapes=[pltpu.VMEM((GROUPS, rows, LANES), F32)],
        name="spectrum_rows",
    )


def pair_sum(local, table_ref, tiles):
    pairs = [(index, tile) for index, (order, tile) in enumerate(PAIRS) if order == local]
    left = [table_ref[index, DEVICES * local :, :] for index, _ in pairs]
    right = [tiles[tile] for _, tile in pairs]
    if len(pairs) == 1:
        return dot(left[0], right[0])
    return dot(jnp.concatenate(left, axis=1), jnp.concatenate(right, axis=0))


def tile_sum(tile, table_ref, first, second):
    left = jnp.concatenate([table_ref[2 * tile], table_ref[2 * tile + 1]], axis=1)
    return dot(left, jnp.concatenate([first, second], axis=0))


def spectral_kernel(recv_ref, *refs):
    a_refs, st_refs = refs[0:3], refs[3:6]
    gain_ref, mix_ref = refs[6:8]
    scaled_ref, payload_ref, recv, payload = refs[8:12]
    a_buffers, st_buffers, scaled_buffers = refs[12:15], refs[15:18], refs[18:21]
    in_sems, out_sems = refs[21:23]
    schedule = (2, 0, 1)
    arrivals, departures = {}, []
    for group in schedule:
        tiles = pl.ds(GROUP_TILES * group, GROUP_TILES)
        arrivals[group] = [
            pltpu.make_async_copy(recv_ref.at[:, tiles], recv.at[group], in_sems.at[group, 0]),
            pltpu.make_async_copy(a_refs[group], a_buffers[group], in_sems.at[group, 1]),
            pltpu.make_async_copy(st_refs[group], st_buffers[group], in_sems.at[group, 2]),
        ]
        for copy in arrivals[group]:
            copy.start()
    for group in schedule:
        for copy in arrivals[group]:
            copy.wait()
        tiles = [recv[group, :, tile].reshape(SPAN, 2 * C) for tile in range(GROUP_TILES)]
        mixed = []
        for local in range(GROUP_ORDERS):
            skipped = DEVICES * local
            coef = pair_sum(local, a_buffers[group], tiles)
            scaled = (gain_ref[LANES * group + skipped :, :] * coef).astype(BF16)
            scaled_buffers[group][packed_rows(group)[local], :] = scaled
            product = dot(scaled, mix_ref[...]).astype(BF16)
            if skipped:
                zeros = jnp.zeros((skipped, 2 * C), BF16)
                product = jnp.concatenate([zeros, product], axis=0)
            mixed.append(product)
        for tile in range(GROUP_TILES):
            grid = tile_sum(tile, st_buffers[group], mixed[tile], mixed[tile + 1])
            payload[group, :, tile] = grid.astype(BF16).reshape(DEVICES, TILE, 2 * C)
        tiles = pl.ds(GROUP_TILES * group, GROUP_TILES)
        copies = (
            pltpu.make_async_copy(
                payload.at[group], payload_ref.at[:, tiles], out_sems.at[group, 0]
            ),
            pltpu.make_async_copy(
                scaled_buffers[group],
                scaled_ref.at[pl.ds(BASES[group], PACKED[group])],
                out_sems.at[group, 1],
            ),
        )
        for copy in copies:
            copy.start()
            departures.append(copy)
    for copy in departures:
        copy.wait()


def spectral_forward(recv, a, st, gain, mix, after=()):
    slots = (GROUPS, DEVICES, GROUP_TILES, TILE, 2 * C)
    return call(
        spectral_kernel,
        (recv, *a, *st, gain, mix),
        [HELD] * 7 + [whole(gain.shape), whole(mix.shape)],
        [HELD] * 2,
        [
            jax.ShapeDtypeStruct((sum(PACKED), 2 * C), BF16),
            jax.ShapeDtypeStruct(recv.shape, BF16),
        ],
        (1,),
        after,
        scratch_shapes=[pltpu.VMEM(slots, BF16), pltpu.VMEM(slots, BF16)]
        + [pltpu.VMEM(value.shape, BF16) for value in a]
        + [pltpu.VMEM(value.shape, BF16) for value in st]
        + [pltpu.VMEM((rows, 2 * C), BF16) for rows in PACKED]
        + [pltpu.SemaphoreType.DMA((GROUPS, 3)), pltpu.SemaphoreType.DMA((GROUPS, 2))],
        name="spectral_forward",
    )


def normal_cumulative(value, bell):
    denominator = 1.0 + (0.3275911 / math.sqrt(2.0)) * jnp.abs(value)
    inverse = pl.reciprocal(denominator, approx=True)
    inverse = inverse * (2.0 - denominator * inverse)
    series = 0.5 * 1.061405429 * inverse - 0.5 * 1.453152027
    series = series * inverse + 0.5 * 1.421413741
    series = series * inverse - 0.5 * 0.284496736
    series = series * inverse + 0.5 * 0.254829592
    tail = series * inverse * bell
    return jnp.where(value < 0.0, tail, 1.0 - tail)


def grid_kernel(
    recv_ref, up_ref, turned_ref, proj_ref, table_ref, turned_table_ref,
    out_ref, grad_ref, scratch, out_scratch, act_scratch, pre_scratch,
):
    step = pl.program_id(1)
    low = half_lanes((MODES, LANES))
    block = 128

    @pl.when(step == 0)
    def _():
        scratch[...] = recv_ref[...].astype(F32)
        grad_ref[...] = jnp.zeros_like(grad_ref)

    columns = []
    for pair in range(2):
        first = scratch[pl.ds(step * 4 + 2 * pair, MODES, stride=LAT_LOCAL), :]
        second = scratch[pl.ds(step * 4 + 2 * pair + 1, MODES, stride=LAT_LOCAL), :]
        real = jnp.where(low, first, pltpu.roll(second, HALF, 1))
        imag = jnp.where(low, pltpu.roll(first, HALF, 1), second)
        columns.append(jnp.concatenate([real, imag], axis=0).astype(BF16))
    modes = jnp.concatenate(columns, axis=1)
    low_block = half_lanes((block, LANES))
    for part in range(NLON // block):
        rows = slice(part * block, (part + 1) * block)
        pre = dot(turned_table_ref[rows, :], modes)
        grad_act = jnp.concatenate(
            [
                jnp.where(
                    low_block,
                    dot(turned_ref[2 * pair, rows, :], proj_ref[...]),
                    dot(turned_ref[2 * pair + 1, rows, :], proj_ref[...]),
                )
                for pair in range(2)
            ],
            axis=1,
        )
        bell = jnp.exp(-0.5 * pre * pre)
        cumulative = normal_cumulative(pre, bell)
        slope = cumulative + pre * bell * (1.0 / math.sqrt(2.0 * math.pi))
        act_scratch[rows, :] = (pre * cumulative).astype(BF16)
        pre_scratch[rows, :] = (grad_act * slope).astype(BF16)
    low_grad = half_lanes((C, LANES))
    for pair in range(2):
        lanes = slice(pair * LANES, (pair + 1) * LANES)
        act = act_scratch[:, lanes]
        grad_ref[...] += jnp.where(
            low_grad, dot(up_ref[2 * pair], act), dot(up_ref[2 * pair + 1], act)
        )
    grad_modes = dot(table_ref[...], pre_scratch[...])
    for pair in range(2):
        lanes = slice(pair * LANES, (pair + 1) * LANES)
        real, imag = grad_modes[:MODES, lanes], grad_modes[MODES:, lanes]
        out_scratch[pl.ds(step * 4 + 2 * pair, MODES, stride=LAT_LOCAL), :] = jnp.where(
            low, real, pltpu.roll(imag, HALF, 1)
        )
        out_scratch[pl.ds(step * 4 + 2 * pair + 1, MODES, stride=LAT_LOCAL), :] = jnp.where(
            low, pltpu.roll(real, HALF, 1), imag
        )

    @pl.when(step == LAT_LOCAL // 4 - 1)
    def _():
        out_ref[...] = out_scratch[...].astype(BF16)


def grid_stage(first, blocks, recv, up, turned, proj, table, turned_table, after=()):
    rows = MODES * LAT_LOCAL
    lanes_spec = pl.BlockSpec((rows, LANES), lambda q, b: (0, q))
    grad_spec = pl.BlockSpec((C, LANES), lambda q, b: (0, q))
    return call(
        grid_kernel,
        (recv, up, turned, proj, table, turned_table),
        [
            pl.BlockSpec((rows, LANES), lambda q, b: (0, q + first)),
            pl.BlockSpec((4, C, NLON), lambda q, b: (b, 0, 0)),
            pl.BlockSpec((4, NLON, C), lambda q, b: (b, 0, 0)),
            pl.BlockSpec((C, LANES), lambda q, b: (0, q + first)),
            whole(table.shape),
            whole(turned_table.shape),
        ],
        [lanes_spec, grad_spec],
        [
            jax.ShapeDtypeStruct((rows, LANES * blocks), BF16),
            jax.ShapeDtypeStruct((C, LANES * blocks), F32),
        ],
        (blocks, LAT_LOCAL // 4),
        after,
        scratch_shapes=[
            pltpu.VMEM((rows, LANES), F32),
            pltpu.VMEM((rows, LANES), F32),
            pltpu.VMEM((NLON, 2 * LANES), BF16),
            pltpu.VMEM((NLON, 2 * LANES), BF16),
        ],
        name=f"grid_stage_{blocks}",
    )


def backward_kernel(groups, *refs):
    recv_ref, table_refs, out_ref = refs[0], refs[1 : 1 + len(groups)], refs[1 + len(groups)]
    buffers, sems = refs[2 + len(groups) : -1], refs[-1]
    copies = [
        pltpu.make_async_copy(table_refs[place], buffers[place], sems.at[place])
        for place in range(len(groups))
    ]
    for copy in copies:
        copy.start()
    lanes = recv_ref.shape[-1]
    first = 0
    for place, group in enumerate(groups):
        start = GROUP_TILES * place
        tiles = [
            recv_ref[:, start + tile].reshape(SPAN, lanes) for tile in range(GROUP_TILES)
        ]
        copies[place].wait()
        for local, rows in enumerate(packed_rows(group)):
            mixed = pair_sum(local, buffers[place], tiles).astype(BF16)
            out_ref[first + rows.start : first + rows.stop, :] = mixed
        first += PACKED[group]


def spectral_backward(groups, recv, tables, after=()):
    lanes = recv.shape[-1]
    tiles = GROUP_TILES * len(groups)
    block = groups[0] if len(groups) == 1 else 0
    out = (sum(PACKED[group] for group in groups), lanes)
    return call(
        functools.partial(backward_kernel, groups),
        (recv, *tables),
        [
            pl.BlockSpec(
                (DEVICES, tiles, TILE, lanes),
                lambda b: (0, block, 0, 0),
                pipeline_mode=pl.Buffered(1),
            )
        ]
        + [HELD] * len(groups),
        whole(out),
        jax.ShapeDtypeStruct(out, BF16),
        (1,),
        after,
        scratch_shapes=[pltpu.VMEM(table.shape, BF16) for table in tables]
        + [pltpu.SemaphoreType.DMA((len(groups),))],
        vmem=20,
        name="spectral_backward_" + "_".join(str(group) for group in groups),
    )


def hold_kernel(value_ref, out_ref):
    pass


def hold(value, after):
    held = pl.BlockSpec(memory_space=pl.ANY)
    return call(
        hold_kernel,
        (value,),
        [held],
        held,
        jax.ShapeDtypeStruct(value.shape, value.dtype),
        (1,),
        after,
        aliases={0: 0},
        vmem=1,
        name="hold",
    )


def synthesis_kernel(group, table_ref, small_ref, large_ref, gain_ref, mix_ref, *refs):
    extra, (out_ref, coeff_ref, at_ref, part_ref, sems) = refs[:-5], refs[-5:]
    degrees = degrees_of(group)
    copies = (
        pltpu.make_async_copy(
            small_ref.at[pl.ds(BASES[group], PACKED[group])], part_ref, sems.at[0]
        ),
        pltpu.make_async_copy(table_ref, at_ref, sems.at[1]),
    )
    for copy in copies:
        copy.start()
    copies[0].wait()
    for local, rows in enumerate(packed_rows(group)):
        first = local * degrees
        skipped = DEVICES * local
        mixed = jnp.concatenate([part_ref[rows, :], large_ref[rows, :]], axis=1)
        scaled = dot_nt(mixed, mix_ref[...])
        if skipped:
            coeff_ref[first : first + skipped, :] = jnp.zeros((skipped, 2 * C), BF16)
        coeff_ref[first + skipped : first + degrees, :] = (
            gain_ref[LANES * group + skipped :, :] * scaled
        ).astype(BF16)
    copies[1].wait()
    for tile in range(GROUP_TILES):
        first = coeff_ref[tile * degrees : (tile + 1) * degrees, :]
        second = coeff_ref[(tile + 1) * degrees : (tile + 2) * degrees, :]
        out = tile_sum(tile, at_ref, first, second)
        out_ref[:, tile] = out.astype(BF16).reshape(DEVICES, TILE, 2 * C)
    if extra:
        out_ref[:, GROUP_TILES] = extra[0][...]


def analysis_back(group, at, small, large, gain, mix, tiles, extra=(), after=()):
    inputs = (at, small, large, gain, mix, *extra)
    return call(
        functools.partial(synthesis_kernel, group),
        inputs,
        [HELD] * 2 + [whole(value.shape) for value in inputs[2:]],
        whole((DEVICES, GROUP_TILES + len(extra), TILE, 2 * C)),
        jax.ShapeDtypeStruct((DEVICES, tiles, TILE, 2 * C), BF16),
        (1,),
        after,
        scratch_shapes=[
            pltpu.VMEM((GROUP_ORDERS * degrees_of(group), 2 * C), BF16),
            pltpu.VMEM(at.shape, BF16),
            pltpu.VMEM((PACKED[group], LANES), BF16),
            pltpu.SemaphoreType.DMA((2,)),
        ],
        vmem=20,
        name=f"analysis_back_{group}",
    )


def fold(tile):
    return tile + pltpu.roll(tile, HALF, 1)


def weight_kernel(held_ref, small_ref, *refs):
    large_refs, (mix_ref, factor_ref, proj_small, proj_large) = refs[:3], refs[3:7]
    out_ref, gain, packed, spaced, scaled_ref, sem = refs[7:]
    copy = pltpu.make_async_copy(held_ref, scaled_ref, sem)
    copy.start()
    copy.wait()
    block = None
    for group in range(GROUPS):
        rows = slice(BASES[group], BASES[group] + PACKED[group])
        mixed = jnp.concatenate([small_ref[rows, :], large_refs[group][...]], axis=1)
        part = lax.dot_general(
            scaled_ref[rows, :], mixed, (((0,), (0,)), ((), ())), preferred_element_type=F32
        )
        block = part if block is None else block + part
        for local, rows in enumerate(packed_rows(group)):
            here = slice(BASES[group] + rows.start, BASES[group] + rows.stop)
            mixed = jnp.concatenate([small_ref[here, :], large_refs[group][rows, :]], axis=1)
            part = dot_nt(mixed, mix_ref[...]) * scaled_ref[here, :].astype(F32)
            first = LANES * group + DEVICES * local
            if first:
                gain[first:, :] += part
            else:
                gain[...] = part
    gain[...] = gain[...] / factor_ref[...]
    low = half_lanes((HALF, LANES))
    low_gain = half_lanes((C, LANES))
    low_proj = half_lanes((C // 2, LANES))
    for index in range(GROUPS):
        lanes = slice(index * LANES, (index + 1) * LANES)
        for row_block in range(GROUPS):
            start = row_block * LANES
            first = block[start : start + HALF, lanes]
            second = pltpu.roll(block[start + HALF : start + LANES, lanes], HALF, 1)
            packed[index, row_block * HALF : (row_block + 1) * HALF, :] = jnp.where(
                low, first + second, first - second
            )
        packed[index, C : 2 * C, :] = jnp.where(
            low_gain, fold(gain[:C, lanes]), fold(gain[C:, lanes])
        )
        if index == 0:
            proj = fold(proj_small[...])
        else:
            proj = fold(proj_large[:, (index - 1) * LANES : index * LANES])
        packed[index, 2 * C :, :] = jnp.where(low_proj, proj[: C // 2], proj[C // 2 :])
        for row in range(TILE - 1):
            spaced[index, pl.ds(row, DEVICES, stride=TILE), :] = packed[
                index, row * DEVICES : (row + 1) * DEVICES, :
            ]
        spaced[index, pl.ds(TILE - 1, DEVICES, stride=TILE), :] = jnp.zeros((DEVICES, LANES), F32)
        out_ref[:, :, lanes] = spaced[index].astype(BF16).reshape(DEVICES, TILE, LANES)


def weight_grads(scaled, small, large, mix, gain, proj_small, proj_large, after=()):
    out = (DEVICES, TILE, 2 * C)
    inputs = (scaled, small, *large, mix, gain, proj_small, proj_large)
    return call(
        weight_kernel,
        inputs,
        [HELD] + [whole(value.shape) for value in inputs[1:]],
        whole(out),
        jax.ShapeDtypeStruct(out, BF16),
        (1,),
        after,
        scratch_shapes=[
            pltpu.VMEM((MODES, 2 * C), F32),
            pltpu.VMEM((GROUPS, 15 * DEVICES, LANES), F32),
            pltpu.VMEM((GROUPS, TILE * DEVICES, LANES), F32),
            pltpu.VMEM(scaled.shape, BF16),
            pltpu.SemaphoreType.DMA,
        ],
        vmem=24,
        name="weight_grads",
    )


def total_kernel(recv_ref, payload_ref, out_ref):
    total = jnp.sum(recv_ref[:, 0].astype(F32), axis=0)
    out_ref[:, 0] = jnp.broadcast_to(total.astype(BF16)[None], (DEVICES, TILE, 2 * C))


def attach_totals(recv, payload):
    spec = pl.BlockSpec((DEVICES, 1, TILE, 2 * C), lambda b: (0, GROUP_TILES, 0, 0))
    return call(
        total_kernel,
        (recv, payload),
        [spec, pl.BlockSpec(memory_space=pl.ANY)],
        spec,
        jax.ShapeDtypeStruct(payload.shape, BF16),
        (1,),
        aliases={1: 0},
        vmem=8,
        name="attach_totals",
    )


def unpack_totals(recv_ref, proj_ref, mix_ref, gain_ref, spaced, packed):
    grid_scale = 1.0 / math.sqrt(NLAT * NLON)
    mode_scale = 1.0 / math.sqrt(MODES)
    lows, highs = [], []
    for index in range(GROUPS):
        lanes = slice(index * LANES, (index + 1) * LANES)
        spaced[index] = recv_ref[:, GROUP_TILES, :, lanes].reshape(DEVICES * TILE, LANES).astype(F32)
        for row in range(TILE - 1):
            packed[index, row * DEVICES : (row + 1) * DEVICES, :] = spaced[
                index, pl.ds(row, DEVICES, stride=TILE), :
            ]
        lows.append(packed[index, :, :HALF])
        highs.append(packed[index, :, HALF:])
    low = jnp.concatenate(lows, axis=1)
    high = jnp.concatenate(highs, axis=1)
    mix_ref[0] = grid_scale * low[:C]
    mix_ref[1] = grid_scale * high[:C]
    gain = jnp.concatenate([low[C : 2 * C], high[C : 2 * C]], axis=0)
    gain_ref[...] = mode_scale * gain.T
    proj = jnp.concatenate([low[2 * C :], high[2 * C :]], axis=0)
    proj_ref[...] = grid_scale * proj.T


def field_kernel(recv_ref, table_ref, base_ref, out_ref, *refs):
    totals, (scratch, *unpacking) = refs[:3] if len(refs) > 1 else (), refs[3:] or refs
    step = pl.program_id(0)
    orders = DEVICES * GROUP_ORDERS
    rows = orders * LAT_LOCAL

    @pl.when(step == 0)
    def _():
        for index in range(GROUPS):
            lanes = slice(index * LANES, (index + 1) * LANES)
            values = recv_ref[:, :GROUP_TILES, :, lanes].astype(F32)
            scratch[index] = values.reshape(rows, LANES)
        if totals:
            unpack_totals(recv_ref, *totals, *unpacking)

    lefts = []
    for inner in range(4):
        real, imag = [], []
        for index in range(GROUPS):
            values = scratch[index, pl.ds(step * 4 + inner, orders, stride=LAT_LOCAL), :]
            turned = values.T.astype(BF16)
            real.append(turned[:HALF])
            imag.append(turned[HALF:])
        lefts.append(
            jnp.concatenate(
                [jnp.concatenate(real, axis=0), jnp.concatenate(imag, axis=0)], axis=1
            )
        )
    product = dot(jnp.concatenate(lefts, axis=0), table_ref[...])
    for inner in range(4):
        total = base_ref[inner].astype(F32) + product[inner * C : (inner + 1) * C]
        out_ref[inner] = total.astype(out_ref.dtype)


def field_stage(recv, table, base, unpacked=False, after=()):
    rows = DEVICES * GROUP_ORDERS * LAT_LOCAL
    block = pl.BlockSpec((4, C, NLON), lambda b: (b, 0, 0))
    tiles = GROUP_TILES + int(unpacked)
    totals = ((C, C), (2, C, C), (C, MODES)) if unpacked else ()
    scratch_shapes = [pltpu.VMEM((GROUPS, rows, LANES), F32)]
    if unpacked:
        scratch_shapes += [
            pltpu.VMEM((GROUPS, TILE * DEVICES, LANES), F32),
            pltpu.VMEM((GROUPS, 15 * DEVICES, LANES), F32),
        ]
    return call(
        field_kernel,
        (recv, table, base),
        [
            pl.BlockSpec(
                (DEVICES, tiles, TILE, 2 * C),
                lambda b: (0, 0, 0, 0),
                pipeline_mode=pl.Buffered(1),
            ),
            whole(table.shape),
            block,
        ],
        [block] + [whole(shape) for shape in totals],
        [jax.ShapeDtypeStruct((LAT_LOCAL, C, NLON), BF16)]
        + [jax.ShapeDtypeStruct(shape, F32) for shape in totals],
        (LAT_LOCAL // 4,),
        after,
        scratch_shapes=scratch_shapes,
        vmem=24 if unpacked else 20,
        name="field_stage",
    )


def exchange(payload):
    tiles, lanes = payload.shape[1], payload.shape[3]
    flat = payload.reshape(DEVICES, tiles * TILE, lanes)
    moved = lax.all_to_all(flat, "lat", split_axis=0, concat_axis=0, tiled=True)
    return moved.reshape(DEVICES, tiles, TILE, lanes)


def shards(saved_input, incoming, spectral_gain, mix_weight, proj_weight):
    device = lax.axis_index("lat")
    section_count = lax.axis_size("section")
    shift = [(source, (source - 1) % section_count) for source in range(section_count)]

    forward_all = forward_rows(0, GROUPS)
    forward = [forward_rows(group, 1) for group in range(GROUPS)]
    inverse_np = inverse_rows()
    inverse = jnp.asarray(inverse_np)
    inverse_turned = jnp.asarray(np.ascontiguousarray(inverse_np.T))
    spread, spread_turned = spread_tables()
    lat = jnp.asarray(latitude_rows())
    starts, numbers = log_starts()
    start = lax.dynamic_index_in_dim(jnp.asarray(starts), device, 0, keepdims=False)
    order = lax.dynamic_index_in_dim(jnp.asarray(numbers), device, 0, keepdims=False)

    field = saved_input[0]
    upstream = incoming[0]
    upstream_next = lax.ppermute(upstream, "section", shift)
    turned = jnp.swapaxes(upstream, 1, 2)
    rows = MODES * LAT_LOCAL
    spectrum = spectrum_rows(field, forward_all)
    recv = exchange(spectrum.reshape(DEVICES, TILES, TILE, 2 * C))
    gain, mix, proj = prepare(
        jnp.swapaxes(spectral_gain[0], 0, 1), mix_weight[0], proj_weight[0], (spectrum,)
    )
    gain_next, mix_next, _ = prepare(
        lax.ppermute(jnp.swapaxes(spectral_gain[0], 0, 1), "section", shift),
        lax.ppermute(mix_weight[0], "section", shift),
        proj_weight[0],
        (spectrum,),
    )
    tables = legendre_tables(start, order, lat, spread, spread_turned, (spectrum,))
    behind = [tables[4 * group + 2 : 4 * group + 4] for group in range(GROUPS)]
    scaled, payload = spectral_forward(
        recv, tables[0::4], tables[1::4], gain, mix, (turned, proj)
    )
    recv = exchange(payload).reshape(rows, 2 * C)
    small_rows, proj_small = grid_stage(
        0,
        1,
        recv,
        upstream,
        turned,
        proj,
        inverse,
        inverse_turned,
        (upstream_next, gain_next, mix_next),
    )
    small = exchange(small_rows.reshape(DEVICES, TILES, TILE, LANES))
    large, proj_large = grid_stage(
        1, 2, recv, upstream, turned, proj, inverse, inverse_turned, (small_rows,)
    )
    large = exchange(large.reshape(DEVICES, TILES, TILE, 2 * LANES))

    mixeds, moved = [None] * GROUPS, [None] * GROUPS
    every = tuple(range(GROUPS))
    mixed_small = spectral_backward(every, small, [table[0] for table in behind])
    moved_small = lax.ppermute(mixed_small, "section", shift)
    mixed_2 = spectral_backward((2,), large, [behind[2][0]], (moved_small,))
    moved_2 = lax.ppermute(mixed_2, "section", shift)
    out_2 = analysis_back(
        2, behind[2][1], moved_small, moved_2, gain_next, mix_next, GROUP_TILES
    )
    recv_2 = exchange(out_2)
    mixed_0 = spectral_backward((0,), large, [behind[0][0]], (out_2,))
    moved_0 = lax.ppermute(mixed_0, "section", shift)
    mixed_1 = spectral_backward((1,), large, [behind[1][0]], (mixed_0,))
    moved_1 = lax.ppermute(hold(mixed_1, (moved_0,)), "section", shift)
    partial_grads = weight_grads(
        scaled, mixed_small, (mixed_0, mixed_1, mixed_2), mix, gain, proj_small, proj_large
    )
    out_0 = analysis_back(
        0,
        behind[0][1],
        moved_small,
        moved_0,
        gain_next,
        mix_next,
        GROUP_TILES + 1,
        (partial_grads,),
    )
    out_0 = hold(out_0, (recv_2,))
    recv_0 = exchange(out_0)
    out_1 = analysis_back(
        1,
        behind[1][1],
        moved_small,
        moved_1,
        gain_next,
        mix_next,
        GROUP_TILES + 1,
        after=(recv_2,),
    )
    out_1 = attach_totals(recv_0, out_1)
    recv_1 = exchange(out_1)
    (base,) = field_stage(recv_2, forward[2], upstream_next, after=(out_1,))
    (base,) = field_stage(recv_0, forward[0], base)
    received, grad_w2, grad_mix, grad_gain = field_stage(recv_1, forward[1], base, True)
    return (
        received[None],
        grad_w2[None],
        grad_mix[None],
        jnp.swapaxes(grad_gain, 0, 1)[None],
    )


def solution(mesh):
    in_specs = (
        P("section", "lat", None, None),
        P("section", "lat", None, None),
        P("section", None, None),
        P("section", None, None, None),
        P("section", None, None),
    )
    out_specs = (
        P("section", "lat", None, None),
        P("section", None, None),
        P("section", None, None, None),
        P("section", None, None),
    )
    return jax.shard_map(shards, mesh=mesh, in_specs=in_specs, out_specs=out_specs, check_vma=False)
```

```python
import functools
import math

import jax
import jax.numpy as jnp
import ml_dtypes
import numpy as np
from jax import lax
from jax.experimental import pallas as pl
from jax.experimental.pallas import tpu as pltpu
from jax.sharding import PartitionSpec as P

NLAT = 384
NLON = 768
MODES = 384
C = 192
DEVICES = 32
LAT_LOCAL = 12
ORDERS = 12
GROUPS = 3
GROUP_ORDERS = 4
HALF = 64
LANES = 128
TILE = 16
TILES = 9
GROUP_TILES = 3
SPAN = DEVICES * TILE
LAT_BLOCKS = 4
BLOCK_LATS = NLAT // LAT_BLOCKS
MIB = 1024 * 1024
F32 = jnp.float32
BF16 = jnp.bfloat16
NT = (((1,), (1,)), ((), ()))

PAIRS = ((0, 0), (1, 0), (1, 1), (2, 1), (2, 2), (3, 2))


def degrees_of(group):
    return MODES - LANES * group


def half_lanes(shape):
    return lax.broadcasted_iota(jnp.int32, shape, 1) < HALF


def packed_rows(group):
    rows, first = [], 0
    for local in range(GROUP_ORDERS):
        rows.append(slice(first, first + degrees_of(group) - DEVICES * local))
        first = rows[-1].stop
    return rows


PACKED = [packed_rows(group)[-1].stop for group in range(GROUPS)]
BASES = [sum(PACKED[:group]) for group in range(GROUPS)]


def dot(left, right):
    return jnp.dot(left, right, preferred_element_type=F32)


def dot_nt(left, right):
    return lax.dot_general(left, right, NT, preferred_element_type=F32)


def whole(shape):
    return pl.BlockSpec(shape, lambda *_: (0,) * len(shape), pipeline_mode=pl.Buffered(1))


HELD = pl.BlockSpec(memory_space=pltpu.HBM)


def call(
    kernel, inputs, in_specs, out_specs, out_shape, grid, after=(), aliases=None, vmem=56, **extra
):
    count = len(inputs)

    def body(*refs):
        kernel(*refs[:count], *refs[count + len(after) :])

    return pl.pallas_call(
        body,
        grid=grid,
        in_specs=list(in_specs) + [pl.BlockSpec(memory_space=pl.ANY)] * len(after),
        out_specs=out_specs,
        out_shape=out_shape,
        input_output_aliases=aliases or {},
        compiler_params=pltpu.CompilerParams(vmem_limit_bytes=vmem * MIB),
        cost_estimate=pl.CostEstimate(flops=1, bytes_accessed=1, transcendentals=0),
        **extra,
    )(*inputs, *after)


def order_rows(first, count):
    device = np.arange(DEVICES)[:, None]
    local = np.arange(GROUP_ORDERS * count)[None, :] + GROUP_ORDERS * first
    return (DEVICES * local + device).reshape(-1)


def fourier_rows(orders):
    phase = (orders[:, None] * np.arange(NLON)[None, :]) % NLON
    angle = phase * (2.0 * math.pi / NLON)
    return np.cos(angle), -np.sin(angle)


def forward_rows(first, count):
    cosine, sine = fourier_rows(order_rows(first, count))
    table = np.concatenate([cosine, sine], axis=0)
    return jnp.asarray(table.astype(np.float32).astype(ml_dtypes.bfloat16))


def inverse_rows():
    device = np.arange(DEVICES)[:, None]
    orders = (DEVICES * np.arange(ORDERS)[None, :] + device).reshape(-1)
    factor = np.where(orders == 0, 1.0, 2.0)[:, None] / NLON
    cosine, sine = fourier_rows(orders)
    table = np.concatenate([factor * cosine, factor * sine], axis=0)
    return table.astype(np.float32).astype(ml_dtypes.bfloat16)


def spread_tables():
    rows = np.arange(LANES)
    source, inner = rows // TILE, rows % TILE
    tables = np.zeros((len(PAIRS), LANES, LANES), np.float32)
    for index, (order, tile) in enumerate(PAIRS):
        lat = TILE * tile + inner - LAT_LOCAL * order
        valid = (lat >= 0) & (lat < LAT_LOCAL)
        tables[index, (source * LAT_LOCAL + lat)[valid], rows[valid]] = 1.0
    flat = jnp.asarray(tables.astype(ml_dtypes.bfloat16))
    turned = jnp.asarray(np.swapaxes(tables, 1, 2).astype(ml_dtypes.bfloat16))
    return flat, turned


def log_starts():
    table = np.zeros((DEVICES, TILE, LANES), np.float32)
    numbers = np.zeros((DEVICES, TILE, LANES), np.float32)
    for device in range(DEVICES):
        for local in range(ORDERS):
            order = DEVICES * local + device
            numbers[device, local] = order
            table[device, local] = 0.5 * math.log((2.0 * order + 1.0) / 2.0) + 0.5 * (
                math.lgamma(order + 0.5) - math.lgamma(0.5) - math.lgamma(order + 1.0)
            )
    return table, numbers


def latitude_rows():
    colatitude = (np.arange(NLAT) + 0.5) * (math.pi / NLAT)
    harmonic = np.arange(1, NLAT // 2 + 1)
    terms = np.cos(2.0 * harmonic[None, :] * colatitude[:, None]) / (4.0 * harmonic**2 - 1.0)
    weight = 2.0 / NLAT * (1.0 - 2.0 * np.sum(terms, axis=1))
    rows = np.stack([np.cos(colatitude), np.log(np.sin(colatitude)), weight])
    rows = np.concatenate([rows, np.zeros((5, NLAT))]).reshape(8, LAT_BLOCKS, BLOCK_LATS)
    rows = np.pad(rows, ((0, 0), (0, 0), (0, LANES - BLOCK_LATS)))
    return rows.reshape(8, SPAN).astype(np.float32)


def legendre_rows(start_ref, order_ref, lat_ref, rows_ref):
    order = jnp.concatenate([order_ref[...]] * LAT_BLOCKS, axis=1)
    cosine = jnp.broadcast_to(lat_ref[0:1, :], (TILE, SPAN))
    log_sin = jnp.broadcast_to(lat_ref[1:2, :], (TILE, SPAN))
    log_start = jnp.concatenate([start_ref[...]] * LAT_BLOCKS, axis=1) + order * log_sin
    narrow = order_ref[...]
    narrow_square = narrow * narrow
    second_factor = jnp.concatenate([jnp.sqrt(2.0 * narrow + 3.0)] * LAT_BLOCKS, axis=1)
    zeros = jnp.zeros((TILE, SPAN), F32)

    def block(index, state):
        previous, current, log_scale = state
        scale = jnp.exp(log_scale)
        for inner in range(16):
            row = index * 16 + inner
            degree = row.astype(F32)
            lower = degree - 1.0
            up = jnp.sqrt(
                jnp.maximum(4.0 * degree * degree - 1.0, 1.0)
                / jnp.maximum(degree * degree - narrow_square, 1.0)
            )
            down = jnp.sqrt(
                jnp.maximum(lower * lower - narrow_square, 0.0)
                / jnp.maximum(4.0 * lower * lower - 1.0, 1.0)
            )
            up = jnp.concatenate([up] * LAT_BLOCKS, axis=1)
            down = jnp.concatenate([down] * LAT_BLOCKS, axis=1)
            general = up * (cosine * current - down * previous)
            second = second_factor * cosine * current
            new_row = jnp.where(
                degree == order,
                1.0,
                jnp.where(
                    degree == order + 1.0, second, jnp.where(degree > order + 1.0, general, 0.0)
                ),
            )
            scaled = new_row * scale
            for part in range(LAT_BLOCKS):
                rows_ref[part, row] = scaled[:, part * LANES : (part + 1) * LANES]
            previous, current = current, new_row
        largest = jnp.maximum(jnp.abs(previous), jnp.abs(current))
        largest = jnp.where(largest > 0.0, largest, 1.0)
        return previous / largest, current / largest, log_scale + jnp.log(largest)

    lax.fori_loop(0, MODES // 16, block, (zeros, zeros, log_start))


def table_kernel(start_ref, order_ref, lat_ref, flat_ref, turned_ref, *rest):
    outs, rows_ref, buffers, sems = rest[:12], rest[12], rest[13:25], rest[25]
    legendre_rows(start_ref, order_ref, lat_ref, rows_ref)
    copies = []
    for group in range(GROUPS):
        ahead_flat, ahead_turned, behind_flat, behind_turned = buffers[4 * group : 4 * group + 4]

        def part_step(part, carry):
            lats = pl.ds(pl.multiple_of(part * LANES, LANES), LANES)
            weight = lat_ref[2:3, lats]
            for local in range(GROUP_ORDERS):
                legendre = rows_ref[part, LANES * group :, GROUP_ORDERS * group + local, :]
                synthesis = legendre.astype(BF16)
                analysis = (weight * legendre).astype(BF16)
                pairs = [index for index, (order, _) in enumerate(PAIRS) if order == local]
                flat = jnp.concatenate([flat_ref[index] for index in pairs], axis=1)
                turned = jnp.concatenate([turned_ref[index] for index in pairs], axis=0)
                products = (
                    dot(analysis, flat).astype(BF16),
                    dot_nt(turned, synthesis).astype(BF16),
                    dot(synthesis, flat).astype(BF16),
                    dot_nt(turned, analysis).astype(BF16),
                )
                for place, index in enumerate(pairs):
                    cut = slice(place * LANES, (place + 1) * LANES)
                    ahead_flat[index, :, lats] = products[0][:, cut]
                    ahead_turned[index, lats, :] = products[1][cut]
                    behind_flat[index, :, lats] = products[2][:, cut]
                    behind_turned[index, lats, :] = products[3][cut]
            return carry

        lax.fori_loop(0, LAT_BLOCKS, part_step, 0)
        for place in range(4):
            at = 4 * group + place
            copy = pltpu.make_async_copy(buffers[at], outs[at], sems.at[at])
            copy.start()
            copies.append(copy)
    for copy in copies:
        copy.wait()


def legendre_tables(start, order, lat, flat, turned, after):
    shapes = []
    for group in range(GROUPS):
        degrees = degrees_of(group)
        shapes += [(len(PAIRS), degrees, SPAN), (len(PAIRS), SPAN, degrees)] * 2
    inputs = (start, order, lat, flat, turned)
    return call(
        table_kernel,
        inputs,
        [whole(value.shape) for value in inputs],
        [HELD] * len(shapes),
        [jax.ShapeDtypeStruct(shape, BF16) for shape in shapes],
        (1,),
        after,
        scratch_shapes=[pltpu.VMEM((LAT_BLOCKS, MODES, TILE, LANES), F32)]
        + [pltpu.VMEM(shape, BF16) for shape in shapes]
        + [pltpu.SemaphoreType.DMA((len(shapes),))],
        name="legendre_tables",
    )


def blocks_of(value):
    return [value[:, index * HALF : (index + 1) * HALF] for index in range(GROUPS)]


def interleave(first, second):
    pairs = zip(blocks_of(first), blocks_of(second))
    return jnp.concatenate([block for pair in pairs for block in pair], axis=1)


def prepare_kernel(gain_ref, mix_ref, proj_ref, gain_out, mix_out, proj_out):
    gain = gain_ref[...].T
    gain_out[...] = interleave(gain, gain)
    real, imag = mix_ref[0].astype(F32), mix_ref[1].astype(F32)
    upper, lower = interleave(real, imag), interleave(-imag, real)
    for index in range(GROUPS):
        rows = slice(index * HALF, (index + 1) * HALF)
        start = index * LANES
        mix_out[start : start + HALF, :] = upper[rows].astype(BF16)
        mix_out[start + HALF : start + LANES, :] = lower[rows].astype(BF16)
    proj = proj_ref[...].astype(F32).T
    proj_out[...] = interleave(proj, proj).astype(BF16)


def prepare(gain, mix, proj, after):
    shapes = ((MODES, 2 * C), (2 * C, 2 * C), (C, 2 * C))
    kinds = (F32, BF16, BF16)
    return call(
        prepare_kernel,
        (gain, mix, proj),
        [whole(gain.shape), whole(mix.shape), whole(proj.shape)],
        [whole(shape) for shape in shapes],
        [jax.ShapeDtypeStruct(shape, kind) for shape, kind in zip(shapes, kinds)],
        (1,),
        after,
        name="prepare",
    )


def spectrum_kernel(field_ref, table_ref, out_ref, scratch):
    step = pl.program_id(0)
    rows = table_ref.shape[0] // 2
    low = half_lanes((rows, LANES))
    fields = field_ref[...].reshape(4 * C, NLON)
    product = dot_nt(table_ref[...], fields)
    for block in range(4 * GROUPS):
        inner, index = block // GROUPS, block % GROUPS
        lanes = slice(block // 2 * LANES, (block // 2 + 1) * LANES)
        real, imag = product[:rows, lanes], product[rows:, lanes]
        if block % 2:
            tile = jnp.where(low, pltpu.roll(real, HALF, 1), imag)
        else:
            tile = jnp.where(low, real, pltpu.roll(imag, HALF, 1))
        scratch[index, pl.ds(step * 4 + inner, rows, stride=LAT_LOCAL), :] = tile

    @pl.when(step == LAT_LOCAL // 4 - 1)
    def _():
        for index in range(GROUPS):
            out_ref[:, index * LANES : (index + 1) * LANES] = scratch[index].astype(BF16)


def spectrum_rows(field, table, after=()):
    rows = table.shape[0] // 2 * LAT_LOCAL
    return call(
        spectrum_kernel,
        (field, table),
        [pl.BlockSpec((4, C, NLON), lambda b: (b, 0, 0)), whole(table.shape)],
        whole((rows, 2 * C)),
        jax.ShapeDtypeStruct((rows, 2 * C), BF16),
        (LAT_LOCAL // 4,),
        after,
        scratch_shapes=[pltpu.VMEM((GROUPS, rows, LANES), F32)],
        name="spectrum_rows",
    )


def order_sums(group, table_ref, tiles):
    totals = [None] * GROUP_ORDERS
    for tile in range(GROUP_TILES):
        left = [table_ref[2 * tile + place, DEVICES * (tile + place) :, :] for place in range(2)]
        product = dot(jnp.concatenate(left, axis=0), tiles[tile])
        middle = left[0].shape[0]
        for order, part in ((tile, product[:middle]), (tile + 1, product[middle:])):
            totals[order] = part if totals[order] is None else totals[order] + part
    return totals


def tile_sum(tile, table_ref, first, second):
    left = jnp.concatenate([table_ref[2 * tile], table_ref[2 * tile + 1]], axis=1)
    return dot(left, jnp.concatenate([first, second], axis=0))


def spectral_kernel(recv_ref, *refs):
    a_refs, st_refs = refs[0:3], refs[3:6]
    gain_ref, mix_ref = refs[6:8]
    scaled_ref, payload_ref, recv, payload = refs[8:12]
    a_buffers, st_buffers, scaled_buffers = refs[12:15], refs[15:18], refs[18:21]
    in_sems, out_sems = refs[21:23]
    schedule = (2, 0, 1)
    arrivals, departures = {}, []
    for group in schedule:
        tiles = pl.ds(GROUP_TILES * group, GROUP_TILES)
        arrivals[group] = [
            pltpu.make_async_copy(recv_ref.at[:, tiles], recv.at[group], in_sems.at[group, 0]),
            pltpu.make_async_copy(a_refs[group], a_buffers[group], in_sems.at[group, 1]),
            pltpu.make_async_copy(st_refs[group], st_buffers[group], in_sems.at[group, 2]),
        ]
        for copy in arrivals[group]:
            copy.start()
    for group in schedule:
        for copy in arrivals[group]:
            copy.wait()
        tiles = [recv[group, :, tile].reshape(SPAN, 2 * C) for tile in range(GROUP_TILES)]
        held = scaled_buffers[group]
        for local, coef in enumerate(order_sums(group, a_buffers[group], tiles)):
            skipped = DEVICES * local
            held[packed_rows(group)[local], :] = (
                gain_ref[LANES * group + skipped :, :] * coef
            ).astype(BF16)
        product = dot(held[...], mix_ref[...]).astype(BF16)
        mixed = []
        for local, rows in enumerate(packed_rows(group)):
            zeros = jnp.zeros((DEVICES * local, 2 * C), BF16)
            mixed.append(
                jnp.concatenate([zeros, product[rows]], axis=0) if local else product[rows]
            )
        for tile in range(GROUP_TILES):
            grid = tile_sum(tile, st_buffers[group], mixed[tile], mixed[tile + 1])
            payload[group, :, tile] = grid.astype(BF16).reshape(DEVICES, TILE, 2 * C)
        tiles = pl.ds(GROUP_TILES * group, GROUP_TILES)
        copies = (
            pltpu.make_async_copy(
                payload.at[group], payload_ref.at[:, tiles], out_sems.at[group, 0]
            ),
            pltpu.make_async_copy(
                scaled_buffers[group],
                scaled_ref.at[pl.ds(BASES[group], PACKED[group])],
                out_sems.at[group, 1],
            ),
        )
        for copy in copies:
            copy.start()
            departures.append(copy)
    for copy in departures:
        copy.wait()


def spectral_forward(recv, a, st, gain, mix, after=()):
    slots = (GROUPS, DEVICES, GROUP_TILES, TILE, 2 * C)
    return call(
        spectral_kernel,
        (recv, *a, *st, gain, mix),
        [HELD] * 7 + [whole(gain.shape), whole(mix.shape)],
        [HELD] * 2,
        [
            jax.ShapeDtypeStruct((sum(PACKED), 2 * C), BF16),
            jax.ShapeDtypeStruct(recv.shape, BF16),
        ],
        (1,),
        after,
        scratch_shapes=[pltpu.VMEM(slots, BF16), pltpu.VMEM(slots, BF16)]
        + [pltpu.VMEM(value.shape, BF16) for value in a]
        + [pltpu.VMEM(value.shape, BF16) for value in st]
        + [pltpu.VMEM((rows, 2 * C), BF16) for rows in PACKED]
        + [pltpu.SemaphoreType.DMA((GROUPS, 3)), pltpu.SemaphoreType.DMA((GROUPS, 2))],
        name="spectral_forward",
    )


def normal_cumulative(value, bell):
    denominator = 1.0 + (0.3275911 / math.sqrt(2.0)) * jnp.abs(value)
    inverse = pl.reciprocal(denominator, approx=True)
    inverse = inverse * (2.0 - denominator * inverse)
    series = 0.5 * 1.061405429 * inverse - 0.5 * 1.453152027
    series = series * inverse + 0.5 * 1.421413741
    series = series * inverse - 0.5 * 0.284496736
    series = series * inverse + 0.5 * 0.254829592
    tail = series * inverse * bell
    return jnp.where(value < 0.0, tail, 1.0 - tail)


def grid_kernel(
    recv_ref, up_ref, turned_ref, proj_ref, table_ref, turned_table_ref,
    out_ref, grad_ref, scratch, out_scratch, act_scratch, pre_scratch,
):
    step = pl.program_id(1)
    low = half_lanes((MODES, LANES))
    block = 128

    @pl.when(step == 0)
    def _():
        scratch[...] = recv_ref[...].astype(F32)
        grad_ref[...] = jnp.zeros_like(grad_ref)

    columns = []
    for pair in range(2):
        first = scratch[pl.ds(step * 4 + 2 * pair, MODES, stride=LAT_LOCAL), :]
        second = scratch[pl.ds(step * 4 + 2 * pair + 1, MODES, stride=LAT_LOCAL), :]
        real = jnp.where(low, first, pltpu.roll(second, HALF, 1))
        imag = jnp.where(low, pltpu.roll(first, HALF, 1), second)
        columns.append(jnp.concatenate([real, imag], axis=0).astype(BF16))
    modes = jnp.concatenate(columns, axis=1)
    low_block = half_lanes((block, LANES))
    for part in range(NLON // block):
        rows = slice(part * block, (part + 1) * block)
        pre = dot(turned_table_ref[rows, :], modes)
        grad_act = jnp.concatenate(
            [
                jnp.where(
                    low_block,
                    dot(turned_ref[2 * pair, rows, :], proj_ref[...]),
                    dot(turned_ref[2 * pair + 1, rows, :], proj_ref[...]),
                )
                for pair in range(2)
            ],
            axis=1,
        )
        bell = jnp.exp(-0.5 * pre * pre)
        cumulative = normal_cumulative(pre, bell)
        slope = cumulative + pre * bell * (1.0 / math.sqrt(2.0 * math.pi))
        act_scratch[rows, :] = (pre * cumulative).astype(BF16)
        pre_scratch[rows, :] = (grad_act * slope).astype(BF16)
    low_grad = half_lanes((C, LANES))
    for pair in range(2):
        act = act_scratch[:, pair * LANES : (pair + 1) * LANES]
        ups = up_ref[2 * pair : 2 * pair + 2].reshape(2 * C, NLON)
        grads = dot(ups, act)
        grad_ref[...] += jnp.where(low_grad, grads[:C], grads[C:])
    grad_modes = dot(table_ref[...], pre_scratch[...])
    for pair in range(2):
        lanes = slice(pair * LANES, (pair + 1) * LANES)
        real, imag = grad_modes[:MODES, lanes], grad_modes[MODES:, lanes]
        out_scratch[pl.ds(step * 4 + 2 * pair, MODES, stride=LAT_LOCAL), :] = jnp.where(
            low, real, pltpu.roll(imag, HALF, 1)
        )
        out_scratch[pl.ds(step * 4 + 2 * pair + 1, MODES, stride=LAT_LOCAL), :] = jnp.where(
            low, pltpu.roll(real, HALF, 1), imag
        )

    @pl.when(step == LAT_LOCAL // 4 - 1)
    def _():
        out_ref[...] = out_scratch[...].astype(BF16)


def grid_stage(first, blocks, recv, up, turned, proj, table, turned_table, after=()):
    rows = MODES * LAT_LOCAL
    lanes_spec = pl.BlockSpec((rows, LANES), lambda q, b: (0, q))
    grad_spec = pl.BlockSpec((C, LANES), lambda q, b: (0, q))
    return call(
        grid_kernel,
        (recv, up, turned, proj, table, turned_table),
        [
            pl.BlockSpec((rows, LANES), lambda q, b: (0, q + first)),
            pl.BlockSpec((4, C, NLON), lambda q, b: (b, 0, 0)),
            pl.BlockSpec((4, NLON, C), lambda q, b: (b, 0, 0)),
            pl.BlockSpec((C, LANES), lambda q, b: (0, q + first)),
            whole(table.shape),
            whole(turned_table.shape),
        ],
        [lanes_spec, grad_spec],
        [
            jax.ShapeDtypeStruct((rows, LANES * blocks), BF16),
            jax.ShapeDtypeStruct((C, LANES * blocks), F32),
        ],
        (blocks, LAT_LOCAL // 4),
        after,
        scratch_shapes=[
            pltpu.VMEM((rows, LANES), F32),
            pltpu.VMEM((rows, LANES), F32),
            pltpu.VMEM((NLON, 2 * LANES), BF16),
            pltpu.VMEM((NLON, 2 * LANES), BF16),
        ],
        name=f"grid_stage_{blocks}",
    )


def backward_kernel(groups, *refs):
    recv_ref, table_refs, out_ref = refs[0], refs[1 : 1 + len(groups)], refs[1 + len(groups)]
    buffers, sems = refs[2 + len(groups) : -1], refs[-1]
    copies = [
        pltpu.make_async_copy(table_refs[place], buffers[place], sems.at[place])
        for place in range(len(groups))
    ]
    for copy in copies:
        copy.start()
    lanes = recv_ref.shape[-1]
    first = 0
    for place, group in enumerate(groups):
        start = GROUP_TILES * group if recv_ref.shape[1] == TILES else 0
        tiles = [
            recv_ref[:, start + tile].reshape(SPAN, lanes) for tile in range(GROUP_TILES)
        ]
        copies[place].wait()
        sums = order_sums(group, buffers[place], tiles)
        for total, rows in zip(sums, packed_rows(group)):
            out_ref[first + rows.start : first + rows.stop, :] = total.astype(BF16)
        first += PACKED[group]


def spectral_backward(groups, recv, tables, after=()):
    lanes = recv.shape[-1]
    tiles = GROUP_TILES if len(groups) == 1 else TILES
    block = groups[0] if len(groups) == 1 else 0
    out = (sum(PACKED[group] for group in groups), lanes)
    return call(
        functools.partial(backward_kernel, groups),
        (recv, *tables),
        [
            pl.BlockSpec(
                (DEVICES, tiles, TILE, lanes),
                lambda b: (0, block, 0, 0),
                pipeline_mode=pl.Buffered(1),
            )
        ]
        + [HELD] * len(groups),
        whole(out),
        jax.ShapeDtypeStruct(out, BF16),
        (1,),
        after,
        scratch_shapes=[pltpu.VMEM(table.shape, BF16) for table in tables]
        + [pltpu.SemaphoreType.DMA((len(groups),))],
        vmem=20,
        name="spectral_backward_" + "_".join(str(group) for group in groups),
    )


def hold_kernel(value_ref, out_ref):
    pass


def hold(value, after):
    held = pl.BlockSpec(memory_space=pl.ANY)
    return call(
        hold_kernel,
        (value,),
        [held],
        held,
        jax.ShapeDtypeStruct(value.shape, value.dtype),
        (1,),
        after,
        aliases={0: 0},
        vmem=1,
        name="hold",
    )


def synthesis_kernel(group, large_rows, table_ref, small_ref, large_ref, gain_ref, mix_ref, *refs):
    out_ref, coeff_ref, at_ref, part_ref, sems = refs[-5:]
    degrees = degrees_of(group)
    copies = (
        pltpu.make_async_copy(
            small_ref.at[pl.ds(BASES[group], PACKED[group])], part_ref, sems.at[0]
        ),
        pltpu.make_async_copy(table_ref, at_ref, sems.at[1]),
    )
    for copy in copies:
        copy.start()
    copies[0].wait()
    product = dot_nt(jnp.concatenate([part_ref[...], large_ref[large_rows, :]], axis=1), mix_ref[...])
    for local, rows in enumerate(packed_rows(group)):
        first = local * degrees
        skipped = DEVICES * local
        if skipped:
            coeff_ref[first : first + skipped, :] = jnp.zeros((skipped, 2 * C), BF16)
        coeff_ref[first + skipped : first + degrees, :] = (
            gain_ref[LANES * group + skipped :, :] * product[rows]
        ).astype(BF16)
    copies[1].wait()
    for tile in range(GROUP_TILES):
        first = coeff_ref[tile * degrees : (tile + 1) * degrees, :]
        second = coeff_ref[(tile + 1) * degrees : (tile + 2) * degrees, :]
        out = tile_sum(tile, at_ref, first, second)
        out_ref[:, tile] = out.astype(BF16).reshape(DEVICES, TILE, 2 * C)


def analysis_back(group, at, small, large, first, gain, mix, tiles, block, payload=(), after=()):
    inputs = (at, small, large, gain, mix, *payload)
    return call(
        functools.partial(synthesis_kernel, group, slice(first, first + PACKED[group])),
        inputs,
        [HELD] * 2 + [whole(value.shape) for value in inputs[2:5]] + [HELD] * len(payload),
        pl.BlockSpec((DEVICES, GROUP_TILES, TILE, 2 * C), lambda b: (0, block, 0, 0)),
        jax.ShapeDtypeStruct((DEVICES, tiles, TILE, 2 * C), BF16),
        (1,),
        after,
        aliases={5: 0} if payload else {},
        scratch_shapes=[
            pltpu.VMEM((GROUP_ORDERS * degrees_of(group), 2 * C), BF16),
            pltpu.VMEM(at.shape, BF16),
            pltpu.VMEM((PACKED[group], LANES), BF16),
            pltpu.SemaphoreType.DMA((2,)),
        ],
        vmem=20,
        name=f"analysis_back_{group}",
    )


def fold(tile):
    return tile + pltpu.roll(tile, HALF, 1)


def weight_kernel(held_ref, small_ref, *refs):
    first_ref, rest_ref, mix_ref, factor_ref, proj_small, proj_large = refs[:6]
    out_ref, gain, packed, spaced, scaled_ref, sem = refs[6:]
    large = (first_ref[...], rest_ref[: PACKED[1], :], rest_ref[PACKED[1] :, :])
    copy = pltpu.make_async_copy(held_ref, scaled_ref, sem)
    copy.start()
    copy.wait()
    block = None
    for group in range(GROUPS):
        rows = slice(BASES[group], BASES[group] + PACKED[group])
        mixed = jnp.concatenate([small_ref[rows, :], large[group]], axis=1)
        part = lax.dot_general(
            scaled_ref[rows, :], mixed, (((0,), (0,)), ((), ())), preferred_element_type=F32
        )
        block = part if block is None else block + part
        product = dot_nt(mixed, mix_ref[...]) * scaled_ref[rows, :].astype(F32)
        for local, rows in enumerate(packed_rows(group)):
            part = product[rows]
            first = LANES * group + DEVICES * local
            if first:
                gain[first:, :] += part
            else:
                gain[...] = part
    gain[...] = gain[...] / factor_ref[...]
    low = half_lanes((HALF, LANES))
    low_gain = half_lanes((C, LANES))
    low_proj = half_lanes((C // 2, LANES))
    for index in range(GROUPS):
        lanes = slice(index * LANES, (index + 1) * LANES)
        for row_block in range(GROUPS):
            start = row_block * LANES
            first = block[start : start + HALF, lanes]
            second = pltpu.roll(block[start + HALF : start + LANES, lanes], HALF, 1)
            packed[index, row_block * HALF : (row_block + 1) * HALF, :] = jnp.where(
                low, first + second, first - second
            )
        packed[index, C : 2 * C, :] = jnp.where(
            low_gain, fold(gain[:C, lanes]), fold(gain[C:, lanes])
        )
        if index == 0:
            proj = fold(proj_small[...])
        else:
            proj = fold(proj_large[:, (index - 1) * LANES : index * LANES])
        packed[index, 2 * C :, :] = jnp.where(low_proj, proj[: C // 2], proj[C // 2 :])
        for row in range(TILE - 1):
            spaced[index, pl.ds(row, DEVICES, stride=TILE), :] = packed[
                index, row * DEVICES : (row + 1) * DEVICES, :
            ]
        spaced[index, pl.ds(TILE - 1, DEVICES, stride=TILE), :] = jnp.zeros((DEVICES, LANES), F32)
        out_ref[:, 0, :, lanes] = spaced[index].astype(BF16).reshape(DEVICES, TILE, LANES)


def weight_grads(scaled, small, large, mix, gain, proj_small, proj_large, after=()):
    tiles = 2 * GROUP_TILES
    inputs = (scaled, small, *large, mix, gain, proj_small, proj_large)
    return call(
        weight_kernel,
        inputs,
        [HELD] + [whole(value.shape) for value in inputs[1:]],
        pl.BlockSpec((DEVICES, 1, TILE, 2 * C), lambda b: (0, tiles, 0, 0)),
        jax.ShapeDtypeStruct((DEVICES, tiles + 1, TILE, 2 * C), BF16),
        (1,),
        after,
        scratch_shapes=[
            pltpu.VMEM((MODES, 2 * C), F32),
            pltpu.VMEM((GROUPS, 15 * DEVICES, LANES), F32),
            pltpu.VMEM((GROUPS, TILE * DEVICES, LANES), F32),
            pltpu.VMEM(scaled.shape, BF16),
            pltpu.SemaphoreType.DMA,
        ],
        vmem=24,
        name="weight_grads",
    )


def total_kernel(recv_ref, payload_ref, out_ref):
    total = jnp.sum(recv_ref[:, 0].astype(F32), axis=0)
    out_ref[:, 0] = jnp.broadcast_to(total.astype(BF16)[None], (DEVICES, TILE, 2 * C))


def attach_totals(recv, payload):
    def last(value):
        tile = value.shape[1] - 1
        return pl.BlockSpec((DEVICES, 1, TILE, 2 * C), lambda b: (0, tile, 0, 0))

    return call(
        total_kernel,
        (recv, payload),
        [last(recv), pl.BlockSpec(memory_space=pl.ANY)],
        last(payload),
        jax.ShapeDtypeStruct(payload.shape, BF16),
        (1,),
        aliases={1: 0},
        vmem=8,
        name="attach_totals",
    )


def unpack_totals(recv_ref, proj_ref, mix_ref, gain_ref, spaced, packed):
    grid_scale = 1.0 / math.sqrt(NLAT * NLON)
    mode_scale = 1.0 / math.sqrt(MODES)
    lows, highs = [], []
    for index in range(GROUPS):
        lanes = slice(index * LANES, (index + 1) * LANES)
        spaced[index] = recv_ref[:, GROUP_TILES, :, lanes].reshape(DEVICES * TILE, LANES).astype(F32)
        for row in range(TILE - 1):
            packed[index, row * DEVICES : (row + 1) * DEVICES, :] = spaced[
                index, pl.ds(row, DEVICES, stride=TILE), :
            ]
        lows.append(packed[index, :, :HALF])
        highs.append(packed[index, :, HALF:])
    low = jnp.concatenate(lows, axis=1)
    high = jnp.concatenate(highs, axis=1)
    mix_ref[0] = grid_scale * low[:C]
    mix_ref[1] = grid_scale * high[:C]
    gain = jnp.concatenate([low[C : 2 * C], high[C : 2 * C]], axis=0)
    gain_ref[...] = mode_scale * gain.T
    proj = jnp.concatenate([low[2 * C :], high[2 * C :]], axis=0)
    proj_ref[...] = grid_scale * proj.T


def field_kernel(recv_ref, table_ref, base_ref, out_ref, *refs):
    totals, (scratch, *unpacking) = refs[:3] if len(refs) > 1 else (), refs[3:] or refs
    step = pl.program_id(0)
    orders = DEVICES * GROUP_ORDERS
    rows = orders * LAT_LOCAL

    @pl.when(step == 0)
    def _():
        for index in range(GROUPS):
            lanes = slice(index * LANES, (index + 1) * LANES)
            values = recv_ref[:, :GROUP_TILES, :, lanes].astype(F32)
            scratch[index] = values.reshape(rows, LANES)
        if totals:
            unpack_totals(recv_ref, *totals, *unpacking)

    lefts = []
    for inner in range(4):
        real, imag = [], []
        for index in range(GROUPS):
            values = scratch[index, pl.ds(step * 4 + inner, orders, stride=LAT_LOCAL), :]
            turned = values.T.astype(BF16)
            real.append(turned[:HALF])
            imag.append(turned[HALF:])
        lefts.append(
            jnp.concatenate(
                [jnp.concatenate(real, axis=0), jnp.concatenate(imag, axis=0)], axis=1
            )
        )
    product = dot(jnp.concatenate(lefts, axis=0), table_ref[...])
    for inner in range(4):
        total = base_ref[inner].astype(F32) + product[inner * C : (inner + 1) * C]
        out_ref[inner] = total.astype(out_ref.dtype)


def field_stage(recv, at, table, base, unpacked=False, after=()):
    rows = DEVICES * GROUP_ORDERS * LAT_LOCAL
    block = pl.BlockSpec((4, C, NLON), lambda b: (b, 0, 0))
    tiles = GROUP_TILES + int(unpacked)
    totals = ((C, C), (2, C, C), (C, MODES)) if unpacked else ()
    scratch_shapes = [pltpu.VMEM((GROUPS, rows, LANES), F32)]
    if unpacked:
        scratch_shapes += [
            pltpu.VMEM((GROUPS, TILE * DEVICES, LANES), F32),
            pltpu.VMEM((GROUPS, 15 * DEVICES, LANES), F32),
        ]
    return call(
        field_kernel,
        (recv, table, base),
        [
            pl.BlockSpec(
                (DEVICES, tiles, TILE, 2 * C),
                lambda b: (0, at, 0, 0),
                pipeline_mode=pl.Buffered(1),
            ),
            whole(table.shape),
            block,
        ],
        [block] + [whole(shape) for shape in totals],
        [jax.ShapeDtypeStruct((LAT_LOCAL, C, NLON), BF16)]
        + [jax.ShapeDtypeStruct(shape, F32) for shape in totals],
        (LAT_LOCAL // 4,),
        after,
        scratch_shapes=scratch_shapes,
        vmem=24 if unpacked else 20,
        name="field_stage",
    )


def exchange(payload):
    tiles, lanes = payload.shape[1], payload.shape[3]
    flat = payload.reshape(DEVICES, tiles * TILE, lanes)
    moved = lax.all_to_all(flat, "lat", split_axis=0, concat_axis=0, tiled=True)
    return moved.reshape(DEVICES, tiles, TILE, lanes)


def shards(saved_input, incoming, spectral_gain, mix_weight, proj_weight):
    device = lax.axis_index("lat")
    section_count = lax.axis_size("section")
    shift = [(source, (source - 1) % section_count) for source in range(section_count)]

    forward_all = forward_rows(0, GROUPS)
    forward = [forward_rows(group, 1) for group in range(GROUPS)]
    inverse_np = inverse_rows()
    inverse = jnp.asarray(inverse_np)
    inverse_turned = jnp.asarray(np.ascontiguousarray(inverse_np.T))
    spread, spread_turned = spread_tables()
    lat = jnp.asarray(latitude_rows())
    starts, numbers = log_starts()
    start = lax.dynamic_index_in_dim(jnp.asarray(starts), device, 0, keepdims=False)
    order = lax.dynamic_index_in_dim(jnp.asarray(numbers), device, 0, keepdims=False)

    field = saved_input[0]
    upstream = incoming[0]
    upstream_next = lax.ppermute(upstream, "section", shift)
    turned = jnp.swapaxes(upstream, 1, 2)
    rows = MODES * LAT_LOCAL
    spectrum = spectrum_rows(field, forward_all)
    recv = exchange(spectrum.reshape(DEVICES, TILES, TILE, 2 * C))
    gain, mix, proj = prepare(
        jnp.swapaxes(spectral_gain[0], 0, 1), mix_weight[0], proj_weight[0], (spectrum,)
    )
    gain_next, mix_next, _ = prepare(
        lax.ppermute(jnp.swapaxes(spectral_gain[0], 0, 1), "section", shift),
        lax.ppermute(mix_weight[0], "section", shift),
        proj_weight[0],
        (spectrum,),
    )
    tables = legendre_tables(start, order, lat, spread, spread_turned, (spectrum,))
    behind = [tables[4 * group + 2 : 4 * group + 4] for group in range(GROUPS)]
    scaled, payload = spectral_forward(
        recv, tables[0::4], tables[1::4], gain, mix, (turned, proj)
    )
    recv = exchange(payload).reshape(rows, 2 * C)
    small_rows, proj_small = grid_stage(
        0,
        1,
        recv,
        upstream,
        turned,
        proj,
        inverse,
        inverse_turned,
        (upstream_next, gain_next, mix_next),
    )
    small = exchange(small_rows.reshape(DEVICES, TILES, TILE, LANES))
    large, proj_large = grid_stage(
        1, 2, recv, upstream, turned, proj, inverse, inverse_turned, (small_rows,)
    )
    large = exchange(large.reshape(DEVICES, TILES, TILE, 2 * LANES))

    mixeds, moved = [None] * GROUPS, [None] * GROUPS
    every = tuple(range(GROUPS))
    mixed_small = spectral_backward(every, small, [table[0] for table in behind])
    moved_small = lax.ppermute(mixed_small, "section", shift)
    mixed_rest = spectral_backward((1, 2), large, [behind[1][0], behind[2][0]], (moved_small,))
    moved_rest = lax.ppermute(mixed_rest, "section", shift)
    mixed_0 = spectral_backward((0,), large, [behind[0][0]], (mixed_rest,))
    out_rest = weight_grads(
        scaled, mixed_small, (mixed_0, mixed_rest), mix, gain, proj_small, proj_large
    )
    for block, group in enumerate((1, 2)):
        out_rest = analysis_back(
            group,
            behind[group][1],
            moved_small,
            moved_rest,
            block * PACKED[1],
            gain_next,
            mix_next,
            2 * GROUP_TILES + 1,
            block,
            (out_rest,),
        )
    moved_0 = lax.ppermute(hold(mixed_0, (moved_rest,)), "section", shift)
    recv_rest = exchange(out_rest)
    out_0 = analysis_back(
        0, behind[0][1], moved_small, moved_0, 0, gain_next, mix_next, GROUP_TILES + 1, 0
    )
    out_0 = attach_totals(recv_rest, out_0)
    recv_0 = exchange(out_0)
    (base,) = field_stage(recv_rest, 0, forward[1], upstream_next, after=(out_0,))
    (base,) = field_stage(recv_rest, 1, forward[2], base)
    received, grad_w2, grad_mix, grad_gain = field_stage(recv_0, 0, forward[0], base, True)
    return (
        received[None],
        grad_w2[None],
        grad_mix[None],
        jnp.swapaxes(grad_gain, 0, 1)[None],
    )


def solution(mesh):
    in_specs = (
        P("section", "lat", None, None),
        P("section", "lat", None, None),
        P("section", None, None),
        P("section", None, None, None),
        P("section", None, None),
    )
    out_specs = (
        P("section", "lat", None, None),
        P("section", None, None),
        P("section", None, None, None),
        P("section", None, None),
    )
    return jax.shard_map(shards, mesh=mesh, in_specs=in_specs, out_specs=out_specs, check_vma=False)
```

```python
import functools
import math

import jax
import jax.numpy as jnp
import ml_dtypes
import numpy as np
from jax import lax
from jax.experimental import pallas as pl
from jax.experimental.pallas import tpu as pltpu
from jax.sharding import PartitionSpec as P

NLAT = 384
NLON = 768
MODES = 384
C = 192
DEVICES = 32
LAT_LOCAL = 12
ORDERS = 12
GROUPS = 3
GROUP_ORDERS = 4
HALF = 64
LANES = 128
TILE = 16
TILES = 9
GROUP_TILES = 3
SPAN = DEVICES * TILE
LAT_BLOCKS = 4
BLOCK_LATS = NLAT // LAT_BLOCKS
MIB = 1024 * 1024
F32 = jnp.float32
BF16 = jnp.bfloat16
NT = (((1,), (1,)), ((), ()))

PAIRS = ((0, 0), (1, 0), (1, 1), (2, 1), (2, 2), (3, 2))


def degrees_of(group):
    return MODES - LANES * group


def half_lanes(shape):
    return lax.broadcasted_iota(jnp.int32, shape, 1) < HALF


def packed_rows(group):
    rows, first = [], 0
    for local in range(GROUP_ORDERS):
        rows.append(slice(first, first + degrees_of(group) - DEVICES * local))
        first = rows[-1].stop
    return rows


PACKED = [packed_rows(group)[-1].stop for group in range(GROUPS)]
BASES = [sum(PACKED[:group]) for group in range(GROUPS)]


def dot(left, right):
    return jnp.dot(left, right, preferred_element_type=F32)


def dot_nt(left, right):
    return lax.dot_general(left, right, NT, preferred_element_type=F32)


def whole(shape):
    return pl.BlockSpec(shape, lambda *_: (0,) * len(shape), pipeline_mode=pl.Buffered(1))


HELD = pl.BlockSpec(memory_space=pltpu.HBM)


def call(
    kernel, inputs, in_specs, out_specs, out_shape, grid, after=(), aliases=None, vmem=56, **extra
):
    count = len(inputs)

    def body(*refs):
        kernel(*refs[:count], *refs[count + len(after) :])

    return pl.pallas_call(
        body,
        grid=grid,
        in_specs=list(in_specs) + [pl.BlockSpec(memory_space=pl.ANY)] * len(after),
        out_specs=out_specs,
        out_shape=out_shape,
        input_output_aliases=aliases or {},
        compiler_params=pltpu.CompilerParams(vmem_limit_bytes=vmem * MIB),
        cost_estimate=pl.CostEstimate(flops=1, bytes_accessed=1, transcendentals=0),
        **extra,
    )(*inputs, *after)


def order_rows(first, count):
    device = np.arange(DEVICES)[:, None]
    local = np.arange(GROUP_ORDERS * count)[None, :] + GROUP_ORDERS * first
    return (DEVICES * local + device).reshape(-1)


def fourier_rows(orders):
    phase = (orders[:, None] * np.arange(NLON)[None, :]) % NLON
    angle = phase * (2.0 * math.pi / NLON)
    return np.cos(angle), -np.sin(angle)


def forward_rows(first, count):
    cosine, sine = fourier_rows(order_rows(first, count))
    table = np.concatenate([cosine, sine], axis=0)
    return jnp.asarray(table.astype(np.float32).astype(ml_dtypes.bfloat16))


def inverse_rows():
    device = np.arange(DEVICES)[:, None]
    orders = (DEVICES * np.arange(ORDERS)[None, :] + device).reshape(-1)
    factor = np.where(orders == 0, 1.0, 2.0)[:, None] / NLON
    cosine, sine = fourier_rows(orders)
    table = np.concatenate([factor * cosine, factor * sine], axis=0)
    return table.astype(np.float32).astype(ml_dtypes.bfloat16)


def spread_tables():
    rows = np.arange(LANES)
    source, inner = rows // TILE, rows % TILE
    tables = np.zeros((len(PAIRS), LANES, LANES), np.float32)
    for index, (order, tile) in enumerate(PAIRS):
        lat = TILE * tile + inner - LAT_LOCAL * order
        valid = (lat >= 0) & (lat < LAT_LOCAL)
        tables[index, (source * LAT_LOCAL + lat)[valid], rows[valid]] = 1.0
    flat = jnp.asarray(tables.astype(ml_dtypes.bfloat16))
    turned = jnp.asarray(np.swapaxes(tables, 1, 2).astype(ml_dtypes.bfloat16))
    return flat, turned


def log_starts():
    table = np.zeros((DEVICES, TILE, LANES), np.float32)
    numbers = np.zeros((DEVICES, TILE, LANES), np.float32)
    for device in range(DEVICES):
        for local in range(ORDERS):
            order = DEVICES * local + device
            numbers[device, local] = order
            table[device, local] = 0.5 * math.log((2.0 * order + 1.0) / 2.0) + 0.5 * (
                math.lgamma(order + 0.5) - math.lgamma(0.5) - math.lgamma(order + 1.0)
            )
    return table, numbers


def latitude_rows():
    colatitude = (np.arange(NLAT) + 0.5) * (math.pi / NLAT)
    harmonic = np.arange(1, NLAT // 2 + 1)
    terms = np.cos(2.0 * harmonic[None, :] * colatitude[:, None]) / (4.0 * harmonic**2 - 1.0)
    weight = 2.0 / NLAT * (1.0 - 2.0 * np.sum(terms, axis=1))
    rows = np.stack([np.cos(colatitude), np.log(np.sin(colatitude)), weight])
    rows = np.concatenate([rows, np.zeros((5, NLAT))]).reshape(8, LAT_BLOCKS, BLOCK_LATS)
    rows = np.pad(rows, ((0, 0), (0, 0), (0, LANES - BLOCK_LATS)))
    return rows.reshape(8, SPAN).astype(np.float32)


def legendre_rows(start_ref, order_ref, lat_ref, rows_ref):
    order = jnp.concatenate([order_ref[...]] * LAT_BLOCKS, axis=1)
    cosine = jnp.broadcast_to(lat_ref[0:1, :], (TILE, SPAN))
    log_sin = jnp.broadcast_to(lat_ref[1:2, :], (TILE, SPAN))
    log_start = jnp.concatenate([start_ref[...]] * LAT_BLOCKS, axis=1) + order * log_sin
    narrow = order_ref[...]
    narrow_square = narrow * narrow
    second_factor = jnp.concatenate([jnp.sqrt(2.0 * narrow + 3.0)] * LAT_BLOCKS, axis=1)
    zeros = jnp.zeros((TILE, SPAN), F32)

    def block(index, state):
        previous, current, log_scale = state
        scale = jnp.exp(log_scale)
        for inner in range(16):
            row = index * 16 + inner
            degree = row.astype(F32)
            lower = degree - 1.0
            up = jnp.sqrt(
                jnp.maximum(4.0 * degree * degree - 1.0, 1.0)
                / jnp.maximum(degree * degree - narrow_square, 1.0)
            )
            down = jnp.sqrt(
                jnp.maximum(lower * lower - narrow_square, 0.0)
                / jnp.maximum(4.0 * lower * lower - 1.0, 1.0)
            )
            up = jnp.concatenate([up] * LAT_BLOCKS, axis=1)
            down = jnp.concatenate([down] * LAT_BLOCKS, axis=1)
            general = up * (cosine * current - down * previous)
            second = second_factor * cosine * current
            new_row = jnp.where(
                degree == order,
                1.0,
                jnp.where(
                    degree == order + 1.0, second, jnp.where(degree > order + 1.0, general, 0.0)
                ),
            )
            scaled = new_row * scale
            for part in range(LAT_BLOCKS):
                rows_ref[part, row] = scaled[:, part * LANES : (part + 1) * LANES]
            previous, current = current, new_row
        largest = jnp.maximum(jnp.abs(previous), jnp.abs(current))
        largest = jnp.where(largest > 0.0, largest, 1.0)
        return previous / largest, current / largest, log_scale + jnp.log(largest)

    lax.fori_loop(0, MODES // 16, block, (zeros, zeros, log_start))


def table_kernel(start_ref, order_ref, lat_ref, flat_ref, turned_ref, *rest):
    outs, rows_ref, buffers, sems = rest[:12], rest[12], rest[13:25], rest[25]
    legendre_rows(start_ref, order_ref, lat_ref, rows_ref)
    copies = []
    for group in range(GROUPS):
        ahead_flat, ahead_turned, behind_flat, behind_turned = buffers[4 * group : 4 * group + 4]

        def part_step(part, carry):
            lats = pl.ds(pl.multiple_of(part * LANES, LANES), LANES)
            weight = lat_ref[2:3, lats]
            for local in range(GROUP_ORDERS):
                legendre = rows_ref[part, LANES * group :, GROUP_ORDERS * group + local, :]
                synthesis = legendre.astype(BF16)
                analysis = (weight * legendre).astype(BF16)
                pairs = [index for index, (order, _) in enumerate(PAIRS) if order == local]
                flat = jnp.concatenate([flat_ref[index] for index in pairs], axis=1)
                turned = jnp.concatenate([turned_ref[index] for index in pairs], axis=0)
                products = (
                    dot(analysis, flat).astype(BF16),
                    dot_nt(turned, synthesis).astype(BF16),
                    dot(synthesis, flat).astype(BF16),
                    dot_nt(turned, analysis).astype(BF16),
                )
                for place, index in enumerate(pairs):
                    cut = slice(place * LANES, (place + 1) * LANES)
                    ahead_flat[index, :, lats] = products[0][:, cut]
                    ahead_turned[index, lats, :] = products[1][cut]
                    behind_flat[index, :, lats] = products[2][:, cut]
                    behind_turned[index, lats, :] = products[3][cut]
            return carry

        lax.fori_loop(0, LAT_BLOCKS, part_step, 0)
        for place in range(4):
            at = 4 * group + place
            copy = pltpu.make_async_copy(buffers[at], outs[at], sems.at[at])
            copy.start()
            copies.append(copy)
    for copy in copies:
        copy.wait()


def legendre_tables(start, order, lat, flat, turned, after):
    shapes = []
    for group in range(GROUPS):
        degrees = degrees_of(group)
        shapes += [(len(PAIRS), degrees, SPAN), (len(PAIRS), SPAN, degrees)] * 2
    inputs = (start, order, lat, flat, turned)
    return call(
        table_kernel,
        inputs,
        [whole(value.shape) for value in inputs],
        [HELD] * len(shapes),
        [jax.ShapeDtypeStruct(shape, BF16) for shape in shapes],
        (1,),
        after,
        scratch_shapes=[pltpu.VMEM((LAT_BLOCKS, MODES, TILE, LANES), F32)]
        + [pltpu.VMEM(shape, BF16) for shape in shapes]
        + [pltpu.SemaphoreType.DMA((len(shapes),))],
        name="legendre_tables",
    )


def blocks_of(value):
    return [value[:, index * HALF : (index + 1) * HALF] for index in range(GROUPS)]


def interleave(first, second):
    pairs = zip(blocks_of(first), blocks_of(second))
    return jnp.concatenate([block for pair in pairs for block in pair], axis=1)


def prepare_kernel(gain_ref, mix_ref, proj_ref, gain_out, mix_out, proj_out):
    gain = gain_ref[...].T
    gain_out[...] = interleave(gain, gain)
    real, imag = mix_ref[0].astype(F32), mix_ref[1].astype(F32)
    upper, lower = interleave(real, imag), interleave(-imag, real)
    for index in range(GROUPS):
        rows = slice(index * HALF, (index + 1) * HALF)
        start = index * LANES
        mix_out[start : start + HALF, :] = upper[rows].astype(BF16)
        mix_out[start + HALF : start + LANES, :] = lower[rows].astype(BF16)
    proj = proj_ref[...].astype(F32).T
    proj_out[...] = interleave(proj, proj).astype(BF16)


def prepare(gain, mix, proj, after):
    shapes = ((MODES, 2 * C), (2 * C, 2 * C), (C, 2 * C))
    kinds = (F32, BF16, BF16)
    return call(
        prepare_kernel,
        (gain, mix, proj),
        [whole(gain.shape), whole(mix.shape), whole(proj.shape)],
        [whole(shape) for shape in shapes],
        [jax.ShapeDtypeStruct(shape, kind) for shape, kind in zip(shapes, kinds)],
        (1,),
        after,
        name="prepare",
    )


def spectrum_kernel(field_ref, table_ref, out_ref, scratch):
    step = pl.program_id(0)
    rows = table_ref.shape[0] // 2
    low = half_lanes((rows, LANES))
    fields = field_ref[...].reshape(4 * C, NLON)
    product = dot_nt(table_ref[...], fields)
    for block in range(4 * GROUPS):
        inner, index = block // GROUPS, block % GROUPS
        lanes = slice(block // 2 * LANES, (block // 2 + 1) * LANES)
        real, imag = product[:rows, lanes], product[rows:, lanes]
        if block % 2:
            tile = jnp.where(low, pltpu.roll(real, HALF, 1), imag)
        else:
            tile = jnp.where(low, real, pltpu.roll(imag, HALF, 1))
        scratch[index, pl.ds(step * 4 + inner, rows, stride=LAT_LOCAL), :] = tile

    @pl.when(step == LAT_LOCAL // 4 - 1)
    def _():
        for index in range(GROUPS):
            out_ref[:, index * LANES : (index + 1) * LANES] = scratch[index].astype(BF16)


def spectrum_rows(field, table, after=()):
    rows = table.shape[0] // 2 * LAT_LOCAL
    return call(
        spectrum_kernel,
        (field, table),
        [pl.BlockSpec((4, C, NLON), lambda b: (b, 0, 0)), whole(table.shape)],
        whole((rows, 2 * C)),
        jax.ShapeDtypeStruct((rows, 2 * C), BF16),
        (LAT_LOCAL // 4,),
        after,
        scratch_shapes=[pltpu.VMEM((GROUPS, rows, LANES), F32)],
        name="spectrum_rows",
    )


def order_sums(group, table_ref, tiles):
    totals = [None] * GROUP_ORDERS
    for tile in range(GROUP_TILES):
        left = [table_ref[2 * tile + place, DEVICES * (tile + place) :, :] for place in range(2)]
        product = dot(jnp.concatenate(left, axis=0), tiles[tile])
        middle = left[0].shape[0]
        for order, part in ((tile, product[:middle]), (tile + 1, product[middle:])):
            totals[order] = part if totals[order] is None else totals[order] + part
    return totals


def tile_sum(tile, table_ref, first, second):
    left = jnp.concatenate([table_ref[2 * tile], table_ref[2 * tile + 1]], axis=1)
    return dot(left, jnp.concatenate([first, second], axis=0))


def spectral_kernel(recv_ref, *refs):
    a_refs, st_refs = refs[0:3], refs[3:6]
    gain_ref, mix_ref = refs[6:8]
    scaled_ref, payload_ref, recv, payload = refs[8:12]
    a_buffers, st_buffers, scaled_buffers = refs[12:15], refs[15:18], refs[18:21]
    in_sems, out_sems = refs[21:23]
    schedule = (2, 0, 1)
    arrivals, departures = {}, []
    for group in schedule:
        tiles = pl.ds(GROUP_TILES * group, GROUP_TILES)
        arrivals[group] = [
            pltpu.make_async_copy(recv_ref.at[:, tiles], recv.at[group], in_sems.at[group, 0]),
            pltpu.make_async_copy(a_refs[group], a_buffers[group], in_sems.at[group, 1]),
            pltpu.make_async_copy(st_refs[group], st_buffers[group], in_sems.at[group, 2]),
        ]
        for copy in arrivals[group]:
            copy.start()
    for group in schedule:
        for copy in arrivals[group]:
            copy.wait()
        tiles = [recv[group, :, tile].reshape(SPAN, 2 * C) for tile in range(GROUP_TILES)]
        held = scaled_buffers[group]
        for local, coef in enumerate(order_sums(group, a_buffers[group], tiles)):
            skipped = DEVICES * local
            held[packed_rows(group)[local], :] = (
                gain_ref[LANES * group + skipped :, :] * coef
            ).astype(BF16)
        product = dot(held[...], mix_ref[...]).astype(BF16)
        mixed = []
        for local, rows in enumerate(packed_rows(group)):
            zeros = jnp.zeros((DEVICES * local, 2 * C), BF16)
            mixed.append(
                jnp.concatenate([zeros, product[rows]], axis=0) if local else product[rows]
            )
        for tile in range(GROUP_TILES):
            grid = tile_sum(tile, st_buffers[group], mixed[tile], mixed[tile + 1])
            payload[group, :, tile] = grid.astype(BF16).reshape(DEVICES, TILE, 2 * C)
        tiles = pl.ds(GROUP_TILES * group, GROUP_TILES)
        copies = (
            pltpu.make_async_copy(
                payload.at[group], payload_ref.at[:, tiles], out_sems.at[group, 0]
            ),
            pltpu.make_async_copy(
                scaled_buffers[group],
                scaled_ref.at[pl.ds(BASES[group], PACKED[group])],
                out_sems.at[group, 1],
            ),
        )
        for copy in copies:
            copy.start()
            departures.append(copy)
    for copy in departures:
        copy.wait()


def spectral_forward(recv, a, st, gain, mix, after=()):
    slots = (GROUPS, DEVICES, GROUP_TILES, TILE, 2 * C)
    return call(
        spectral_kernel,
        (recv, *a, *st, gain, mix),
        [HELD] * 7 + [whole(gain.shape), whole(mix.shape)],
        [HELD] * 2,
        [
            jax.ShapeDtypeStruct((sum(PACKED), 2 * C), BF16),
            jax.ShapeDtypeStruct(recv.shape, BF16),
        ],
        (1,),
        after,
        scratch_shapes=[pltpu.VMEM(slots, BF16), pltpu.VMEM(slots, BF16)]
        + [pltpu.VMEM(value.shape, BF16) for value in a]
        + [pltpu.VMEM(value.shape, BF16) for value in st]
        + [pltpu.VMEM((rows, 2 * C), BF16) for rows in PACKED]
        + [pltpu.SemaphoreType.DMA((GROUPS, 3)), pltpu.SemaphoreType.DMA((GROUPS, 2))],
        name="spectral_forward",
    )


def normal_cumulative(value, bell):
    denominator = 1.0 + (0.3275911 / math.sqrt(2.0)) * jnp.abs(value)
    inverse = pl.reciprocal(denominator, approx=True)
    inverse = inverse * (2.0 - denominator * inverse)
    series = 0.5 * 1.061405429 * inverse - 0.5 * 1.453152027
    series = series * inverse + 0.5 * 1.421413741
    series = series * inverse - 0.5 * 0.284496736
    series = series * inverse + 0.5 * 0.254829592
    tail = series * inverse * bell
    return jnp.where(value < 0.0, tail, 1.0 - tail)


def grid_kernel(
    recv_ref, up_ref, turned_ref, proj_ref, table_ref, turned_table_ref,
    out_ref, grad_ref, scratch, out_scratch, act_scratch, pre_scratch,
):
    step = pl.program_id(1)
    low = half_lanes((MODES, LANES))
    block = 128

    @pl.when(step == 0)
    def _():
        scratch[...] = recv_ref[...].astype(F32)
        grad_ref[...] = jnp.zeros_like(grad_ref)

    columns = []
    for pair in range(2):
        first = scratch[pl.ds(step * 4 + 2 * pair, MODES, stride=LAT_LOCAL), :]
        second = scratch[pl.ds(step * 4 + 2 * pair + 1, MODES, stride=LAT_LOCAL), :]
        real = jnp.where(low, first, pltpu.roll(second, HALF, 1))
        imag = jnp.where(low, pltpu.roll(first, HALF, 1), second)
        columns.append(jnp.concatenate([real, imag], axis=0).astype(BF16))
    modes = jnp.concatenate(columns, axis=1)
    low_block = half_lanes((block, LANES))
    for part in range(NLON // block):
        rows = slice(part * block, (part + 1) * block)
        pre = dot(turned_table_ref[rows, :], modes)
        grad_act = jnp.concatenate(
            [
                jnp.where(
                    low_block,
                    dot(turned_ref[2 * pair, rows, :], proj_ref[...]),
                    dot(turned_ref[2 * pair + 1, rows, :], proj_ref[...]),
                )
                for pair in range(2)
            ],
            axis=1,
        )
        bell = jnp.exp(-0.5 * pre * pre)
        cumulative = normal_cumulative(pre, bell)
        slope = cumulative + pre * bell * (1.0 / math.sqrt(2.0 * math.pi))
        act_scratch[rows, :] = (pre * cumulative).astype(BF16)
        pre_scratch[rows, :] = (grad_act * slope).astype(BF16)
    low_grad = half_lanes((C, LANES))
    for pair in range(2):
        act = act_scratch[:, pair * LANES : (pair + 1) * LANES]
        ups = up_ref[2 * pair : 2 * pair + 2].reshape(2 * C, NLON)
        grads = dot(ups, act)
        grad_ref[...] += jnp.where(low_grad, grads[:C], grads[C:])
    grad_modes = dot(table_ref[...], pre_scratch[...])
    for pair in range(2):
        lanes = slice(pair * LANES, (pair + 1) * LANES)
        real, imag = grad_modes[:MODES, lanes], grad_modes[MODES:, lanes]
        out_scratch[pl.ds(step * 4 + 2 * pair, MODES, stride=LAT_LOCAL), :] = jnp.where(
            low, real, pltpu.roll(imag, HALF, 1)
        )
        out_scratch[pl.ds(step * 4 + 2 * pair + 1, MODES, stride=LAT_LOCAL), :] = jnp.where(
            low, pltpu.roll(real, HALF, 1), imag
        )

    @pl.when(step == LAT_LOCAL // 4 - 1)
    def _():
        out_ref[...] = out_scratch[...].astype(BF16)


def grid_stage(first, blocks, recv, up, turned, proj, table, turned_table, after=()):
    rows = MODES * LAT_LOCAL
    lanes_spec = pl.BlockSpec((rows, LANES), lambda q, b: (0, q))
    grad_spec = pl.BlockSpec((C, LANES), lambda q, b: (0, q))
    return call(
        grid_kernel,
        (recv, up, turned, proj, table, turned_table),
        [
            pl.BlockSpec((rows, LANES), lambda q, b: (0, q + first)),
            pl.BlockSpec((4, C, NLON), lambda q, b: (b, 0, 0)),
            pl.BlockSpec((4, NLON, C), lambda q, b: (b, 0, 0)),
            pl.BlockSpec((C, LANES), lambda q, b: (0, q + first)),
            whole(table.shape),
            whole(turned_table.shape),
        ],
        [lanes_spec, grad_spec],
        [
            jax.ShapeDtypeStruct((rows, LANES * blocks), BF16),
            jax.ShapeDtypeStruct((C, LANES * blocks), F32),
        ],
        (blocks, LAT_LOCAL // 4),
        after,
        scratch_shapes=[
            pltpu.VMEM((rows, LANES), F32),
            pltpu.VMEM((rows, LANES), F32),
            pltpu.VMEM((NLON, 2 * LANES), BF16),
            pltpu.VMEM((NLON, 2 * LANES), BF16),
        ],
        name=f"grid_stage_{blocks}",
    )


def backward_kernel(groups, *refs):
    recv_ref, table_refs, out_ref = refs[0], refs[1 : 1 + len(groups)], refs[1 + len(groups)]
    buffers, sems = refs[2 + len(groups) : -1], refs[-1]
    copies = [
        pltpu.make_async_copy(table_refs[place], buffers[place], sems.at[place])
        for place in range(len(groups))
    ]
    for copy in copies:
        copy.start()
    lanes = recv_ref.shape[-1]
    first = 0
    for place, group in enumerate(groups):
        start = GROUP_TILES * group if recv_ref.shape[1] == TILES else 0
        tiles = [
            recv_ref[:, start + tile].reshape(SPAN, lanes) for tile in range(GROUP_TILES)
        ]
        copies[place].wait()
        sums = order_sums(group, buffers[place], tiles)
        for total, rows in zip(sums, packed_rows(group)):
            out_ref[first + rows.start : first + rows.stop, :] = total.astype(BF16)
        first += PACKED[group]


def spectral_backward(groups, recv, tables, after=()):
    lanes = recv.shape[-1]
    tiles = GROUP_TILES if len(groups) == 1 else TILES
    block = groups[0] if len(groups) == 1 else 0
    out = (sum(PACKED[group] for group in groups), lanes)
    return call(
        functools.partial(backward_kernel, groups),
        (recv, *tables),
        [
            pl.BlockSpec(
                (DEVICES, tiles, TILE, lanes),
                lambda b: (0, block, 0, 0),
                pipeline_mode=pl.Buffered(1),
            )
        ]
        + [HELD] * len(groups),
        whole(out),
        jax.ShapeDtypeStruct(out, BF16),
        (1,),
        after,
        scratch_shapes=[pltpu.VMEM(table.shape, BF16) for table in tables]
        + [pltpu.SemaphoreType.DMA((len(groups),))],
        vmem=20,
        name="spectral_backward_" + "_".join(str(group) for group in groups),
    )


def hold_kernel(value_ref, out_ref):
    pass


def hold(value, after):
    held = pl.BlockSpec(memory_space=pl.ANY)
    return call(
        hold_kernel,
        (value,),
        [held],
        held,
        jax.ShapeDtypeStruct(value.shape, value.dtype),
        (1,),
        after,
        aliases={0: 0},
        vmem=1,
        name="hold",
    )


def synthesis_kernel(group, large_rows, table_ref, small_ref, large_ref, gain_ref, mix_ref, *refs):
    out_ref, coeff_ref, at_ref, part_ref, sems = refs[-5:]
    degrees = degrees_of(group)
    copies = (
        pltpu.make_async_copy(
            small_ref.at[pl.ds(BASES[group], PACKED[group])], part_ref, sems.at[0]
        ),
        pltpu.make_async_copy(table_ref, at_ref, sems.at[1]),
    )
    for copy in copies:
        copy.start()
    copies[0].wait()
    product = dot_nt(jnp.concatenate([part_ref[...], large_ref[large_rows, :]], axis=1), mix_ref[...])
    for local, rows in enumerate(packed_rows(group)):
        first = local * degrees
        skipped = DEVICES * local
        if skipped:
            coeff_ref[first : first + skipped, :] = jnp.zeros((skipped, 2 * C), BF16)
        coeff_ref[first + skipped : first + degrees, :] = (
            gain_ref[LANES * group + skipped :, :] * product[rows]
        ).astype(BF16)
    copies[1].wait()
    for tile in range(GROUP_TILES):
        first = coeff_ref[tile * degrees : (tile + 1) * degrees, :]
        second = coeff_ref[(tile + 1) * degrees : (tile + 2) * degrees, :]
        out = tile_sum(tile, at_ref, first, second)
        out_ref[:, tile] = out.astype(BF16).reshape(DEVICES, TILE, 2 * C)


def analysis_back(group, at, small, large, first, gain, mix, tiles, block, payload=(), after=()):
    inputs = (at, small, large, gain, mix, *payload)
    return call(
        functools.partial(synthesis_kernel, group, slice(first, first + PACKED[group])),
        inputs,
        [HELD] * 2 + [whole(value.shape) for value in inputs[2:5]] + [HELD] * len(payload),
        pl.BlockSpec((DEVICES, GROUP_TILES, TILE, 2 * C), lambda b: (0, block, 0, 0)),
        pltpu.HBM((DEVICES, tiles, TILE, 2 * C), BF16),
        (1,),
        after,
        aliases={5: 0} if payload else {},
        scratch_shapes=[
            pltpu.VMEM((GROUP_ORDERS * degrees_of(group), 2 * C), BF16),
            pltpu.VMEM(at.shape, BF16),
            pltpu.VMEM((PACKED[group], LANES), BF16),
            pltpu.SemaphoreType.DMA((2,)),
        ],
        vmem=20,
        name=f"analysis_back_{group}",
    )


def fold(tile):
    return tile + pltpu.roll(tile, HALF, 1)


def weight_kernel(held_ref, small_ref, *refs):
    first_ref, rest_ref, mix_ref, factor_ref, proj_small, proj_large = refs[:6]
    out_ref, gain, packed, spaced, scaled_ref, sem = refs[6:]
    large = (first_ref[...], rest_ref[: PACKED[1], :], rest_ref[PACKED[1] :, :])
    copy = pltpu.make_async_copy(held_ref, scaled_ref, sem)
    copy.start()
    copy.wait()
    block = None
    for group in range(GROUPS):
        rows = slice(BASES[group], BASES[group] + PACKED[group])
        mixed = jnp.concatenate([small_ref[rows, :], large[group]], axis=1)
        part = lax.dot_general(
            scaled_ref[rows, :], mixed, (((0,), (0,)), ((), ())), preferred_element_type=F32
        )
        block = part if block is None else block + part
        product = dot_nt(mixed, mix_ref[...]) * scaled_ref[rows, :].astype(F32)
        for local, rows in enumerate(packed_rows(group)):
            part = product[rows]
            first = LANES * group + DEVICES * local
            if first:
                gain[first:, :] += part
            else:
                gain[...] = part
    gain[...] = gain[...] / factor_ref[...]
    low = half_lanes((HALF, LANES))
    low_gain = half_lanes((C, LANES))
    low_proj = half_lanes((C // 2, LANES))
    for index in range(GROUPS):
        lanes = slice(index * LANES, (index + 1) * LANES)
        for row_block in range(GROUPS):
            start = row_block * LANES
            first = block[start : start + HALF, lanes]
            second = pltpu.roll(block[start + HALF : start + LANES, lanes], HALF, 1)
            packed[index, row_block * HALF : (row_block + 1) * HALF, :] = jnp.where(
                low, first + second, first - second
            )
        packed[index, C : 2 * C, :] = jnp.where(
            low_gain, fold(gain[:C, lanes]), fold(gain[C:, lanes])
        )
        if index == 0:
            proj = fold(proj_small[...])
        else:
            proj = fold(proj_large[:, (index - 1) * LANES : index * LANES])
        packed[index, 2 * C :, :] = jnp.where(low_proj, proj[: C // 2], proj[C // 2 :])
        for row in range(TILE - 1):
            spaced[index, pl.ds(row, DEVICES, stride=TILE), :] = packed[
                index, row * DEVICES : (row + 1) * DEVICES, :
            ]
        spaced[index, pl.ds(TILE - 1, DEVICES, stride=TILE), :] = jnp.zeros((DEVICES, LANES), F32)
        out_ref[:, 0, :, lanes] = spaced[index].astype(BF16).reshape(DEVICES, TILE, LANES)


def weight_grads(scaled, small, large, mix, gain, proj_small, proj_large, after=()):
    tiles = 2 * GROUP_TILES
    inputs = (scaled, small, *large, mix, gain, proj_small, proj_large)
    return call(
        weight_kernel,
        inputs,
        [HELD] + [whole(value.shape) for value in inputs[1:]],
        pl.BlockSpec((DEVICES, 1, TILE, 2 * C), lambda b: (0, tiles, 0, 0)),
        pltpu.HBM((DEVICES, tiles + 1, TILE, 2 * C), BF16),
        (1,),
        after,
        scratch_shapes=[
            pltpu.VMEM((MODES, 2 * C), F32),
            pltpu.VMEM((GROUPS, 15 * DEVICES, LANES), F32),
            pltpu.VMEM((GROUPS, TILE * DEVICES, LANES), F32),
            pltpu.VMEM(scaled.shape, BF16),
            pltpu.SemaphoreType.DMA,
        ],
        vmem=24,
        name="weight_grads",
    )


def total_kernel(recv_ref, payload_ref, out_ref, token_ref):
    token_ref[...] = jnp.zeros((8, LANES), F32)
    total = jnp.sum(recv_ref[:, 0].astype(F32), axis=0)
    out_ref[:, 0] = jnp.broadcast_to(total.astype(BF16)[None], (DEVICES, TILE, 2 * C))


def attach_totals(recv, payload):
    def last(value):
        tile = value.shape[1] - 1
        return pl.BlockSpec((DEVICES, 1, TILE, 2 * C), lambda b: (0, tile, 0, 0))

    return call(
        total_kernel,
        (recv, payload),
        [last(recv), pl.BlockSpec(memory_space=pl.ANY)],
        [last(payload), whole((8, LANES))],
        [pltpu.HBM(payload.shape, BF16), jax.ShapeDtypeStruct((8, LANES), F32)],
        (1,),
        aliases={1: 0},
        vmem=8,
        name="attach_totals",
    )


def unpack_totals(recv_ref, proj_ref, mix_ref, gain_ref, spaced, packed):
    grid_scale = 1.0 / math.sqrt(NLAT * NLON)
    mode_scale = 1.0 / math.sqrt(MODES)
    lows, highs = [], []
    for index in range(GROUPS):
        lanes = slice(index * LANES, (index + 1) * LANES)
        spaced[index] = recv_ref[:, GROUP_TILES, :, lanes].reshape(DEVICES * TILE, LANES).astype(F32)
        for row in range(TILE - 1):
            packed[index, row * DEVICES : (row + 1) * DEVICES, :] = spaced[
                index, pl.ds(row, DEVICES, stride=TILE), :
            ]
        lows.append(packed[index, :, :HALF])
        highs.append(packed[index, :, HALF:])
    low = jnp.concatenate(lows, axis=1)
    high = jnp.concatenate(highs, axis=1)
    mix_ref[0] = grid_scale * low[:C]
    mix_ref[1] = grid_scale * high[:C]
    gain = jnp.concatenate([low[C : 2 * C], high[C : 2 * C]], axis=0)
    gain_ref[...] = mode_scale * gain.T
    proj = jnp.concatenate([low[2 * C :], high[2 * C :]], axis=0)
    proj_ref[...] = grid_scale * proj.T


def field_kernel(recv_ref, table_ref, base_ref, out_ref, *refs):
    totals, (scratch, *unpacking) = refs[:3] if len(refs) > 1 else (), refs[3:] or refs
    step = pl.program_id(0)
    orders = DEVICES * GROUP_ORDERS
    rows = orders * LAT_LOCAL

    @pl.when(step == 0)
    def _():
        for index in range(GROUPS):
            lanes = slice(index * LANES, (index + 1) * LANES)
            values = recv_ref[:, :GROUP_TILES, :, lanes].astype(F32)
            scratch[index] = values.reshape(rows, LANES)
        if totals:
            unpack_totals(recv_ref, *totals, *unpacking)

    lefts = []
    for inner in range(4):
        real, imag = [], []
        for index in range(GROUPS):
            values = scratch[index, pl.ds(step * 4 + inner, orders, stride=LAT_LOCAL), :]
            turned = values.T.astype(BF16)
            real.append(turned[:HALF])
            imag.append(turned[HALF:])
        lefts.append(
            jnp.concatenate(
                [jnp.concatenate(real, axis=0), jnp.concatenate(imag, axis=0)], axis=1
            )
        )
    product = dot(jnp.concatenate(lefts, axis=0), table_ref[...])
    for inner in range(4):
        total = base_ref[inner].astype(F32) + product[inner * C : (inner + 1) * C]
        out_ref[inner] = total.astype(out_ref.dtype)


def field_stage(recv, at, table, base, unpacked=False, after=()):
    rows = DEVICES * GROUP_ORDERS * LAT_LOCAL
    block = pl.BlockSpec((4, C, NLON), lambda b: (b, 0, 0))
    tiles = GROUP_TILES + int(unpacked)
    totals = ((C, C), (2, C, C), (C, MODES)) if unpacked else ()
    scratch_shapes = [pltpu.VMEM((GROUPS, rows, LANES), F32)]
    if unpacked:
        scratch_shapes += [
            pltpu.VMEM((GROUPS, TILE * DEVICES, LANES), F32),
            pltpu.VMEM((GROUPS, 15 * DEVICES, LANES), F32),
        ]
    return call(
        field_kernel,
        (recv, table, base),
        [
            pl.BlockSpec(
                (DEVICES, tiles, TILE, 2 * C),
                lambda b: (0, at, 0, 0),
                pipeline_mode=pl.Buffered(1),
            ),
            whole(table.shape),
            block,
        ],
        [block] + [whole(shape) for shape in totals],
        [pltpu.HBM((LAT_LOCAL, C, NLON), BF16)]
        + [jax.ShapeDtypeStruct(shape, F32) for shape in totals],
        (LAT_LOCAL // 4,),
        after,
        scratch_shapes=scratch_shapes,
        vmem=56 if unpacked else 20,
        name="field_stage",
    )


def exchange(payload):
    tiles, lanes = payload.shape[1], payload.shape[3]
    flat = payload.reshape(DEVICES, tiles * TILE, lanes)
    moved = lax.all_to_all(flat, "lat", split_axis=0, concat_axis=0, tiled=True)
    return moved.reshape(DEVICES, tiles, TILE, lanes)


def shards(saved_input, incoming, spectral_gain, mix_weight, proj_weight):
    device = lax.axis_index("lat")
    section_count = lax.axis_size("section")
    shift = [(source, (source - 1) % section_count) for source in range(section_count)]

    forward_all = forward_rows(0, GROUPS)
    forward = [forward_rows(group, 1) for group in range(GROUPS)]
    inverse_np = inverse_rows()
    inverse = jnp.asarray(inverse_np)
    inverse_turned = jnp.asarray(np.ascontiguousarray(inverse_np.T))
    spread, spread_turned = spread_tables()
    lat = jnp.asarray(latitude_rows())
    starts, numbers = log_starts()
    start = lax.dynamic_index_in_dim(jnp.asarray(starts), device, 0, keepdims=False)
    order = lax.dynamic_index_in_dim(jnp.asarray(numbers), device, 0, keepdims=False)

    field = saved_input[0]
    upstream = incoming[0]
    upstream_next = lax.ppermute(upstream, "section", shift)
    turned = jnp.swapaxes(upstream, 1, 2)
    rows = MODES * LAT_LOCAL
    spectrum = spectrum_rows(field, forward_all)
    recv = exchange(spectrum.reshape(DEVICES, TILES, TILE, 2 * C))
    gain, mix, proj = prepare(
        jnp.swapaxes(spectral_gain[0], 0, 1), mix_weight[0], proj_weight[0], (spectrum,)
    )
    gain_next, mix_next, _ = prepare(
        lax.ppermute(jnp.swapaxes(spectral_gain[0], 0, 1), "section", shift),
        lax.ppermute(mix_weight[0], "section", shift),
        proj_weight[0],
        (spectrum,),
    )
    tables = legendre_tables(start, order, lat, spread, spread_turned, (spectrum,))
    behind = [tables[4 * group + 2 : 4 * group + 4] for group in range(GROUPS)]
    scaled, payload = spectral_forward(
        recv, tables[0::4], tables[1::4], gain, mix, (turned, proj)
    )
    recv = exchange(payload).reshape(rows, 2 * C)
    small_rows, proj_small = grid_stage(
        0,
        1,
        recv,
        upstream,
        turned,
        proj,
        inverse,
        inverse_turned,
        (upstream_next, gain_next, mix_next),
    )
    small = exchange(small_rows.reshape(DEVICES, TILES, TILE, LANES))
    large, proj_large = grid_stage(
        1, 2, recv, upstream, turned, proj, inverse, inverse_turned, (small_rows,)
    )
    large = exchange(large.reshape(DEVICES, TILES, TILE, 2 * LANES))

    mixeds, moved = [None] * GROUPS, [None] * GROUPS
    every = tuple(range(GROUPS))
    mixed_small = spectral_backward(every, small, [table[0] for table in behind])
    moved_small = lax.ppermute(mixed_small, "section", shift)
    mixed_rest = spectral_backward((1, 2), large, [behind[1][0], behind[2][0]], (moved_small,))
    moved_rest = lax.ppermute(mixed_rest, "section", shift)
    mixed_0 = spectral_backward((0,), large, [behind[0][0]], (mixed_rest,))
    out_rest = weight_grads(
        scaled, mixed_small, (mixed_0, mixed_rest), mix, gain, proj_small, proj_large
    )
    for block, group in enumerate((1, 2)):
        out_rest = analysis_back(
            group,
            behind[group][1],
            moved_small,
            moved_rest,
            block * PACKED[1],
            gain_next,
            mix_next,
            2 * GROUP_TILES + 1,
            block,
            (out_rest,),
        )
    moved_0 = lax.ppermute(hold(mixed_0, (moved_rest,)), "section", shift)
    recv_rest = exchange(out_rest)
    out_0 = analysis_back(
        0, behind[0][1], moved_small, moved_0, 0, gain_next, mix_next, GROUP_TILES + 1, 0
    )
    out_0, token = attach_totals(recv_rest, out_0)
    recv_0 = exchange(out_0)
    (base,) = field_stage(recv_rest, 0, forward[1], upstream_next, after=(token,))
    (base,) = field_stage(recv_rest, 1, forward[2], base)
    received, grad_w2, grad_mix, grad_gain = field_stage(recv_0, 0, forward[0], base, True)
    return (
        received[None],
        grad_w2[None],
        grad_mix[None],
        jnp.swapaxes(grad_gain, 0, 1)[None],
    )


def solution(mesh):
    in_specs = (
        P("section", "lat", None, None),
        P("section", "lat", None, None),
        P("section", None, None),
        P("section", None, None, None),
        P("section", None, None),
    )
    out_specs = (
        P("section", "lat", None, None),
        P("section", None, None),
        P("section", None, None, None),
        P("section", None, None),
    )
    return jax.shard_map(shards, mesh=mesh, in_specs=in_specs, out_specs=out_specs, check_vma=False)
```

```python
import functools
import math

import jax
import jax.numpy as jnp
import ml_dtypes
import numpy as np
from jax import lax
from jax.experimental import pallas as pl
from jax.experimental.pallas import tpu as pltpu
from jax.sharding import PartitionSpec as P

NLAT = 384
NLON = 768
MODES = 384
C = 192
DEVICES = 32
LAT_LOCAL = 12
ORDERS = 12
GROUPS = 3
GROUP_ORDERS = 4
HALF = 64
LANES = 128
TILE = 16
TILES = 9
GROUP_TILES = 3
SPAN = DEVICES * TILE
LAT_BLOCKS = 4
BLOCK_LATS = NLAT // LAT_BLOCKS
MIB = 1024 * 1024
F32 = jnp.float32
BF16 = jnp.bfloat16
NT = (((1,), (1,)), ((), ()))

PAIRS = ((0, 0), (1, 0), (1, 1), (2, 1), (2, 2), (3, 2))


def degrees_of(group):
    return MODES - LANES * group


def half_lanes(shape):
    return lax.broadcasted_iota(jnp.int32, shape, 1) < HALF


def packed_rows(group):
    rows, first = [], 0
    for local in range(GROUP_ORDERS):
        rows.append(slice(first, first + degrees_of(group) - DEVICES * local))
        first = rows[-1].stop
    return rows


PACKED = [packed_rows(group)[-1].stop for group in range(GROUPS)]
BASES = [sum(PACKED[:group]) for group in range(GROUPS)]


def dot(left, right):
    return jnp.dot(left, right, preferred_element_type=F32)


def dot_nt(left, right):
    return lax.dot_general(left, right, NT, preferred_element_type=F32)


def whole(shape):
    return pl.BlockSpec(shape, lambda *_: (0,) * len(shape), pipeline_mode=pl.Buffered(1))


HELD = pl.BlockSpec(memory_space=pltpu.HBM)


def call(
    kernel, inputs, in_specs, out_specs, out_shape, grid, after=(), aliases=None, vmem=56, **extra
):
    count = len(inputs)

    def body(*refs):
        kernel(*refs[:count], *refs[count + len(after) :])

    return pl.pallas_call(
        body,
        grid=grid,
        in_specs=list(in_specs) + [pl.BlockSpec(memory_space=pl.ANY)] * len(after),
        out_specs=out_specs,
        out_shape=out_shape,
        input_output_aliases=aliases or {},
        compiler_params=pltpu.CompilerParams(vmem_limit_bytes=vmem * MIB),
        cost_estimate=pl.CostEstimate(flops=1, bytes_accessed=1, transcendentals=0),
        **extra,
    )(*inputs, *after)


def order_rows(first, count):
    device = np.arange(DEVICES)[:, None]
    local = np.arange(GROUP_ORDERS * count)[None, :] + GROUP_ORDERS * first
    return (DEVICES * local + device).reshape(-1)


def fourier_rows(orders):
    phase = (orders[:, None] * np.arange(NLON)[None, :]) % NLON
    angle = phase * (2.0 * math.pi / NLON)
    return np.cos(angle), -np.sin(angle)


def forward_rows(first, count):
    cosine, sine = fourier_rows(order_rows(first, count))
    table = np.concatenate([cosine, sine], axis=0)
    return jnp.asarray(table.astype(np.float32).astype(ml_dtypes.bfloat16))


def inverse_rows():
    device = np.arange(DEVICES)[:, None]
    orders = (DEVICES * np.arange(ORDERS)[None, :] + device).reshape(-1)
    factor = np.where(orders == 0, 1.0, 2.0)[:, None] / NLON
    cosine, sine = fourier_rows(orders)
    table = np.concatenate([factor * cosine, factor * sine], axis=0)
    return table.astype(np.float32).astype(ml_dtypes.bfloat16)


def spread_tables():
    rows = np.arange(LANES)
    source, inner = rows // TILE, rows % TILE
    tables = np.zeros((len(PAIRS), LANES, LANES), np.float32)
    for index, (order, tile) in enumerate(PAIRS):
        lat = TILE * tile + inner - LAT_LOCAL * order
        valid = (lat >= 0) & (lat < LAT_LOCAL)
        tables[index, (source * LAT_LOCAL + lat)[valid], rows[valid]] = 1.0
    flat = jnp.asarray(tables.astype(ml_dtypes.bfloat16))
    turned = jnp.asarray(np.swapaxes(tables, 1, 2).astype(ml_dtypes.bfloat16))
    return flat, turned


def log_starts():
    table = np.zeros((DEVICES, TILE, LANES), np.float32)
    numbers = np.zeros((DEVICES, TILE, LANES), np.float32)
    for device in range(DEVICES):
        for local in range(ORDERS):
            order = DEVICES * local + device
            numbers[device, local] = order
            table[device, local] = 0.5 * math.log((2.0 * order + 1.0) / 2.0) + 0.5 * (
                math.lgamma(order + 0.5) - math.lgamma(0.5) - math.lgamma(order + 1.0)
            )
    return table, numbers


def latitude_rows():
    colatitude = (np.arange(NLAT) + 0.5) * (math.pi / NLAT)
    harmonic = np.arange(1, NLAT // 2 + 1)
    terms = np.cos(2.0 * harmonic[None, :] * colatitude[:, None]) / (4.0 * harmonic**2 - 1.0)
    weight = 2.0 / NLAT * (1.0 - 2.0 * np.sum(terms, axis=1))
    rows = np.stack([np.cos(colatitude), np.log(np.sin(colatitude)), weight])
    rows = np.concatenate([rows, np.zeros((5, NLAT))]).reshape(8, LAT_BLOCKS, BLOCK_LATS)
    rows = np.pad(rows, ((0, 0), (0, 0), (0, LANES - BLOCK_LATS)))
    return rows.reshape(8, SPAN).astype(np.float32)


def legendre_rows(start_ref, order_ref, lat_ref, rows_ref):
    order = jnp.concatenate([order_ref[...]] * LAT_BLOCKS, axis=1)
    cosine = jnp.broadcast_to(lat_ref[0:1, :], (TILE, SPAN))
    log_sin = jnp.broadcast_to(lat_ref[1:2, :], (TILE, SPAN))
    log_start = jnp.concatenate([start_ref[...]] * LAT_BLOCKS, axis=1) + order * log_sin
    narrow = order_ref[...]
    narrow_square = narrow * narrow
    second_factor = jnp.concatenate([jnp.sqrt(2.0 * narrow + 3.0)] * LAT_BLOCKS, axis=1)
    zeros = jnp.zeros((TILE, SPAN), F32)

    def block(index, state):
        previous, current, log_scale = state
        scale = jnp.exp(log_scale)
        for inner in range(16):
            row = index * 16 + inner
            degree = row.astype(F32)
            lower = degree - 1.0
            up = jnp.sqrt(
                jnp.maximum(4.0 * degree * degree - 1.0, 1.0)
                / jnp.maximum(degree * degree - narrow_square, 1.0)
            )
            down = jnp.sqrt(
                jnp.maximum(lower * lower - narrow_square, 0.0)
                / jnp.maximum(4.0 * lower * lower - 1.0, 1.0)
            )
            up = jnp.concatenate([up] * LAT_BLOCKS, axis=1)
            down = jnp.concatenate([down] * LAT_BLOCKS, axis=1)
            general = up * (cosine * current - down * previous)
            second = second_factor * cosine * current
            new_row = jnp.where(
                degree == order,
                1.0,
                jnp.where(
                    degree == order + 1.0, second, jnp.where(degree > order + 1.0, general, 0.0)
                ),
            )
            scaled = new_row * scale
            for part in range(LAT_BLOCKS):
                rows_ref[part, row] = scaled[:, part * LANES : (part + 1) * LANES]
            previous, current = current, new_row
        largest = jnp.maximum(jnp.abs(previous), jnp.abs(current))
        largest = jnp.where(largest > 0.0, largest, 1.0)
        return previous / largest, current / largest, log_scale + jnp.log(largest)

    lax.fori_loop(0, MODES // 16, block, (zeros, zeros, log_start))


def table_kernel(start_ref, order_ref, lat_ref, flat_ref, turned_ref, *rest):
    outs, rows_ref, buffers, sems = rest[:12], rest[12], rest[13:25], rest[25]
    legendre_rows(start_ref, order_ref, lat_ref, rows_ref)
    copies = []
    for group in range(GROUPS):
        ahead_flat, ahead_turned, behind_flat, behind_turned = buffers[4 * group : 4 * group + 4]

        def part_step(part, carry):
            lats = pl.ds(pl.multiple_of(part * LANES, LANES), LANES)
            weight = lat_ref[2:3, lats]
            for local in range(GROUP_ORDERS):
                legendre = rows_ref[part, LANES * group :, GROUP_ORDERS * group + local, :]
                synthesis = legendre.astype(BF16)
                analysis = (weight * legendre).astype(BF16)
                pairs = [index for index, (order, _) in enumerate(PAIRS) if order == local]
                flat = jnp.concatenate([flat_ref[index] for index in pairs], axis=1)
                turned = jnp.concatenate([turned_ref[index] for index in pairs], axis=0)
                products = (
                    dot(analysis, flat).astype(BF16),
                    dot_nt(turned, synthesis).astype(BF16),
                    dot(synthesis, flat).astype(BF16),
                    dot_nt(turned, analysis).astype(BF16),
                )
                for place, index in enumerate(pairs):
                    cut = slice(place * LANES, (place + 1) * LANES)
                    ahead_flat[index, :, lats] = products[0][:, cut]
                    ahead_turned[index, lats, :] = products[1][cut]
                    behind_flat[index, :, lats] = products[2][:, cut]
                    behind_turned[index, lats, :] = products[3][cut]
            return carry

        lax.fori_loop(0, LAT_BLOCKS, part_step, 0)
        for place in range(4):
            at = 4 * group + place
            copy = pltpu.make_async_copy(buffers[at], outs[at], sems.at[at])
            copy.start()
            copies.append(copy)
    for copy in copies:
        copy.wait()


def legendre_tables(start, order, lat, flat, turned, after):
    shapes = []
    for group in range(GROUPS):
        degrees = degrees_of(group)
        shapes += [(len(PAIRS), degrees, SPAN), (len(PAIRS), SPAN, degrees)] * 2
    inputs = (start, order, lat, flat, turned)
    return call(
        table_kernel,
        inputs,
        [whole(value.shape) for value in inputs],
        [HELD] * len(shapes),
        [jax.ShapeDtypeStruct(shape, BF16) for shape in shapes],
        (1,),
        after,
        scratch_shapes=[pltpu.VMEM((LAT_BLOCKS, MODES, TILE, LANES), F32)]
        + [pltpu.VMEM(shape, BF16) for shape in shapes]
        + [pltpu.SemaphoreType.DMA((len(shapes),))],
        name="legendre_tables",
    )


def blocks_of(value):
    return [value[:, index * HALF : (index + 1) * HALF] for index in range(GROUPS)]


def interleave(first, second):
    pairs = zip(blocks_of(first), blocks_of(second))
    return jnp.concatenate([block for pair in pairs for block in pair], axis=1)


def prepare_kernel(gain_ref, mix_ref, proj_ref, gain_out, mix_out, proj_out):
    gain = gain_ref[...].T
    gain_out[...] = interleave(gain, gain)
    real, imag = mix_ref[0].astype(F32), mix_ref[1].astype(F32)
    upper, lower = interleave(real, imag), interleave(-imag, real)
    for index in range(GROUPS):
        rows = slice(index * HALF, (index + 1) * HALF)
        start = index * LANES
        mix_out[start : start + HALF, :] = upper[rows].astype(BF16)
        mix_out[start + HALF : start + LANES, :] = lower[rows].astype(BF16)
    proj = proj_ref[...].astype(F32).T
    proj_out[...] = interleave(proj, proj).astype(BF16)


def prepare(gain, mix, proj, after):
    shapes = ((MODES, 2 * C), (2 * C, 2 * C), (C, 2 * C))
    kinds = (F32, BF16, BF16)
    return call(
        prepare_kernel,
        (gain, mix, proj),
        [whole(gain.shape), whole(mix.shape), whole(proj.shape)],
        [whole(shape) for shape in shapes],
        [jax.ShapeDtypeStruct(shape, kind) for shape, kind in zip(shapes, kinds)],
        (1,),
        after,
        name="prepare",
    )


def spectrum_kernel(field_ref, table_ref, out_ref, scratch):
    step = pl.program_id(0)
    rows = table_ref.shape[0] // 2
    low = half_lanes((rows, LANES))
    fields = field_ref[...].reshape(4 * C, NLON)
    product = dot_nt(table_ref[...], fields)
    for block in range(4 * GROUPS):
        inner, index = block // GROUPS, block % GROUPS
        lanes = slice(block // 2 * LANES, (block // 2 + 1) * LANES)
        real, imag = product[:rows, lanes], product[rows:, lanes]
        if block % 2:
            tile = jnp.where(low, pltpu.roll(real, HALF, 1), imag)
        else:
            tile = jnp.where(low, real, pltpu.roll(imag, HALF, 1))
        scratch[index, pl.ds(step * 4 + inner, rows, stride=LAT_LOCAL), :] = tile

    @pl.when(step == LAT_LOCAL // 4 - 1)
    def _():
        for index in range(GROUPS):
            out_ref[:, index * LANES : (index + 1) * LANES] = scratch[index].astype(BF16)


def spectrum_rows(field, table, after=()):
    rows = table.shape[0] // 2 * LAT_LOCAL
    return call(
        spectrum_kernel,
        (field, table),
        [pl.BlockSpec((4, C, NLON), lambda b: (b, 0, 0)), whole(table.shape)],
        whole((rows, 2 * C)),
        jax.ShapeDtypeStruct((rows, 2 * C), BF16),
        (LAT_LOCAL // 4,),
        after,
        scratch_shapes=[pltpu.VMEM((GROUPS, rows, LANES), F32)],
        name="spectrum_rows",
    )


def order_sums(group, table_ref, tiles):
    totals = [None] * GROUP_ORDERS
    for tile in range(GROUP_TILES):
        left = [table_ref[2 * tile + place, DEVICES * (tile + place) :, :] for place in range(2)]
        product = dot(jnp.concatenate(left, axis=0), tiles[tile])
        middle = left[0].shape[0]
        for order, part in ((tile, product[:middle]), (tile + 1, product[middle:])):
            totals[order] = part if totals[order] is None else totals[order] + part
    return totals


def tile_sum(tile, table_ref, first, second):
    left = jnp.concatenate([table_ref[2 * tile], table_ref[2 * tile + 1]], axis=1)
    return dot(left, jnp.concatenate([first, second], axis=0))


def spectral_kernel(recv_ref, *refs):
    a_refs, st_refs = refs[0:3], refs[3:6]
    gain_ref, mix_ref = refs[6:8]
    scaled_ref, payload_ref, recv, payload = refs[8:12]
    a_buffers, st_buffers, scaled_buffers = refs[12:15], refs[15:18], refs[18:21]
    in_sems, out_sems = refs[21:23]
    schedule = (2, 1, 0)
    arrivals, departures = {}, []
    for group in schedule:
        tiles = pl.ds(GROUP_TILES * group, GROUP_TILES)
        arrivals[group] = [
            pltpu.make_async_copy(recv_ref.at[:, tiles], recv.at[group], in_sems.at[group, 0]),
            pltpu.make_async_copy(a_refs[group], a_buffers[group], in_sems.at[group, 1]),
            pltpu.make_async_copy(st_refs[group], st_buffers[group], in_sems.at[group, 2]),
        ]
        for copy in arrivals[group]:
            copy.start()
    for group in schedule:
        for copy in arrivals[group][:2]:
            copy.wait()
        tiles = [recv[group, :, tile].reshape(SPAN, 2 * C) for tile in range(GROUP_TILES)]
        held = scaled_buffers[group]
        for local, coef in enumerate(order_sums(group, a_buffers[group], tiles)):
            skipped = DEVICES * local
            held[packed_rows(group)[local], :] = (
                gain_ref[LANES * group + skipped :, :] * coef
            ).astype(BF16)
        product = dot(held[...], mix_ref[...]).astype(BF16)
        mixed = []
        for local, rows in enumerate(packed_rows(group)):
            zeros = jnp.zeros((DEVICES * local, 2 * C), BF16)
            mixed.append(
                jnp.concatenate([zeros, product[rows]], axis=0) if local else product[rows]
            )
        arrivals[group][2].wait()
        for tile in range(GROUP_TILES):
            grid = tile_sum(tile, st_buffers[group], mixed[tile], mixed[tile + 1])
            payload[group, :, tile] = grid.astype(BF16).reshape(DEVICES, TILE, 2 * C)
        tiles = pl.ds(GROUP_TILES * group, GROUP_TILES)
        copies = (
            pltpu.make_async_copy(
                payload.at[group], payload_ref.at[:, tiles], out_sems.at[group, 0]
            ),
            pltpu.make_async_copy(
                scaled_buffers[group],
                scaled_ref.at[pl.ds(BASES[group], PACKED[group])],
                out_sems.at[group, 1],
            ),
        )
        for copy in copies:
            copy.start()
            departures.append(copy)
    for copy in departures:
        copy.wait()


def spectral_forward(recv, a, st, gain, mix, after=()):
    slots = (GROUPS, DEVICES, GROUP_TILES, TILE, 2 * C)
    return call(
        spectral_kernel,
        (recv, *a, *st, gain, mix),
        [HELD] * 7 + [whole(gain.shape), whole(mix.shape)],
        [HELD] * 2,
        [
            jax.ShapeDtypeStruct((sum(PACKED), 2 * C), BF16),
            jax.ShapeDtypeStruct(recv.shape, BF16),
        ],
        (1,),
        after,
        scratch_shapes=[pltpu.VMEM(slots, BF16), pltpu.VMEM(slots, BF16)]
        + [pltpu.VMEM(value.shape, BF16) for value in a]
        + [pltpu.VMEM(value.shape, BF16) for value in st]
        + [pltpu.VMEM((rows, 2 * C), BF16) for rows in PACKED]
        + [pltpu.SemaphoreType.DMA((GROUPS, 3)), pltpu.SemaphoreType.DMA((GROUPS, 2))],
        name="spectral_forward",
    )


def normal_cumulative(value, bell):
    denominator = 1.0 + (0.3275911 / math.sqrt(2.0)) * jnp.abs(value)
    inverse = pl.reciprocal(denominator, approx=True)
    inverse = inverse * (2.0 - denominator * inverse)
    series = 0.5 * 1.061405429 * inverse - 0.5 * 1.453152027
    series = series * inverse + 0.5 * 1.421413741
    series = series * inverse - 0.5 * 0.284496736
    series = series * inverse + 0.5 * 0.254829592
    tail = series * inverse * bell
    return jnp.where(value < 0.0, tail, 1.0 - tail)


def grid_kernel(
    recv_ref, up_ref, turned_ref, proj_ref, held_ref, turned_table_ref,
    out_ref, grad_ref, scratch, out_scratch, act_scratch, pre_scratch, table_ref, sem,
):
    step = pl.program_id(1)
    opening = jnp.logical_and(pl.program_id(0) == 0, step == 0)

    @pl.when(opening)
    def _():
        pltpu.make_async_copy(held_ref, table_ref, sem).start()

    low = half_lanes((MODES, LANES))
    block = 128

    @pl.when(step == 0)
    def _():
        scratch[...] = recv_ref[...].astype(F32)
        grad_ref[...] = jnp.zeros_like(grad_ref)

    columns = []
    for pair in range(2):
        first = scratch[pl.ds(step * 4 + 2 * pair, MODES, stride=LAT_LOCAL), :]
        second = scratch[pl.ds(step * 4 + 2 * pair + 1, MODES, stride=LAT_LOCAL), :]
        real = jnp.where(low, first, pltpu.roll(second, HALF, 1))
        imag = jnp.where(low, pltpu.roll(first, HALF, 1), second)
        columns.append(jnp.concatenate([real, imag], axis=0).astype(BF16))
    modes = jnp.concatenate(columns, axis=1)
    low_block = half_lanes((block, LANES))
    for part in range(NLON // block):
        rows = slice(part * block, (part + 1) * block)
        pre = dot(turned_table_ref[rows, :], modes)
        grad_act = jnp.concatenate(
            [
                jnp.where(
                    low_block,
                    dot(turned_ref[2 * pair, rows, :], proj_ref[...]),
                    dot(turned_ref[2 * pair + 1, rows, :], proj_ref[...]),
                )
                for pair in range(2)
            ],
            axis=1,
        )
        bell = jnp.exp(-0.5 * pre * pre)
        cumulative = normal_cumulative(pre, bell)
        slope = cumulative + pre * bell * (1.0 / math.sqrt(2.0 * math.pi))
        act_scratch[rows, :] = (pre * cumulative).astype(BF16)
        pre_scratch[rows, :] = (grad_act * slope).astype(BF16)
    low_grad = half_lanes((C, LANES))
    for pair in range(2):
        act = act_scratch[:, pair * LANES : (pair + 1) * LANES]
        ups = up_ref[2 * pair : 2 * pair + 2].reshape(2 * C, NLON)
        grads = dot(ups, act)
        grad_ref[...] += jnp.where(low_grad, grads[:C], grads[C:])

    @pl.when(opening)
    def _():
        pltpu.make_async_copy(held_ref, table_ref, sem).wait()

    grad_modes = dot(table_ref[...], pre_scratch[...])
    for pair in range(2):
        lanes = slice(pair * LANES, (pair + 1) * LANES)
        real, imag = grad_modes[:MODES, lanes], grad_modes[MODES:, lanes]
        out_scratch[pl.ds(step * 4 + 2 * pair, MODES, stride=LAT_LOCAL), :] = jnp.where(
            low, real, pltpu.roll(imag, HALF, 1)
        )
        out_scratch[pl.ds(step * 4 + 2 * pair + 1, MODES, stride=LAT_LOCAL), :] = jnp.where(
            low, pltpu.roll(real, HALF, 1), imag
        )

    @pl.when(step == LAT_LOCAL // 4 - 1)
    def _():
        out_ref[...] = out_scratch[...].astype(BF16)


def grid_stage(first, blocks, recv, up, turned, proj, table, turned_table, after=()):
    rows = MODES * LAT_LOCAL
    lanes_spec = pl.BlockSpec((rows, LANES), lambda q, b: (0, q))
    grad_spec = pl.BlockSpec((C, LANES), lambda q, b: (0, q))
    return call(
        grid_kernel,
        (recv, up, turned, proj, table, turned_table),
        [
            pl.BlockSpec((rows, LANES), lambda q, b: (0, q + first)),
            pl.BlockSpec((4, C, NLON), lambda q, b: (b, 0, 0)),
            pl.BlockSpec((4, NLON, C), lambda q, b: (b, 0, 0)),
            pl.BlockSpec((C, LANES), lambda q, b: (0, q + first)),
            HELD,
            whole(turned_table.shape),
        ],
        [lanes_spec, grad_spec],
        [
            jax.ShapeDtypeStruct((rows, LANES * blocks), BF16),
            jax.ShapeDtypeStruct((C, LANES * blocks), F32),
        ],
        (blocks, LAT_LOCAL // 4),
        after,
        scratch_shapes=[
            pltpu.VMEM((rows, LANES), F32),
            pltpu.VMEM((rows, LANES), F32),
            pltpu.VMEM((NLON, 2 * LANES), BF16),
            pltpu.VMEM((NLON, 2 * LANES), BF16),
            pltpu.VMEM(table.shape, BF16),
            pltpu.SemaphoreType.DMA,
        ],
        name=f"grid_stage_{blocks}",
    )


def backward_kernel(groups, *refs):
    recv_ref, table_refs, out_ref = refs[0], refs[1 : 1 + len(groups)], refs[1 + len(groups)]
    buffers, sems = refs[2 + len(groups) : -1], refs[-1]
    copies = [
        pltpu.make_async_copy(table_refs[place], buffers[place], sems.at[place])
        for place in range(len(groups))
    ]
    for copy in copies:
        copy.start()
    lanes = recv_ref.shape[-1]
    first = 0
    for place, group in enumerate(groups):
        start = GROUP_TILES * group if recv_ref.shape[1] == TILES else 0
        tiles = [
            recv_ref[:, start + tile].reshape(SPAN, lanes) for tile in range(GROUP_TILES)
        ]
        copies[place].wait()
        sums = order_sums(group, buffers[place], tiles)
        for total, rows in zip(sums, packed_rows(group)):
            out_ref[first + rows.start : first + rows.stop, :] = total.astype(BF16)
        first += PACKED[group]


def spectral_backward(groups, recv, tables, after=()):
    lanes = recv.shape[-1]
    tiles = GROUP_TILES if len(groups) == 1 else TILES
    block = groups[0] if len(groups) == 1 else 0
    out = (sum(PACKED[group] for group in groups), lanes)
    return call(
        functools.partial(backward_kernel, groups),
        (recv, *tables),
        [
            pl.BlockSpec(
                (DEVICES, tiles, TILE, lanes),
                lambda b: (0, block, 0, 0),
                pipeline_mode=pl.Buffered(1),
            )
        ]
        + [HELD] * len(groups),
        whole(out),
        jax.ShapeDtypeStruct(out, BF16),
        (1,),
        after,
        scratch_shapes=[pltpu.VMEM(table.shape, BF16) for table in tables]
        + [pltpu.SemaphoreType.DMA((len(groups),))],
        vmem=20,
        name="spectral_backward_" + "_".join(str(group) for group in groups),
    )


def hold_kernel(value_ref, out_ref):
    pass


def hold(value, after):
    held = pl.BlockSpec(memory_space=pl.ANY)
    return call(
        hold_kernel,
        (value,),
        [held],
        held,
        jax.ShapeDtypeStruct(value.shape, value.dtype),
        (1,),
        after,
        aliases={0: 0},
        vmem=1,
        name="hold",
    )


def synthesis_kernel(groups, small_ref, large_ref, gain_ref, mix_ref, *refs):
    count = len(groups)
    table_refs, refs = refs[:count], refs[-3 * count - 2 :]
    out_ref, coeff_refs, at_refs = refs[0], refs[1 : 1 + count], refs[1 + count : 1 + 2 * count]
    part_refs, sems = refs[1 + 2 * count : -1], refs[-1]
    copies = []
    for place, group in enumerate(groups):
        rows = pl.ds(BASES[group], PACKED[group])
        copies.append(
            (
                pltpu.make_async_copy(small_ref.at[rows], part_refs[place], sems.at[0, place]),
                pltpu.make_async_copy(table_refs[place], at_refs[place], sems.at[1, place]),
            )
        )
    for pair in copies:
        for copy in pair:
            copy.start()
    start = 0
    for place, group in enumerate(groups):
        coeff_ref, at_ref = coeff_refs[place], at_refs[place]
        degrees = degrees_of(group)
        copies[place][0].wait()
        large = large_ref[start : start + PACKED[group], :]
        start += PACKED[group]
        mixed = jnp.concatenate([part_refs[place][...], large], axis=1)
        product = dot_nt(mixed, mix_ref[...])
        for local, rows in enumerate(packed_rows(group)):
            first = local * degrees
            skipped = DEVICES * local
            if skipped:
                coeff_ref[first : first + skipped, :] = jnp.zeros((skipped, 2 * C), BF16)
            coeff_ref[first + skipped : first + degrees, :] = (
                gain_ref[LANES * group + skipped :, :] * product[rows]
            ).astype(BF16)
        copies[place][1].wait()
        for tile in range(GROUP_TILES):
            first = coeff_ref[tile * degrees : (tile + 1) * degrees, :]
            second = coeff_ref[(tile + 1) * degrees : (tile + 2) * degrees, :]
            out = tile_sum(tile, at_ref, first, second).astype(BF16)
            out_ref[:, GROUP_TILES * place + tile] = out.reshape(DEVICES, TILE, 2 * C)


def analysis_back(groups, tables, small, large, gain, mix, tiles, payload=(), after=()):
    inputs = (small, large, gain, mix, *tables, *payload)
    count = len(groups)
    return call(
        functools.partial(synthesis_kernel, groups),
        inputs,
        [HELD] + [whole(value.shape) for value in inputs[1:4]] + [HELD] * len(inputs[4:]),
        whole((DEVICES, GROUP_TILES * count, TILE, 2 * C)),
        pltpu.HBM((DEVICES, tiles, TILE, 2 * C), BF16),
        (1,),
        after,
        aliases={4 + count: 0} if payload else {},
        scratch_shapes=[
            pltpu.VMEM((GROUP_ORDERS * degrees_of(group), 2 * C), BF16) for group in groups
        ]
        + [pltpu.VMEM(table.shape, BF16) for table in tables]
        + [pltpu.VMEM((PACKED[group], LANES), BF16) for group in groups]
        + [pltpu.SemaphoreType.DMA((2, count))],
        vmem=24,
        name="analysis_back_" + "_".join(str(group) for group in groups),
    )


def fold(tile):
    return tile + pltpu.roll(tile, HALF, 1)


def weight_kernel(held_ref, small_ref, *refs):
    first_ref, rest_ref, mix_ref, factor_ref, proj_small, proj_large = refs[:6]
    out_ref, gain, packed, spaced, scaled_ref, sem = refs[6:]
    large = (first_ref[...], rest_ref[: PACKED[1], :], rest_ref[PACKED[1] :, :])
    copy = pltpu.make_async_copy(held_ref, scaled_ref, sem)
    copy.start()
    copy.wait()
    block = None
    for group in range(GROUPS):
        rows = slice(BASES[group], BASES[group] + PACKED[group])
        mixed = jnp.concatenate([small_ref[rows, :], large[group]], axis=1)
        part = lax.dot_general(
            scaled_ref[rows, :], mixed, (((0,), (0,)), ((), ())), preferred_element_type=F32
        )
        block = part if block is None else block + part
        product = dot_nt(mixed, mix_ref[...]) * scaled_ref[rows, :].astype(F32)
        for local, rows in enumerate(packed_rows(group)):
            part = product[rows]
            first = LANES * group + DEVICES * local
            if first:
                gain[first:, :] += part
            else:
                gain[...] = part
    gain[...] = gain[...] / factor_ref[...]
    low = half_lanes((HALF, LANES))
    low_gain = half_lanes((C, LANES))
    low_proj = half_lanes((C // 2, LANES))
    for index in range(GROUPS):
        lanes = slice(index * LANES, (index + 1) * LANES)
        for row_block in range(GROUPS):
            start = row_block * LANES
            first = block[start : start + HALF, lanes]
            second = pltpu.roll(block[start + HALF : start + LANES, lanes], HALF, 1)
            packed[index, row_block * HALF : (row_block + 1) * HALF, :] = jnp.where(
                low, first + second, first - second
            )
        packed[index, C : 2 * C, :] = jnp.where(
            low_gain, fold(gain[:C, lanes]), fold(gain[C:, lanes])
        )
        if index == 0:
            proj = fold(proj_small[...])
        else:
            proj = fold(proj_large[:, (index - 1) * LANES : index * LANES])
        packed[index, 2 * C :, :] = jnp.where(low_proj, proj[: C // 2], proj[C // 2 :])
        for row in range(TILE - 1):
            spaced[index, pl.ds(row, DEVICES, stride=TILE), :] = packed[
                index, row * DEVICES : (row + 1) * DEVICES, :
            ]
        spaced[index, pl.ds(TILE - 1, DEVICES, stride=TILE), :] = jnp.zeros((DEVICES, LANES), F32)
        out_ref[:, 0, :, lanes] = spaced[index].astype(BF16).reshape(DEVICES, TILE, LANES)


def weight_grads(scaled, small, large, mix, gain, proj_small, proj_large, after=()):
    tiles = 2 * GROUP_TILES
    inputs = (scaled, small, *large, mix, gain, proj_small, proj_large)
    return call(
        weight_kernel,
        inputs,
        [HELD] + [whole(value.shape) for value in inputs[1:]],
        pl.BlockSpec((DEVICES, 1, TILE, 2 * C), lambda b: (0, tiles, 0, 0)),
        pltpu.HBM((DEVICES, tiles + 1, TILE, 2 * C), BF16),
        (1,),
        after,
        scratch_shapes=[
            pltpu.VMEM((MODES, 2 * C), F32),
            pltpu.VMEM((GROUPS, 15 * DEVICES, LANES), F32),
            pltpu.VMEM((GROUPS, TILE * DEVICES, LANES), F32),
            pltpu.VMEM(scaled.shape, BF16),
            pltpu.SemaphoreType.DMA,
        ],
        vmem=24,
        name="weight_grads",
    )


def total_kernel(recv_ref, payload_ref, out_ref, token_ref):
    token_ref[...] = jnp.zeros((8, LANES), F32)
    total = jnp.sum(recv_ref[:, 0].astype(F32), axis=0)
    out_ref[:, 0] = jnp.broadcast_to(total.astype(BF16)[None], (DEVICES, TILE, 2 * C))


def attach_totals(recv, payload):
    def last(value):
        tile = value.shape[1] - 1
        return pl.BlockSpec((DEVICES, 1, TILE, 2 * C), lambda b: (0, tile, 0, 0))

    return call(
        total_kernel,
        (recv, payload),
        [last(recv), pl.BlockSpec(memory_space=pl.ANY)],
        [last(payload), whole((8, LANES))],
        [pltpu.HBM(payload.shape, BF16), jax.ShapeDtypeStruct((8, LANES), F32)],
        (1,),
        aliases={1: 0},
        vmem=8,
        name="attach_totals",
    )


def unpack_totals(recv_ref, proj_ref, mix_ref, gain_ref, spaced, packed):
    grid_scale = 1.0 / math.sqrt(NLAT * NLON)
    mode_scale = 1.0 / math.sqrt(MODES)
    lows, highs = [], []
    for index in range(GROUPS):
        lanes = slice(index * LANES, (index + 1) * LANES)
        spaced[index] = recv_ref[:, GROUP_TILES, :, lanes].reshape(DEVICES * TILE, LANES).astype(F32)
        for row in range(TILE - 1):
            packed[index, row * DEVICES : (row + 1) * DEVICES, :] = spaced[
                index, pl.ds(row, DEVICES, stride=TILE), :
            ]
        lows.append(packed[index, :, :HALF])
        highs.append(packed[index, :, HALF:])
    low = jnp.concatenate(lows, axis=1)
    high = jnp.concatenate(highs, axis=1)
    mix_ref[0] = grid_scale * low[:C]
    mix_ref[1] = grid_scale * high[:C]
    gain = jnp.concatenate([low[C : 2 * C], high[C : 2 * C]], axis=0)
    gain_ref[...] = mode_scale * gain.T
    proj = jnp.concatenate([low[2 * C :], high[2 * C :]], axis=0)
    proj_ref[...] = grid_scale * proj.T


def field_kernel(recv_ref, table_ref, base_ref, out_ref, *refs):
    totals, (scratch, *unpacking) = refs[:3] if len(refs) > 1 else (), refs[3:] or refs
    step = pl.program_id(0)
    orders = DEVICES * GROUP_ORDERS
    rows = orders * LAT_LOCAL

    @pl.when(step == 0)
    def _():
        for index in range(GROUPS):
            lanes = slice(index * LANES, (index + 1) * LANES)
            values = recv_ref[:, :GROUP_TILES, :, lanes].astype(F32)
            scratch[index] = values.reshape(rows, LANES)
        if totals:
            unpack_totals(recv_ref, *totals, *unpacking)

    lefts = []
    for inner in range(4):
        real, imag = [], []
        for index in range(GROUPS):
            values = scratch[index, pl.ds(step * 4 + inner, orders, stride=LAT_LOCAL), :]
            turned = values.T.astype(BF16)
            real.append(turned[:HALF])
            imag.append(turned[HALF:])
        lefts.append(
            jnp.concatenate(
                [jnp.concatenate(real, axis=0), jnp.concatenate(imag, axis=0)], axis=1
            )
        )
    product = dot(jnp.concatenate(lefts, axis=0), table_ref[...])
    for inner in range(4):
        total = base_ref[inner].astype(F32) + product[inner * C : (inner + 1) * C]
        out_ref[inner] = total.astype(out_ref.dtype)


def field_stage(recv, at, table, base, unpacked=False, after=()):
    rows = DEVICES * GROUP_ORDERS * LAT_LOCAL
    block = pl.BlockSpec((4, C, NLON), lambda b: (b, 0, 0))
    tiles = GROUP_TILES + int(unpacked)
    totals = ((C, C), (2, C, C), (C, MODES)) if unpacked else ()
    scratch_shapes = [pltpu.VMEM((GROUPS, rows, LANES), F32)]
    if unpacked:
        scratch_shapes += [
            pltpu.VMEM((GROUPS, TILE * DEVICES, LANES), F32),
            pltpu.VMEM((GROUPS, 15 * DEVICES, LANES), F32),
        ]
    return call(
        field_kernel,
        (recv, table, base),
        [
            pl.BlockSpec(
                (DEVICES, tiles, TILE, 2 * C),
                lambda b: (0, at, 0, 0),
                pipeline_mode=pl.Buffered(1),
            ),
            whole(table.shape),
            block,
        ],
        [block] + [whole(shape) for shape in totals],
        [pltpu.HBM((LAT_LOCAL, C, NLON), BF16)]
        + [jax.ShapeDtypeStruct(shape, F32) for shape in totals],
        (LAT_LOCAL // 4,),
        after,
        scratch_shapes=scratch_shapes,
        vmem=56 if unpacked else 20,
        name="field_stage",
    )


def exchange(payload):
    tiles, lanes = payload.shape[1], payload.shape[3]
    flat = payload.reshape(DEVICES, tiles * TILE, lanes)
    moved = lax.all_to_all(flat, "lat", split_axis=0, concat_axis=0, tiled=True)
    return moved.reshape(DEVICES, tiles, TILE, lanes)


def shards(saved_input, incoming, spectral_gain, mix_weight, proj_weight):
    device = lax.axis_index("lat")
    section_count = lax.axis_size("section")
    shift = [(source, (source - 1) % section_count) for source in range(section_count)]

    forward_all = forward_rows(0, GROUPS)
    forward = [forward_rows(group, 1) for group in range(GROUPS)]
    inverse_np = inverse_rows()
    inverse = jnp.asarray(inverse_np)
    inverse_turned = jnp.asarray(np.ascontiguousarray(inverse_np.T))
    spread, spread_turned = spread_tables()
    lat = jnp.asarray(latitude_rows())
    starts, numbers = log_starts()
    start = lax.dynamic_index_in_dim(jnp.asarray(starts), device, 0, keepdims=False)
    order = lax.dynamic_index_in_dim(jnp.asarray(numbers), device, 0, keepdims=False)

    field = saved_input[0]
    upstream = incoming[0]
    upstream_next = lax.ppermute(upstream, "section", shift)
    turned = jnp.swapaxes(upstream, 1, 2)
    rows = MODES * LAT_LOCAL
    spectrum = spectrum_rows(field, forward_all)
    recv = exchange(spectrum.reshape(DEVICES, TILES, TILE, 2 * C))
    gain, mix, proj = prepare(
        jnp.swapaxes(spectral_gain[0], 0, 1), mix_weight[0], proj_weight[0], (spectrum,)
    )
    gain_next, mix_next, _ = prepare(
        lax.ppermute(jnp.swapaxes(spectral_gain[0], 0, 1), "section", shift),
        lax.ppermute(mix_weight[0], "section", shift),
        proj_weight[0],
        (spectrum,),
    )
    tables = legendre_tables(start, order, lat, spread, spread_turned, (spectrum,))
    behind = [tables[4 * group + 2 : 4 * group + 4] for group in range(GROUPS)]
    scaled, payload = spectral_forward(
        recv, tables[0::4], tables[1::4], gain, mix, (turned, proj)
    )
    recv = exchange(payload).reshape(rows, 2 * C)
    small_rows, proj_small = grid_stage(
        0,
        1,
        recv,
        upstream,
        turned,
        proj,
        inverse,
        inverse_turned,
        (upstream_next, gain_next, mix_next),
    )
    small = exchange(small_rows.reshape(DEVICES, TILES, TILE, LANES))
    large, proj_large = grid_stage(
        1, 2, recv, upstream, turned, proj, inverse, inverse_turned, (small_rows,)
    )
    large = exchange(large.reshape(DEVICES, TILES, TILE, 2 * LANES))

    mixeds, moved = [None] * GROUPS, [None] * GROUPS
    every = tuple(range(GROUPS))
    mixed_small = spectral_backward(every, small, [table[0] for table in behind])
    moved_small = lax.ppermute(mixed_small, "section", shift)
    mixed_rest = spectral_backward((1, 2), large, [behind[1][0], behind[2][0]], (moved_small,))
    moved_rest = lax.ppermute(mixed_rest, "section", shift)
    mixed_0 = spectral_backward((0,), large, [behind[0][0]], (mixed_rest,))
    out_rest = weight_grads(
        scaled, mixed_small, (mixed_0, mixed_rest), mix, gain, proj_small, proj_large
    )
    out_rest = analysis_back(
        (1, 2),
        [behind[1][1], behind[2][1]],
        moved_small,
        moved_rest,
        gain_next,
        mix_next,
        2 * GROUP_TILES + 1,
        (out_rest,),
    )
    moved_0 = lax.ppermute(hold(mixed_0, (moved_rest,)), "section", shift)
    recv_rest = exchange(out_rest)
    out_0 = analysis_back(
        (0,), [behind[0][1]], moved_small, moved_0, gain_next, mix_next, GROUP_TILES + 1
    )
    out_0, token = attach_totals(recv_rest, out_0)
    recv_0 = exchange(out_0)
    (base,) = field_stage(recv_rest, 0, forward[1], upstream_next, after=(token,))
    (base,) = field_stage(recv_rest, 1, forward[2], base)
    received, grad_w2, grad_mix, grad_gain = field_stage(recv_0, 0, forward[0], base, True)
    return (
        received[None],
        grad_w2[None],
        grad_mix[None],
        jnp.swapaxes(grad_gain, 0, 1)[None],
    )


def solution(mesh):
    in_specs = (
        P("section", "lat", None, None),
        P("section", "lat", None, None),
        P("section", None, None),
        P("section", None, None, None),
        P("section", None, None),
    )
    out_specs = (
        P("section", "lat", None, None),
        P("section", None, None),
        P("section", None, None, None),
        P("section", None, None),
    )
    return jax.shard_map(shards, mesh=mesh, in_specs=in_specs, out_specs=out_specs, check_vma=False)
```

```python
import functools
import math

import jax
import jax.numpy as jnp
import ml_dtypes
import numpy as np
from jax import lax
from jax.experimental import pallas as pl
from jax.experimental.pallas import tpu as pltpu
from jax.sharding import PartitionSpec as P

NLAT = 384
NLON = 768
MODES = 384
C = 192
DEVICES = 32
LAT_LOCAL = 12
ORDERS = 12
GROUPS = 3
GROUP_ORDERS = 4
HALF = 64
LANES = 128
TILE = 16
TILES = 9
GROUP_TILES = 3
SPAN = DEVICES * TILE
LAT_BLOCKS = 4
BLOCK_LATS = NLAT // LAT_BLOCKS
MIB = 1024 * 1024
F32 = jnp.float32
BF16 = jnp.bfloat16
NT = (((1,), (1,)), ((), ()))

PAIRS = ((0, 0), (1, 0), (1, 1), (2, 1), (2, 2), (3, 2))


def degrees_of(group):
    return MODES - LANES * group


def half_lanes(shape):
    return lax.broadcasted_iota(jnp.int32, shape, 1) < HALF


def packed_rows(group):
    rows, first = [], 0
    for local in range(GROUP_ORDERS):
        rows.append(slice(first, first + degrees_of(group) - DEVICES * local))
        first = rows[-1].stop
    return rows


PACKED = [packed_rows(group)[-1].stop for group in range(GROUPS)]
BASES = [sum(PACKED[:group]) for group in range(GROUPS)]


def dot(left, right):
    return jnp.dot(left, right, preferred_element_type=F32)


def dot_nt(left, right):
    return lax.dot_general(left, right, NT, preferred_element_type=F32)


def whole(shape):
    return pl.BlockSpec(shape, lambda *_: (0,) * len(shape), pipeline_mode=pl.Buffered(1))


HELD = pl.BlockSpec(memory_space=pltpu.HBM)


def call(
    kernel, inputs, in_specs, out_specs, out_shape, grid, after=(), aliases=None, vmem=56, **extra
):
    count = len(inputs)

    def body(*refs):
        kernel(*refs[:count], *refs[count + len(after) :])

    return pl.pallas_call(
        body,
        grid=grid,
        in_specs=list(in_specs) + [pl.BlockSpec(memory_space=pl.ANY)] * len(after),
        out_specs=out_specs,
        out_shape=out_shape,
        input_output_aliases=aliases or {},
        compiler_params=pltpu.CompilerParams(vmem_limit_bytes=vmem * MIB),
        cost_estimate=pl.CostEstimate(flops=1, bytes_accessed=1, transcendentals=0),
        **extra,
    )(*inputs, *after)


def order_rows(first, count):
    device = np.arange(DEVICES)[:, None]
    local = np.arange(GROUP_ORDERS * count)[None, :] + GROUP_ORDERS * first
    return (DEVICES * local + device).reshape(-1)


def fourier_rows(orders):
    phase = (orders[:, None] * np.arange(NLON)[None, :]) % NLON
    angle = phase * (2.0 * math.pi / NLON)
    return np.cos(angle), -np.sin(angle)


def forward_rows(first, count):
    cosine, sine = fourier_rows(order_rows(first, count))
    table = np.concatenate([cosine, sine], axis=0)
    return jnp.asarray(table.astype(np.float32).astype(ml_dtypes.bfloat16))


def inverse_rows():
    device = np.arange(DEVICES)[:, None]
    orders = (DEVICES * np.arange(ORDERS)[None, :] + device).reshape(-1)
    factor = np.where(orders == 0, 1.0, 2.0)[:, None] / NLON
    cosine, sine = fourier_rows(orders)
    table = np.concatenate([factor * cosine, factor * sine], axis=0)
    return table.astype(np.float32).astype(ml_dtypes.bfloat16)


def spread_tables():
    rows = np.arange(LANES)
    source, inner = rows // TILE, rows % TILE
    tables = np.zeros((len(PAIRS), LANES, LANES), np.float32)
    for index, (order, tile) in enumerate(PAIRS):
        lat = TILE * tile + inner - LAT_LOCAL * order
        valid = (lat >= 0) & (lat < LAT_LOCAL)
        tables[index, (source * LAT_LOCAL + lat)[valid], rows[valid]] = 1.0
    flat = jnp.asarray(tables.astype(ml_dtypes.bfloat16))
    turned = jnp.asarray(np.swapaxes(tables, 1, 2).astype(ml_dtypes.bfloat16))
    return flat, turned


def log_starts():
    table = np.zeros((DEVICES, TILE, LANES), np.float32)
    numbers = np.zeros((DEVICES, TILE, LANES), np.float32)
    for device in range(DEVICES):
        for local in range(ORDERS):
            order = DEVICES * local + device
            numbers[device, local] = order
            table[device, local] = 0.5 * math.log((2.0 * order + 1.0) / 2.0) + 0.5 * (
                math.lgamma(order + 0.5) - math.lgamma(0.5) - math.lgamma(order + 1.0)
            )
    return table, numbers


def latitude_rows():
    colatitude = (np.arange(NLAT) + 0.5) * (math.pi / NLAT)
    harmonic = np.arange(1, NLAT // 2 + 1)
    terms = np.cos(2.0 * harmonic[None, :] * colatitude[:, None]) / (4.0 * harmonic**2 - 1.0)
    weight = 2.0 / NLAT * (1.0 - 2.0 * np.sum(terms, axis=1))
    rows = np.stack([np.cos(colatitude), np.log(np.sin(colatitude)), weight])
    rows = np.concatenate([rows, np.zeros((5, NLAT))]).reshape(8, LAT_BLOCKS, BLOCK_LATS)
    rows = np.pad(rows, ((0, 0), (0, 0), (0, LANES - BLOCK_LATS)))
    return rows.reshape(8, SPAN).astype(np.float32)


def legendre_rows(start_ref, order_ref, lat_ref, rows_ref):
    order = jnp.concatenate([order_ref[...]] * LAT_BLOCKS, axis=1)
    cosine = jnp.broadcast_to(lat_ref[0:1, :], (TILE, SPAN))
    log_sin = jnp.broadcast_to(lat_ref[1:2, :], (TILE, SPAN))
    log_start = jnp.concatenate([start_ref[...]] * LAT_BLOCKS, axis=1) + order * log_sin
    narrow = order_ref[...]
    narrow_square = narrow * narrow
    second_factor = jnp.concatenate([jnp.sqrt(2.0 * narrow + 3.0)] * LAT_BLOCKS, axis=1)
    zeros = jnp.zeros((TILE, SPAN), F32)

    def block(index, state):
        previous, current, log_scale = state
        scale = jnp.exp(log_scale)
        for inner in range(16):
            row = index * 16 + inner
            degree = row.astype(F32)
            lower = degree - 1.0
            up = jnp.sqrt(
                jnp.maximum(4.0 * degree * degree - 1.0, 1.0)
                / jnp.maximum(degree * degree - narrow_square, 1.0)
            )
            down = jnp.sqrt(
                jnp.maximum(lower * lower - narrow_square, 0.0)
                / jnp.maximum(4.0 * lower * lower - 1.0, 1.0)
            )
            up = jnp.concatenate([up] * LAT_BLOCKS, axis=1)
            down = jnp.concatenate([down] * LAT_BLOCKS, axis=1)
            general = up * (cosine * current - down * previous)
            second = second_factor * cosine * current
            new_row = jnp.where(
                degree == order,
                1.0,
                jnp.where(
                    degree == order + 1.0, second, jnp.where(degree > order + 1.0, general, 0.0)
                ),
            )
            scaled = new_row * scale
            for part in range(LAT_BLOCKS):
                rows_ref[part, row] = scaled[:, part * LANES : (part + 1) * LANES]
            previous, current = current, new_row
        largest = jnp.maximum(jnp.abs(previous), jnp.abs(current))
        largest = jnp.where(largest > 0.0, largest, 1.0)
        return previous / largest, current / largest, log_scale + jnp.log(largest)

    lax.fori_loop(0, MODES // 16, block, (zeros, zeros, log_start))


def table_kernel(start_ref, order_ref, lat_ref, flat_ref, turned_ref, *rest):
    outs, rows_ref, buffers, sems = rest[:12], rest[12], rest[13:25], rest[25]
    legendre_rows(start_ref, order_ref, lat_ref, rows_ref)
    copies = []
    for group in range(GROUPS):
        ahead_flat, ahead_turned, behind_flat, behind_turned = buffers[4 * group : 4 * group + 4]

        def part_step(part, carry):
            lats = pl.ds(pl.multiple_of(part * LANES, LANES), LANES)
            weight = lat_ref[2:3, lats]
            for local in range(GROUP_ORDERS):
                legendre = rows_ref[part, LANES * group :, GROUP_ORDERS * group + local, :]
                synthesis = legendre.astype(BF16)
                analysis = (weight * legendre).astype(BF16)
                pairs = [index for index, (order, _) in enumerate(PAIRS) if order == local]
                flat = jnp.concatenate([flat_ref[index] for index in pairs], axis=1)
                turned = jnp.concatenate([turned_ref[index] for index in pairs], axis=0)
                products = (
                    dot(analysis, flat).astype(BF16),
                    dot_nt(turned, synthesis).astype(BF16),
                    dot(synthesis, flat).astype(BF16),
                    dot_nt(turned, analysis).astype(BF16),
                )
                for place, index in enumerate(pairs):
                    cut = slice(place * LANES, (place + 1) * LANES)
                    ahead_flat[index, :, lats] = products[0][:, cut]
                    ahead_turned[index, lats, :] = products[1][cut]
                    behind_flat[index, :, lats] = products[2][:, cut]
                    behind_turned[index, lats, :] = products[3][cut]
            return carry

        lax.fori_loop(0, LAT_BLOCKS, part_step, 0)
        for place in range(4):
            at = 4 * group + place
            copy = pltpu.make_async_copy(buffers[at], outs[at], sems.at[at])
            copy.start()
            copies.append(copy)
    for copy in copies:
        copy.wait()


def legendre_tables(start, order, lat, flat, turned, after):
    shapes = []
    for group in range(GROUPS):
        degrees = degrees_of(group)
        shapes += [(len(PAIRS), degrees, SPAN), (len(PAIRS), SPAN, degrees)] * 2
    inputs = (start, order, lat, flat, turned)
    return call(
        table_kernel,
        inputs,
        [whole(value.shape) for value in inputs],
        [HELD] * len(shapes),
        [jax.ShapeDtypeStruct(shape, BF16) for shape in shapes],
        (1,),
        after,
        scratch_shapes=[pltpu.VMEM((LAT_BLOCKS, MODES, TILE, LANES), F32)]
        + [pltpu.VMEM(shape, BF16) for shape in shapes]
        + [pltpu.SemaphoreType.DMA((len(shapes),))],
        name="legendre_tables",
    )


def blocks_of(value):
    return [value[:, index * HALF : (index + 1) * HALF] for index in range(GROUPS)]


def interleave(first, second):
    pairs = zip(blocks_of(first), blocks_of(second))
    return jnp.concatenate([block for pair in pairs for block in pair], axis=1)


def prepare_kernel(gain_ref, mix_ref, proj_ref, gain_out, mix_out, proj_out):
    gain = gain_ref[...].T
    gain_out[...] = interleave(gain, gain)
    real, imag = mix_ref[0].astype(F32), mix_ref[1].astype(F32)
    upper, lower = interleave(real, imag), interleave(-imag, real)
    for index in range(GROUPS):
        rows = slice(index * HALF, (index + 1) * HALF)
        start = index * LANES
        mix_out[start : start + HALF, :] = upper[rows].astype(BF16)
        mix_out[start + HALF : start + LANES, :] = lower[rows].astype(BF16)
    proj = proj_ref[...].astype(F32).T
    proj_out[...] = interleave(proj, proj).astype(BF16)


def prepare(gain, mix, proj, after):
    shapes = ((MODES, 2 * C), (2 * C, 2 * C), (C, 2 * C))
    kinds = (F32, BF16, BF16)
    return call(
        prepare_kernel,
        (gain, mix, proj),
        [whole(gain.shape), whole(mix.shape), whole(proj.shape)],
        [whole(shape) for shape in shapes],
        [jax.ShapeDtypeStruct(shape, kind) for shape, kind in zip(shapes, kinds)],
        (1,),
        after,
        name="prepare",
    )


def spectrum_kernel(field_ref, table_ref, out_ref, scratch):
    step = pl.program_id(0)
    rows = table_ref.shape[0] // 2
    low = half_lanes((rows, LANES))
    fields = field_ref[...].reshape(4 * C, NLON)
    product = dot_nt(table_ref[...], fields)
    for block in range(4 * GROUPS):
        inner, index = block // GROUPS, block % GROUPS
        lanes = slice(block // 2 * LANES, (block // 2 + 1) * LANES)
        real, imag = product[:rows, lanes], product[rows:, lanes]
        if block % 2:
            tile = jnp.where(low, pltpu.roll(real, HALF, 1), imag)
        else:
            tile = jnp.where(low, real, pltpu.roll(imag, HALF, 1))
        scratch[index, pl.ds(step * 4 + inner, rows, stride=LAT_LOCAL), :] = tile

    @pl.when(step == LAT_LOCAL // 4 - 1)
    def _():
        for index in range(GROUPS):
            out_ref[:, index * LANES : (index + 1) * LANES] = scratch[index].astype(BF16)


def spectrum_rows(field, table, after=()):
    rows = table.shape[0] // 2 * LAT_LOCAL
    return call(
        spectrum_kernel,
        (field, table),
        [pl.BlockSpec((4, C, NLON), lambda b: (b, 0, 0)), whole(table.shape)],
        whole((rows, 2 * C)),
        jax.ShapeDtypeStruct((rows, 2 * C), BF16),
        (LAT_LOCAL // 4,),
        after,
        scratch_shapes=[pltpu.VMEM((GROUPS, rows, LANES), F32)],
        name="spectrum_rows",
    )


def order_sums(group, table_ref, tiles):
    totals = [None] * GROUP_ORDERS
    for tile in range(GROUP_TILES):
        left = [table_ref[2 * tile + place, DEVICES * (tile + place) :, :] for place in range(2)]
        product = dot(jnp.concatenate(left, axis=0), tiles[tile])
        middle = left[0].shape[0]
        for order, part in ((tile, product[:middle]), (tile + 1, product[middle:])):
            totals[order] = part if totals[order] is None else totals[order] + part
    return totals


def tile_sum(tile, table_ref, first, second):
    left = jnp.concatenate([table_ref[2 * tile], table_ref[2 * tile + 1]], axis=1)
    return dot(left, jnp.concatenate([first, second], axis=0))


def spectral_kernel(recv_ref, *refs):
    a_refs, st_refs = refs[0:3], refs[3:6]
    gain_ref, mix_ref = refs[6:8]
    scaled_ref, payload_ref, recv, payload = refs[8:12]
    a_buffers, st_buffers, scaled_buffers = refs[12:15], refs[15:18], refs[18:21]
    in_sems, out_sems = refs[21:23]
    schedule = (2, 1, 0)
    arrivals, departures = {}, []
    for group in schedule:
        tiles = pl.ds(GROUP_TILES * group, GROUP_TILES)
        arrivals[group] = [
            pltpu.make_async_copy(recv_ref.at[:, tiles], recv.at[group], in_sems.at[group, 0]),
            pltpu.make_async_copy(a_refs[group], a_buffers[group], in_sems.at[group, 1]),
            pltpu.make_async_copy(st_refs[group], st_buffers[group], in_sems.at[group, 2]),
        ]
        for copy in arrivals[group]:
            copy.start()
    for group in schedule:
        for copy in arrivals[group][:2]:
            copy.wait()
        tiles = [recv[group, :, tile].reshape(SPAN, 2 * C) for tile in range(GROUP_TILES)]
        held = scaled_buffers[group]
        for local, coef in enumerate(order_sums(group, a_buffers[group], tiles)):
            skipped = DEVICES * local
            held[packed_rows(group)[local], :] = (
                gain_ref[LANES * group + skipped :, :] * coef
            ).astype(BF16)
        product = dot(held[...], mix_ref[...]).astype(BF16)
        mixed = []
        for local, rows in enumerate(packed_rows(group)):
            zeros = jnp.zeros((DEVICES * local, 2 * C), BF16)
            mixed.append(
                jnp.concatenate([zeros, product[rows]], axis=0) if local else product[rows]
            )
        arrivals[group][2].wait()
        for tile in range(GROUP_TILES):
            grid = tile_sum(tile, st_buffers[group], mixed[tile], mixed[tile + 1])
            payload[group, :, tile] = grid.astype(BF16).reshape(DEVICES, TILE, 2 * C)
        tiles = pl.ds(GROUP_TILES * group, GROUP_TILES)
        copies = (
            pltpu.make_async_copy(
                payload.at[group], payload_ref.at[:, tiles], out_sems.at[group, 0]
            ),
            pltpu.make_async_copy(
                scaled_buffers[group],
                scaled_ref.at[pl.ds(BASES[group], PACKED[group])],
                out_sems.at[group, 1],
            ),
        )
        for copy in copies:
            copy.start()
            departures.append(copy)
    for copy in departures:
        copy.wait()


def spectral_forward(recv, a, st, gain, mix, after=()):
    slots = (GROUPS, DEVICES, GROUP_TILES, TILE, 2 * C)
    return call(
        spectral_kernel,
        (recv, *a, *st, gain, mix),
        [HELD] * 7 + [whole(gain.shape), whole(mix.shape)],
        [HELD] * 2,
        [
            jax.ShapeDtypeStruct((sum(PACKED), 2 * C), BF16),
            jax.ShapeDtypeStruct(recv.shape, BF16),
        ],
        (1,),
        after,
        scratch_shapes=[pltpu.VMEM(slots, BF16), pltpu.VMEM(slots, BF16)]
        + [pltpu.VMEM(value.shape, BF16) for value in a]
        + [pltpu.VMEM(value.shape, BF16) for value in st]
        + [pltpu.VMEM((rows, 2 * C), BF16) for rows in PACKED]
        + [pltpu.SemaphoreType.DMA((GROUPS, 3)), pltpu.SemaphoreType.DMA((GROUPS, 2))],
        name="spectral_forward",
    )


def normal_cumulative(value, bell):
    denominator = 1.0 + (0.3275911 / math.sqrt(2.0)) * jnp.abs(value)
    inverse = pl.reciprocal(denominator, approx=True)
    inverse = inverse * (2.0 - denominator * inverse)
    series = 0.5 * 1.061405429 * inverse - 0.5 * 1.453152027
    series = series * inverse + 0.5 * 1.421413741
    series = series * inverse - 0.5 * 0.284496736
    series = series * inverse + 0.5 * 0.254829592
    tail = series * inverse * bell
    return jnp.where(value < 0.0, tail, 1.0 - tail)


def grid_kernel(
    recv_ref, up_ref, turned_ref, proj_ref, held_ref, turned_table_ref,
    out_ref, grad_ref, scratch, out_scratch, act_scratch, pre_scratch, table_ref, sem,
):
    step = pl.program_id(1)
    opening = jnp.logical_and(pl.program_id(0) == 0, step == 0)

    @pl.when(opening)
    def _():
        pltpu.make_async_copy(held_ref, table_ref, sem).start()

    low = half_lanes((MODES, LANES))
    block = 256

    @pl.when(step == 0)
    def _():
        scratch[...] = recv_ref[...].astype(F32)
        grad_ref[...] = jnp.zeros_like(grad_ref)

    columns = []
    for pair in range(2):
        first = scratch[pl.ds(step * 4 + 2 * pair, MODES, stride=LAT_LOCAL), :]
        second = scratch[pl.ds(step * 4 + 2 * pair + 1, MODES, stride=LAT_LOCAL), :]
        real = jnp.where(low, first, pltpu.roll(second, HALF, 1))
        imag = jnp.where(low, pltpu.roll(first, HALF, 1), second)
        columns.append(jnp.concatenate([real, imag], axis=0).astype(BF16))
    modes = jnp.concatenate(columns, axis=1)
    low_block = half_lanes((block, LANES))
    for part in range(NLON // block):
        rows = slice(part * block, (part + 1) * block)
        pre = dot(turned_table_ref[rows, :], modes)
        grad_act = jnp.concatenate(
            [
                jnp.where(
                    low_block,
                    dot(turned_ref[2 * pair, rows, :], proj_ref[...]),
                    dot(turned_ref[2 * pair + 1, rows, :], proj_ref[...]),
                )
                for pair in range(2)
            ],
            axis=1,
        )
        bell = jnp.exp(-0.5 * pre * pre)
        cumulative = normal_cumulative(pre, bell)
        slope = cumulative + pre * bell * (1.0 / math.sqrt(2.0 * math.pi))
        act_scratch[rows, :] = (pre * cumulative).astype(BF16)
        pre_scratch[rows, :] = (grad_act * slope).astype(BF16)
    low_grad = half_lanes((C, LANES))
    for pair in range(2):
        act = act_scratch[:, pair * LANES : (pair + 1) * LANES]
        ups = up_ref[2 * pair : 2 * pair + 2].reshape(2 * C, NLON)
        grads = dot(ups, act)
        grad_ref[...] += jnp.where(low_grad, grads[:C], grads[C:])

    @pl.when(opening)
    def _():
        pltpu.make_async_copy(held_ref, table_ref, sem).wait()

    grad_modes = dot(table_ref[...], pre_scratch[...])
    for pair in range(2):
        lanes = slice(pair * LANES, (pair + 1) * LANES)
        real, imag = grad_modes[:MODES, lanes], grad_modes[MODES:, lanes]
        out_scratch[pl.ds(step * 4 + 2 * pair, MODES, stride=LAT_LOCAL), :] = jnp.where(
            low, real, pltpu.roll(imag, HALF, 1)
        )
        out_scratch[pl.ds(step * 4 + 2 * pair + 1, MODES, stride=LAT_LOCAL), :] = jnp.where(
            low, pltpu.roll(real, HALF, 1), imag
        )

    @pl.when(step == LAT_LOCAL // 4 - 1)
    def _():
        out_ref[...] = out_scratch[...].astype(BF16)


def grid_stage(first, blocks, recv, up, turned, proj, table, turned_table, after=()):
    rows = MODES * LAT_LOCAL
    lanes_spec = pl.BlockSpec((rows, LANES), lambda q, b: (0, q))
    grad_spec = pl.BlockSpec((C, LANES), lambda q, b: (0, q))
    return call(
        grid_kernel,
        (recv, up, turned, proj, table, turned_table),
        [
            pl.BlockSpec((rows, LANES), lambda q, b: (0, q + first)),
            pl.BlockSpec((4, C, NLON), lambda q, b: (b, 0, 0)),
            pl.BlockSpec((4, NLON, C), lambda q, b: (b, 0, 0)),
            pl.BlockSpec((C, LANES), lambda q, b: (0, q + first)),
            HELD,
            whole(turned_table.shape),
        ],
        [lanes_spec, grad_spec],
        [
            jax.ShapeDtypeStruct((rows, LANES * blocks), BF16),
            jax.ShapeDtypeStruct((C, LANES * blocks), F32),
        ],
        (blocks, LAT_LOCAL // 4),
        after,
        scratch_shapes=[
            pltpu.VMEM((rows, LANES), F32),
            pltpu.VMEM((rows, LANES), F32),
            pltpu.VMEM((NLON, 2 * LANES), BF16),
            pltpu.VMEM((NLON, 2 * LANES), BF16),
            pltpu.VMEM(table.shape, BF16),
            pltpu.SemaphoreType.DMA,
        ],
        name=f"grid_stage_{blocks}",
    )


def backward_kernel(groups, *refs):
    recv_ref, table_refs, out_ref = refs[0], refs[1 : 1 + len(groups)], refs[1 + len(groups)]
    buffers, sems = refs[-1 - len(groups) : -1], refs[-1]
    copies = [
        pltpu.make_async_copy(table_refs[place], buffers[place], sems.at[place])
        for place in range(len(groups))
    ]
    for copy in copies:
        copy.start()
    lanes = recv_ref.shape[-1]
    first = 0
    for place, group in enumerate(groups):
        start = GROUP_TILES * group if recv_ref.shape[1] == TILES else 0
        tiles = [
            recv_ref[:, start + tile].reshape(SPAN, lanes) for tile in range(GROUP_TILES)
        ]
        copies[place].wait()
        sums = order_sums(group, buffers[place], tiles)
        for total, rows in zip(sums, packed_rows(group)):
            out_ref[first + rows.start : first + rows.stop, :] = total.astype(BF16)
        first += PACKED[group]


def spectral_backward(groups, recv, tables, after=(), last=False):
    lanes = recv.shape[-1]
    tiles = GROUP_TILES if len(groups) == 1 else TILES
    block = groups[0] if len(groups) == 1 else 0
    out = (sum(PACKED[group] for group in groups), lanes)
    return call(
        functools.partial(backward_kernel, groups),
        (recv, *tables),
        [
            pl.BlockSpec(
                (DEVICES, tiles, TILE, lanes),
                lambda b: (0, block, 0, 0),
                pipeline_mode=pl.Buffered(1),
            )
        ]
        + [HELD] * len(groups),
        [whole(out)] + [HELD] * len(groups) * last,
        [jax.ShapeDtypeStruct(out, BF16)]
        + [pltpu.HBM(table.shape, BF16) for table in tables] * last,
        (1,),
        after,
        aliases={1 + place: 1 + place for place in range(len(groups))} if last else {},
        scratch_shapes=[pltpu.VMEM(table.shape, BF16) for table in tables]
        + [pltpu.SemaphoreType.DMA((len(groups),))],
        vmem=20,
        name="spectral_backward_" + "_".join(str(group) for group in groups),
    )[0]


def hold_kernel(value_ref, out_ref):
    pass


def hold(value, after):
    held = pl.BlockSpec(memory_space=pl.ANY)
    return call(
        hold_kernel,
        (value,),
        [held],
        held,
        jax.ShapeDtypeStruct(value.shape, value.dtype),
        (1,),
        after,
        aliases={0: 0},
        vmem=1,
        name="hold",
    )


def synthesis_kernel(groups, small_ref, large_ref, gain_ref, mix_ref, *refs):
    count = len(groups)
    table_refs, refs = refs[:count], refs[-3 * count - 2 :]
    out_ref, coeff_refs, at_refs = refs[0], refs[1 : 1 + count], refs[1 + count : 1 + 2 * count]
    part_refs, sems = refs[1 + 2 * count : -1], refs[-1]
    copies = []
    for place, group in enumerate(groups):
        rows = pl.ds(BASES[group], PACKED[group])
        copies.append(
            (
                pltpu.make_async_copy(small_ref.at[rows], part_refs[place], sems.at[0, place]),
                pltpu.make_async_copy(table_refs[place], at_refs[place], sems.at[1, place]),
            )
        )
    for pair in copies:
        for copy in pair:
            copy.start()
    start = 0
    for place, group in enumerate(groups):
        coeff_ref, at_ref = coeff_refs[place], at_refs[place]
        degrees = degrees_of(group)
        copies[place][0].wait()
        large = large_ref[start : start + PACKED[group], :]
        start += PACKED[group]
        mixed = jnp.concatenate([part_refs[place][...], large], axis=1)
        product = dot_nt(mixed, mix_ref[...])
        for local, rows in enumerate(packed_rows(group)):
            first = local * degrees
            skipped = DEVICES * local
            if skipped:
                coeff_ref[first : first + skipped, :] = jnp.zeros((skipped, 2 * C), BF16)
            coeff_ref[first + skipped : first + degrees, :] = (
                gain_ref[LANES * group + skipped :, :] * product[rows]
            ).astype(BF16)
        copies[place][1].wait()
        for tile in range(GROUP_TILES):
            first = coeff_ref[tile * degrees : (tile + 1) * degrees, :]
            second = coeff_ref[(tile + 1) * degrees : (tile + 2) * degrees, :]
            out = tile_sum(tile, at_ref, first, second).astype(BF16)
            out_ref[:, GROUP_TILES * place + tile] = out.reshape(DEVICES, TILE, 2 * C)


def analysis_back(groups, tables, small, large, gain, mix, tiles, payload=(), after=()):
    inputs = (small, large, gain, mix, *tables, *payload)
    count = len(groups)
    return call(
        functools.partial(synthesis_kernel, groups),
        inputs,
        [HELD] + [whole(value.shape) for value in inputs[1:4]] + [HELD] * len(inputs[4:]),
        whole((DEVICES, GROUP_TILES * count, TILE, 2 * C)),
        pltpu.HBM((DEVICES, tiles, TILE, 2 * C), BF16),
        (1,),
        after,
        aliases={4 + count: 0} if payload else {},
        scratch_shapes=[
            pltpu.VMEM((GROUP_ORDERS * degrees_of(group), 2 * C), BF16) for group in groups
        ]
        + [pltpu.VMEM(table.shape, BF16) for table in tables]
        + [pltpu.VMEM((PACKED[group], LANES), BF16) for group in groups]
        + [pltpu.SemaphoreType.DMA((2, count))],
        vmem=24,
        name="analysis_back_" + "_".join(str(group) for group in groups),
    )


def fold(tile):
    return tile + pltpu.roll(tile, HALF, 1)


def weight_kernel(held_ref, small_ref, *refs):
    first_ref, rest_ref, mix_ref, factor_ref, proj_small, proj_large = refs[:6]
    out_ref, gain, packed, spaced, scaled_ref, sem = refs[6:]
    large = (first_ref[...], rest_ref[: PACKED[1], :], rest_ref[PACKED[1] :, :])
    copy = pltpu.make_async_copy(held_ref, scaled_ref, sem)
    copy.start()
    copy.wait()
    block = None
    for group in range(GROUPS):
        rows = slice(BASES[group], BASES[group] + PACKED[group])
        mixed = jnp.concatenate([small_ref[rows, :], large[group]], axis=1)
        part = lax.dot_general(
            scaled_ref[rows, :], mixed, (((0,), (0,)), ((), ())), preferred_element_type=F32
        )
        block = part if block is None else block + part
        product = dot_nt(mixed, mix_ref[...]) * scaled_ref[rows, :].astype(F32)
        for local, rows in enumerate(packed_rows(group)):
            part = product[rows]
            first = LANES * group + DEVICES * local
            if first:
                gain[first:, :] += part
            else:
                gain[...] = part
    gain[...] = gain[...] / factor_ref[...]
    low = half_lanes((HALF, LANES))
    low_gain = half_lanes((C, LANES))
    low_proj = half_lanes((C // 2, LANES))
    for index in range(GROUPS):
        lanes = slice(index * LANES, (index + 1) * LANES)
        for row_block in range(GROUPS):
            start = row_block * LANES
            first = block[start : start + HALF, lanes]
            second = pltpu.roll(block[start + HALF : start + LANES, lanes], HALF, 1)
            packed[index, row_block * HALF : (row_block + 1) * HALF, :] = jnp.where(
                low, first + second, first - second
            )
        packed[index, C : 2 * C, :] = jnp.where(
            low_gain, fold(gain[:C, lanes]), fold(gain[C:, lanes])
        )
        if index == 0:
            proj = fold(proj_small[...])
        else:
            proj = fold(proj_large[:, (index - 1) * LANES : index * LANES])
        packed[index, 2 * C :, :] = jnp.where(low_proj, proj[: C // 2], proj[C // 2 :])
        for row in range(TILE - 1):
            spaced[index, pl.ds(row, DEVICES, stride=TILE), :] = packed[
                index, row * DEVICES : (row + 1) * DEVICES, :
            ]
        spaced[index, pl.ds(TILE - 1, DEVICES, stride=TILE), :] = jnp.zeros((DEVICES, LANES), F32)
        out_ref[:, 0, :, lanes] = spaced[index].astype(BF16).reshape(DEVICES, TILE, LANES)


def weight_grads(scaled, small, large, mix, gain, proj_small, proj_large, after=()):
    tiles = 2 * GROUP_TILES
    inputs = (scaled, small, *large, mix, gain, proj_small, proj_large)
    return call(
        weight_kernel,
        inputs,
        [HELD] + [whole(value.shape) for value in inputs[1:]],
        pl.BlockSpec((DEVICES, 1, TILE, 2 * C), lambda b: (0, tiles, 0, 0)),
        pltpu.HBM((DEVICES, tiles + 1, TILE, 2 * C), BF16),
        (1,),
        after,
        scratch_shapes=[
            pltpu.VMEM((MODES, 2 * C), F32),
            pltpu.VMEM((GROUPS, 15 * DEVICES, LANES), F32),
            pltpu.VMEM((GROUPS, TILE * DEVICES, LANES), F32),
            pltpu.VMEM(scaled.shape, BF16),
            pltpu.SemaphoreType.DMA,
        ],
        vmem=24,
        name="weight_grads",
    )


def total_kernel(recv_ref, payload_ref, out_ref, token_ref):
    token_ref[...] = jnp.zeros((8, LANES), F32)
    total = jnp.sum(recv_ref[:, 0].astype(F32), axis=0)
    out_ref[:, 0] = jnp.broadcast_to(total.astype(BF16)[None], (DEVICES, TILE, 2 * C))


def attach_totals(recv, payload):
    def last(value):
        tile = value.shape[1] - 1
        return pl.BlockSpec((DEVICES, 1, TILE, 2 * C), lambda b: (0, tile, 0, 0))

    return call(
        total_kernel,
        (recv, payload),
        [last(recv), pl.BlockSpec(memory_space=pl.ANY)],
        [last(payload), whole((8, LANES))],
        [pltpu.HBM(payload.shape, BF16), jax.ShapeDtypeStruct((8, LANES), F32)],
        (1,),
        aliases={1: 0},
        vmem=8,
        name="attach_totals",
    )


def unpack_totals(recv_ref, proj_ref, mix_ref, gain_ref, spaced, packed):
    grid_scale = 1.0 / math.sqrt(NLAT * NLON)
    mode_scale = 1.0 / math.sqrt(MODES)
    lows, highs = [], []
    for index in range(GROUPS):
        lanes = slice(index * LANES, (index + 1) * LANES)
        spaced[index] = recv_ref[:, GROUP_TILES, :, lanes].reshape(DEVICES * TILE, LANES).astype(F32)
        for row in range(TILE - 1):
            packed[index, row * DEVICES : (row + 1) * DEVICES, :] = spaced[
                index, pl.ds(row, DEVICES, stride=TILE), :
            ]
        lows.append(packed[index, :, :HALF])
        highs.append(packed[index, :, HALF:])
    low = jnp.concatenate(lows, axis=1)
    high = jnp.concatenate(highs, axis=1)
    mix_ref[0] = grid_scale * low[:C]
    mix_ref[1] = grid_scale * high[:C]
    gain = jnp.concatenate([low[C : 2 * C], high[C : 2 * C]], axis=0)
    gain_ref[...] = mode_scale * gain.T
    proj = jnp.concatenate([low[2 * C :], high[2 * C :]], axis=0)
    proj_ref[...] = grid_scale * proj.T


def field_kernel(recv_ref, table_ref, base_ref, out_ref, *refs):
    totals, (scratch, *unpacking) = refs[:3] if len(refs) > 1 else (), refs[3:] or refs
    step = pl.program_id(0)
    orders = DEVICES * GROUP_ORDERS
    rows = orders * LAT_LOCAL

    @pl.when(step == 0)
    def _():
        for index in range(GROUPS):
            lanes = slice(index * LANES, (index + 1) * LANES)
            values = recv_ref[:, :GROUP_TILES, :, lanes].astype(F32)
            scratch[index] = values.reshape(rows, LANES)
        if totals:
            unpack_totals(recv_ref, *totals, *unpacking)

    lefts = []
    for inner in range(4):
        real, imag = [], []
        for index in range(GROUPS):
            values = scratch[index, pl.ds(step * 4 + inner, orders, stride=LAT_LOCAL), :]
            turned = values.T.astype(BF16)
            real.append(turned[:HALF])
            imag.append(turned[HALF:])
        lefts.append(
            jnp.concatenate(
                [jnp.concatenate(real, axis=0), jnp.concatenate(imag, axis=0)], axis=1
            )
        )
    product = dot(jnp.concatenate(lefts, axis=0), table_ref[...])
    for inner in range(4):
        total = base_ref[inner].astype(F32) + product[inner * C : (inner + 1) * C]
        out_ref[inner] = total.astype(out_ref.dtype)


def field_stage(recv, at, table, base, unpacked=False, after=()):
    rows = DEVICES * GROUP_ORDERS * LAT_LOCAL
    block = pl.BlockSpec((4, C, NLON), lambda b: (b, 0, 0))
    tiles = GROUP_TILES + int(unpacked)
    totals = ((C, C), (2, C, C), (C, MODES)) if unpacked else ()
    scratch_shapes = [pltpu.VMEM((GROUPS, rows, LANES), F32)]
    if unpacked:
        scratch_shapes += [
            pltpu.VMEM((GROUPS, TILE * DEVICES, LANES), F32),
            pltpu.VMEM((GROUPS, 15 * DEVICES, LANES), F32),
        ]
    return call(
        field_kernel,
        (recv, table, base),
        [
            pl.BlockSpec(
                (DEVICES, tiles, TILE, 2 * C),
                lambda b: (0, at, 0, 0),
                pipeline_mode=pl.Buffered(1),
            ),
            whole(table.shape),
            block,
        ],
        [block] + [whole(shape) for shape in totals],
        [pltpu.HBM((LAT_LOCAL, C, NLON), BF16)]
        + [jax.ShapeDtypeStruct(shape, F32) for shape in totals],
        (LAT_LOCAL // 4,),
        after,
        scratch_shapes=scratch_shapes,
        vmem=56 if unpacked else 20,
        name="field_stage",
    )


def exchange(payload):
    tiles, lanes = payload.shape[1], payload.shape[3]
    flat = payload.reshape(DEVICES, tiles * TILE, lanes)
    moved = lax.all_to_all(flat, "lat", split_axis=0, concat_axis=0, tiled=True)
    return moved.reshape(DEVICES, tiles, TILE, lanes)


def shards(saved_input, incoming, spectral_gain, mix_weight, proj_weight):
    device = lax.axis_index("lat")
    section_count = lax.axis_size("section")
    shift = [(source, (source - 1) % section_count) for source in range(section_count)]

    forward_all = forward_rows(0, GROUPS)
    forward = [forward_rows(group, 1) for group in range(GROUPS)]
    inverse_np = inverse_rows()
    inverse = jnp.asarray(inverse_np)
    inverse_turned = jnp.asarray(np.ascontiguousarray(inverse_np.T))
    spread, spread_turned = spread_tables()
    lat = jnp.asarray(latitude_rows())
    starts, numbers = log_starts()
    start = lax.dynamic_index_in_dim(jnp.asarray(starts), device, 0, keepdims=False)
    order = lax.dynamic_index_in_dim(jnp.asarray(numbers), device, 0, keepdims=False)

    field = saved_input[0]
    upstream = incoming[0]
    upstream_next = lax.ppermute(upstream, "section", shift)
    turned = jnp.swapaxes(upstream, 1, 2)
    rows = MODES * LAT_LOCAL
    spectrum = spectrum_rows(field, forward_all)
    recv = exchange(spectrum.reshape(DEVICES, TILES, TILE, 2 * C))
    gain, mix, proj = prepare(
        jnp.swapaxes(spectral_gain[0], 0, 1), mix_weight[0], proj_weight[0], (spectrum,)
    )
    gain_next, mix_next, _ = prepare(
        lax.ppermute(jnp.swapaxes(spectral_gain[0], 0, 1), "section", shift),
        lax.ppermute(mix_weight[0], "section", shift),
        proj_weight[0],
        (spectrum,),
    )
    tables = legendre_tables(start, order, lat, spread, spread_turned, (spectrum,))
    behind = [tables[4 * group + 2 : 4 * group + 4] for group in range(GROUPS)]
    scaled, payload = spectral_forward(
        recv, tables[0::4], tables[1::4], gain, mix, (turned, proj)
    )
    recv = exchange(payload).reshape(rows, 2 * C)
    small_rows, proj_small = grid_stage(
        0,
        1,
        recv,
        upstream,
        turned,
        proj,
        inverse,
        inverse_turned,
        (upstream_next, gain_next, mix_next),
    )
    small = exchange(small_rows.reshape(DEVICES, TILES, TILE, LANES))
    large, proj_large = grid_stage(
        1, 2, recv, upstream, turned, proj, inverse, inverse_turned, (small_rows,)
    )
    large = exchange(large.reshape(DEVICES, TILES, TILE, 2 * LANES))

    mixeds, moved = [None] * GROUPS, [None] * GROUPS
    every = tuple(range(GROUPS))
    mixed_small = spectral_backward(every, small, [table[0] for table in behind])
    moved_small = lax.ppermute(mixed_small, "section", shift)
    mixed_rest = spectral_backward((1, 2), large, [behind[1][0], behind[2][0]], (moved_small,), True)
    moved_rest = lax.ppermute(mixed_rest, "section", shift)
    mixed_0 = spectral_backward((0,), large, [behind[0][0]], (mixed_rest,))
    out_rest = weight_grads(
        scaled, mixed_small, (mixed_0, mixed_rest), mix, gain, proj_small, proj_large
    )
    out_rest = analysis_back(
        (1, 2),
        [behind[1][1], behind[2][1]],
        moved_small,
        moved_rest,
        gain_next,
        mix_next,
        2 * GROUP_TILES + 1,
        (out_rest,),
    )
    moved_0 = lax.ppermute(hold(mixed_0, (moved_rest,)), "section", shift)
    recv_rest = exchange(out_rest)
    out_0 = analysis_back(
        (0,), [behind[0][1]], moved_small, moved_0, gain_next, mix_next, GROUP_TILES + 1
    )
    out_0, token = attach_totals(recv_rest, out_0)
    recv_0 = exchange(out_0)
    (base,) = field_stage(recv_rest, 0, forward[1], upstream_next, after=(token,))
    (base,) = field_stage(recv_rest, 1, forward[2], base)
    received, grad_w2, grad_mix, grad_gain = field_stage(recv_0, 0, forward[0], base, True)
    return (
        received[None],
        grad_w2[None],
        grad_mix[None],
        jnp.swapaxes(grad_gain, 0, 1)[None],
    )


def solution(mesh):
    in_specs = (
        P("section", "lat", None, None),
        P("section", "lat", None, None),
        P("section", None, None),
        P("section", None, None, None),
        P("section", None, None),
    )
    out_specs = (
        P("section", "lat", None, None),
        P("section", None, None),
        P("section", None, None, None),
        P("section", None, None),
    )
    return jax.shard_map(shards, mesh=mesh, in_specs=in_specs, out_specs=out_specs, check_vma=False)
```

```python
import functools
import math

import jax
import jax.numpy as jnp
import ml_dtypes
import numpy as np
from jax import lax
from jax.experimental import pallas as pl
from jax.experimental.pallas import tpu as pltpu
from jax.sharding import PartitionSpec as P

NLAT = 384
NLON = 768
MODES = 384
C = 192
DEVICES = 32
LAT_LOCAL = 12
ORDERS = 12
GROUPS = 3
GROUP_ORDERS = 4
HALF = 64
LANES = 128
TILE = 16
TILES = 9
GROUP_TILES = 3
SPAN = DEVICES * TILE
LAT_BLOCKS = 4
BLOCK_LATS = NLAT // LAT_BLOCKS
MIB = 1024 * 1024
F32 = jnp.float32
BF16 = jnp.bfloat16
NT = (((1,), (1,)), ((), ()))

PAIRS = ((0, 0), (1, 0), (1, 1), (2, 1), (2, 2), (3, 2))


def degrees_of(group):
    return MODES - LANES * group


def half_lanes(shape):
    return lax.broadcasted_iota(jnp.int32, shape, 1) < HALF


def packed_rows(group):
    rows, first = [], 0
    for local in range(GROUP_ORDERS):
        rows.append(slice(first, first + degrees_of(group) - DEVICES * local))
        first = rows[-1].stop
    return rows


PACKED = [packed_rows(group)[-1].stop for group in range(GROUPS)]
BASES = [sum(PACKED[:group]) for group in range(GROUPS)]


def dot(left, right):
    return jnp.dot(left, right, preferred_element_type=F32)


def dot_nt(left, right):
    return lax.dot_general(left, right, NT, preferred_element_type=F32)


def whole(shape):
    return pl.BlockSpec(shape, lambda *_: (0,) * len(shape), pipeline_mode=pl.Buffered(1))


HELD = pl.BlockSpec(memory_space=pltpu.HBM)


def call(
    kernel, inputs, in_specs, out_specs, out_shape, grid, after=(), aliases=None, vmem=56, **extra
):
    count = len(inputs)

    def body(*refs):
        kernel(*refs[:count], *refs[count + len(after) :])

    return pl.pallas_call(
        body,
        grid=grid,
        in_specs=list(in_specs) + [pl.BlockSpec(memory_space=pl.ANY)] * len(after),
        out_specs=out_specs,
        out_shape=out_shape,
        input_output_aliases=aliases or {},
        compiler_params=pltpu.CompilerParams(vmem_limit_bytes=vmem * MIB),
        cost_estimate=pl.CostEstimate(flops=1, bytes_accessed=1, transcendentals=0),
        **extra,
    )(*inputs, *after)


def order_rows(first, count):
    device = np.arange(DEVICES)[:, None]
    local = np.arange(GROUP_ORDERS * count)[None, :] + GROUP_ORDERS * first
    return (DEVICES * local + device).reshape(-1)


def fourier_rows(orders):
    phase = (orders[:, None] * np.arange(NLON)[None, :]) % NLON
    angle = phase * (2.0 * math.pi / NLON)
    return np.cos(angle), -np.sin(angle)


def forward_rows(first, count):
    cosine, sine = fourier_rows(order_rows(first, count))
    table = np.concatenate([cosine, sine], axis=0)
    return jnp.asarray(table.astype(np.float32).astype(ml_dtypes.bfloat16))


def inverse_rows():
    device = np.arange(DEVICES)[:, None]
    orders = (DEVICES * np.arange(ORDERS)[None, :] + device).reshape(-1)
    factor = np.where(orders == 0, 1.0, 2.0)[:, None] / NLON
    cosine, sine = fourier_rows(orders)
    table = np.concatenate([factor * cosine, factor * sine], axis=0)
    return table.astype(np.float32).astype(ml_dtypes.bfloat16)


def spread_tables():
    rows = np.arange(LANES)
    source, inner = rows // TILE, rows % TILE
    tables = np.zeros((len(PAIRS), LANES, LANES), np.float32)
    for index, (order, tile) in enumerate(PAIRS):
        lat = TILE * tile + inner - LAT_LOCAL * order
        valid = (lat >= 0) & (lat < LAT_LOCAL)
        tables[index, (source * LAT_LOCAL + lat)[valid], rows[valid]] = 1.0
    flat = jnp.asarray(tables.astype(ml_dtypes.bfloat16))
    turned = jnp.asarray(np.swapaxes(tables, 1, 2).astype(ml_dtypes.bfloat16))
    return flat, turned


def log_starts():
    table = np.zeros((DEVICES, TILE, LANES), np.float32)
    numbers = np.zeros((DEVICES, TILE, LANES), np.float32)
    for device in range(DEVICES):
        for local in range(ORDERS):
            order = DEVICES * local + device
            numbers[device, local] = order
            table[device, local] = 0.5 * math.log((2.0 * order + 1.0) / 2.0) + 0.5 * (
                math.lgamma(order + 0.5) - math.lgamma(0.5) - math.lgamma(order + 1.0)
            )
    return table, numbers


def latitude_rows():
    colatitude = (np.arange(NLAT) + 0.5) * (math.pi / NLAT)
    harmonic = np.arange(1, NLAT // 2 + 1)
    terms = np.cos(2.0 * harmonic[None, :] * colatitude[:, None]) / (4.0 * harmonic**2 - 1.0)
    weight = 2.0 / NLAT * (1.0 - 2.0 * np.sum(terms, axis=1))
    rows = np.stack([np.cos(colatitude), np.log(np.sin(colatitude)), weight])
    rows = np.concatenate([rows, np.zeros((5, NLAT))]).reshape(8, LAT_BLOCKS, BLOCK_LATS)
    rows = np.pad(rows, ((0, 0), (0, 0), (0, LANES - BLOCK_LATS)))
    return rows.reshape(8, SPAN).astype(np.float32)


def legendre_rows(start_ref, order_ref, lat_ref, rows_ref):
    order = jnp.concatenate([order_ref[...]] * LAT_BLOCKS, axis=1)
    cosine = jnp.broadcast_to(lat_ref[0:1, :], (TILE, SPAN))
    log_sin = jnp.broadcast_to(lat_ref[1:2, :], (TILE, SPAN))
    log_start = jnp.concatenate([start_ref[...]] * LAT_BLOCKS, axis=1) + order * log_sin
    narrow = order_ref[...]
    narrow_square = narrow * narrow
    second_factor = jnp.concatenate([jnp.sqrt(2.0 * narrow + 3.0)] * LAT_BLOCKS, axis=1)
    zeros = jnp.zeros((TILE, SPAN), F32)

    def block(index, state):
        previous, current, log_scale = state
        scale = jnp.exp(log_scale)
        for inner in range(16):
            row = index * 16 + inner
            degree = row.astype(F32)
            lower = degree - 1.0
            up = jnp.sqrt(
                jnp.maximum(4.0 * degree * degree - 1.0, 1.0)
                / jnp.maximum(degree * degree - narrow_square, 1.0)
            )
            down = jnp.sqrt(
                jnp.maximum(lower * lower - narrow_square, 0.0)
                / jnp.maximum(4.0 * lower * lower - 1.0, 1.0)
            )
            up = jnp.concatenate([up] * LAT_BLOCKS, axis=1)
            down = jnp.concatenate([down] * LAT_BLOCKS, axis=1)
            general = up * (cosine * current - down * previous)
            second = second_factor * cosine * current
            new_row = jnp.where(
                degree == order,
                1.0,
                jnp.where(
                    degree == order + 1.0, second, jnp.where(degree > order + 1.0, general, 0.0)
                ),
            )
            scaled = new_row * scale
            for part in range(LAT_BLOCKS):
                rows_ref[part, row] = scaled[:, part * LANES : (part + 1) * LANES]
            previous, current = current, new_row
        largest = jnp.maximum(jnp.abs(previous), jnp.abs(current))
        largest = jnp.where(largest > 0.0, largest, 1.0)
        return previous / largest, current / largest, log_scale + jnp.log(largest)

    lax.fori_loop(0, MODES // 16, block, (zeros, zeros, log_start))


def table_kernel(start_ref, order_ref, lat_ref, flat_ref, turned_ref, *rest):
    outs, rows_ref, buffers, sems = rest[:12], rest[12], rest[13:25], rest[25]
    legendre_rows(start_ref, order_ref, lat_ref, rows_ref)
    copies = []
    for group in range(GROUPS):
        ahead_flat, ahead_turned, behind_flat, behind_turned = buffers[4 * group : 4 * group + 4]

        def part_step(part, carry):
            lats = pl.ds(pl.multiple_of(part * LANES, LANES), LANES)
            weight = lat_ref[2:3, lats]
            for local in range(GROUP_ORDERS):
                legendre = rows_ref[part, LANES * group :, GROUP_ORDERS * group + local, :]
                synthesis = legendre.astype(BF16)
                analysis = (weight * legendre).astype(BF16)
                pairs = [index for index, (order, _) in enumerate(PAIRS) if order == local]
                flat = jnp.concatenate([flat_ref[index] for index in pairs], axis=1)
                turned = jnp.concatenate([turned_ref[index] for index in pairs], axis=0)
                products = (
                    dot(analysis, flat).astype(BF16),
                    dot_nt(turned, synthesis).astype(BF16),
                    dot(synthesis, flat).astype(BF16),
                    dot_nt(turned, analysis).astype(BF16),
                )
                for place, index in enumerate(pairs):
                    cut = slice(place * LANES, (place + 1) * LANES)
                    ahead_flat[index, :, lats] = products[0][:, cut]
                    ahead_turned[index, lats, :] = products[1][cut]
                    behind_flat[index, :, lats] = products[2][:, cut]
                    behind_turned[index, lats, :] = products[3][cut]
            return carry

        lax.fori_loop(0, LAT_BLOCKS, part_step, 0)
        for place in range(4):
            at = 4 * group + place
            copy = pltpu.make_async_copy(buffers[at], outs[at], sems.at[at])
            copy.start()
            copies.append(copy)
    for copy in copies:
        copy.wait()


def legendre_tables(start, order, lat, flat, turned, after):
    shapes = []
    for group in range(GROUPS):
        degrees = degrees_of(group)
        shapes += [(len(PAIRS), degrees, SPAN), (len(PAIRS), SPAN, degrees)] * 2
    inputs = (start, order, lat, flat, turned)
    return call(
        table_kernel,
        inputs,
        [whole(value.shape) for value in inputs],
        [HELD] * len(shapes),
        [jax.ShapeDtypeStruct(shape, BF16) for shape in shapes],
        (1,),
        after,
        scratch_shapes=[pltpu.VMEM((LAT_BLOCKS, MODES, TILE, LANES), F32)]
        + [pltpu.VMEM(shape, BF16) for shape in shapes]
        + [pltpu.SemaphoreType.DMA((len(shapes),))],
        name="legendre_tables",
    )


def blocks_of(value):
    return [value[:, index * HALF : (index + 1) * HALF] for index in range(GROUPS)]


def interleave(first, second):
    pairs = zip(blocks_of(first), blocks_of(second))
    return jnp.concatenate([block for pair in pairs for block in pair], axis=1)


def prepare_kernel(gain_ref, mix_ref, proj_ref, gain_out, mix_out, proj_out):
    gain = gain_ref[...].T
    gain_out[...] = interleave(gain, gain)
    real, imag = mix_ref[0].astype(F32), mix_ref[1].astype(F32)
    upper, lower = interleave(real, imag), interleave(-imag, real)
    for index in range(GROUPS):
        rows = slice(index * HALF, (index + 1) * HALF)
        start = index * LANES
        mix_out[start : start + HALF, :] = upper[rows].astype(BF16)
        mix_out[start + HALF : start + LANES, :] = lower[rows].astype(BF16)
    proj = proj_ref[...].astype(F32).T
    proj_out[...] = interleave(proj, proj).astype(BF16)


def prepare(gain, mix, proj, after):
    shapes = ((MODES, 2 * C), (2 * C, 2 * C), (C, 2 * C))
    kinds = (F32, BF16, BF16)
    return call(
        prepare_kernel,
        (gain, mix, proj),
        [whole(gain.shape), whole(mix.shape), whole(proj.shape)],
        [whole(shape) for shape in shapes],
        [jax.ShapeDtypeStruct(shape, kind) for shape, kind in zip(shapes, kinds)],
        (1,),
        after,
        name="prepare",
    )


def spectrum_kernel(field_ref, table_ref, out_ref, scratch):
    rows = table_ref.shape[0] // 2
    low = half_lanes((rows, LANES))
    fields = field_ref[...].reshape(LAT_LOCAL * HALF, NLON)
    product = dot_nt(table_ref[...], fields)
    for lat in range(LAT_LOCAL):
        lanes = slice(lat // 2 * LANES, (lat // 2 + 1) * LANES)
        real, imag = product[:rows, lanes], product[rows:, lanes]
        if lat % 2:
            tile = jnp.where(low, pltpu.roll(real, HALF, 1), imag)
        else:
            tile = jnp.where(low, real, pltpu.roll(imag, HALF, 1))
        scratch[pl.ds(lat, rows, stride=LAT_LOCAL), :] = tile
    out_ref[...] = scratch[...].astype(BF16)


def spectrum_rows(field, table, after=()):
    rows = table.shape[0] // 2 * LAT_LOCAL
    return call(
        spectrum_kernel,
        (field, table),
        [pl.BlockSpec((LAT_LOCAL, HALF, NLON), lambda q: (0, q, 0)), whole(table.shape)],
        pl.BlockSpec((rows, LANES), lambda q: (0, q)),
        jax.ShapeDtypeStruct((rows, 2 * C), BF16),
        (GROUPS,),
        after,
        scratch_shapes=[pltpu.VMEM((rows, LANES), F32)],
        name="spectrum_rows",
    )


def order_sums(group, table_ref, tiles):
    totals = [None] * GROUP_ORDERS
    for tile in range(GROUP_TILES):
        left = [table_ref[2 * tile + place, DEVICES * (tile + place) :, :] for place in range(2)]
        product = dot(jnp.concatenate(left, axis=0), tiles[tile])
        middle = left[0].shape[0]
        for order, part in ((tile, product[:middle]), (tile + 1, product[middle:])):
            totals[order] = part if totals[order] is None else totals[order] + part
    return totals


def tile_sum(tile, table_ref, first, second):
    left = jnp.concatenate([table_ref[2 * tile], table_ref[2 * tile + 1]], axis=1)
    return dot(left, jnp.concatenate([first, second], axis=0))


def spectral_kernel(recv_ref, *refs):
    a_refs, st_refs = refs[0:3], refs[3:6]
    gain_ref, mix_ref = refs[6:8]
    scaled_ref, payload_ref, recv, payload = refs[8:12]
    a_buffers, st_buffers, scaled_buffers = refs[12:15], refs[15:18], refs[18:21]
    in_sems, out_sems = refs[21:23]
    schedule = (2, 1, 0)
    arrivals, departures = {}, []
    for group in schedule:
        tiles = pl.ds(GROUP_TILES * group, GROUP_TILES)
        arrivals[group] = [
            pltpu.make_async_copy(recv_ref.at[:, tiles], recv.at[group], in_sems.at[group, 0]),
            pltpu.make_async_copy(a_refs[group], a_buffers[group], in_sems.at[group, 1]),
            pltpu.make_async_copy(st_refs[group], st_buffers[group], in_sems.at[group, 2]),
        ]
        for copy in arrivals[group]:
            copy.start()
    for group in schedule:
        for copy in arrivals[group][:2]:
            copy.wait()
        tiles = [recv[group, :, tile].reshape(SPAN, 2 * C) for tile in range(GROUP_TILES)]
        held = scaled_buffers[group]
        for local, coef in enumerate(order_sums(group, a_buffers[group], tiles)):
            skipped = DEVICES * local
            held[packed_rows(group)[local], :] = (
                gain_ref[LANES * group + skipped :, :] * coef
            ).astype(BF16)
        product = dot(held[...], mix_ref[...]).astype(BF16)
        mixed = []
        for local, rows in enumerate(packed_rows(group)):
            zeros = jnp.zeros((DEVICES * local, 2 * C), BF16)
            mixed.append(
                jnp.concatenate([zeros, product[rows]], axis=0) if local else product[rows]
            )
        arrivals[group][2].wait()
        for tile in range(GROUP_TILES):
            grid = tile_sum(tile, st_buffers[group], mixed[tile], mixed[tile + 1])
            payload[group, :, tile] = grid.astype(BF16).reshape(DEVICES, TILE, 2 * C)
        tiles = pl.ds(GROUP_TILES * group, GROUP_TILES)
        copies = (
            pltpu.make_async_copy(
                payload.at[group], payload_ref.at[:, tiles], out_sems.at[group, 0]
            ),
            pltpu.make_async_copy(
                scaled_buffers[group],
                scaled_ref.at[pl.ds(BASES[group], PACKED[group])],
                out_sems.at[group, 1],
            ),
        )
        for copy in copies:
            copy.start()
            departures.append(copy)
    for copy in departures:
        copy.wait()


def spectral_forward(recv, a, st, gain, mix, after=()):
    slots = (GROUPS, DEVICES, GROUP_TILES, TILE, 2 * C)
    return call(
        spectral_kernel,
        (recv, *a, *st, gain, mix),
        [HELD] * 7 + [whole(gain.shape), whole(mix.shape)],
        [HELD] * 2,
        [
            jax.ShapeDtypeStruct((sum(PACKED), 2 * C), BF16),
            jax.ShapeDtypeStruct(recv.shape, BF16),
        ],
        (1,),
        after,
        scratch_shapes=[pltpu.VMEM(slots, BF16), pltpu.VMEM(slots, BF16)]
        + [pltpu.VMEM(value.shape, BF16) for value in a]
        + [pltpu.VMEM(value.shape, BF16) for value in st]
        + [pltpu.VMEM((rows, 2 * C), BF16) for rows in PACKED]
        + [pltpu.SemaphoreType.DMA((GROUPS, 3)), pltpu.SemaphoreType.DMA((GROUPS, 2))],
        name="spectral_forward",
    )


def normal_cumulative(value, bell):
    denominator = 1.0 + (0.3275911 / math.sqrt(2.0)) * jnp.abs(value)
    inverse = pl.reciprocal(denominator, approx=True)
    inverse = inverse * (2.0 - denominator * inverse)
    series = 0.5 * 1.061405429 * inverse - 0.5 * 1.453152027
    series = series * inverse + 0.5 * 1.421413741
    series = series * inverse - 0.5 * 0.284496736
    series = series * inverse + 0.5 * 0.254829592
    tail = series * inverse * bell
    return jnp.where(value < 0.0, tail, 1.0 - tail)


def grid_kernel(
    recv_ref, up_ref, turned_ref, proj_ref, held_ref, turned_table_ref,
    out_ref, grad_ref, scratch, out_scratch, act_scratch, pre_scratch, table_ref, sem,
):
    step = pl.program_id(1)
    opening = jnp.logical_and(pl.program_id(0) == 0, step == 0)

    @pl.when(opening)
    def _():
        pltpu.make_async_copy(held_ref, table_ref, sem).start()

    low = half_lanes((MODES, LANES))
    block = 256

    @pl.when(step == 0)
    def _():
        scratch[...] = recv_ref[...].astype(F32)
        grad_ref[...] = jnp.zeros_like(grad_ref)

    columns = []
    for pair in range(2):
        first = scratch[pl.ds(step * 4 + 2 * pair, MODES, stride=LAT_LOCAL), :]
        second = scratch[pl.ds(step * 4 + 2 * pair + 1, MODES, stride=LAT_LOCAL), :]
        real = jnp.where(low, first, pltpu.roll(second, HALF, 1))
        imag = jnp.where(low, pltpu.roll(first, HALF, 1), second)
        columns.append(jnp.concatenate([real, imag], axis=0).astype(BF16))
    modes = jnp.concatenate(columns, axis=1)
    low_block = half_lanes((block, LANES))
    for part in range(NLON // block):
        rows = slice(part * block, (part + 1) * block)
        pre = dot(turned_table_ref[rows, :], modes)
        grad_act = jnp.concatenate(
            [
                jnp.where(
                    low_block,
                    dot(turned_ref[2 * pair, rows, :], proj_ref[...]),
                    dot(turned_ref[2 * pair + 1, rows, :], proj_ref[...]),
                )
                for pair in range(2)
            ],
            axis=1,
        )
        bell = jnp.exp(-0.5 * pre * pre)
        cumulative = normal_cumulative(pre, bell)
        slope = cumulative + pre * bell * (1.0 / math.sqrt(2.0 * math.pi))
        act_scratch[rows, :] = (pre * cumulative).astype(BF16)
        pre_scratch[rows, :] = (grad_act * slope).astype(BF16)
    low_grad = half_lanes((C, LANES))
    for pair in range(2):
        act = act_scratch[:, pair * LANES : (pair + 1) * LANES]
        ups = up_ref[2 * pair : 2 * pair + 2].reshape(2 * C, NLON)
        grads = dot(ups, act)
        grad_ref[...] += jnp.where(low_grad, grads[:C], grads[C:])

    @pl.when(opening)
    def _():
        pltpu.make_async_copy(held_ref, table_ref, sem).wait()

    grad_modes = dot(table_ref[...], pre_scratch[...])
    for pair in range(2):
        lanes = slice(pair * LANES, (pair + 1) * LANES)
        real, imag = grad_modes[:MODES, lanes], grad_modes[MODES:, lanes]
        out_scratch[pl.ds(step * 4 + 2 * pair, MODES, stride=LAT_LOCAL), :] = jnp.where(
            low, real, pltpu.roll(imag, HALF, 1)
        )
        out_scratch[pl.ds(step * 4 + 2 * pair + 1, MODES, stride=LAT_LOCAL), :] = jnp.where(
            low, pltpu.roll(real, HALF, 1), imag
        )

    @pl.when(step == LAT_LOCAL // 4 - 1)
    def _():
        out_ref[...] = out_scratch[...].astype(BF16)


def grid_stage(first, blocks, recv, up, turned, proj, table, turned_table, after=()):
    rows = MODES * LAT_LOCAL
    lanes_spec = pl.BlockSpec((rows, LANES), lambda q, b: (0, q))
    grad_spec = pl.BlockSpec((C, LANES), lambda q, b: (0, q))
    return call(
        grid_kernel,
        (recv, up, turned, proj, table, turned_table),
        [
            pl.BlockSpec((rows, LANES), lambda q, b: (0, q + first)),
            pl.BlockSpec((4, C, NLON), lambda q, b: (b, 0, 0)),
            pl.BlockSpec((4, NLON, C), lambda q, b: (b, 0, 0)),
            pl.BlockSpec((C, LANES), lambda q, b: (0, q + first)),
            HELD,
            whole(turned_table.shape),
        ],
        [lanes_spec, grad_spec],
        [
            jax.ShapeDtypeStruct((rows, LANES * blocks), BF16),
            jax.ShapeDtypeStruct((C, LANES * blocks), F32),
        ],
        (blocks, LAT_LOCAL // 4),
        after,
        scratch_shapes=[
            pltpu.VMEM((rows, LANES), F32),
            pltpu.VMEM((rows, LANES), F32),
            pltpu.VMEM((NLON, 2 * LANES), BF16),
            pltpu.VMEM((NLON, 2 * LANES), BF16),
            pltpu.VMEM(table.shape, BF16),
            pltpu.SemaphoreType.DMA,
        ],
        name=f"grid_stage_{blocks}",
    )


def backward_kernel(groups, *refs):
    recv_ref, table_refs, out_ref = refs[0], refs[1 : 1 + len(groups)], refs[1 + len(groups)]
    buffers, sems = refs[-1 - len(groups) : -1], refs[-1]
    copies = [
        pltpu.make_async_copy(table_refs[place], buffers[place], sems.at[place])
        for place in range(len(groups))
    ]
    for copy in copies:
        copy.start()
    lanes = recv_ref.shape[-1]
    first = 0
    for place, group in enumerate(groups):
        start = GROUP_TILES * group if recv_ref.shape[1] == TILES else 0
        tiles = [
            recv_ref[:, start + tile].reshape(SPAN, lanes) for tile in range(GROUP_TILES)
        ]
        copies[place].wait()
        sums = order_sums(group, buffers[place], tiles)
        for total, rows in zip(sums, packed_rows(group)):
            out_ref[first + rows.start : first + rows.stop, :] = total.astype(BF16)
        first += PACKED[group]


def spectral_backward(groups, recv, tables, after=(), last=False):
    lanes = recv.shape[-1]
    tiles = GROUP_TILES if len(groups) == 1 else TILES
    block = groups[0] if len(groups) == 1 else 0
    out = (sum(PACKED[group] for group in groups), lanes)
    return call(
        functools.partial(backward_kernel, groups),
        (recv, *tables),
        [
            pl.BlockSpec(
                (DEVICES, tiles, TILE, lanes),
                lambda b: (0, block, 0, 0),
                pipeline_mode=pl.Buffered(1),
            )
        ]
        + [HELD] * len(groups),
        [whole(out)] + [HELD] * len(groups) * last,
        [jax.ShapeDtypeStruct(out, BF16)]
        + [pltpu.HBM(table.shape, BF16) for table in tables] * last,
        (1,),
        after,
        aliases={1 + place: 1 + place for place in range(len(groups))} if last else {},
        scratch_shapes=[pltpu.VMEM(table.shape, BF16) for table in tables]
        + [pltpu.SemaphoreType.DMA((len(groups),))],
        vmem=20,
        name="spectral_backward_" + "_".join(str(group) for group in groups),
    )[0]


def hold_kernel(value_ref, out_ref):
    pass


def hold(value, after):
    held = pl.BlockSpec(memory_space=pl.ANY)
    return call(
        hold_kernel,
        (value,),
        [held],
        held,
        jax.ShapeDtypeStruct(value.shape, value.dtype),
        (1,),
        after,
        aliases={0: 0},
        vmem=1,
        name="hold",
    )


def synthesis_kernel(groups, small_ref, large_ref, gain_ref, mix_ref, *refs):
    count = len(groups)
    table_refs, refs = refs[:count], refs[-3 * count - 2 :]
    out_ref, coeff_refs, at_refs = refs[0], refs[1 : 1 + count], refs[1 + count : 1 + 2 * count]
    part_refs, sems = refs[1 + 2 * count : -1], refs[-1]
    copies = []
    for place, group in enumerate(groups):
        rows = pl.ds(BASES[group], PACKED[group])
        copies.append(
            (
                pltpu.make_async_copy(small_ref.at[rows], part_refs[place], sems.at[0, place]),
                pltpu.make_async_copy(table_refs[place], at_refs[place], sems.at[1, place]),
            )
        )
    for pair in copies:
        for copy in pair:
            copy.start()
    start = 0
    for place, group in enumerate(groups):
        coeff_ref, at_ref = coeff_refs[place], at_refs[place]
        degrees = degrees_of(group)
        copies[place][0].wait()
        large = large_ref[start : start + PACKED[group], :]
        start += PACKED[group]
        mixed = jnp.concatenate([part_refs[place][...], large], axis=1)
        product = dot_nt(mixed, mix_ref[...])
        for local, rows in enumerate(packed_rows(group)):
            first = local * degrees
            skipped = DEVICES * local
            if skipped:
                coeff_ref[first : first + skipped, :] = jnp.zeros((skipped, 2 * C), BF16)
            coeff_ref[first + skipped : first + degrees, :] = (
                gain_ref[LANES * group + skipped :, :] * product[rows]
            ).astype(BF16)
        copies[place][1].wait()
        for tile in range(GROUP_TILES):
            first = coeff_ref[tile * degrees : (tile + 1) * degrees, :]
            second = coeff_ref[(tile + 1) * degrees : (tile + 2) * degrees, :]
            out = tile_sum(tile, at_ref, first, second).astype(BF16)
            out_ref[:, GROUP_TILES * place + tile] = out.reshape(DEVICES, TILE, 2 * C)


def analysis_back(groups, tables, small, large, gain, mix, tiles, payload=(), after=()):
    inputs = (small, large, gain, mix, *tables, *payload)
    count = len(groups)
    return call(
        functools.partial(synthesis_kernel, groups),
        inputs,
        [HELD] + [whole(value.shape) for value in inputs[1:4]] + [HELD] * len(inputs[4:]),
        whole((DEVICES, GROUP_TILES * count, TILE, 2 * C)),
        pltpu.HBM((DEVICES, tiles, TILE, 2 * C), BF16),
        (1,),
        after,
        aliases={4 + count: 0} if payload else {},
        scratch_shapes=[
            pltpu.VMEM((GROUP_ORDERS * degrees_of(group), 2 * C), BF16) for group in groups
        ]
        + [pltpu.VMEM(table.shape, BF16) for table in tables]
        + [pltpu.VMEM((PACKED[group], LANES), BF16) for group in groups]
        + [pltpu.SemaphoreType.DMA((2, count))],
        vmem=24,
        name="analysis_back_" + "_".join(str(group) for group in groups),
    )


def fold(tile):
    return tile + pltpu.roll(tile, HALF, 1)


def weight_kernel(held_ref, small_ref, *refs):
    first_ref, rest_ref, mix_ref, factor_ref, proj_small, proj_large = refs[:6]
    out_ref, gain, packed, spaced, scaled_ref, sem = refs[6:]
    large = (first_ref[...], rest_ref[: PACKED[1], :], rest_ref[PACKED[1] :, :])
    copy = pltpu.make_async_copy(held_ref, scaled_ref, sem)
    copy.start()
    copy.wait()
    block = None
    for group in range(GROUPS):
        rows = slice(BASES[group], BASES[group] + PACKED[group])
        mixed = jnp.concatenate([small_ref[rows, :], large[group]], axis=1)
        part = lax.dot_general(
            scaled_ref[rows, :], mixed, (((0,), (0,)), ((), ())), preferred_element_type=F32
        )
        block = part if block is None else block + part
        product = dot_nt(mixed, mix_ref[...]) * scaled_ref[rows, :].astype(F32)
        for local, rows in enumerate(packed_rows(group)):
            part = product[rows]
            first = LANES * group + DEVICES * local
            if first:
                gain[first:, :] += part
            else:
                gain[...] = part
    gain[...] = gain[...] / factor_ref[...]
    low = half_lanes((HALF, LANES))
    low_gain = half_lanes((C, LANES))
    low_proj = half_lanes((C // 2, LANES))
    for index in range(GROUPS):
        lanes = slice(index * LANES, (index + 1) * LANES)
        for row_block in range(GROUPS):
            start = row_block * LANES
            first = block[start : start + HALF, lanes]
            second = pltpu.roll(block[start + HALF : start + LANES, lanes], HALF, 1)
            packed[index, row_block * HALF : (row_block + 1) * HALF, :] = jnp.where(
                low, first + second, first - second
            )
        packed[index, C : 2 * C, :] = jnp.where(
            low_gain, fold(gain[:C, lanes]), fold(gain[C:, lanes])
        )
        if index == 0:
            proj = fold(proj_small[...])
        else:
            proj = fold(proj_large[:, (index - 1) * LANES : index * LANES])
        packed[index, 2 * C :, :] = jnp.where(low_proj, proj[: C // 2], proj[C // 2 :])
        for row in range(TILE - 1):
            spaced[index, pl.ds(row, DEVICES, stride=TILE), :] = packed[
                index, row * DEVICES : (row + 1) * DEVICES, :
            ]
        spaced[index, pl.ds(TILE - 1, DEVICES, stride=TILE), :] = jnp.zeros((DEVICES, LANES), F32)
        out_ref[:, 0, :, lanes] = spaced[index].astype(BF16).reshape(DEVICES, TILE, LANES)


def weight_grads(scaled, small, large, mix, gain, proj_small, proj_large, after=()):
    tiles = 2 * GROUP_TILES
    inputs = (scaled, small, *large, mix, gain, proj_small, proj_large)
    return call(
        weight_kernel,
        inputs,
        [HELD] + [whole(value.shape) for value in inputs[1:]],
        pl.BlockSpec((DEVICES, 1, TILE, 2 * C), lambda b: (0, tiles, 0, 0)),
        pltpu.HBM((DEVICES, tiles + 1, TILE, 2 * C), BF16),
        (1,),
        after,
        scratch_shapes=[
            pltpu.VMEM((MODES, 2 * C), F32),
            pltpu.VMEM((GROUPS, 15 * DEVICES, LANES), F32),
            pltpu.VMEM((GROUPS, TILE * DEVICES, LANES), F32),
            pltpu.VMEM(scaled.shape, BF16),
            pltpu.SemaphoreType.DMA,
        ],
        vmem=24,
        name="weight_grads",
    )


def total_kernel(recv_ref, payload_ref, out_ref, token_ref):
    token_ref[...] = jnp.zeros((8, LANES), F32)
    total = jnp.sum(recv_ref[:, 0].astype(F32), axis=0)
    out_ref[:, 0] = jnp.broadcast_to(total.astype(BF16)[None], (DEVICES, TILE, 2 * C))


def attach_totals(recv, payload):
    def last(value):
        tile = value.shape[1] - 1
        return pl.BlockSpec((DEVICES, 1, TILE, 2 * C), lambda b: (0, tile, 0, 0))

    return call(
        total_kernel,
        (recv, payload),
        [last(recv), pl.BlockSpec(memory_space=pl.ANY)],
        [last(payload), whole((8, LANES))],
        [pltpu.HBM(payload.shape, BF16), jax.ShapeDtypeStruct((8, LANES), F32)],
        (1,),
        aliases={1: 0},
        vmem=8,
        name="attach_totals",
    )


def unpack_totals(recv_ref, proj_ref, mix_ref, gain_ref, spaced, packed):
    grid_scale = 1.0 / math.sqrt(NLAT * NLON)
    mode_scale = 1.0 / math.sqrt(MODES)
    lows, highs = [], []
    for index in range(GROUPS):
        lanes = slice(index * LANES, (index + 1) * LANES)
        spaced[index] = recv_ref[:, GROUP_TILES, :, lanes].reshape(DEVICES * TILE, LANES).astype(F32)
        for row in range(TILE - 1):
            packed[index, row * DEVICES : (row + 1) * DEVICES, :] = spaced[
                index, pl.ds(row, DEVICES, stride=TILE), :
            ]
        lows.append(packed[index, :, :HALF])
        highs.append(packed[index, :, HALF:])
    low = jnp.concatenate(lows, axis=1)
    high = jnp.concatenate(highs, axis=1)
    mix_ref[0] = grid_scale * low[:C]
    mix_ref[1] = grid_scale * high[:C]
    gain = jnp.concatenate([low[C : 2 * C], high[C : 2 * C]], axis=0)
    gain_ref[...] = mode_scale * gain.T
    proj = jnp.concatenate([low[2 * C :], high[2 * C :]], axis=0)
    proj_ref[...] = grid_scale * proj.T


def field_kernel(recv_ref, table_ref, base_ref, out_ref, *refs):
    totals, (scratch, *unpacking) = refs[:3] if len(refs) > 1 else (), refs[3:] or refs
    step = pl.program_id(0)
    orders = DEVICES * GROUP_ORDERS
    rows = orders * LAT_LOCAL

    @pl.when(step == 0)
    def _():
        for index in range(GROUPS):
            lanes = slice(index * LANES, (index + 1) * LANES)
            values = recv_ref[:, :GROUP_TILES, :, lanes].astype(F32)
            scratch[index] = values.reshape(rows, LANES)
        if totals:
            unpack_totals(recv_ref, *totals, *unpacking)

    lefts = []
    for inner in range(4):
        real, imag = [], []
        for index in range(GROUPS):
            values = scratch[index, pl.ds(step * 4 + inner, orders, stride=LAT_LOCAL), :]
            turned = values.T.astype(BF16)
            real.append(turned[:HALF])
            imag.append(turned[HALF:])
        lefts.append(
            jnp.concatenate(
                [jnp.concatenate(real, axis=0), jnp.concatenate(imag, axis=0)], axis=1
            )
        )
    product = dot(jnp.concatenate(lefts, axis=0), table_ref[...])
    for inner in range(4):
        total = base_ref[inner].astype(F32) + product[inner * C : (inner + 1) * C]
        out_ref[inner] = total.astype(out_ref.dtype)


def field_stage(recv, at, table, base, unpacked=False, after=()):
    rows = DEVICES * GROUP_ORDERS * LAT_LOCAL
    block = pl.BlockSpec((4, C, NLON), lambda b: (b, 0, 0))
    tiles = GROUP_TILES + int(unpacked)
    totals = ((C, C), (2, C, C), (C, MODES)) if unpacked else ()
    scratch_shapes = [pltpu.VMEM((GROUPS, rows, LANES), F32)]
    if unpacked:
        scratch_shapes += [
            pltpu.VMEM((GROUPS, TILE * DEVICES, LANES), F32),
            pltpu.VMEM((GROUPS, 15 * DEVICES, LANES), F32),
        ]
    return call(
        field_kernel,
        (recv, table, base),
        [
            pl.BlockSpec(
                (DEVICES, tiles, TILE, 2 * C),
                lambda b: (0, at, 0, 0),
                pipeline_mode=pl.Buffered(1),
            ),
            whole(table.shape),
            block,
        ],
        [block] + [whole(shape) for shape in totals],
        [pltpu.HBM((LAT_LOCAL, C, NLON), BF16)]
        + [jax.ShapeDtypeStruct(shape, F32) for shape in totals],
        (LAT_LOCAL // 4,),
        after,
        scratch_shapes=scratch_shapes,
        vmem=56 if unpacked else 20,
        name="field_stage",
    )


def exchange(payload):
    tiles, lanes = payload.shape[1], payload.shape[3]
    flat = payload.reshape(DEVICES, tiles * TILE, lanes)
    moved = lax.all_to_all(flat, "lat", split_axis=0, concat_axis=0, tiled=True)
    return moved.reshape(DEVICES, tiles, TILE, lanes)


def shards(saved_input, incoming, spectral_gain, mix_weight, proj_weight):
    device = lax.axis_index("lat")
    section_count = lax.axis_size("section")
    shift = [(source, (source - 1) % section_count) for source in range(section_count)]

    forward_all = forward_rows(0, GROUPS)
    forward = [forward_rows(group, 1) for group in range(GROUPS)]
    inverse_np = inverse_rows()
    inverse = jnp.asarray(inverse_np)
    inverse_turned = jnp.asarray(np.ascontiguousarray(inverse_np.T))
    spread, spread_turned = spread_tables()
    lat = jnp.asarray(latitude_rows())
    starts, numbers = log_starts()
    start = lax.dynamic_index_in_dim(jnp.asarray(starts), device, 0, keepdims=False)
    order = lax.dynamic_index_in_dim(jnp.asarray(numbers), device, 0, keepdims=False)

    field = saved_input[0]
    upstream = incoming[0]
    upstream_next = lax.ppermute(upstream, "section", shift)
    turned = jnp.swapaxes(upstream, 1, 2)
    rows = MODES * LAT_LOCAL
    spectrum = spectrum_rows(field, forward_all)
    recv = exchange(spectrum.reshape(DEVICES, TILES, TILE, 2 * C))
    gain, mix, proj = prepare(
        jnp.swapaxes(spectral_gain[0], 0, 1), mix_weight[0], proj_weight[0], (spectrum,)
    )
    gain_next, mix_next, _ = prepare(
        lax.ppermute(jnp.swapaxes(spectral_gain[0], 0, 1), "section", shift),
        lax.ppermute(mix_weight[0], "section", shift),
        proj_weight[0],
        (spectrum,),
    )
    tables = legendre_tables(start, order, lat, spread, spread_turned, (spectrum,))
    behind = [tables[4 * group + 2 : 4 * group + 4] for group in range(GROUPS)]
    scaled, payload = spectral_forward(
        recv, tables[0::4], tables[1::4], gain, mix, (turned, proj)
    )
    recv = exchange(payload).reshape(rows, 2 * C)
    small_rows, proj_small = grid_stage(
        0,
        1,
        recv,
        upstream,
        turned,
        proj,
        inverse,
        inverse_turned,
        (upstream_next, gain_next, mix_next),
    )
    small = exchange(small_rows.reshape(DEVICES, TILES, TILE, LANES))
    large, proj_large = grid_stage(
        1, 2, recv, upstream, turned, proj, inverse, inverse_turned, (small_rows,)
    )
    large = exchange(large.reshape(DEVICES, TILES, TILE, 2 * LANES))

    mixeds, moved = [None] * GROUPS, [None] * GROUPS
    every = tuple(range(GROUPS))
    mixed_small = spectral_backward(every, small, [table[0] for table in behind])
    moved_small = lax.ppermute(mixed_small, "section", shift)
    mixed_rest = spectral_backward((1, 2), large, [behind[1][0], behind[2][0]], (moved_small,), True)
    moved_rest = lax.ppermute(mixed_rest, "section", shift)
    mixed_0 = spectral_backward((0,), large, [behind[0][0]], (mixed_rest,))
    out_rest = weight_grads(
        scaled, mixed_small, (mixed_0, mixed_rest), mix, gain, proj_small, proj_large
    )
    out_rest = analysis_back(
        (1, 2),
        [behind[1][1], behind[2][1]],
        moved_small,
        moved_rest,
        gain_next,
        mix_next,
        2 * GROUP_TILES + 1,
        (out_rest,),
    )
    moved_0 = lax.ppermute(hold(mixed_0, (moved_rest,)), "section", shift)
    recv_rest = exchange(out_rest)
    out_0 = analysis_back(
        (0,), [behind[0][1]], moved_small, moved_0, gain_next, mix_next, GROUP_TILES + 1
    )
    out_0, token = attach_totals(recv_rest, out_0)
    recv_0 = exchange(out_0)
    (base,) = field_stage(recv_rest, 0, forward[1], upstream_next, after=(token,))
    (base,) = field_stage(recv_rest, 1, forward[2], base)
    received, grad_w2, grad_mix, grad_gain = field_stage(recv_0, 0, forward[0], base, True)
    return (
        received[None],
        grad_w2[None],
        grad_mix[None],
        jnp.swapaxes(grad_gain, 0, 1)[None],
    )


def solution(mesh):
    in_specs = (
        P("section", "lat", None, None),
        P("section", "lat", None, None),
        P("section", None, None),
        P("section", None, None, None),
        P("section", None, None),
    )
    out_specs = (
        P("section", "lat", None, None),
        P("section", None, None),
        P("section", None, None, None),
        P("section", None, None),
    )
    return jax.shard_map(shards, mesh=mesh, in_specs=in_specs, out_specs=out_specs, check_vma=False)
```
